32 devices in a mesh: pipe: 2 (over x), dp: 16 (over z, y, core).
Axes of the slice: x: 2, y: 2, z: 4, core: 2. Of those that a mesh axis runs over, the one named last changes fastest.
Arguments:
- samples: bfloat16 [80, 3, 32, 640], P('dp'), may hold values from -6 to 6
- timesteps: int32 [80], P('dp'), may hold values from 0 to 999
- cotangent: bfloat16 [80, 3, 32, 640], P('dp'), may hold values from -0.059814453 to 0.059814453
- spatial_weight: bfloat16 [2, 5760, 640], P('pipe', 'dp'), may hold values from -0.078125 to 0.078125
- temporal_weight: bfloat16 [2, 1920, 640], P('pipe', 'dp'), may hold values from -0.125 to 0.125
Outputs:
- spatial_grad: float32 [2, 5760, 640], P('pipe', 'dp')
- temporal_grad: float32 [2, 1920, 640], P('pipe', 'dp')
The draws below stay inside these ranges and needn't reach their ends.
All inputs are finite; a program needn't handle non-finite values.
Results may differ from the reference program's by a relative error of at most 0.034.
Values may be sent and summed in bfloat16 or wider, within the bound.
No kernel may reach another device: no remote copies, remote signals or barrier semaphores. Data moves between devices by JAX's collectives and lax.ppermute only.
A program may use at most 128 MiB of HBM per device.

```python
import math
import jax
import jax.numpy as jnp
from jax import lax

C = 640
FRAMES = 3
HEIGHT = 8
WIDTH = 4
MICRO = 5
STEPS = 1000
PIXELS = 32
SAMPLES = 80
N_PIPE = 2
N_DP = 16


def touch_ends(entries, stream_key, least, largest):
    extent = entries.shape
    place = [jax.random.randint(jax.random.fold_in(stream_key, axis), (), 0, extent[axis]) for axis in range(len(extent))]
    entries = entries.at[tuple(place)].set(least)
    longest = extent.index(max(extent))
    place[longest] = (place[longest] + 1) % extent[longest]
    return entries.at[tuple(place)].set(largest)


def steps_of(own_key, dims, cuts, low, top_value):
    loudness, own = 1.0, jax.random.fold_in(own_key, 6)
    for position, blocks in cuts:
        draws = jnp.exp(jax.random.uniform(jax.random.fold_in(own, position), (blocks,), jnp.float32, low / len(cuts), top_value / len(cuts)))
        loudness = loudness * jnp.repeat(draws, dims[position] // blocks).reshape([-1 if axis == position else 1 for axis in range(len(dims))])
    return loudness


def bell_draw(key, extent, deviation, limit, cuts=(), held_as=jnp.bfloat16):
    factor_of = steps_of(key, extent, cuts, -0.22, 0.18) if cuts else 1.0
    result = jax.random.normal(key, extent, jnp.float32) * deviation * factor_of
    return jnp.minimum(jnp.maximum(result, -limit), limit).astype(held_as)


def setup_inputs(seed: int = 0) -> dict:
    key_of = jax.random.split(jax.random.key(seed), 6)
    return {
        "samples": bell_draw(key_of[0], (SAMPLES, FRAMES, PIXELS, C), 1.0, 6.0, ((0, 16),)),
        "timesteps": touch_ends(jax.random.randint(key_of[1], (SAMPLES,), 0, STEPS), jax.random.fold_in(key_of[1], 1), 0, STEPS - 1).astype(jnp.int32),
        "cotangent": bell_draw(key_of[2], (SAMPLES, FRAMES, PIXELS, C), 0.01, 0.059814453, ((0, 16),)),
        "spatial_weight": bell_draw(key_of[3], (N_PIPE, 9 * C, C), (9 * C) ** -0.5, 0.078125, ((0, 2), (1, 16))),
        "temporal_weight": bell_draw(key_of[4], (N_PIPE, 3 * C, C), (3 * C) ** -0.5, 0.125, ((0, 2), (1, 16))),
    }


def embedding_of(step, channels):
    half_width = channels // 2
    frequency = jnp.exp(-math.log(10000.0) * jnp.arange(half_width, dtype=jnp.float32) / half_width)
    phases = step.astype(jnp.float32) * frequency
    return jnp.concatenate([jnp.sin(phases), jnp.cos(phases)])

def normalize(summed):
    return summed * lax.rsqrt(lax.optimization_barrier(jnp.mean(summed * summed, axis=-1, keepdims=True)) + 1e-06)

def spatial_columns(normed):
    frames, pixels, channels = normed.shape
    grid = normed.reshape(frames, HEIGHT, WIDTH, channels)
    padded = jnp.pad(grid, ((0, 0), (1, 1), (1, 1), (0, 0)))
    pieces = [padded[:, row:row + HEIGHT, col:col + WIDTH, :] for row in range(3) for col in range(3)]
    return jnp.concatenate(pieces, axis=-1).reshape(frames * pixels, 9 * channels)

def spatial_fold(grads, frames, channels):
    parts = grads.reshape(frames, HEIGHT, WIDTH, 9, channels)
    padded = jnp.zeros((frames, HEIGHT + 2, WIDTH + 2, channels), jnp.float32)
    for row in range(3):
        for col in range(3):
            padded = padded.at[:, row:row + HEIGHT, col:col + WIDTH, :].add(parts[:, :, :, row * 3 + col, :])
    return padded[:, 1:HEIGHT + 1, 1:WIDTH + 1, :].reshape(frames, HEIGHT * WIDTH, channels)

def temporal_columns(activated):
    frames, pixels, channels = activated.shape
    padded = jnp.pad(activated, ((1, 1), (0, 0), (0, 0)))
    pieces = [padded[tap:tap + frames] for tap in range(3)]
    return jnp.concatenate(pieces, axis=-1).reshape(frames * pixels, 3 * channels)

def temporal_fold(grads, frames, pixels, channels):
    parts = grads.reshape(frames, pixels, 3, channels)
    padded = jnp.zeros((frames + 2, pixels, channels), jnp.float32)
    for tap in range(3):
        padded = padded.at[tap:tap + frames].add(parts[:, :, tap, :])
    return padded[1:frames + 1]

def section_forward(block_in, embedding, spatial, temporal):
    frames, pixels, channels = block_in.shape
    summed = block_in.astype(jnp.float32) + embedding
    normed = normalize(summed).astype(jnp.bfloat16)
    preact = jnp.dot(spatial_columns(normed), spatial, preferred_element_type=jnp.float32)
    activated = jax.nn.silu(preact).astype(jnp.bfloat16).reshape(frames, pixels, channels)
    mixed = jnp.dot(temporal_columns(activated), temporal, preferred_element_type=jnp.float32)
    return (block_in.astype(jnp.float32) + mixed.reshape(frames, pixels, channels)).astype(jnp.bfloat16)

def section_backward(block_in, embedding, spatial, temporal, upstream):
    frames, pixels, channels = block_in.shape
    summed = block_in.astype(jnp.float32) + embedding
    normed = normalize(summed).astype(jnp.bfloat16)
    columns = spatial_columns(normed)
    preact = jnp.dot(columns, spatial, preferred_element_type=jnp.float32)
    activated = jax.nn.silu(preact).astype(jnp.bfloat16).reshape(frames, pixels, channels)
    tcolumns = temporal_columns(activated)
    upstream_flat = upstream.reshape(frames * pixels, channels)
    temporal_term = jnp.dot(tcolumns.T, upstream_flat, preferred_element_type=jnp.float32)
    act_grad = temporal_fold(jnp.dot(upstream_flat, temporal.T, preferred_element_type=jnp.float32), frames, pixels, channels)
    logistic = jax.nn.sigmoid(preact)
    slope = logistic * (1.0 + preact * (1.0 - logistic))
    pre_grad = (act_grad.reshape(frames * pixels, channels) * slope).astype(jnp.bfloat16)
    spatial_term = jnp.dot(columns.T, pre_grad, preferred_element_type=jnp.float32)
    norm_grad = spatial_fold(jnp.dot(pre_grad, spatial.T, preferred_element_type=jnp.float32), frames, channels)
    _, pullback = jax.vjp(normalize, summed)
    back_input = (upstream.astype(jnp.float32) + pullback(norm_grad)[0]).astype(jnp.bfloat16)
    return (back_input, spatial_term, temporal_term)

def one_sample(sample, step, upstream, spatial_weight, temporal_weight):
    embedding = embedding_of(step, sample.shape[-1])

    def forward(hidden, weights):
        return (section_forward(hidden, embedding, weights[0], weights[1]), hidden)
    _, inputs = lax.scan(forward, sample, (spatial_weight, temporal_weight))

    def backward(carried, pieces):
        back_input, spatial_term, temporal_term = section_backward(pieces[0], embedding, pieces[1], pieces[2], carried)
        return (back_input, (spatial_term, temporal_term))
    _, terms = lax.scan(backward, upstream, (inputs, spatial_weight, temporal_weight), reverse=True)
    return terms

def reference(samples, timesteps, cotangent, spatial_weight, temporal_weight):
    shard_samples = samples.reshape((N_DP, MICRO) + samples.shape[1:])
    shard_steps = timesteps.reshape(N_DP, MICRO)
    shard_cots = cotangent.reshape((N_DP, MICRO) + cotangent.shape[1:])
    zero_sp = jnp.zeros(spatial_weight.shape, jnp.float32)
    zero_tm = jnp.zeros(temporal_weight.shape, jnp.float32)

    def per_shard(totals, shard):

        def per_sample(partial_value, item):
            spatial_term, temporal_term = one_sample(item[0], item[1], item[2], spatial_weight, temporal_weight)
            return ((partial_value[0] + spatial_term, partial_value[1] + temporal_term), None)
        partial_value, _ = lax.scan(per_sample, (zero_sp, zero_tm), shard)
        rounded = lax.optimization_barrier((partial_value[0].astype(jnp.bfloat16), partial_value[1].astype(jnp.bfloat16)))
        return ((totals[0] + rounded[0].astype(jnp.float32), totals[1] + rounded[1].astype(jnp.float32)), None)
    totals, _ = lax.scan(per_shard, (zero_sp, zero_tm), (shard_samples, shard_steps, shard_cots))
    return (totals[0], totals[1])
```

```python
import functools
import math

import jax
import jax.numpy as jnp
from jax import lax
from jax.experimental import pallas as pl
from jax.experimental.pallas import tpu as pltpu
from jax.sharding import PartitionSpec as P

HEIGHT = 8
WIDTH = 4
F32 = jnp.float32
BF16 = jnp.bfloat16
GRID = (4, 2, 2)
LANES = 128


def passed_along(value, axis, steps):
    count = lax.axis_size(axis)
    first, last = (max(0, -steps), min(count, count - steps))
    return lax.ppermute(value, axis, [(source, source + steps) for source in range(first, last)])


def embedding_of(step, channels):
    half_width = channels // 2
    frequency = jnp.exp(-math.log(10000.0) * jnp.arange(half_width, dtype=jnp.float32) / half_width)
    phases = step.astype(jnp.float32) * frequency
    return jnp.concatenate([jnp.sin(phases), jnp.cos(phases)])


def normalize(summed):
    return summed * lax.rsqrt(jnp.mean(summed * summed, axis=-1, keepdims=True) + 1e-06)


def spatial_columns(normed):
    frames, pixels, channels = normed.shape
    grid = normed.reshape(frames, HEIGHT, WIDTH, channels)
    padded = jnp.pad(grid, ((0, 0), (1, 1), (1, 1), (0, 0)))
    pieces = [
        padded[:, row : row + HEIGHT, col : col + WIDTH, :] for row in range(3) for col in range(3)
    ]
    return jnp.concatenate(pieces, axis=-1).reshape(frames * pixels, 9 * channels)


def spatial_fold(grads, frames, channels):
    parts = grads.reshape(frames, HEIGHT, WIDTH, 9, channels)
    padded = jnp.zeros((frames, HEIGHT + 2, WIDTH + 2, channels), jnp.float32)
    for row in range(3):
        for col in range(3):
            padded = padded.at[:, row : row + HEIGHT, col : col + WIDTH, :].add(
                parts[:, :, :, row * 3 + col, :]
            )
    return padded[:, 1 : HEIGHT + 1, 1 : WIDTH + 1, :].reshape(frames, HEIGHT * WIDTH, channels)


def temporal_columns(activated):
    frames, pixels, channels = activated.shape
    padded = jnp.pad(activated, ((1, 1), (0, 0), (0, 0)))
    pieces = [padded[tap : tap + frames] for tap in range(3)]
    return jnp.concatenate(pieces, axis=-1).reshape(frames * pixels, 3 * channels)


def temporal_fold(grads, frames, pixels, channels):
    parts = grads.reshape(frames, pixels, 3, channels)
    padded = jnp.zeros((frames + 2, pixels, channels), jnp.float32)
    for tap in range(3):
        padded = padded.at[tap : tap + frames].add(parts[:, :, tap, :])
    return padded[1 : frames + 1]


def section_forward(block_in, embedding, spatial, temporal):
    frames, pixels, channels = block_in.shape
    summed = block_in.astype(jnp.float32) + embedding
    normed = normalize(summed).astype(jnp.bfloat16)
    preact = jnp.dot(spatial_columns(normed), spatial, preferred_element_type=jnp.float32)
    activated = jax.nn.silu(preact).astype(jnp.bfloat16).reshape(frames, pixels, channels)
    mixed = jnp.dot(temporal_columns(activated), temporal, preferred_element_type=jnp.float32)
    return (block_in.astype(jnp.float32) + mixed.reshape(frames, pixels, channels)).astype(
        jnp.bfloat16
    )


def backward_first(block_in, embedding, spatial, temporal, upstream):
    frames, pixels, channels = block_in.shape
    summed = block_in.astype(jnp.float32) + embedding
    normed = normalize(summed).astype(jnp.bfloat16)
    columns = spatial_columns(normed)
    preact = jnp.dot(columns, spatial, preferred_element_type=jnp.float32)
    activated = jax.nn.silu(preact).astype(jnp.bfloat16).reshape(frames, pixels, channels)
    tcolumns = temporal_columns(activated)
    upstream_flat = upstream.reshape(frames * pixels, channels)
    temporal_term = jnp.dot(tcolumns.T, upstream_flat, preferred_element_type=jnp.float32)
    act_grad = temporal_fold(
        jnp.dot(upstream_flat, temporal.T, preferred_element_type=jnp.float32),
        frames,
        pixels,
        channels,
    )
    logistic = jax.nn.sigmoid(preact)
    slope = logistic * (1.0 + preact * (1.0 - logistic))
    pre_grad = (act_grad.reshape(frames * pixels, channels) * slope).astype(jnp.bfloat16)
    return (temporal_term, pre_grad, columns)


def backward_second(block_in, embedding, spatial, upstream, pre_grad, columns):
    frames, pixels, channels = block_in.shape
    summed = block_in.astype(jnp.float32) + embedding
    spatial_term = jnp.dot(columns.T, pre_grad, preferred_element_type=jnp.float32)
    norm_grad = spatial_fold(
        jnp.dot(pre_grad, spatial.T, preferred_element_type=jnp.float32), frames, channels
    )
    _, pullback = jax.vjp(normalize, summed)
    back_input = (upstream.astype(jnp.float32) + pullback(norm_grad)[0]).astype(jnp.bfloat16)
    return (back_input, spatial_term)


def section_backward(block_in, embedding, spatial, temporal, upstream):
    temporal_term, pre_grad, columns = backward_first(
        block_in, embedding, spatial, temporal, upstream
    )
    back_input, spatial_term = backward_second(
        block_in, embedding, spatial, upstream, pre_grad, columns
    )
    return (back_input, spatial_term, temporal_term)


def per_device(samples, timesteps, cotangent, spatial_weight, temporal_weight):
    sections = lax.axis_size("pipe")
    section_index = lax.axis_index("pipe")
    micro_count = samples.shape[0]
    frames, pixels, channels = (samples.shape[1], samples.shape[2], samples.shape[3])
    moments = jnp.arange(micro_count + sections - 1, dtype=jnp.int32)
    blank = jnp.zeros((frames, pixels, channels), jnp.bfloat16)
    full_spatial, full_temporal = (
        lax.all_gather(spatial_weight[0], "dp", axis=0, tiled=True),
        lax.all_gather(temporal_weight[0], "dp", axis=0, tiled=True),
    )

    def forward_step(carry, moment):
        incoming, stash = carry
        position = moment - section_index
        active = (position >= 0) & (position < micro_count)
        picked = jnp.clip(position, 0, micro_count - 1)
        own = lax.dynamic_index_in_dim(samples, picked, 0, keepdims=False)
        embedding = embedding_of(
            lax.dynamic_index_in_dim(timesteps, picked, 0, keepdims=False), channels
        )
        block_in = jnp.where(section_index == 0, own, incoming)
        result = lax.cond(
            active & (section_index < sections - 1),
            lambda: section_forward(block_in, embedding, full_spatial, full_temporal),
            lambda: blank,
        )
        stash = jnp.where(
            active, lax.dynamic_update_index_in_dim(stash, block_in, picked, 0), stash
        )
        passed = passed_along(result, "pipe", 1)
        return ((passed, stash), None)

    (_, stash), _ = lax.scan(forward_step, (blank, jnp.zeros_like(samples)), moments)
    back_spatial, back_temporal = (full_spatial, full_temporal)

    def inputs_at(moment, incoming):
        position = moment - (sections - 1 - section_index)
        active = (position >= 0) & (position < micro_count)
        picked = jnp.clip(position, 0, micro_count - 1)
        block_in = lax.dynamic_index_in_dim(stash, picked, 0, keepdims=False)
        embedding = embedding_of(
            lax.dynamic_index_in_dim(timesteps, picked, 0, keepdims=False), channels
        )
        given = lax.dynamic_index_in_dim(cotangent, picked, 0, keepdims=False)
        upstream = jnp.where(section_index == sections - 1, given, incoming)
        return (active, block_in, embedding, upstream)

    def backward_step(carry, moment):
        incoming, grad_spatial, grad_temporal = carry
        active, block_in, embedding, upstream = inputs_at(moment, incoming)

        def working():
            back_input, spatial_term, temporal_term = section_backward(
                block_in, embedding, back_spatial, back_temporal, upstream
            )
            return (back_input, grad_spatial + spatial_term, grad_temporal + temporal_term)

        def waiting():
            return (blank, grad_spatial, grad_temporal)

        back_input, grad_spatial, grad_temporal = lax.cond(active, working, waiting)
        passed = passed_along(back_input, "pipe", -1)
        return ((passed, grad_spatial, grad_temporal), None)

    start = (
        blank,
        jnp.zeros(back_spatial.shape, jnp.float32),
        jnp.zeros(back_temporal.shape, jnp.float32),
    )
    (_, grad_spatial, grad_temporal), _ = lax.scan(backward_step, start, moments)
    share_spatial, share_temporal = (
        lax.psum_scatter(
            grad_spatial.astype(jnp.bfloat16).astype(jnp.float32).astype(jnp.bfloat16),
            "dp",
            scatter_dimension=0,
            tiled=True,
        ).astype(jnp.float32),
        lax.psum_scatter(
            grad_temporal.astype(jnp.bfloat16).astype(jnp.float32).astype(jnp.bfloat16),
            "dp",
            scatter_dimension=0,
            tiled=True,
        ).astype(jnp.float32),
    )
    return (share_spatial[None], share_temporal[None])


def coordinates():
    index = lax.axis_index("dp")
    return index // (GRID[1] * GRID[2]), (index // GRID[2]) % GRID[1], index % GRID[2]


def shifted(value, dz=0, dy=0, dc=0):
    pairs = []
    for z in range(GRID[0]):
        for y in range(GRID[1]):
            for c in range(GRID[2]):
                place = ((z + dz) % GRID[0], (y + dy) % GRID[1], (c + dc) % GRID[2])
                pairs.append(
                    (
                        (z * GRID[1] + y) * GRID[2] + c,
                        (place[0] * GRID[1] + place[1]) * GRID[2] + place[2],
                    )
                )
    return lax.ppermute(value, "dp", pairs)


def swapped(value):
    return lax.ppermute(value, "pipe", [(0, 1), (1, 0)])


def part_of(value, index, axis):
    return lax.dynamic_index_in_dim(value, index, axis, keepdims=False)


def vmem_call(body, outs, scratch=(), flops=0, moved=0):
    return pl.pallas_call(
        body,
        out_shape=outs,
        scratch_shapes=list(scratch),
        compiler_params=pltpu.CompilerParams(vmem_limit_bytes=40 * 2**20),
        cost_estimate=pl.CostEstimate(flops=flops, bytes_accessed=moved, transcendentals=0),
    )


def place_blocks(place_ref, blocks_ref, out_ref):
    rows = blocks_ref.shape[1]
    for block in range(blocks_ref.shape[0]):
        start = pl.multiple_of(place_ref[block] * rows, 16)
        out_ref[pl.ds(start, rows), :] = blocks_ref[block]


def gathered(value):
    rows, lanes = value.shape
    z, y, c = coordinates()
    line = jnp.stack([value] + [shifted(value, dz=step) for step in range(1, GRID[0])])
    plane = jnp.stack([line, shifted(line, dy=1)])
    other = shifted(plane, dc=1)
    pair = jnp.where(c == 0, jnp.stack([plane, other], 2), jnp.stack([other, plane], 2))
    blocks = pair.reshape(GRID[0] * GRID[1], GRID[2] * rows, lanes)
    places = jnp.stack(
        [
            ((z - step) % GRID[0]) * GRID[1] + (y + dy) % GRID[1]
            for dy in range(GRID[1])
            for step in range(GRID[0])
        ]
    ).astype(jnp.int32)
    total = GRID[0] * GRID[1] * GRID[2] * rows
    return pl.pallas_call(
        place_blocks,
        out_shape=jax.ShapeDtypeStruct((total, lanes), value.dtype),
        in_specs=[
            pl.BlockSpec(memory_space=pltpu.SMEM),
            pl.BlockSpec(memory_space=pltpu.VMEM),
        ],
        compiler_params=pltpu.CompilerParams(vmem_limit_bytes=40 * 2**20),
        cost_estimate=pl.CostEstimate(
            flops=0, bytes_accessed=4 * total * lanes, transcendentals=0
        ),
    )(places, blocks)


def added(*terms):
    return sum(term.astype(F32) for term in terms)


def summed_on_chip(value):
    _, _, c = coordinates()
    sent = shifted(part_of(value, 1 - c, 2), dc=1)
    return added(part_of(value, c, 2), sent).astype(BF16)


def summed_over_chips(value):
    z, y, _ = coordinates()
    sent = shifted(part_of(value, 1 - y, 1), dy=1)
    line = added(part_of(value, y, 1), sent).astype(BF16)
    terms = [part_of(line, z, 0)] + [
        shifted(part_of(line, (z + step) % GRID[0], 0), dz=step) for step in range(1, GRID[0])
    ]
    return added(*terms)


def scattered(value):
    lanes = value.shape[1]
    return summed_over_chips(summed_on_chip(value.reshape(*GRID, -1, lanes)))


def pixel_masks(rows):
    row = lax.broadcasted_iota(jnp.int32, (rows, 1), 0)
    high, wide = (row // WIDTH) % HEIGHT, row % WIDTH
    masks = []
    for dr in (-1, 0, 1):
        for dc in (-1, 0, 1):
            inside = (high + dr >= 0) & (high + dr < HEIGHT) & (wide + dc >= 0) & (wide + dc < WIDTH)
            masks.append((dr * WIDTH + dc, inside))
    return masks


def frame_masks(rows, frames):
    pixels = HEIGHT * WIDTH
    row = lax.broadcasted_iota(jnp.int32, (rows, 1), 0)
    frame = (row // pixels) % frames
    return [
        (step * pixels, (frame + step >= 0) & (frame + step < frames)) for step in (-1, 0, 1)
    ]


def moved_rows(value, move):
    shift, inside = move
    if shift:
        value = pltpu.roll(value, (-shift) % value.shape[0], 0)
    return jnp.where(inside, value, 0.0)


def dot(left, right, dims=((1,), (0,))):
    return lax.dot_general(left, right, (dims, ((), ())), preferred_element_type=F32)


def with_embedding(hidden, embedding_ref, samples):
    per = hidden.shape[0] // samples
    return jnp.concatenate(
        [hidden[s * per : (s + 1) * per] + embedding_ref[s : s + 1, :] for s in range(samples)]
    )


def scale_of(summed):
    return lax.rsqrt(jnp.mean(summed * summed, axis=-1, keepdims=True) + 1e-06)


def silu_parts(preact):
    logistic = 1.0 / (1.0 + jnp.exp(-preact))
    return logistic, preact * logistic


def convolved(normed, weight_ref, masks):
    rows, channels = normed.shape
    normed = normed.astype(F32)
    total = None
    for tap in range(9):
        term = dot(
            moved_rows(normed, masks[tap]).astype(BF16),
            weight_ref[tap * channels : (tap + 1) * channels, :],
        )
        total = term if total is None else total + term
    return total


def first_forward(frames, hidden_ref, embedding_ref, keep_ref, spatial_ref, temporal_ref, *outs):
    normed_ref, preact_ref, mixed_ref = outs
    rows = hidden_ref.shape[0]
    width = keep_ref.shape[1]
    summed = with_embedding(hidden_ref[...].astype(F32), embedding_ref, embedding_ref.shape[0])
    normed = (summed * scale_of(summed)).astype(BF16)
    normed_ref[...] = normed
    preact = convolved(normed, spatial_ref, pixel_masks(rows))
    preact_ref[...] = preact
    activated = silu_parts(preact)[1].astype(BF16).astype(F32) * keep_ref[...]
    mixed = None
    for tap, move in enumerate(frame_masks(rows, frames)):
        term = dot(
            moved_rows(activated, move).astype(BF16),
            temporal_ref[tap * width : (tap + 1) * width, :],
        )
        mixed = term if mixed is None else mixed + term
    mixed_ref[...] = mixed.astype(BF16)


def slope_of(preact):
    logistic, _ = silu_parts(preact)
    return logistic * (1.0 + preact * (1.0 - logistic))


def act_grad_of(upstream, temporal_ref, width, frames):
    upstream = upstream.astype(F32)
    moves = frame_masks(upstream.shape[0], frames)
    total = None
    for tap in range(3):
        term = dot(
            moved_rows(upstream, moves[2 - tap]).astype(BF16),
            temporal_ref[tap * width : (tap + 1) * width, :],
            ((1,), (1,)),
        )
        total = term if total is None else total + term
    return total


def store_temporal_terms(activated, upstream, frames, out_ref):
    width = activated.shape[1]
    upstream = upstream.astype(F32)
    moves = frame_masks(upstream.shape[0], frames)
    for tap in range(3):
        out_ref[tap * width : (tap + 1) * width, :] = dot(
            activated, moved_rows(upstream, moves[2 - tap]).astype(BF16), ((0,), (0,))
        ).astype(BF16)


def store_spatial_terms(normed, pre_grad, out_ref):
    channels = normed.shape[1]
    pre_grad = pre_grad.astype(F32)
    masks = pixel_masks(pre_grad.shape[0])
    for tap in range(9):
        out_ref[tap * channels : (tap + 1) * channels, :] = dot(
            normed, moved_rows(pre_grad, masks[8 - tap]).astype(BF16), ((0,), (0,))
        ).astype(BF16)


def second_forward(
    frames, hidden_ref, own_ref, sent_ref, embedding_ref, keep_ref, upstream_ref, spatial_ref,
    temporal_ref, next_ref, normed_ref, activated_ref, pre_grad_ref, back_ref,
):
    rows, channels = hidden_ref.shape
    width = keep_ref.shape[1]
    masks = pixel_masks(rows)
    mixed = own_ref[...].astype(F32) + sent_ref[...].astype(F32)
    hidden = (hidden_ref[...].astype(F32) + mixed).astype(BF16)
    next_ref[...] = hidden
    summed = with_embedding(hidden.astype(F32), embedding_ref, embedding_ref.shape[0])
    normed = (summed * scale_of(summed)).astype(BF16)
    normed_ref[...] = normed
    preact = convolved(normed, spatial_ref, masks)
    activated_ref[...] = (silu_parts(preact)[1] * keep_ref[...]).astype(BF16)
    act_grad = act_grad_of(upstream_ref[...], temporal_ref, width, frames)
    pre_grad = (act_grad * slope_of(preact) * keep_ref[...]).astype(BF16)
    pre_grad_ref[...] = pre_grad
    pre_grad = pre_grad.astype(F32)
    back = None
    for tap in range(9):
        term = dot(
            moved_rows(pre_grad, masks[8 - tap]).astype(BF16),
            spatial_ref[tap * channels : (tap + 1) * channels, :],
            ((1,), (1,)),
        )
        back = term if back is None else back + term
    back_ref[...] = back.astype(BF16)


def second_terms(frames, normed_ref, pre_grad_ref, activated_ref, upstream_ref, *outs):
    spatial_ref, temporal_ref = outs
    store_spatial_terms(normed_ref[...], pre_grad_ref[...], spatial_ref)
    store_temporal_terms(activated_ref[...], upstream_ref[...], frames, temporal_ref)


def first_terms(
    frames, hidden_ref, embedding_ref, upstream_ref, own_ref, sent_ref, normed_ref, preact_ref,
    keep_ref, temporal_ref, spatial_out, temporal_out,
):
    width = keep_ref.shape[1]
    channels = hidden_ref.shape[1]
    summed = with_embedding(hidden_ref[...].astype(F32), embedding_ref, embedding_ref.shape[0])
    scale = scale_of(summed)
    grad = own_ref[...].astype(F32) + sent_ref[...].astype(F32)
    inner = jnp.sum(grad * summed, axis=-1, keepdims=True)
    back = grad * scale - summed * (scale * scale * scale) * (inner / channels)
    upstream = (upstream_ref[...].astype(F32) + back).astype(BF16)
    preact = preact_ref[...]
    activated = (silu_parts(preact)[1] * keep_ref[...]).astype(BF16)
    act_grad = act_grad_of(upstream, temporal_ref, width, frames)
    pre_grad = (act_grad * slope_of(preact) * keep_ref[...]).astype(BF16)
    store_spatial_terms(normed_ref[...], pre_grad, spatial_out)
    store_temporal_terms(activated, upstream, frames, temporal_out)


def paired_device(samples, timesteps, cotangent, spatial_weight, temporal_weight):
    me = lax.axis_index("pipe")
    first = me == 0
    _, _, c = coordinates()
    count, frames, pixels, channels = samples.shape
    rows = count * frames * pixels
    main = 2 * LANES
    width = main + LANES
    hidden = samples.reshape(rows, channels)
    upstream = cotangent.reshape(rows, channels)
    embedding = jax.vmap(lambda step: embedding_of(step, channels))(timesteps)
    lane = jnp.arange(LANES)
    keep_own = jnp.concatenate([jnp.ones(main), lane < LANES // 2]).astype(F32)[None]
    keep_other = jnp.concatenate([jnp.ones(main), lane >= LANES // 2]).astype(F32)[None]
    keep_first = jnp.where(first, keep_own, keep_other)
    keep_second = jnp.where(first, keep_other, keep_own)
    tail = lane[None] < LANES // 2

    def main_of(value, index, axis):
        return lax.dynamic_slice_in_dim(value, index * main, main, axis)

    temporal_own = gathered(temporal_weight[0]).reshape(3, channels, channels)
    spatial_own = spatial_weight[0]
    given = swapped(
        jnp.concatenate([main_of(spatial_own, 1 - me, 1), spatial_own[:, 2 * main :]], 1)
    )
    main_own, main_given = main_of(spatial_own, me, 1), given[:, :main]
    tails = jnp.where(tail, spatial_own[:, 2 * main :], given[:, main:])
    spatial_first = gathered(jnp.concatenate([jnp.where(first, main_own, main_given), tails], 1))
    main_second = gathered(jnp.where(first, main_given, main_own))
    spatial_second = jnp.concatenate([main_second, spatial_first[:, main:]], 1)

    def local_rows(index):
        return jnp.concatenate(
            [main_of(temporal_own, index, 1), temporal_own[:, 2 * main :]], 1
        ).reshape(GRID[2], -1, channels)

    half = swapped(part_of(local_rows(1 - me), c, 0))
    other_half = shifted(half, dc=1)
    temporal_other = jnp.where(
        c == 0, jnp.concatenate([half, other_half]), jnp.concatenate([other_half, half])
    )
    temporal_mine = local_rows(me).reshape(3 * width, channels)
    temporal_first = jnp.where(first, temporal_mine, temporal_other)
    temporal_second = jnp.where(first, temporal_other, temporal_mine)

    def shape(extent, dtype=BF16):
        return jax.ShapeDtypeStruct(extent, dtype)

    spatial_flops = 2 * rows * 9 * channels * width
    temporal_flops = 2 * rows * 3 * channels * width
    spatial_bytes = 2 * 9 * channels * width
    temporal_bytes = 2 * 3 * channels * width
    normed_first, preact_first, mixed = vmem_call(
        functools.partial(first_forward, frames),
        (shape((rows, channels)), shape((rows, width), F32), shape((rows, channels))),
        flops=spatial_flops + temporal_flops,
        moved=spatial_bytes + temporal_bytes,
    )(hidden, embedding, keep_first, spatial_first, temporal_first)
    hidden_second, normed_second, activated_second, pre_grad_second, back = vmem_call(
        functools.partial(second_forward, frames),
        (
            shape((rows, channels)),
            shape((rows, channels)),
            shape((rows, width)),
            shape((rows, width)),
            shape((rows, channels)),
        ),
        flops=2 * spatial_flops + temporal_flops,
        moved=spatial_bytes + temporal_bytes,
    )(
        hidden, mixed, swapped(mixed), embedding, keep_second, upstream, spatial_second,
        temporal_second,
    )

    back_given = swapped(back)
    spatial_terms_second, temporal_terms_second = vmem_call(
        functools.partial(second_terms, frames),
        (shape((9 * channels, width)), shape((3 * width, channels))),
        flops=spatial_flops + temporal_flops,
        moved=spatial_bytes + temporal_bytes,
    )(normed_second, pre_grad_second, activated_second, upstream)
    grad_second = scattered(spatial_terms_second[:, :main])
    spatial_terms_first, temporal_terms_first = vmem_call(
        functools.partial(first_terms, frames),
        (shape((9 * channels, width)), shape((3 * width, channels))),
        flops=spatial_flops + 2 * temporal_flops,
        moved=spatial_bytes + 2 * temporal_bytes,
    )(
        hidden_second, embedding, upstream, back, back_given, normed_first, preact_first,
        keep_first, temporal_first,
    )
    tail_terms = spatial_terms_first[:, main:] + spatial_terms_second[:, main:]
    grad_first = scattered(jnp.concatenate([spatial_terms_first[:, :main], tail_terms], 1))

    terms = jnp.stack(
        [
            jnp.where(first, temporal_terms_first, temporal_terms_second),
            jnp.where(first, temporal_terms_second, temporal_terms_first),
        ]
    ).reshape(2, GRID[2], -1, channels)
    sent = shifted(part_of(terms, 1 - c, 1), dc=1)
    halves = added(part_of(terms, c, 1), sent).astype(BF16)
    halves = jnp.stack([halves[0], swapped(halves[1])])
    other_halves = shifted(halves, dc=1)
    both = jnp.where(
        c == 0,
        jnp.stack([halves, other_halves], 1),
        jnp.stack([other_halves, halves], 1),
    ).reshape(2, 3, width, channels)
    mine, theirs = both[0], both[1]
    full = jnp.concatenate(
        [
            jnp.where(first, mine[:, :main], theirs[:, :main]),
            jnp.where(first, theirs[:, :main], mine[:, :main]),
            mine[:, main:] + theirs[:, main:],
        ],
        1,
    )
    share_temporal = summed_over_chips(part_of(full.reshape(*GRID, -1, channels), c, 2))

    kept = jnp.where(first, grad_first[:, :main], grad_second)
    passed = jnp.where(first, grad_second, grad_first[:, :main])
    given = swapped(jnp.concatenate([passed, grad_first[:, main:]], 1).astype(BF16)).astype(F32)
    share_spatial = jnp.concatenate(
        [
            jnp.where(first, kept, given[:, :main]),
            jnp.where(first, given[:, :main], kept),
            jnp.where(tail, grad_first[:, main:], given[:, main:]),
        ],
        1,
    )
    return (share_spatial[None], share_temporal[None])


def solution(mesh):
    paired = mesh.shape["pipe"] == 2 and mesh.shape["dp"] == math.prod(GRID)
    return jax.shard_map(
        paired_device if paired else per_device,
        mesh=mesh,
        in_specs=(
            P("dp", None, None, None),
            P("dp"),
            P("dp", None, None, None),
            P("pipe", "dp", None),
            P("pipe", "dp", None),
        ),
        out_specs=(P("pipe", "dp", None), P("pipe", "dp", None)),
        check_vma=False,
    )
```

```python
import functools
import math

import jax
import jax.numpy as jnp
from jax import lax
from jax.experimental import pallas as pl
from jax.experimental.pallas import tpu as pltpu
from jax.sharding import PartitionSpec as P

HEIGHT = 8
WIDTH = 4
F32 = jnp.float32
BF16 = jnp.bfloat16
GRID = (4, 2, 2)
LANES = 128


def passed_along(value, axis, steps):
    count = lax.axis_size(axis)
    first, last = (max(0, -steps), min(count, count - steps))
    return lax.ppermute(value, axis, [(source, source + steps) for source in range(first, last)])


def embedding_of(step, channels):
    half_width = channels // 2
    frequency = jnp.exp(-math.log(10000.0) * jnp.arange(half_width, dtype=jnp.float32) / half_width)
    phases = step.astype(jnp.float32) * frequency
    return jnp.concatenate([jnp.sin(phases), jnp.cos(phases)])


def normalize(summed):
    return summed * lax.rsqrt(jnp.mean(summed * summed, axis=-1, keepdims=True) + 1e-06)


def spatial_columns(normed):
    frames, pixels, channels = normed.shape
    grid = normed.reshape(frames, HEIGHT, WIDTH, channels)
    padded = jnp.pad(grid, ((0, 0), (1, 1), (1, 1), (0, 0)))
    pieces = [
        padded[:, row : row + HEIGHT, col : col + WIDTH, :] for row in range(3) for col in range(3)
    ]
    return jnp.concatenate(pieces, axis=-1).reshape(frames * pixels, 9 * channels)


def spatial_fold(grads, frames, channels):
    parts = grads.reshape(frames, HEIGHT, WIDTH, 9, channels)
    padded = jnp.zeros((frames, HEIGHT + 2, WIDTH + 2, channels), jnp.float32)
    for row in range(3):
        for col in range(3):
            padded = padded.at[:, row : row + HEIGHT, col : col + WIDTH, :].add(
                parts[:, :, :, row * 3 + col, :]
            )
    return padded[:, 1 : HEIGHT + 1, 1 : WIDTH + 1, :].reshape(frames, HEIGHT * WIDTH, channels)


def temporal_columns(activated):
    frames, pixels, channels = activated.shape
    padded = jnp.pad(activated, ((1, 1), (0, 0), (0, 0)))
    pieces = [padded[tap : tap + frames] for tap in range(3)]
    return jnp.concatenate(pieces, axis=-1).reshape(frames * pixels, 3 * channels)


def temporal_fold(grads, frames, pixels, channels):
    parts = grads.reshape(frames, pixels, 3, channels)
    padded = jnp.zeros((frames + 2, pixels, channels), jnp.float32)
    for tap in range(3):
        padded = padded.at[tap : tap + frames].add(parts[:, :, tap, :])
    return padded[1 : frames + 1]


def section_forward(block_in, embedding, spatial, temporal):
    frames, pixels, channels = block_in.shape
    summed = block_in.astype(jnp.float32) + embedding
    normed = normalize(summed).astype(jnp.bfloat16)
    preact = jnp.dot(spatial_columns(normed), spatial, preferred_element_type=jnp.float32)
    activated = jax.nn.silu(preact).astype(jnp.bfloat16).reshape(frames, pixels, channels)
    mixed = jnp.dot(temporal_columns(activated), temporal, preferred_element_type=jnp.float32)
    return (block_in.astype(jnp.float32) + mixed.reshape(frames, pixels, channels)).astype(
        jnp.bfloat16
    )


def backward_first(block_in, embedding, spatial, temporal, upstream):
    frames, pixels, channels = block_in.shape
    summed = block_in.astype(jnp.float32) + embedding
    normed = normalize(summed).astype(jnp.bfloat16)
    columns = spatial_columns(normed)
    preact = jnp.dot(columns, spatial, preferred_element_type=jnp.float32)
    activated = jax.nn.silu(preact).astype(jnp.bfloat16).reshape(frames, pixels, channels)
    tcolumns = temporal_columns(activated)
    upstream_flat = upstream.reshape(frames * pixels, channels)
    temporal_term = jnp.dot(tcolumns.T, upstream_flat, preferred_element_type=jnp.float32)
    act_grad = temporal_fold(
        jnp.dot(upstream_flat, temporal.T, preferred_element_type=jnp.float32),
        frames,
        pixels,
        channels,
    )
    logistic = jax.nn.sigmoid(preact)
    slope = logistic * (1.0 + preact * (1.0 - logistic))
    pre_grad = (act_grad.reshape(frames * pixels, channels) * slope).astype(jnp.bfloat16)
    return (temporal_term, pre_grad, columns)


def backward_second(block_in, embedding, spatial, upstream, pre_grad, columns):
    frames, pixels, channels = block_in.shape
    summed = block_in.astype(jnp.float32) + embedding
    spatial_term = jnp.dot(columns.T, pre_grad, preferred_element_type=jnp.float32)
    norm_grad = spatial_fold(
        jnp.dot(pre_grad, spatial.T, preferred_element_type=jnp.float32), frames, channels
    )
    _, pullback = jax.vjp(normalize, summed)
    back_input = (upstream.astype(jnp.float32) + pullback(norm_grad)[0]).astype(jnp.bfloat16)
    return (back_input, spatial_term)


def section_backward(block_in, embedding, spatial, temporal, upstream):
    temporal_term, pre_grad, columns = backward_first(
        block_in, embedding, spatial, temporal, upstream
    )
    back_input, spatial_term = backward_second(
        block_in, embedding, spatial, upstream, pre_grad, columns
    )
    return (back_input, spatial_term, temporal_term)


def per_device(samples, timesteps, cotangent, spatial_weight, temporal_weight):
    sections = lax.axis_size("pipe")
    section_index = lax.axis_index("pipe")
    micro_count = samples.shape[0]
    frames, pixels, channels = (samples.shape[1], samples.shape[2], samples.shape[3])
    moments = jnp.arange(micro_count + sections - 1, dtype=jnp.int32)
    blank = jnp.zeros((frames, pixels, channels), jnp.bfloat16)
    full_spatial, full_temporal = (
        lax.all_gather(spatial_weight[0], "dp", axis=0, tiled=True),
        lax.all_gather(temporal_weight[0], "dp", axis=0, tiled=True),
    )

    def forward_step(carry, moment):
        incoming, stash = carry
        position = moment - section_index
        active = (position >= 0) & (position < micro_count)
        picked = jnp.clip(position, 0, micro_count - 1)
        own = lax.dynamic_index_in_dim(samples, picked, 0, keepdims=False)
        embedding = embedding_of(
            lax.dynamic_index_in_dim(timesteps, picked, 0, keepdims=False), channels
        )
        block_in = jnp.where(section_index == 0, own, incoming)
        result = lax.cond(
            active & (section_index < sections - 1),
            lambda: section_forward(block_in, embedding, full_spatial, full_temporal),
            lambda: blank,
        )
        stash = jnp.where(
            active, lax.dynamic_update_index_in_dim(stash, block_in, picked, 0), stash
        )
        passed = passed_along(result, "pipe", 1)
        return ((passed, stash), None)

    (_, stash), _ = lax.scan(forward_step, (blank, jnp.zeros_like(samples)), moments)
    back_spatial, back_temporal = (full_spatial, full_temporal)

    def inputs_at(moment, incoming):
        position = moment - (sections - 1 - section_index)
        active = (position >= 0) & (position < micro_count)
        picked = jnp.clip(position, 0, micro_count - 1)
        block_in = lax.dynamic_index_in_dim(stash, picked, 0, keepdims=False)
        embedding = embedding_of(
            lax.dynamic_index_in_dim(timesteps, picked, 0, keepdims=False), channels
        )
        given = lax.dynamic_index_in_dim(cotangent, picked, 0, keepdims=False)
        upstream = jnp.where(section_index == sections - 1, given, incoming)
        return (active, block_in, embedding, upstream)

    def backward_step(carry, moment):
        incoming, grad_spatial, grad_temporal = carry
        active, block_in, embedding, upstream = inputs_at(moment, incoming)

        def working():
            back_input, spatial_term, temporal_term = section_backward(
                block_in, embedding, back_spatial, back_temporal, upstream
            )
            return (back_input, grad_spatial + spatial_term, grad_temporal + temporal_term)

        def waiting():
            return (blank, grad_spatial, grad_temporal)

        back_input, grad_spatial, grad_temporal = lax.cond(active, working, waiting)
        passed = passed_along(back_input, "pipe", -1)
        return ((passed, grad_spatial, grad_temporal), None)

    start = (
        blank,
        jnp.zeros(back_spatial.shape, jnp.float32),
        jnp.zeros(back_temporal.shape, jnp.float32),
    )
    (_, grad_spatial, grad_temporal), _ = lax.scan(backward_step, start, moments)
    share_spatial, share_temporal = (
        lax.psum_scatter(
            grad_spatial.astype(jnp.bfloat16).astype(jnp.float32).astype(jnp.bfloat16),
            "dp",
            scatter_dimension=0,
            tiled=True,
        ).astype(jnp.float32),
        lax.psum_scatter(
            grad_temporal.astype(jnp.bfloat16).astype(jnp.float32).astype(jnp.bfloat16),
            "dp",
            scatter_dimension=0,
            tiled=True,
        ).astype(jnp.float32),
    )
    return (share_spatial[None], share_temporal[None])


def coordinates():
    index = lax.axis_index("dp")
    return index // (GRID[1] * GRID[2]), (index // GRID[2]) % GRID[1], index % GRID[2]


def shifted(value, dz=0, dy=0, dc=0):
    pairs = []
    for z in range(GRID[0]):
        for y in range(GRID[1]):
            for c in range(GRID[2]):
                place = ((z + dz) % GRID[0], (y + dy) % GRID[1], (c + dc) % GRID[2])
                pairs.append(
                    (
                        (z * GRID[1] + y) * GRID[2] + c,
                        (place[0] * GRID[1] + place[1]) * GRID[2] + place[2],
                    )
                )
    return lax.ppermute(value, "dp", pairs)


def swapped(value):
    return lax.ppermute(value, "pipe", [(0, 1), (1, 0)])


def part_of(value, index, axis):
    return lax.dynamic_index_in_dim(value, index, axis, keepdims=False)


def vmem_call(body, outs, scratch=(), flops=0, moved=0):
    return pl.pallas_call(
        body,
        out_shape=outs,
        scratch_shapes=list(scratch),
        compiler_params=pltpu.CompilerParams(vmem_limit_bytes=40 * 2**20),
        cost_estimate=pl.CostEstimate(flops=flops, bytes_accessed=moved, transcendentals=0),
    )


def after(value, earlier):
    return value if earlier is None else lax.optimization_barrier((value, earlier))[0]


def in_order(swap, own, other, axis):
    return jnp.where(
        swap, jnp.concatenate([other, own], axis), jnp.concatenate([own, other], axis)
    )


def over_z(value, pairs):
    moves = []
    for source, target in pairs:
        for rest in range(GRID[1] * GRID[2]):
            moves.append(tuple(z * GRID[1] * GRID[2] + rest for z in (source, target)))
    return lax.ppermute(value, "dp", moves)


def gathered(values):
    z, y, c = coordinates()
    pair_sent, sides = None, []
    results = []
    for chunk, value in enumerate(values):
        rows, lanes = value.shape
        pair_sent = over_z(after(value, pair_sent), [(0, 1), (1, 0), (2, 3), (3, 2)])
        near = in_order(z % 2 == 1, value[None], pair_sent[None], 0)
        middle = over_z(near, [(1, 2), (2, 1)])
        outer = over_z(middle, [(1, 0), (2, 3)])
        far = jnp.where((z == 1) | (z == 2), middle, outer)
        if chunk == 0:
            side = [shifted(near, dy=1), shifted(far, dy=1)]
            line = in_order(z >= 2, near, far, 0)
            side = in_order(z >= 2, side[0], side[1], 0)
        else:
            line = in_order(z >= 2, near, far, 0)
            side = shifted(after(line, sides[-2] if len(sides) > 1 else None), dy=1)
        sides.append(side)
        plane = in_order(y == 1, line[:, None], side[:, None], 1)
        whole = in_order(c == 1, plane[:, :, None], shifted(plane, dc=1)[:, :, None], 2)
        results.append(whole.reshape(-1, lanes))
    return results


def added(*terms):
    return sum(term.astype(F32) for term in terms)


def summed_on_chip(value):
    _, _, c = coordinates()
    sent = shifted(part_of(value, 1 - c, 2), dc=1)
    return added(part_of(value, c, 2), sent).astype(BF16)


def summed_over_chips(value, earlier):
    z, y, _ = coordinates()
    sent = shifted(after(part_of(value, 1 - y, 1), earlier), dy=1)
    line = added(part_of(value, y, 1), sent).astype(BF16)
    terms = [part_of(line, z, 0)] + [
        shifted(part_of(line, (z + step) % GRID[0], 0), dz=step) for step in range(1, GRID[0])
    ]
    return added(*terms), sent


def pixel_masks(rows):
    row = lax.broadcasted_iota(jnp.int32, (rows, 1), 0)
    high, wide = (row // WIDTH) % HEIGHT, row % WIDTH
    masks = []
    for dr in (-1, 0, 1):
        for dc in (-1, 0, 1):
            inside = (high + dr >= 0) & (high + dr < HEIGHT) & (wide + dc >= 0) & (wide + dc < WIDTH)
            masks.append((dr * WIDTH + dc, inside))
    return masks


def frame_masks(rows, frames):
    pixels = HEIGHT * WIDTH
    row = lax.broadcasted_iota(jnp.int32, (rows, 1), 0)
    frame = (row // pixels) % frames
    return [
        (step * pixels, (frame + step >= 0) & (frame + step < frames)) for step in (-1, 0, 1)
    ]


def moved_rows(value, move):
    shift, inside = move
    if shift:
        value = pltpu.roll(value, (-shift) % value.shape[0], 0)
    return jnp.where(inside, value, 0.0)


def dot(left, right, dims=((1,), (0,))):
    return lax.dot_general(left, right, (dims, ((), ())), preferred_element_type=F32)


def with_embedding(hidden, embedding_ref, samples):
    per = hidden.shape[0] // samples
    return jnp.concatenate(
        [hidden[s * per : (s + 1) * per] + embedding_ref[s : s + 1, :] for s in range(samples)]
    )


def scale_of(summed):
    return lax.rsqrt(jnp.mean(summed * summed, axis=-1, keepdims=True) + 1e-06)


def silu_parts(preact):
    logistic = 1.0 / (1.0 + jnp.exp(-preact))
    return logistic, preact * logistic


def tap_weight(weight_refs, tap, channels):
    return jnp.concatenate(
        [ref[tap * channels : (tap + 1) * channels, :] for ref in weight_refs], 1
    )


def convolved(normed, weight_refs, masks):
    rows, channels = normed.shape
    normed = normed.astype(F32)
    total = None
    for tap in range(9):
        term = dot(
            moved_rows(normed, masks[tap]).astype(BF16),
            tap_weight(weight_refs, tap, channels),
        )
        total = term if total is None else total + term
    return total


def first_forward(frames, hidden_ref, embedding_ref, keep_ref, temporal_ref, *refs):
    *spatial_refs, normed_ref, preact_ref, mixed_ref = refs
    rows = hidden_ref.shape[0]
    width = keep_ref.shape[1]
    summed = with_embedding(hidden_ref[...].astype(F32), embedding_ref, embedding_ref.shape[0])
    normed = (summed * scale_of(summed)).astype(BF16)
    normed_ref[...] = normed
    preact = convolved(normed, spatial_refs, pixel_masks(rows))
    preact_ref[...] = preact
    activated = silu_parts(preact)[1].astype(BF16).astype(F32) * keep_ref[...]
    mixed = None
    for tap, move in enumerate(frame_masks(rows, frames)):
        term = dot(
            moved_rows(activated, move).astype(BF16),
            temporal_ref[tap * width : (tap + 1) * width, :],
        )
        mixed = term if mixed is None else mixed + term
    mixed_ref[...] = mixed.astype(BF16)


def slope_of(preact):
    logistic, _ = silu_parts(preact)
    return logistic * (1.0 + preact * (1.0 - logistic))


def act_grad_of(upstream, temporal_ref, width, frames):
    upstream = upstream.astype(F32)
    moves = frame_masks(upstream.shape[0], frames)
    total = None
    for tap in range(3):
        term = dot(
            moved_rows(upstream, moves[2 - tap]).astype(BF16),
            temporal_ref[tap * width : (tap + 1) * width, :],
            ((1,), (1,)),
        )
        total = term if total is None else total + term
    return total


def store_temporal_terms(activated, upstream, frames, out_ref):
    width = activated.shape[1]
    upstream = upstream.astype(F32)
    moves = frame_masks(upstream.shape[0], frames)
    for tap in range(3):
        out_ref[tap * width : (tap + 1) * width, :] = dot(
            activated, moved_rows(upstream, moves[2 - tap]).astype(BF16), ((0,), (0,))
        ).astype(BF16)


def store_spatial_terms(normed, pre_grad, out_refs):
    channels = normed.shape[1]
    pre_grad = pre_grad.astype(F32)
    masks = pixel_masks(pre_grad.shape[0])
    for tap in range(9):
        term = dot(
            normed, moved_rows(pre_grad, masks[8 - tap]).astype(BF16), ((0,), (0,))
        ).astype(BF16)
        for tile, out_ref in enumerate(out_refs):
            out_ref[tap * channels : (tap + 1) * channels, :] = term[
                :, tile * LANES : (tile + 1) * LANES
            ]


def second_forward(
    frames, hidden_ref, own_ref, sent_ref, embedding_ref, keep_ref, upstream_ref, temporal_ref, *refs
):
    *spatial_refs, next_ref, normed_ref, activated_ref, pre_grad_ref, back_ref = refs
    rows, channels = hidden_ref.shape
    width = keep_ref.shape[1]
    masks = pixel_masks(rows)
    mixed = own_ref[...].astype(F32) + sent_ref[...].astype(F32)
    hidden = (hidden_ref[...].astype(F32) + mixed).astype(BF16)
    next_ref[...] = hidden
    summed = with_embedding(hidden.astype(F32), embedding_ref, embedding_ref.shape[0])
    normed = (summed * scale_of(summed)).astype(BF16)
    normed_ref[...] = normed
    preact = convolved(normed, spatial_refs, masks)
    activated_ref[...] = (silu_parts(preact)[1] * keep_ref[...]).astype(BF16)
    act_grad = act_grad_of(upstream_ref[...], temporal_ref, width, frames)
    pre_grad = (act_grad * slope_of(preact) * keep_ref[...]).astype(BF16)
    pre_grad_ref[...] = pre_grad
    pre_grad = pre_grad.astype(F32)
    back = None
    for tap in range(9):
        term = dot(
            moved_rows(pre_grad, masks[8 - tap]).astype(BF16),
            tap_weight(spatial_refs, tap, channels),
            ((1,), (1,)),
        )
        back = term if back is None else back + term
    back_ref[...] = back.astype(BF16)


def second_terms(frames, normed_ref, pre_grad_ref, activated_ref, upstream_ref, *outs):
    *spatial_refs, temporal_ref = outs
    store_spatial_terms(normed_ref[...], pre_grad_ref[...], spatial_refs)
    store_temporal_terms(activated_ref[...], upstream_ref[...], frames, temporal_ref)


def first_terms(
    frames, hidden_ref, embedding_ref, upstream_ref, own_ref, sent_ref, normed_ref, preact_ref,
    keep_ref, temporal_ref, *outs
):
    *spatial_outs, temporal_out = outs
    width = keep_ref.shape[1]
    channels = hidden_ref.shape[1]
    summed = with_embedding(hidden_ref[...].astype(F32), embedding_ref, embedding_ref.shape[0])
    scale = scale_of(summed)
    grad = own_ref[...].astype(F32) + sent_ref[...].astype(F32)
    inner = jnp.sum(grad * summed, axis=-1, keepdims=True)
    back = grad * scale - summed * (scale * scale * scale) * (inner / channels)
    upstream = (upstream_ref[...].astype(F32) + back).astype(BF16)
    preact = preact_ref[...]
    activated = (silu_parts(preact)[1] * keep_ref[...]).astype(BF16)
    act_grad = act_grad_of(upstream, temporal_ref, width, frames)
    pre_grad = (act_grad * slope_of(preact) * keep_ref[...]).astype(BF16)
    store_spatial_terms(normed_ref[...], pre_grad, spatial_outs)
    store_temporal_terms(activated, upstream, frames, temporal_out)


def paired_device(samples, timesteps, cotangent, spatial_weight, temporal_weight):
    me = lax.axis_index("pipe")
    first = me == 0
    _, _, c = coordinates()
    count, frames, pixels, channels = samples.shape
    rows = count * frames * pixels
    main = 2 * LANES
    width = main + LANES
    hidden = samples.reshape(rows, channels)
    upstream = cotangent.reshape(rows, channels)
    embedding = jax.vmap(lambda step: embedding_of(step, channels))(timesteps)
    lane = jnp.arange(LANES)
    keep_own = jnp.concatenate([jnp.ones(main), lane < LANES // 2]).astype(F32)[None]
    keep_other = jnp.concatenate([jnp.ones(main), lane >= LANES // 2]).astype(F32)[None]
    keep_first = jnp.where(first, keep_own, keep_other)
    keep_second = jnp.where(first, keep_other, keep_own)
    tail = lane[None] < LANES // 2

    def main_of(value, index, axis):
        return lax.dynamic_slice_in_dim(value, index * main, main, axis)

    spatial_own = spatial_weight[0]
    given = swapped(
        jnp.concatenate([main_of(spatial_own, 1 - me, 1), spatial_own[:, 2 * main :]], 1)
    )
    main_own, main_given = main_of(spatial_own, me, 1), given[:, :main]
    tails = jnp.where(tail, spatial_own[:, 2 * main :], given[:, main:])
    main_first = jnp.where(first, main_own, main_given)
    main_second = jnp.where(first, main_given, main_own)
    temporal_own, *mains_first, tails, low, high = gathered(
        [
            temporal_weight[0],
            main_first[:, :LANES],
            main_first[:, LANES:],
            tails,
            main_second[:, :LANES],
            main_second[:, LANES:],
        ]
    )
    temporal_own = temporal_own.reshape(3, channels, channels)
    spatial_first = [*mains_first, tails]
    spatial_second = [low, high, tails]

    def local_rows(index):
        return jnp.concatenate(
            [main_of(temporal_own, index, 1), temporal_own[:, 2 * main :]], 1
        ).reshape(GRID[2], -1, channels)

    half = swapped(part_of(local_rows(1 - me), c, 0))
    other_half = shifted(half, dc=1)
    temporal_other = jnp.where(
        c == 0, jnp.concatenate([half, other_half]), jnp.concatenate([other_half, half])
    )
    temporal_mine = local_rows(me).reshape(3 * width, channels)
    temporal_first = jnp.where(first, temporal_mine, temporal_other)
    temporal_second = jnp.where(first, temporal_other, temporal_mine)

    def shape(extent, dtype=BF16):
        return jax.ShapeDtypeStruct(extent, dtype)

    spatial_flops = 2 * rows * 9 * channels * width
    temporal_flops = 2 * rows * 3 * channels * width
    spatial_bytes = 2 * 9 * channels * width
    temporal_bytes = 2 * 3 * channels * width
    normed_first, preact_first, mixed = vmem_call(
        functools.partial(first_forward, frames),
        (shape((rows, channels)), shape((rows, width), F32), shape((rows, channels))),
        flops=spatial_flops + temporal_flops,
        moved=spatial_bytes + temporal_bytes,
    )(hidden, embedding, keep_first, temporal_first, *spatial_first)
    hidden_second, normed_second, activated_second, pre_grad_second, back = vmem_call(
        functools.partial(second_forward, frames),
        (
            shape((rows, channels)),
            shape((rows, channels)),
            shape((rows, width)),
            shape((rows, width)),
            shape((rows, channels)),
        ),
        flops=2 * spatial_flops + temporal_flops,
        moved=spatial_bytes + temporal_bytes,
    )(
        hidden, mixed, swapped(mixed), embedding, keep_second, upstream, temporal_second,
        *spatial_second,
    )

    def terms_shape():
        return (shape((9 * channels, LANES)),) * 3 + (shape((3 * width, channels)),)

    back_given = swapped(back)
    *spatial_terms_second, temporal_terms_second = vmem_call(
        functools.partial(second_terms, frames),
        terms_shape(),
        flops=spatial_flops + temporal_flops,
        moved=spatial_bytes + temporal_bytes,
    )(normed_second, pre_grad_second, activated_second, upstream)
    *spatial_terms_first, temporal_terms_first = vmem_call(
        functools.partial(first_terms, frames),
        terms_shape(),
        flops=spatial_flops + 2 * temporal_flops,
        moved=spatial_bytes + 2 * temporal_bytes,
    )(
        hidden_second, embedding, upstream, back, back_given, normed_first, preact_first,
        keep_first, temporal_first,
    )
    tail_terms = spatial_terms_first[2] + spatial_terms_second[2]
    sides, shares = [None, None], []
    for terms in (*spatial_terms_second[:2], tail_terms, *spatial_terms_first[:2]):
        share, side = summed_over_chips(
            summed_on_chip(terms.reshape(*GRID, -1, LANES)), sides[-2]
        )
        sides.append(side)
        shares.append(share)

    terms = jnp.stack(
        [
            jnp.where(first, temporal_terms_first, temporal_terms_second),
            jnp.where(first, temporal_terms_second, temporal_terms_first),
        ]
    ).reshape(2, GRID[2], -1, channels)
    sent = shifted(part_of(terms, 1 - c, 1), dc=1)
    halves = added(part_of(terms, c, 1), sent).astype(BF16)
    halves = jnp.stack([halves[0], swapped(halves[1])])
    other_halves = shifted(halves, dc=1)
    both = jnp.where(
        c == 0,
        jnp.stack([halves, other_halves], 1),
        jnp.stack([other_halves, halves], 1),
    ).reshape(2, 3, width, channels)
    mine, theirs = both[0], both[1]
    full = jnp.concatenate(
        [
            jnp.where(first, mine[:, :main], theirs[:, :main]),
            jnp.where(first, theirs[:, :main], mine[:, :main]),
            mine[:, main:] + theirs[:, main:],
        ],
        1,
    )
    share_temporal, _ = summed_over_chips(
        part_of(full.reshape(*GRID, -1, channels), c, 2), sides[-2]
    )

    share_second, share_tails, share_first = (
        jnp.concatenate(shares[:2], 1),
        shares[2],
        jnp.concatenate(shares[3:], 1),
    )
    kept = jnp.where(first, share_first, share_second)
    passed = jnp.where(first, share_second, share_first)
    given = swapped(jnp.concatenate([passed, share_tails], 1).astype(BF16)).astype(F32)
    share_spatial = jnp.concatenate(
        [
            jnp.where(first, kept, given[:, :main]),
            jnp.where(first, given[:, :main], kept),
            jnp.where(tail, share_tails, given[:, main:]),
        ],
        1,
    )
    return (share_spatial[None], share_temporal[None])


def solution(mesh):
    paired = mesh.shape["pipe"] == 2 and mesh.shape["dp"] == math.prod(GRID)
    return jax.shard_map(
        paired_device if paired else per_device,
        mesh=mesh,
        in_specs=(
            P("dp", None, None, None),
            P("dp"),
            P("dp", None, None, None),
            P("pipe", "dp", None),
            P("pipe", "dp", None),
        ),
        out_specs=(P("pipe", "dp", None), P("pipe", "dp", None)),
        check_vma=False,
    )
```

```python
import functools
import math

import jax
import jax.numpy as jnp
from jax import lax
from jax.experimental import pallas as pl
from jax.experimental.pallas import tpu as pltpu
from jax.sharding import PartitionSpec as P

HEIGHT = 8
WIDTH = 4
F32 = jnp.float32
BF16 = jnp.bfloat16
GRID = (4, 2, 2)
LANES = 128


def passed_along(value, axis, steps):
    count = lax.axis_size(axis)
    first, last = (max(0, -steps), min(count, count - steps))
    return lax.ppermute(value, axis, [(source, source + steps) for source in range(first, last)])


def embedding_of(step, channels):
    half_width = channels // 2
    frequency = jnp.exp(-math.log(10000.0) * jnp.arange(half_width, dtype=jnp.float32) / half_width)
    phases = step.astype(jnp.float32) * frequency
    return jnp.concatenate([jnp.sin(phases), jnp.cos(phases)])


def normalize(summed):
    return summed * lax.rsqrt(jnp.mean(summed * summed, axis=-1, keepdims=True) + 1e-06)


def spatial_columns(normed):
    frames, pixels, channels = normed.shape
    grid = normed.reshape(frames, HEIGHT, WIDTH, channels)
    padded = jnp.pad(grid, ((0, 0), (1, 1), (1, 1), (0, 0)))
    pieces = [
        padded[:, row : row + HEIGHT, col : col + WIDTH, :] for row in range(3) for col in range(3)
    ]
    return jnp.concatenate(pieces, axis=-1).reshape(frames * pixels, 9 * channels)


def spatial_fold(grads, frames, channels):
    parts = grads.reshape(frames, HEIGHT, WIDTH, 9, channels)
    padded = jnp.zeros((frames, HEIGHT + 2, WIDTH + 2, channels), jnp.float32)
    for row in range(3):
        for col in range(3):
            padded = padded.at[:, row : row + HEIGHT, col : col + WIDTH, :].add(
                parts[:, :, :, row * 3 + col, :]
            )
    return padded[:, 1 : HEIGHT + 1, 1 : WIDTH + 1, :].reshape(frames, HEIGHT * WIDTH, channels)


def temporal_columns(activated):
    frames, pixels, channels = activated.shape
    padded = jnp.pad(activated, ((1, 1), (0, 0), (0, 0)))
    pieces = [padded[tap : tap + frames] for tap in range(3)]
    return jnp.concatenate(pieces, axis=-1).reshape(frames * pixels, 3 * channels)


def temporal_fold(grads, frames, pixels, channels):
    parts = grads.reshape(frames, pixels, 3, channels)
    padded = jnp.zeros((frames + 2, pixels, channels), jnp.float32)
    for tap in range(3):
        padded = padded.at[tap : tap + frames].add(parts[:, :, tap, :])
    return padded[1 : frames + 1]


def section_forward(block_in, embedding, spatial, temporal):
    frames, pixels, channels = block_in.shape
    summed = block_in.astype(jnp.float32) + embedding
    normed = normalize(summed).astype(jnp.bfloat16)
    preact = jnp.dot(spatial_columns(normed), spatial, preferred_element_type=jnp.float32)
    activated = jax.nn.silu(preact).astype(jnp.bfloat16).reshape(frames, pixels, channels)
    mixed = jnp.dot(temporal_columns(activated), temporal, preferred_element_type=jnp.float32)
    return (block_in.astype(jnp.float32) + mixed.reshape(frames, pixels, channels)).astype(
        jnp.bfloat16
    )


def backward_first(block_in, embedding, spatial, temporal, upstream):
    frames, pixels, channels = block_in.shape
    summed = block_in.astype(jnp.float32) + embedding
    normed = normalize(summed).astype(jnp.bfloat16)
    columns = spatial_columns(normed)
    preact = jnp.dot(columns, spatial, preferred_element_type=jnp.float32)
    activated = jax.nn.silu(preact).astype(jnp.bfloat16).reshape(frames, pixels, channels)
    tcolumns = temporal_columns(activated)
    upstream_flat = upstream.reshape(frames * pixels, channels)
    temporal_term = jnp.dot(tcolumns.T, upstream_flat, preferred_element_type=jnp.float32)
    act_grad = temporal_fold(
        jnp.dot(upstream_flat, temporal.T, preferred_element_type=jnp.float32),
        frames,
        pixels,
        channels,
    )
    logistic = jax.nn.sigmoid(preact)
    slope = logistic * (1.0 + preact * (1.0 - logistic))
    pre_grad = (act_grad.reshape(frames * pixels, channels) * slope).astype(jnp.bfloat16)
    return (temporal_term, pre_grad, columns)


def backward_second(block_in, embedding, spatial, upstream, pre_grad, columns):
    frames, pixels, channels = block_in.shape
    summed = block_in.astype(jnp.float32) + embedding
    spatial_term = jnp.dot(columns.T, pre_grad, preferred_element_type=jnp.float32)
    norm_grad = spatial_fold(
        jnp.dot(pre_grad, spatial.T, preferred_element_type=jnp.float32), frames, channels
    )
    _, pullback = jax.vjp(normalize, summed)
    back_input = (upstream.astype(jnp.float32) + pullback(norm_grad)[0]).astype(jnp.bfloat16)
    return (back_input, spatial_term)


def section_backward(block_in, embedding, spatial, temporal, upstream):
    temporal_term, pre_grad, columns = backward_first(
        block_in, embedding, spatial, temporal, upstream
    )
    back_input, spatial_term = backward_second(
        block_in, embedding, spatial, upstream, pre_grad, columns
    )
    return (back_input, spatial_term, temporal_term)


def per_device(samples, timesteps, cotangent, spatial_weight, temporal_weight):
    sections = lax.axis_size("pipe")
    section_index = lax.axis_index("pipe")
    micro_count = samples.shape[0]
    frames, pixels, channels = (samples.shape[1], samples.shape[2], samples.shape[3])
    moments = jnp.arange(micro_count + sections - 1, dtype=jnp.int32)
    blank = jnp.zeros((frames, pixels, channels), jnp.bfloat16)
    full_spatial, full_temporal = (
        lax.all_gather(spatial_weight[0], "dp", axis=0, tiled=True),
        lax.all_gather(temporal_weight[0], "dp", axis=0, tiled=True),
    )

    def forward_step(carry, moment):
        incoming, stash = carry
        position = moment - section_index
        active = (position >= 0) & (position < micro_count)
        picked = jnp.clip(position, 0, micro_count - 1)
        own = lax.dynamic_index_in_dim(samples, picked, 0, keepdims=False)
        embedding = embedding_of(
            lax.dynamic_index_in_dim(timesteps, picked, 0, keepdims=False), channels
        )
        block_in = jnp.where(section_index == 0, own, incoming)
        result = lax.cond(
            active & (section_index < sections - 1),
            lambda: section_forward(block_in, embedding, full_spatial, full_temporal),
            lambda: blank,
        )
        stash = jnp.where(
            active, lax.dynamic_update_index_in_dim(stash, block_in, picked, 0), stash
        )
        passed = passed_along(result, "pipe", 1)
        return ((passed, stash), None)

    (_, stash), _ = lax.scan(forward_step, (blank, jnp.zeros_like(samples)), moments)
    back_spatial, back_temporal = (full_spatial, full_temporal)

    def inputs_at(moment, incoming):
        position = moment - (sections - 1 - section_index)
        active = (position >= 0) & (position < micro_count)
        picked = jnp.clip(position, 0, micro_count - 1)
        block_in = lax.dynamic_index_in_dim(stash, picked, 0, keepdims=False)
        embedding = embedding_of(
            lax.dynamic_index_in_dim(timesteps, picked, 0, keepdims=False), channels
        )
        given = lax.dynamic_index_in_dim(cotangent, picked, 0, keepdims=False)
        upstream = jnp.where(section_index == sections - 1, given, incoming)
        return (active, block_in, embedding, upstream)

    def backward_step(carry, moment):
        incoming, grad_spatial, grad_temporal = carry
        active, block_in, embedding, upstream = inputs_at(moment, incoming)

        def working():
            back_input, spatial_term, temporal_term = section_backward(
                block_in, embedding, back_spatial, back_temporal, upstream
            )
            return (back_input, grad_spatial + spatial_term, grad_temporal + temporal_term)

        def waiting():
            return (blank, grad_spatial, grad_temporal)

        back_input, grad_spatial, grad_temporal = lax.cond(active, working, waiting)
        passed = passed_along(back_input, "pipe", -1)
        return ((passed, grad_spatial, grad_temporal), None)

    start = (
        blank,
        jnp.zeros(back_spatial.shape, jnp.float32),
        jnp.zeros(back_temporal.shape, jnp.float32),
    )
    (_, grad_spatial, grad_temporal), _ = lax.scan(backward_step, start, moments)
    share_spatial, share_temporal = (
        lax.psum_scatter(
            grad_spatial.astype(jnp.bfloat16).astype(jnp.float32).astype(jnp.bfloat16),
            "dp",
            scatter_dimension=0,
            tiled=True,
        ).astype(jnp.float32),
        lax.psum_scatter(
            grad_temporal.astype(jnp.bfloat16).astype(jnp.float32).astype(jnp.bfloat16),
            "dp",
            scatter_dimension=0,
            tiled=True,
        ).astype(jnp.float32),
    )
    return (share_spatial[None], share_temporal[None])


def coordinates():
    index = lax.axis_index("dp")
    return index // (GRID[1] * GRID[2]), (index // GRID[2]) % GRID[1], index % GRID[2]


def shifted(value, dz=0, dy=0, dc=0):
    pairs = []
    for z in range(GRID[0]):
        for y in range(GRID[1]):
            for c in range(GRID[2]):
                place = ((z + dz) % GRID[0], (y + dy) % GRID[1], (c + dc) % GRID[2])
                pairs.append(
                    (
                        (z * GRID[1] + y) * GRID[2] + c,
                        (place[0] * GRID[1] + place[1]) * GRID[2] + place[2],
                    )
                )
    return lax.ppermute(value, "dp", pairs)


def swapped(value):
    return lax.ppermute(value, "pipe", [(0, 1), (1, 0)])


def part_of(value, index, axis):
    return lax.dynamic_index_in_dim(value, index, axis, keepdims=False)


def vmem_call(body, outs, scratch=(), flops=0, moved=0):
    return pl.pallas_call(
        body,
        out_shape=outs,
        scratch_shapes=list(scratch),
        compiler_params=pltpu.CompilerParams(vmem_limit_bytes=24 * 2**20),
        cost_estimate=pl.CostEstimate(flops=flops, bytes_accessed=moved, transcendentals=0),
    )


def after(value, earlier):
    return value if earlier is None else lax.optimization_barrier((value, earlier))[0]


def in_order(swap, own, other, axis):
    return jnp.where(
        swap, jnp.concatenate([other, own], axis), jnp.concatenate([own, other], axis)
    )


def over_z(value, pairs):
    moves = []
    for source, target in pairs:
        for rest in range(GRID[1] * GRID[2]):
            moves.append(tuple(z * GRID[1] * GRID[2] + rest for z in (source, target)))
    return lax.ppermute(value, "dp", moves)


def gathered_over_z(value, chunks):
    z, _, _ = coordinates()
    pair_sent = over_z(after(value, stage(chunks, "far", 2)), [(0, 1), (1, 0), (2, 3), (3, 2)])
    near = in_order(z % 2 == 1, value[None], pair_sent[None], 0)
    far = over_z(after(near, stage(chunks, "side", 3)), [(0, 2), (2, 0), (1, 3), (3, 1)])
    chunks.append({"far": far})
    return in_order(z >= 2, near, far, 0)


def stage(chunks, name, back):
    return chunks[-back].get(name) if len(chunks) >= back else None


def gathered_over_plane(line, chunks, earlier=None, last=None):
    _, y, c = coordinates()
    side = shifted(after(after(line, stage(chunks, "whole", 3)), earlier), dy=1)
    plane = after(in_order(y == 1, line[:, None], side[:, None], 1), last)
    whole = in_order(c == 1, plane[:, :, None], shifted(plane, dc=1)[:, :, None], 2)
    chunks[-1].update(side=side, whole=whole)
    return whole.reshape(-1, line.shape[2])


def gathered(value, chunks):
    return gathered_over_plane(gathered_over_z(value, chunks), chunks)


def added(*terms):
    return sum(term.astype(F32) for term in terms)


def summed_on_chip(value):
    _, _, c = coordinates()
    sent = shifted(part_of(value, 1 - c, 2), dc=1)
    return added(part_of(value, c, 2), sent).astype(BF16)


def summed_over_y(value, earlier):
    _, y, _ = coordinates()
    sent = shifted(after(part_of(value, 1 - y, 1), earlier), dy=1)
    return added(part_of(value, y, 1), sent).astype(BF16), sent


def summed_over_z(line):
    z, _, _ = coordinates()
    terms = [part_of(line, z, 0)] + [
        shifted(part_of(line, (z + step) % GRID[0], 0), dz=step) for step in range(1, GRID[0])
    ]
    return added(*terms)


def pixel_masks(rows):
    row = lax.broadcasted_iota(jnp.int32, (rows, 1), 0)
    high, wide = (row // WIDTH) % HEIGHT, row % WIDTH
    masks = []
    for dr in (-1, 0, 1):
        for dc in (-1, 0, 1):
            inside = (high + dr >= 0) & (high + dr < HEIGHT) & (wide + dc >= 0) & (wide + dc < WIDTH)
            masks.append((dr * WIDTH + dc, inside))
    return masks


def frame_masks(rows, frames):
    pixels = HEIGHT * WIDTH
    row = lax.broadcasted_iota(jnp.int32, (rows, 1), 0)
    frame = (row // pixels) % frames
    return [
        (step * pixels, (frame + step >= 0) & (frame + step < frames)) for step in (-1, 0, 1)
    ]


def moved_rows(value, move):
    shift, inside = move
    if shift:
        value = pltpu.roll(value, (-shift) % value.shape[0], 0)
    return jnp.where(inside, value, 0.0)


def dot(left, right, dims=((1,), (0,))):
    return lax.dot_general(left, right, (dims, ((), ())), preferred_element_type=F32)


def with_embedding(hidden, embedding_ref, samples):
    per = hidden.shape[0] // samples
    return jnp.concatenate(
        [hidden[s * per : (s + 1) * per] + embedding_ref[s : s + 1, :] for s in range(samples)]
    )


def scale_of(summed):
    return lax.rsqrt(jnp.mean(summed * summed, axis=-1, keepdims=True) + 1e-06)


def silu_parts(preact):
    logistic = 1.0 / (1.0 + jnp.exp(-preact))
    return logistic, preact * logistic


def tap_weight(weight_refs, tap, channels):
    return jnp.concatenate(
        [ref[tap * channels : (tap + 1) * channels, :] for ref in weight_refs], 1
    )


def convolved(normed, weight_refs, masks):
    rows, channels = normed.shape
    normed = normed.astype(F32)
    total = None
    for tap in range(9):
        term = dot(
            moved_rows(normed, masks[tap]).astype(BF16),
            tap_weight(weight_refs, tap, channels),
        )
        total = term if total is None else total + term
    return total


def first_forward(frames, hidden_ref, embedding_ref, keep_ref, temporal_ref, *refs):
    *spatial_refs, normed_ref, preact_ref, mixed_ref = refs
    rows = hidden_ref.shape[0]
    width = keep_ref.shape[1]
    summed = with_embedding(hidden_ref[...].astype(F32), embedding_ref, embedding_ref.shape[0])
    normed = (summed * scale_of(summed)).astype(BF16)
    normed_ref[...] = normed
    preact = convolved(normed, spatial_refs, pixel_masks(rows))
    preact_ref[...] = preact
    activated = silu_parts(preact)[1].astype(BF16).astype(F32) * keep_ref[...]
    mixed = None
    for tap, move in enumerate(frame_masks(rows, frames)):
        term = dot(
            moved_rows(activated, move).astype(BF16),
            temporal_ref[tap * width : (tap + 1) * width, :],
        )
        mixed = term if mixed is None else mixed + term
    mixed_ref[...] = mixed.astype(BF16)


def slope_of(preact):
    logistic, _ = silu_parts(preact)
    return logistic * (1.0 + preact * (1.0 - logistic))


def act_grad_of(upstream, temporal_ref, width, frames):
    upstream = upstream.astype(F32)
    moves = frame_masks(upstream.shape[0], frames)
    total = None
    for tap in range(3):
        term = dot(
            moved_rows(upstream, moves[2 - tap]).astype(BF16),
            temporal_ref[tap * width : (tap + 1) * width, :],
            ((1,), (1,)),
        )
        total = term if total is None else total + term
    return total


def store_temporal_terms(activated, upstream, frames, out_ref):
    width = activated.shape[1]
    upstream = upstream.astype(F32)
    moves = frame_masks(upstream.shape[0], frames)
    for tap in range(3):
        out_ref[tap * width : (tap + 1) * width, :] = dot(
            activated, moved_rows(upstream, moves[2 - tap]).astype(BF16), ((0,), (0,))
        ).astype(BF16)


def store_spatial_terms(normed, pre_grad, out_refs):
    channels = normed.shape[1]
    pre_grad = pre_grad.astype(F32)
    masks = pixel_masks(pre_grad.shape[0])
    for tap in range(9):
        term = dot(
            normed, moved_rows(pre_grad, masks[8 - tap]).astype(BF16), ((0,), (0,))
        ).astype(BF16)
        start = 0
        for out_ref in out_refs:
            end = start + out_ref.shape[1]
            out_ref[tap * channels : (tap + 1) * channels, :] = term[:, start:end]
            start = end


def second_forward(
    frames, hidden_ref, own_ref, sent_ref, embedding_ref, keep_ref, upstream_ref, temporal_ref, *refs
):
    *spatial_refs, next_ref, normed_ref, activated_ref, pre_grad_ref, back_ref = refs
    rows, channels = hidden_ref.shape
    width = keep_ref.shape[1]
    masks = pixel_masks(rows)
    mixed = own_ref[...].astype(F32) + sent_ref[...].astype(F32)
    hidden = (hidden_ref[...].astype(F32) + mixed).astype(BF16)
    next_ref[...] = hidden
    summed = with_embedding(hidden.astype(F32), embedding_ref, embedding_ref.shape[0])
    normed = (summed * scale_of(summed)).astype(BF16)
    normed_ref[...] = normed
    preact = convolved(normed, spatial_refs, masks)
    activated_ref[...] = (silu_parts(preact)[1] * keep_ref[...]).astype(BF16)
    act_grad = act_grad_of(upstream_ref[...], temporal_ref, width, frames)
    pre_grad = (act_grad * slope_of(preact) * keep_ref[...]).astype(BF16)
    pre_grad_ref[...] = pre_grad
    pre_grad = pre_grad.astype(F32)
    back = None
    for tap in range(9):
        term = dot(
            moved_rows(pre_grad, masks[8 - tap]).astype(BF16),
            tap_weight(spatial_refs, tap, channels),
            ((1,), (1,)),
        )
        back = term if back is None else back + term
    back_ref[...] = back.astype(BF16)


def second_terms(frames, normed_ref, pre_grad_ref, activated_ref, upstream_ref, *outs):
    *spatial_refs, temporal_ref = outs
    store_spatial_terms(normed_ref[...], pre_grad_ref[...], spatial_refs)
    store_temporal_terms(activated_ref[...], upstream_ref[...], frames, temporal_ref)


def first_terms(
    frames, hidden_ref, embedding_ref, upstream_ref, own_ref, sent_ref, normed_ref, preact_ref,
    keep_ref, temporal_ref, *outs
):
    *spatial_outs, temporal_out = outs
    width = keep_ref.shape[1]
    channels = hidden_ref.shape[1]
    summed = with_embedding(hidden_ref[...].astype(F32), embedding_ref, embedding_ref.shape[0])
    scale = scale_of(summed)
    grad = own_ref[...].astype(F32) + sent_ref[...].astype(F32)
    inner = jnp.sum(grad * summed, axis=-1, keepdims=True)
    back = grad * scale - summed * (scale * scale * scale) * (inner / channels)
    upstream = (upstream_ref[...].astype(F32) + back).astype(BF16)
    preact = preact_ref[...]
    activated = (silu_parts(preact)[1] * keep_ref[...]).astype(BF16)
    act_grad = act_grad_of(upstream, temporal_ref, width, frames)
    pre_grad = (act_grad * slope_of(preact) * keep_ref[...]).astype(BF16)
    store_spatial_terms(normed_ref[...], pre_grad, spatial_outs)
    store_temporal_terms(activated, upstream, frames, temporal_out)


def paired_device(samples, timesteps, cotangent, spatial_weight, temporal_weight):
    me = lax.axis_index("pipe")
    first = me == 0
    _, _, c = coordinates()
    count, frames, pixels, channels = samples.shape
    rows = count * frames * pixels
    main = 2 * LANES
    width = main + LANES
    hidden = samples.reshape(rows, channels)
    upstream = cotangent.reshape(rows, channels)
    embedding = jax.vmap(lambda step: embedding_of(step, channels))(timesteps)
    lane = jnp.arange(LANES)
    keep_own = jnp.concatenate([jnp.ones(main), lane < LANES // 2]).astype(F32)[None]
    keep_other = jnp.concatenate([jnp.ones(main), lane >= LANES // 2]).astype(F32)[None]
    keep_first = jnp.where(first, keep_own, keep_other)
    keep_second = jnp.where(first, keep_other, keep_own)
    tail = lane[None] < LANES // 2

    def main_of(value, index, axis):
        return lax.dynamic_slice_in_dim(value, index * main, main, axis)

    spatial_own = spatial_weight[0]
    given = swapped(
        jnp.concatenate([main_of(spatial_own, 1 - me, 1), spatial_own[:, 2 * main :]], 1)
    )
    main_own, main_given = main_of(spatial_own, me, 1), given[:, :main]
    tails = jnp.where(tail, spatial_own[:, 2 * main :], given[:, main:])
    main_first = jnp.where(first, main_own, main_given)
    main_second = jnp.where(first, main_given, main_own)
    chunks = []
    temporal_own = gathered(temporal_weight[0], chunks).reshape(3, channels, channels)
    main_first = gathered(main_first, chunks)
    tails = gathered(tails, chunks)
    spatial_first = [main_first, tails]

    def local_rows(index):
        return jnp.concatenate(
            [main_of(temporal_own, index, 1), temporal_own[:, 2 * main :]], 1
        ).reshape(GRID[2], -1, channels)

    half = swapped(part_of(local_rows(1 - me), c, 0))
    other_half = shifted(half, dc=1)
    temporal_other = jnp.where(
        c == 0, jnp.concatenate([half, other_half]), jnp.concatenate([other_half, half])
    )
    temporal_mine = local_rows(me).reshape(3 * width, channels)
    temporal_first = jnp.where(first, temporal_mine, temporal_other)
    temporal_second = jnp.where(first, temporal_other, temporal_mine)

    def shape(extent, dtype=BF16):
        return jax.ShapeDtypeStruct(extent, dtype)

    spatial_flops = 2 * rows * 9 * channels * width
    temporal_flops = 2 * rows * 3 * channels * width
    spatial_bytes = 2 * 9 * channels * width
    temporal_bytes = 2 * 3 * channels * width
    normed_first, preact_first, mixed = vmem_call(
        functools.partial(first_forward, frames),
        (shape((rows, channels)), shape((rows, width), F32), shape((rows, channels))),
        flops=spatial_flops + temporal_flops,
        moved=spatial_bytes + temporal_bytes,
    )(hidden, embedding, keep_first, temporal_first, *spatial_first)
    line_second = gathered_over_z(main_second, chunks)
    low = gathered_over_plane(line_second[..., :LANES], chunks, half)
    mixed_given = swapped(mixed)
    high = gathered_over_plane(line_second[..., LANES:], chunks, mixed, mixed_given)
    spatial_second = [low, high, tails]
    hidden_second, normed_second, activated_second, pre_grad_second, back = vmem_call(
        functools.partial(second_forward, frames),
        (
            shape((rows, channels)),
            shape((rows, channels)),
            shape((rows, width)),
            shape((rows, width)),
            shape((rows, channels)),
        ),
        flops=2 * spatial_flops + temporal_flops,
        moved=spatial_bytes + temporal_bytes,
    )(
        hidden, mixed, mixed_given, embedding, keep_second, upstream, temporal_second,
        *spatial_second,
    )

    def terms_shape():
        return (
            shape((9 * channels, main)),
            shape((9 * channels, width - main)),
            shape((3 * width, channels)),
        )

    def on_chip(terms):
        return summed_on_chip(terms.reshape(*GRID, -1, terms.shape[1]))

    back_given = swapped(back)
    main_terms_second, tail_terms_second, temporal_terms_second = vmem_call(
        functools.partial(second_terms, frames),
        terms_shape(),
        flops=spatial_flops + temporal_flops,
        moved=spatial_bytes + temporal_bytes,
    )(normed_second, pre_grad_second, activated_second, upstream)
    chip_second = on_chip(main_terms_second)
    line_low, side_low = summed_over_y(chip_second[..., :LANES], None)
    line_high, side_second = summed_over_y(chip_second[..., LANES:], None)
    back_given = after(back_given, side_low)
    main_terms_first, tail_terms_first, temporal_terms_first = vmem_call(
        functools.partial(first_terms, frames),
        terms_shape(),
        flops=spatial_flops + 2 * temporal_flops,
        moved=spatial_bytes + 2 * temporal_bytes,
    )(
        hidden_second, embedding, upstream, back, back_given, normed_first, preact_first,
        keep_first, temporal_first,
    )
    chip_tails = on_chip(tail_terms_first + tail_terms_second)
    chip_first = on_chip(main_terms_first)

    terms = jnp.stack(
        [
            jnp.where(first, temporal_terms_first, temporal_terms_second),
            jnp.where(first, temporal_terms_second, temporal_terms_first),
        ]
    ).reshape(2, GRID[2], -1, channels)
    sent = shifted(part_of(terms, 1 - c, 1), dc=1)
    halves = added(part_of(terms, c, 1), sent).astype(BF16)
    half_given = swapped(halves[1])
    halves = jnp.stack([halves[0], half_given])
    other_halves = shifted(halves, dc=1)
    both = jnp.where(
        c == 0,
        jnp.stack([halves, other_halves], 1),
        jnp.stack([other_halves, halves], 1),
    ).reshape(2, 3, width, channels)
    mine, theirs = both[0], both[1]
    full = jnp.concatenate(
        [
            jnp.where(first, mine[:, :main], theirs[:, :main]),
            jnp.where(first, theirs[:, :main], mine[:, :main]),
            mine[:, main:] + theirs[:, main:],
        ],
        1,
    )
    full = part_of(full.reshape(*GRID, -1, channels), c, 2)

    share_second = summed_over_z(jnp.concatenate([line_low, line_high], 2))
    line_tails, side_tails = summed_over_y(chip_tails, (side_second, sent))
    line_first, side_first = summed_over_y(chip_first, side_second)
    share_tails = summed_over_z(line_tails)
    line, side = summed_over_y(full[..., : 3 * LANES], side_tails)
    share_first = summed_over_z(after(line_first, other_halves))
    line_end, _ = summed_over_y(full[..., 3 * LANES :], side_first)
    share_temporal = jnp.concatenate([summed_over_z(line), summed_over_z(line_end)], 1)

    kept = jnp.where(first, share_first, share_second)
    passed = jnp.where(first, share_second, share_first)
    given = swapped(jnp.concatenate([passed, share_tails], 1).astype(BF16)).astype(F32)
    share_spatial = jnp.concatenate(
        [
            jnp.where(first, kept, given[:, :main]),
            jnp.where(first, given[:, :main], kept),
            jnp.where(tail, share_tails, given[:, main:]),
        ],
        1,
    )
    return (share_spatial[None], share_temporal[None])


def solution(mesh):
    paired = mesh.shape["pipe"] == 2 and mesh.shape["dp"] == math.prod(GRID)
    return jax.shard_map(
        paired_device if paired else per_device,
        mesh=mesh,
        in_specs=(
            P("dp", None, None, None),
            P("dp"),
            P("dp", None, None, None),
            P("pipe", "dp", None),
            P("pipe", "dp", None),
        ),
        out_specs=(P("pipe", "dp", None), P("pipe", "dp", None)),
        check_vma=False,
    )
```

```python
import functools
import math

import jax
import jax.numpy as jnp
from jax import lax
from jax.experimental import pallas as pl
from jax.experimental.pallas import tpu as pltpu
from jax.sharding import PartitionSpec as P

HEIGHT = 8
WIDTH = 4
F32 = jnp.float32
BF16 = jnp.bfloat16
GRID = (4, 2, 2)
LANES = 128


def passed_along(value, axis, steps):
    count = lax.axis_size(axis)
    first, last = (max(0, -steps), min(count, count - steps))
    return lax.ppermute(value, axis, [(source, source + steps) for source in range(first, last)])


def embedding_of(step, channels):
    half_width = channels // 2
    frequency = jnp.exp(-math.log(10000.0) * jnp.arange(half_width, dtype=jnp.float32) / half_width)
    phases = step.astype(jnp.float32) * frequency
    return jnp.concatenate([jnp.sin(phases), jnp.cos(phases)])


def normalize(summed):
    return summed * lax.rsqrt(jnp.mean(summed * summed, axis=-1, keepdims=True) + 1e-06)


def spatial_columns(normed):
    frames, pixels, channels = normed.shape
    grid = normed.reshape(frames, HEIGHT, WIDTH, channels)
    padded = jnp.pad(grid, ((0, 0), (1, 1), (1, 1), (0, 0)))
    pieces = [
        padded[:, row : row + HEIGHT, col : col + WIDTH, :] for row in range(3) for col in range(3)
    ]
    return jnp.concatenate(pieces, axis=-1).reshape(frames * pixels, 9 * channels)


def spatial_fold(grads, frames, channels):
    parts = grads.reshape(frames, HEIGHT, WIDTH, 9, channels)
    padded = jnp.zeros((frames, HEIGHT + 2, WIDTH + 2, channels), jnp.float32)
    for row in range(3):
        for col in range(3):
            padded = padded.at[:, row : row + HEIGHT, col : col + WIDTH, :].add(
                parts[:, :, :, row * 3 + col, :]
            )
    return padded[:, 1 : HEIGHT + 1, 1 : WIDTH + 1, :].reshape(frames, HEIGHT * WIDTH, channels)


def temporal_columns(activated):
    frames, pixels, channels = activated.shape
    padded = jnp.pad(activated, ((1, 1), (0, 0), (0, 0)))
    pieces = [padded[tap : tap + frames] for tap in range(3)]
    return jnp.concatenate(pieces, axis=-1).reshape(frames * pixels, 3 * channels)


def temporal_fold(grads, frames, pixels, channels):
    parts = grads.reshape(frames, pixels, 3, channels)
    padded = jnp.zeros((frames + 2, pixels, channels), jnp.float32)
    for tap in range(3):
        padded = padded.at[tap : tap + frames].add(parts[:, :, tap, :])
    return padded[1 : frames + 1]


def section_forward(block_in, embedding, spatial, temporal):
    frames, pixels, channels = block_in.shape
    summed = block_in.astype(jnp.float32) + embedding
    normed = normalize(summed).astype(jnp.bfloat16)
    preact = jnp.dot(spatial_columns(normed), spatial, preferred_element_type=jnp.float32)
    activated = jax.nn.silu(preact).astype(jnp.bfloat16).reshape(frames, pixels, channels)
    mixed = jnp.dot(temporal_columns(activated), temporal, preferred_element_type=jnp.float32)
    return (block_in.astype(jnp.float32) + mixed.reshape(frames, pixels, channels)).astype(
        jnp.bfloat16
    )


def backward_first(block_in, embedding, spatial, temporal, upstream):
    frames, pixels, channels = block_in.shape
    summed = block_in.astype(jnp.float32) + embedding
    normed = normalize(summed).astype(jnp.bfloat16)
    columns = spatial_columns(normed)
    preact = jnp.dot(columns, spatial, preferred_element_type=jnp.float32)
    activated = jax.nn.silu(preact).astype(jnp.bfloat16).reshape(frames, pixels, channels)
    tcolumns = temporal_columns(activated)
    upstream_flat = upstream.reshape(frames * pixels, channels)
    temporal_term = jnp.dot(tcolumns.T, upstream_flat, preferred_element_type=jnp.float32)
    act_grad = temporal_fold(
        jnp.dot(upstream_flat, temporal.T, preferred_element_type=jnp.float32),
        frames,
        pixels,
        channels,
    )
    logistic = jax.nn.sigmoid(preact)
    slope = logistic * (1.0 + preact * (1.0 - logistic))
    pre_grad = (act_grad.reshape(frames * pixels, channels) * slope).astype(jnp.bfloat16)
    return (temporal_term, pre_grad, columns)


def backward_second(block_in, embedding, spatial, upstream, pre_grad, columns):
    frames, pixels, channels = block_in.shape
    summed = block_in.astype(jnp.float32) + embedding
    spatial_term = jnp.dot(columns.T, pre_grad, preferred_element_type=jnp.float32)
    norm_grad = spatial_fold(
        jnp.dot(pre_grad, spatial.T, preferred_element_type=jnp.float32), frames, channels
    )
    _, pullback = jax.vjp(normalize, summed)
    back_input = (upstream.astype(jnp.float32) + pullback(norm_grad)[0]).astype(jnp.bfloat16)
    return (back_input, spatial_term)


def section_backward(block_in, embedding, spatial, temporal, upstream):
    temporal_term, pre_grad, columns = backward_first(
        block_in, embedding, spatial, temporal, upstream
    )
    back_input, spatial_term = backward_second(
        block_in, embedding, spatial, upstream, pre_grad, columns
    )
    return (back_input, spatial_term, temporal_term)


def per_device(samples, timesteps, cotangent, spatial_weight, temporal_weight):
    sections = lax.axis_size("pipe")
    section_index = lax.axis_index("pipe")
    micro_count = samples.shape[0]
    frames, pixels, channels = (samples.shape[1], samples.shape[2], samples.shape[3])
    moments = jnp.arange(micro_count + sections - 1, dtype=jnp.int32)
    blank = jnp.zeros((frames, pixels, channels), jnp.bfloat16)
    full_spatial, full_temporal = (
        lax.all_gather(spatial_weight[0], "dp", axis=0, tiled=True),
        lax.all_gather(temporal_weight[0], "dp", axis=0, tiled=True),
    )

    def forward_step(carry, moment):
        incoming, stash = carry
        position = moment - section_index
        active = (position >= 0) & (position < micro_count)
        picked = jnp.clip(position, 0, micro_count - 1)
        own = lax.dynamic_index_in_dim(samples, picked, 0, keepdims=False)
        embedding = embedding_of(
            lax.dynamic_index_in_dim(timesteps, picked, 0, keepdims=False), channels
        )
        block_in = jnp.where(section_index == 0, own, incoming)
        result = lax.cond(
            active & (section_index < sections - 1),
            lambda: section_forward(block_in, embedding, full_spatial, full_temporal),
            lambda: blank,
        )
        stash = jnp.where(
            active, lax.dynamic_update_index_in_dim(stash, block_in, picked, 0), stash
        )
        passed = passed_along(result, "pipe", 1)
        return ((passed, stash), None)

    (_, stash), _ = lax.scan(forward_step, (blank, jnp.zeros_like(samples)), moments)
    back_spatial, back_temporal = (full_spatial, full_temporal)

    def inputs_at(moment, incoming):
        position = moment - (sections - 1 - section_index)
        active = (position >= 0) & (position < micro_count)
        picked = jnp.clip(position, 0, micro_count - 1)
        block_in = lax.dynamic_index_in_dim(stash, picked, 0, keepdims=False)
        embedding = embedding_of(
            lax.dynamic_index_in_dim(timesteps, picked, 0, keepdims=False), channels
        )
        given = lax.dynamic_index_in_dim(cotangent, picked, 0, keepdims=False)
        upstream = jnp.where(section_index == sections - 1, given, incoming)
        return (active, block_in, embedding, upstream)

    def backward_step(carry, moment):
        incoming, grad_spatial, grad_temporal = carry
        active, block_in, embedding, upstream = inputs_at(moment, incoming)

        def working():
            back_input, spatial_term, temporal_term = section_backward(
                block_in, embedding, back_spatial, back_temporal, upstream
            )
            return (back_input, grad_spatial + spatial_term, grad_temporal + temporal_term)

        def waiting():
            return (blank, grad_spatial, grad_temporal)

        back_input, grad_spatial, grad_temporal = lax.cond(active, working, waiting)
        passed = passed_along(back_input, "pipe", -1)
        return ((passed, grad_spatial, grad_temporal), None)

    start = (
        blank,
        jnp.zeros(back_spatial.shape, jnp.float32),
        jnp.zeros(back_temporal.shape, jnp.float32),
    )
    (_, grad_spatial, grad_temporal), _ = lax.scan(backward_step, start, moments)
    share_spatial, share_temporal = (
        lax.psum_scatter(
            grad_spatial.astype(jnp.bfloat16).astype(jnp.float32).astype(jnp.bfloat16),
            "dp",
            scatter_dimension=0,
            tiled=True,
        ).astype(jnp.float32),
        lax.psum_scatter(
            grad_temporal.astype(jnp.bfloat16).astype(jnp.float32).astype(jnp.bfloat16),
            "dp",
            scatter_dimension=0,
            tiled=True,
        ).astype(jnp.float32),
    )
    return (share_spatial[None], share_temporal[None])


def coordinates():
    index = lax.axis_index("dp")
    return index // (GRID[1] * GRID[2]), (index // GRID[2]) % GRID[1], index % GRID[2]


def shifted(value, dz=0, dy=0, dc=0):
    pairs = []
    for z in range(GRID[0]):
        for y in range(GRID[1]):
            for c in range(GRID[2]):
                place = ((z + dz) % GRID[0], (y + dy) % GRID[1], (c + dc) % GRID[2])
                pairs.append(
                    (
                        (z * GRID[1] + y) * GRID[2] + c,
                        (place[0] * GRID[1] + place[1]) * GRID[2] + place[2],
                    )
                )
    return lax.ppermute(value, "dp", pairs)


def swapped(value):
    return lax.ppermute(value, "pipe", [(0, 1), (1, 0)])


def part_of(value, index, axis):
    return lax.dynamic_index_in_dim(value, index, axis, keepdims=False)


def vmem_call(body, outs, scratch=(), flops=0, moved=0):
    return pl.pallas_call(
        body,
        out_shape=outs,
        scratch_shapes=list(scratch),
        compiler_params=pltpu.CompilerParams(vmem_limit_bytes=24 * 2**20),
        cost_estimate=pl.CostEstimate(flops=flops, bytes_accessed=moved, transcendentals=0),
    )


def after(value, earlier):
    return value if earlier is None else lax.optimization_barrier((value, earlier))[0]


def in_order(swap, own, other, axis):
    return jnp.where(
        swap, jnp.concatenate([other, own], axis), jnp.concatenate([own, other], axis)
    )


def over_z(value, pairs):
    moves = []
    for source, target in pairs:
        for rest in range(GRID[1] * GRID[2]):
            moves.append(tuple(z * GRID[1] * GRID[2] + rest for z in (source, target)))
    return lax.ppermute(value, "dp", moves)


def gathered(value, earlier=None):
    z, y, c = coordinates()
    pair_sent = over_z(value, [(0, 1), (1, 0), (2, 3), (3, 2)])
    near = in_order(z % 2 == 1, value[None], pair_sent[None], 0)
    far = over_z(after(near, earlier), [(0, 2), (2, 0), (1, 3), (3, 1)])
    line = in_order(z >= 2, near, far, 0)
    side = shifted(line, dy=1)
    plane = in_order(y == 1, line[:, None], side[:, None], 1)
    whole = in_order(c == 1, plane[:, :, None], shifted(plane, dc=1)[:, :, None], 2)
    return whole.reshape(-1, value.shape[1]), far


def added(*terms):
    return sum(term.astype(F32) for term in terms)


def summed_on_chip(value):
    _, _, c = coordinates()
    sent = shifted(part_of(value, 1 - c, 2), dc=1)
    return added(part_of(value, c, 2), sent).astype(BF16)


def summed_over_y(value, earlier):
    _, y, _ = coordinates()
    sent = shifted(after(part_of(value, 1 - y, 1), earlier), dy=1)
    return added(part_of(value, y, 1), sent).astype(BF16), sent


def summed_over_z(line):
    z, _, _ = coordinates()
    terms = [part_of(line, z, 0)] + [
        shifted(part_of(line, (z + step) % GRID[0], 0), dz=step) for step in range(1, GRID[0])
    ]
    return added(*terms)


def pixel_masks(rows):
    row = lax.broadcasted_iota(jnp.int32, (rows, 1), 0)
    high, wide = (row // WIDTH) % HEIGHT, row % WIDTH
    masks = []
    for dr in (-1, 0, 1):
        for dc in (-1, 0, 1):
            inside = (high + dr >= 0) & (high + dr < HEIGHT) & (wide + dc >= 0) & (wide + dc < WIDTH)
            masks.append((dr * WIDTH + dc, inside))
    return masks


def frame_masks(rows, frames):
    pixels = HEIGHT * WIDTH
    row = lax.broadcasted_iota(jnp.int32, (rows, 1), 0)
    frame = (row // pixels) % frames
    return [
        (step * pixels, (frame + step >= 0) & (frame + step < frames)) for step in (-1, 0, 1)
    ]


def moved_rows(value, move):
    shift, inside = move
    if shift:
        value = pltpu.roll(value, (-shift) % value.shape[0], 0)
    return jnp.where(inside, value, 0.0)


def dot(left, right, dims=((1,), (0,))):
    return lax.dot_general(left, right, (dims, ((), ())), preferred_element_type=F32)


def with_embedding(hidden, embedding_ref, samples):
    per = hidden.shape[0] // samples
    return jnp.concatenate(
        [hidden[s * per : (s + 1) * per] + embedding_ref[s : s + 1, :] for s in range(samples)]
    )


def scale_of(summed):
    return lax.rsqrt(jnp.mean(summed * summed, axis=-1, keepdims=True) + 1e-06)


def silu_parts(preact):
    logistic = 1.0 / (1.0 + jnp.exp(-preact))
    return logistic, preact * logistic


def tap_weight(weight_refs, tap, channels):
    return jnp.concatenate(
        [ref[tap * channels : (tap + 1) * channels, :] for ref in weight_refs], 1
    )


def convolved(normed, weight_refs, masks):
    rows, channels = normed.shape
    normed = normed.astype(F32)
    total = None
    for tap in range(9):
        term = dot(
            moved_rows(normed, masks[tap]).astype(BF16),
            tap_weight(weight_refs, tap, channels),
        )
        total = term if total is None else total + term
    return total


def first_forward(frames, hidden_ref, embedding_ref, keep_ref, temporal_ref, *refs):
    *spatial_refs, normed_ref, preact_ref, mixed_ref = refs
    rows = hidden_ref.shape[0]
    width = keep_ref.shape[1]
    summed = with_embedding(hidden_ref[...].astype(F32), embedding_ref, embedding_ref.shape[0])
    normed = (summed * scale_of(summed)).astype(BF16)
    normed_ref[...] = normed
    preact = convolved(normed, spatial_refs, pixel_masks(rows))
    preact_ref[...] = preact
    activated = silu_parts(preact)[1].astype(BF16).astype(F32) * keep_ref[...]
    mixed = None
    for tap, move in enumerate(frame_masks(rows, frames)):
        term = dot(
            moved_rows(activated, move).astype(BF16),
            temporal_ref[tap * width : (tap + 1) * width, :],
        )
        mixed = term if mixed is None else mixed + term
    mixed_ref[...] = mixed.astype(BF16)


def slope_of(preact):
    logistic, _ = silu_parts(preact)
    return logistic * (1.0 + preact * (1.0 - logistic))


def act_grad_of(upstream, temporal_ref, width, frames):
    upstream = upstream.astype(F32)
    moves = frame_masks(upstream.shape[0], frames)
    total = None
    for tap in range(3):
        term = dot(
            moved_rows(upstream, moves[2 - tap]).astype(BF16),
            temporal_ref[tap * width : (tap + 1) * width, :],
            ((1,), (1,)),
        )
        total = term if total is None else total + term
    return total


def store_temporal_terms(activated, upstream, frames, out_ref):
    width = activated.shape[1]
    upstream = upstream.astype(F32)
    moves = frame_masks(upstream.shape[0], frames)
    for tap in range(3):
        out_ref[tap * width : (tap + 1) * width, :] = dot(
            activated, moved_rows(upstream, moves[2 - tap]).astype(BF16), ((0,), (0,))
        ).astype(BF16)


def store_spatial_terms(normed, pre_grad, out_refs):
    channels = normed.shape[1]
    pre_grad = pre_grad.astype(F32)
    masks = pixel_masks(pre_grad.shape[0])
    for tap in range(9):
        term = dot(
            normed, moved_rows(pre_grad, masks[8 - tap]).astype(BF16), ((0,), (0,))
        ).astype(BF16)
        start = 0
        for out_ref in out_refs:
            end = start + out_ref.shape[1]
            out_ref[tap * channels : (tap + 1) * channels, :] = term[:, start:end]
            start = end


def second_forward(
    frames, hidden_ref, own_ref, sent_ref, embedding_ref, keep_ref, upstream_ref, temporal_ref, *refs
):
    *spatial_refs, next_ref, normed_ref, activated_ref, pre_grad_ref, back_ref = refs
    rows, channels = hidden_ref.shape
    width = keep_ref.shape[1]
    masks = pixel_masks(rows)
    mixed = own_ref[...].astype(F32) + sent_ref[...].astype(F32)
    hidden = (hidden_ref[...].astype(F32) + mixed).astype(BF16)
    next_ref[...] = hidden
    summed = with_embedding(hidden.astype(F32), embedding_ref, embedding_ref.shape[0])
    normed = (summed * scale_of(summed)).astype(BF16)
    normed_ref[...] = normed
    preact = convolved(normed, spatial_refs, masks)
    activated_ref[...] = (silu_parts(preact)[1] * keep_ref[...]).astype(BF16)
    act_grad = act_grad_of(upstream_ref[...], temporal_ref, width, frames)
    pre_grad = (act_grad * slope_of(preact) * keep_ref[...]).astype(BF16)
    pre_grad_ref[...] = pre_grad
    pre_grad = pre_grad.astype(F32)
    back = None
    for tap in range(9):
        term = dot(
            moved_rows(pre_grad, masks[8 - tap]).astype(BF16),
            tap_weight(spatial_refs, tap, channels),
            ((1,), (1,)),
        )
        back = term if back is None else back + term
    back_ref[...] = back.astype(BF16)


def second_terms(frames, normed_ref, pre_grad_ref, activated_ref, upstream_ref, *outs):
    *spatial_refs, temporal_ref = outs
    store_spatial_terms(normed_ref[...], pre_grad_ref[...], spatial_refs)
    store_temporal_terms(activated_ref[...], upstream_ref[...], frames, temporal_ref)


def first_terms(
    frames, hidden_ref, embedding_ref, upstream_ref, own_ref, sent_ref, normed_ref, preact_ref,
    keep_ref, temporal_ref, *outs
):
    *spatial_outs, temporal_out = outs
    width = keep_ref.shape[1]
    channels = hidden_ref.shape[1]
    summed = with_embedding(hidden_ref[...].astype(F32), embedding_ref, embedding_ref.shape[0])
    scale = scale_of(summed)
    grad = own_ref[...].astype(F32) + sent_ref[...].astype(F32)
    inner = jnp.sum(grad * summed, axis=-1, keepdims=True)
    back = grad * scale - summed * (scale * scale * scale) * (inner / channels)
    upstream = (upstream_ref[...].astype(F32) + back).astype(BF16)
    preact = preact_ref[...]
    activated = (silu_parts(preact)[1] * keep_ref[...]).astype(BF16)
    act_grad = act_grad_of(upstream, temporal_ref, width, frames)
    pre_grad = (act_grad * slope_of(preact) * keep_ref[...]).astype(BF16)
    store_spatial_terms(normed_ref[...], pre_grad, spatial_outs)
    store_temporal_terms(activated, upstream, frames, temporal_out)


def paired_device(samples, timesteps, cotangent, spatial_weight, temporal_weight):
    me = lax.axis_index("pipe")
    first = me == 0
    _, _, c = coordinates()
    count, frames, pixels, channels = samples.shape
    rows = count * frames * pixels
    main = 2 * LANES
    width = main + LANES
    hidden = samples.reshape(rows, channels)
    upstream = cotangent.reshape(rows, channels)
    embedding = jax.vmap(lambda step: embedding_of(step, channels))(timesteps)
    lane = jnp.arange(LANES)
    keep_own = jnp.concatenate([jnp.ones(main), lane < LANES // 2]).astype(F32)[None]
    keep_other = jnp.concatenate([jnp.ones(main), lane >= LANES // 2]).astype(F32)[None]
    keep_first = jnp.where(first, keep_own, keep_other)
    keep_second = jnp.where(first, keep_other, keep_own)
    tail = lane[None] < LANES // 2

    def main_of(value, index, axis):
        return lax.dynamic_slice_in_dim(value, index * main, main, axis)

    spatial_own = spatial_weight[0]
    given = swapped(
        jnp.concatenate([main_of(spatial_own, 1 - me, 1), spatial_own[:, 2 * main :]], 1)
    )
    main_own, main_given = main_of(spatial_own, me, 1), given[:, :main]
    tails = jnp.where(tail, spatial_own[:, 2 * main :], given[:, main:])
    main_first = jnp.where(first, main_own, main_given)
    main_second = jnp.where(first, main_given, main_own)
    temporal_own = lax.all_gather(temporal_weight[0], "dp", axis=0, tiled=True)
    temporal_own = temporal_own.reshape(3, channels, channels)
    main_first, far = gathered(main_first)
    tails, _ = gathered(tails, far)
    main_second = lax.all_gather(main_second, "dp", axis=0, tiled=True)
    spatial_first = [main_first, tails]
    spatial_second = [main_second, tails]

    def local_rows(index):
        return jnp.concatenate(
            [main_of(temporal_own, index, 1), temporal_own[:, 2 * main :]], 1
        ).reshape(GRID[2], -1, channels)

    half = swapped(part_of(local_rows(1 - me), c, 0))
    other_half = shifted(half, dc=1)
    temporal_other = jnp.where(
        c == 0, jnp.concatenate([half, other_half]), jnp.concatenate([other_half, half])
    )
    temporal_mine = local_rows(me).reshape(3 * width, channels)
    temporal_first = jnp.where(first, temporal_mine, temporal_other)
    temporal_second = jnp.where(first, temporal_other, temporal_mine)

    def shape(extent, dtype=BF16):
        return jax.ShapeDtypeStruct(extent, dtype)

    spatial_flops = 2 * rows * 9 * channels * width
    temporal_flops = 2 * rows * 3 * channels * width
    spatial_bytes = 2 * 9 * channels * width
    temporal_bytes = 2 * 3 * channels * width
    normed_first, preact_first, mixed = vmem_call(
        functools.partial(first_forward, frames),
        (shape((rows, channels)), shape((rows, width), F32), shape((rows, channels))),
        flops=spatial_flops + temporal_flops,
        moved=spatial_bytes + temporal_bytes,
    )(hidden, embedding, keep_first, temporal_first, *spatial_first)
    hidden_second, normed_second, activated_second, pre_grad_second, back = vmem_call(
        functools.partial(second_forward, frames),
        (
            shape((rows, channels)),
            shape((rows, channels)),
            shape((rows, width)),
            shape((rows, width)),
            shape((rows, channels)),
        ),
        flops=2 * spatial_flops + temporal_flops,
        moved=spatial_bytes + temporal_bytes,
    )(
        hidden, mixed, swapped(mixed), embedding, keep_second, upstream, temporal_second,
        *spatial_second,
    )

    def terms_shape():
        return (
            shape((9 * channels, main)),
            shape((9 * channels, width - main)),
            shape((3 * width, channels)),
        )

    def on_chip(terms):
        return summed_on_chip(terms.reshape(*GRID, -1, terms.shape[1]))

    back_given = swapped(back)
    main_terms_second, tail_terms_second, temporal_terms_second = vmem_call(
        functools.partial(second_terms, frames),
        terms_shape(),
        flops=spatial_flops + temporal_flops,
        moved=spatial_bytes + temporal_bytes,
    )(normed_second, pre_grad_second, activated_second, upstream)
    share_second = lax.psum_scatter(
        main_terms_second, "dp", scatter_dimension=0, tiled=True
    ).astype(F32)
    main_terms_first, tail_terms_first, temporal_terms_first = vmem_call(
        functools.partial(first_terms, frames),
        terms_shape(),
        flops=spatial_flops + 2 * temporal_flops,
        moved=spatial_bytes + 2 * temporal_bytes,
    )(
        hidden_second, embedding, upstream, back, back_given, normed_first, preact_first,
        keep_first, temporal_first,
    )
    chip_tails = on_chip(tail_terms_first + tail_terms_second)
    chip_first = on_chip(main_terms_first)

    terms = jnp.stack(
        [
            jnp.where(first, temporal_terms_first, temporal_terms_second),
            jnp.where(first, temporal_terms_second, temporal_terms_first),
        ]
    ).reshape(2, GRID[2], -1, channels)
    sent = shifted(part_of(terms, 1 - c, 1), dc=1)
    halves = added(part_of(terms, c, 1), sent).astype(BF16)
    half_given = swapped(halves[1])
    halves = jnp.stack([halves[0], half_given])
    other_halves = shifted(halves, dc=1)
    both = jnp.where(
        c == 0,
        jnp.stack([halves, other_halves], 1),
        jnp.stack([other_halves, halves], 1),
    ).reshape(2, 3, width, channels)
    mine, theirs = both[0], both[1]
    full = jnp.concatenate(
        [
            jnp.where(first, mine[:, :main], theirs[:, :main]),
            jnp.where(first, theirs[:, :main], mine[:, :main]),
            mine[:, main:] + theirs[:, main:],
        ],
        1,
    )
    full = part_of(full.reshape(*GRID, -1, channels), c, 2)

    line_tails, side_tails = summed_over_y(chip_tails, sent)
    line_first, side_first = summed_over_y(chip_first, None)
    share_tails = summed_over_z(line_tails)
    line, _ = summed_over_y(full[..., : 3 * LANES], side_tails)
    share_first = summed_over_z(after(line_first, other_halves))
    line_end, _ = summed_over_y(full[..., 3 * LANES :], side_first)
    share_temporal = jnp.concatenate([summed_over_z(line), summed_over_z(line_end)], 1)

    kept = jnp.where(first, share_first, share_second)
    passed = jnp.where(first, share_second, share_first)
    given = swapped(jnp.concatenate([passed, share_tails], 1).astype(BF16)).astype(F32)
    share_spatial = jnp.concatenate(
        [
            jnp.where(first, kept, given[:, :main]),
            jnp.where(first, given[:, :main], kept),
            jnp.where(tail, share_tails, given[:, main:]),
        ],
        1,
    )
    return (share_spatial[None], share_temporal[None])


def solution(mesh):
    paired = mesh.shape["pipe"] == 2 and mesh.shape["dp"] == math.prod(GRID)
    return jax.shard_map(
        paired_device if paired else per_device,
        mesh=mesh,
        in_specs=(
            P("dp", None, None, None),
            P("dp"),
            P("dp", None, None, None),
            P("pipe", "dp", None),
            P("pipe", "dp", None),
        ),
        out_specs=(P("pipe", "dp", None), P("pipe", "dp", None)),
        check_vma=False,
    )
```

```python
import functools
import math

import jax
import jax.numpy as jnp
from jax import lax
from jax.experimental import pallas as pl
from jax.experimental.pallas import tpu as pltpu
from jax.sharding import PartitionSpec as P

HEIGHT = 8
WIDTH = 4
F32 = jnp.float32
BF16 = jnp.bfloat16
GRID = (4, 2, 2)
LANES = 128


def passed_along(value, axis, steps):
    count = lax.axis_size(axis)
    first, last = (max(0, -steps), min(count, count - steps))
    return lax.ppermute(value, axis, [(source, source + steps) for source in range(first, last)])


def embedding_of(step, channels):
    half_width = channels // 2
    frequency = jnp.exp(-math.log(10000.0) * jnp.arange(half_width, dtype=jnp.float32) / half_width)
    phases = step.astype(jnp.float32) * frequency
    return jnp.concatenate([jnp.sin(phases), jnp.cos(phases)])


def normalize(summed):
    return summed * lax.rsqrt(jnp.mean(summed * summed, axis=-1, keepdims=True) + 1e-06)


def spatial_columns(normed):
    frames, pixels, channels = normed.shape
    grid = normed.reshape(frames, HEIGHT, WIDTH, channels)
    padded = jnp.pad(grid, ((0, 0), (1, 1), (1, 1), (0, 0)))
    pieces = [
        padded[:, row : row + HEIGHT, col : col + WIDTH, :] for row in range(3) for col in range(3)
    ]
    return jnp.concatenate(pieces, axis=-1).reshape(frames * pixels, 9 * channels)


def spatial_fold(grads, frames, channels):
    parts = grads.reshape(frames, HEIGHT, WIDTH, 9, channels)
    padded = jnp.zeros((frames, HEIGHT + 2, WIDTH + 2, channels), jnp.float32)
    for row in range(3):
        for col in range(3):
            padded = padded.at[:, row : row + HEIGHT, col : col + WIDTH, :].add(
                parts[:, :, :, row * 3 + col, :]
            )
    return padded[:, 1 : HEIGHT + 1, 1 : WIDTH + 1, :].reshape(frames, HEIGHT * WIDTH, channels)


def temporal_columns(activated):
    frames, pixels, channels = activated.shape
    padded = jnp.pad(activated, ((1, 1), (0, 0), (0, 0)))
    pieces = [padded[tap : tap + frames] for tap in range(3)]
    return jnp.concatenate(pieces, axis=-1).reshape(frames * pixels, 3 * channels)


def temporal_fold(grads, frames, pixels, channels):
    parts = grads.reshape(frames, pixels, 3, channels)
    padded = jnp.zeros((frames + 2, pixels, channels), jnp.float32)
    for tap in range(3):
        padded = padded.at[tap : tap + frames].add(parts[:, :, tap, :])
    return padded[1 : frames + 1]


def section_forward(block_in, embedding, spatial, temporal):
    frames, pixels, channels = block_in.shape
    summed = block_in.astype(jnp.float32) + embedding
    normed = normalize(summed).astype(jnp.bfloat16)
    preact = jnp.dot(spatial_columns(normed), spatial, preferred_element_type=jnp.float32)
    activated = jax.nn.silu(preact).astype(jnp.bfloat16).reshape(frames, pixels, channels)
    mixed = jnp.dot(temporal_columns(activated), temporal, preferred_element_type=jnp.float32)
    return (block_in.astype(jnp.float32) + mixed.reshape(frames, pixels, channels)).astype(
        jnp.bfloat16
    )


def backward_first(block_in, embedding, spatial, temporal, upstream):
    frames, pixels, channels = block_in.shape
    summed = block_in.astype(jnp.float32) + embedding
    normed = normalize(summed).astype(jnp.bfloat16)
    columns = spatial_columns(normed)
    preact = jnp.dot(columns, spatial, preferred_element_type=jnp.float32)
    activated = jax.nn.silu(preact).astype(jnp.bfloat16).reshape(frames, pixels, channels)
    tcolumns = temporal_columns(activated)
    upstream_flat = upstream.reshape(frames * pixels, channels)
    temporal_term = jnp.dot(tcolumns.T, upstream_flat, preferred_element_type=jnp.float32)
    act_grad = temporal_fold(
        jnp.dot(upstream_flat, temporal.T, preferred_element_type=jnp.float32),
        frames,
        pixels,
        channels,
    )
    logistic = jax.nn.sigmoid(preact)
    slope = logistic * (1.0 + preact * (1.0 - logistic))
    pre_grad = (act_grad.reshape(frames * pixels, channels) * slope).astype(jnp.bfloat16)
    return (temporal_term, pre_grad, columns)


def backward_second(block_in, embedding, spatial, upstream, pre_grad, columns):
    frames, pixels, channels = block_in.shape
    summed = block_in.astype(jnp.float32) + embedding
    spatial_term = jnp.dot(columns.T, pre_grad, preferred_element_type=jnp.float32)
    norm_grad = spatial_fold(
        jnp.dot(pre_grad, spatial.T, preferred_element_type=jnp.float32), frames, channels
    )
    _, pullback = jax.vjp(normalize, summed)
    back_input = (upstream.astype(jnp.float32) + pullback(norm_grad)[0]).astype(jnp.bfloat16)
    return (back_input, spatial_term)


def section_backward(block_in, embedding, spatial, temporal, upstream):
    temporal_term, pre_grad, columns = backward_first(
        block_in, embedding, spatial, temporal, upstream
    )
    back_input, spatial_term = backward_second(
        block_in, embedding, spatial, upstream, pre_grad, columns
    )
    return (back_input, spatial_term, temporal_term)


def per_device(samples, timesteps, cotangent, spatial_weight, temporal_weight):
    sections = lax.axis_size("pipe")
    section_index = lax.axis_index("pipe")
    micro_count = samples.shape[0]
    frames, pixels, channels = (samples.shape[1], samples.shape[2], samples.shape[3])
    moments = jnp.arange(micro_count + sections - 1, dtype=jnp.int32)
    blank = jnp.zeros((frames, pixels, channels), jnp.bfloat16)
    full_spatial, full_temporal = (
        lax.all_gather(spatial_weight[0], "dp", axis=0, tiled=True),
        lax.all_gather(temporal_weight[0], "dp", axis=0, tiled=True),
    )

    def forward_step(carry, moment):
        incoming, stash = carry
        position = moment - section_index
        active = (position >= 0) & (position < micro_count)
        picked = jnp.clip(position, 0, micro_count - 1)
        own = lax.dynamic_index_in_dim(samples, picked, 0, keepdims=False)
        embedding = embedding_of(
            lax.dynamic_index_in_dim(timesteps, picked, 0, keepdims=False), channels
        )
        block_in = jnp.where(section_index == 0, own, incoming)
        result = lax.cond(
            active & (section_index < sections - 1),
            lambda: section_forward(block_in, embedding, full_spatial, full_temporal),
            lambda: blank,
        )
        stash = jnp.where(
            active, lax.dynamic_update_index_in_dim(stash, block_in, picked, 0), stash
        )
        passed = passed_along(result, "pipe", 1)
        return ((passed, stash), None)

    (_, stash), _ = lax.scan(forward_step, (blank, jnp.zeros_like(samples)), moments)
    back_spatial, back_temporal = (full_spatial, full_temporal)

    def inputs_at(moment, incoming):
        position = moment - (sections - 1 - section_index)
        active = (position >= 0) & (position < micro_count)
        picked = jnp.clip(position, 0, micro_count - 1)
        block_in = lax.dynamic_index_in_dim(stash, picked, 0, keepdims=False)
        embedding = embedding_of(
            lax.dynamic_index_in_dim(timesteps, picked, 0, keepdims=False), channels
        )
        given = lax.dynamic_index_in_dim(cotangent, picked, 0, keepdims=False)
        upstream = jnp.where(section_index == sections - 1, given, incoming)
        return (active, block_in, embedding, upstream)

    def backward_step(carry, moment):
        incoming, grad_spatial, grad_temporal = carry
        active, block_in, embedding, upstream = inputs_at(moment, incoming)

        def working():
            back_input, spatial_term, temporal_term = section_backward(
                block_in, embedding, back_spatial, back_temporal, upstream
            )
            return (back_input, grad_spatial + spatial_term, grad_temporal + temporal_term)

        def waiting():
            return (blank, grad_spatial, grad_temporal)

        back_input, grad_spatial, grad_temporal = lax.cond(active, working, waiting)
        passed = passed_along(back_input, "pipe", -1)
        return ((passed, grad_spatial, grad_temporal), None)

    start = (
        blank,
        jnp.zeros(back_spatial.shape, jnp.float32),
        jnp.zeros(back_temporal.shape, jnp.float32),
    )
    (_, grad_spatial, grad_temporal), _ = lax.scan(backward_step, start, moments)
    share_spatial, share_temporal = (
        lax.psum_scatter(
            grad_spatial.astype(jnp.bfloat16).astype(jnp.float32).astype(jnp.bfloat16),
            "dp",
            scatter_dimension=0,
            tiled=True,
        ).astype(jnp.float32),
        lax.psum_scatter(
            grad_temporal.astype(jnp.bfloat16).astype(jnp.float32).astype(jnp.bfloat16),
            "dp",
            scatter_dimension=0,
            tiled=True,
        ).astype(jnp.float32),
    )
    return (share_spatial[None], share_temporal[None])


def coordinates():
    index = lax.axis_index("dp")
    return index // (GRID[1] * GRID[2]), (index // GRID[2]) % GRID[1], index % GRID[2]


def shifted(value, dz=0, dy=0, dc=0):
    pairs = []
    for z in range(GRID[0]):
        for y in range(GRID[1]):
            for c in range(GRID[2]):
                place = ((z + dz) % GRID[0], (y + dy) % GRID[1], (c + dc) % GRID[2])
                pairs.append(
                    (
                        (z * GRID[1] + y) * GRID[2] + c,
                        (place[0] * GRID[1] + place[1]) * GRID[2] + place[2],
                    )
                )
    return lax.ppermute(value, "dp", pairs)


def swapped(value):
    return lax.ppermute(value, "pipe", [(0, 1), (1, 0)])


def part_of(value, index, axis):
    return lax.dynamic_index_in_dim(value, index, axis, keepdims=False)


def vmem_call(body, outs, scratch=(), flops=0, moved=0):
    return pl.pallas_call(
        body,
        out_shape=outs,
        scratch_shapes=list(scratch),
        compiler_params=pltpu.CompilerParams(vmem_limit_bytes=24 * 2**20),
        cost_estimate=pl.CostEstimate(flops=flops, bytes_accessed=moved, transcendentals=0),
    )


def after(value, earlier):
    return value if earlier is None else lax.optimization_barrier((value, earlier))[0]


def in_order(swap, own, other, axis):
    return jnp.where(
        swap, jnp.concatenate([other, own], axis), jnp.concatenate([own, other], axis)
    )


def over_z(value, pairs):
    moves = []
    for source, target in pairs:
        for rest in range(GRID[1] * GRID[2]):
            moves.append(tuple(z * GRID[1] * GRID[2] + rest for z in (source, target)))
    return lax.ppermute(value, "dp", moves)


def gathered(value, chunks, earlier=None, last=None):
    z, y, c = coordinates()
    before = chunks[-1] if chunks else (None, None)
    pair_sent = over_z(after(value, before[0]), [(0, 1), (1, 0), (2, 3), (3, 2)])
    near = in_order(z % 2 == 1, value[None], pair_sent[None], 0)
    middle = over_z(near, [(1, 2), (2, 1)])
    outer = over_z(middle, [(1, 0), (2, 3)])
    far = jnp.where((z == 1) | (z == 2), middle, outer)
    line = in_order(z >= 2, near, far, 0)
    side = shifted(after(after(line, before[1]), earlier), dy=1)
    plane = after(in_order(y == 1, line[:, None], side[:, None], 1), last)
    whole = in_order(c == 1, plane[:, :, None], shifted(plane, dc=1)[:, :, None], 2)
    chunks.append((pair_sent, side))
    return whole.reshape(-1, value.shape[1])


def added(*terms):
    return sum(term.astype(F32) for term in terms)


def summed_on_chip(value):
    _, _, c = coordinates()
    sent = shifted(part_of(value, 1 - c, 2), dc=1)
    return added(part_of(value, c, 2), sent).astype(BF16)


def summed_over_y(value, earlier):
    _, y, _ = coordinates()
    sent = shifted(after(part_of(value, 1 - y, 1), earlier), dy=1)
    return added(part_of(value, y, 1), sent).astype(BF16), sent


def summed_over_z(line):
    z, _, _ = coordinates()
    pairs = line.reshape(2, 2, *line.shape[1:])
    near, far = part_of(pairs, z // 2, 0), part_of(pairs, 1 - z // 2, 0)
    far = added(far, over_z(far, [(0, 1), (3, 2)])).astype(BF16)
    near = added(near, over_z(far, [(1, 2), (2, 1)])).astype(BF16)
    sent = over_z(part_of(near, 1 - z % 2, 0), [(0, 1), (1, 0), (2, 3), (3, 2)])
    return added(part_of(near, z % 2, 0), sent)


def summed_over_z_at_once(line):
    z, _, _ = coordinates()
    terms = [part_of(line, z, 0)] + [
        shifted(part_of(line, (z + step) % GRID[0], 0), dz=step) for step in range(1, GRID[0])
    ]
    return added(*terms)


def pixel_masks(rows):
    row = lax.broadcasted_iota(jnp.int32, (rows, 1), 0)
    high, wide = (row // WIDTH) % HEIGHT, row % WIDTH
    masks = []
    for dr in (-1, 0, 1):
        for dc in (-1, 0, 1):
            inside = (high + dr >= 0) & (high + dr < HEIGHT) & (wide + dc >= 0) & (wide + dc < WIDTH)
            masks.append((dr * WIDTH + dc, inside))
    return masks


def frame_masks(rows, frames):
    pixels = HEIGHT * WIDTH
    row = lax.broadcasted_iota(jnp.int32, (rows, 1), 0)
    frame = (row // pixels) % frames
    return [
        (step * pixels, (frame + step >= 0) & (frame + step < frames)) for step in (-1, 0, 1)
    ]


def moved_rows(value, move):
    shift, inside = move
    if shift:
        value = pltpu.roll(value, (-shift) % value.shape[0], 0)
    return jnp.where(inside, value, 0.0)


def dot(left, right, dims=((1,), (0,))):
    return lax.dot_general(left, right, (dims, ((), ())), preferred_element_type=F32)


def with_embedding(hidden, embedding_ref, samples):
    per = hidden.shape[0] // samples
    return jnp.concatenate(
        [hidden[s * per : (s + 1) * per] + embedding_ref[s : s + 1, :] for s in range(samples)]
    )


def scale_of(summed):
    return lax.rsqrt(jnp.mean(summed * summed, axis=-1, keepdims=True) + 1e-06)


def silu_parts(preact):
    logistic = 1.0 / (1.0 + jnp.exp(-preact))
    return logistic, preact * logistic


def tap_weight(weight_refs, tap, channels):
    return jnp.concatenate(
        [ref[tap * channels : (tap + 1) * channels, :] for ref in weight_refs], 1
    )


def convolved(normed, weight_refs, masks):
    rows, channels = normed.shape
    normed = normed.astype(F32)
    total = None
    for tap in range(9):
        term = dot(
            moved_rows(normed, masks[tap]).astype(BF16),
            tap_weight(weight_refs, tap, channels),
        )
        total = term if total is None else total + term
    return total


def first_forward(frames, hidden_ref, embedding_ref, keep_ref, temporal_ref, *refs):
    *spatial_refs, normed_ref, preact_ref, mixed_ref = refs
    rows = hidden_ref.shape[0]
    width = keep_ref.shape[1]
    summed = with_embedding(hidden_ref[...].astype(F32), embedding_ref, embedding_ref.shape[0])
    normed = (summed * scale_of(summed)).astype(BF16)
    normed_ref[...] = normed
    preact = convolved(normed, spatial_refs, pixel_masks(rows))
    preact_ref[...] = preact
    activated = silu_parts(preact)[1].astype(BF16).astype(F32) * keep_ref[...]
    mixed = None
    for tap, move in enumerate(frame_masks(rows, frames)):
        term = dot(
            moved_rows(activated, move).astype(BF16),
            temporal_ref[tap * width : (tap + 1) * width, :],
        )
        mixed = term if mixed is None else mixed + term
    mixed_ref[...] = mixed.astype(BF16)


def slope_of(preact):
    logistic, _ = silu_parts(preact)
    return logistic * (1.0 + preact * (1.0 - logistic))


def act_grad_of(upstream, temporal_ref, width, frames):
    upstream = upstream.astype(F32)
    moves = frame_masks(upstream.shape[0], frames)
    total = None
    for tap in range(3):
        term = dot(
            moved_rows(upstream, moves[2 - tap]).astype(BF16),
            temporal_ref[tap * width : (tap + 1) * width, :],
            ((1,), (1,)),
        )
        total = term if total is None else total + term
    return total


def store_temporal_terms(activated, upstream, frames, out_ref):
    width = activated.shape[1]
    upstream = upstream.astype(F32)
    moves = frame_masks(upstream.shape[0], frames)
    for tap in range(3):
        out_ref[tap * width : (tap + 1) * width, :] = dot(
            activated, moved_rows(upstream, moves[2 - tap]).astype(BF16), ((0,), (0,))
        ).astype(BF16)


def store_spatial_terms(normed, pre_grad, out_refs):
    channels = normed.shape[1]
    pre_grad = pre_grad.astype(F32)
    masks = pixel_masks(pre_grad.shape[0])
    for tap in range(9):
        term = dot(
            normed, moved_rows(pre_grad, masks[8 - tap]).astype(BF16), ((0,), (0,))
        ).astype(BF16)
        start = 0
        for out_ref in out_refs:
            end = start + out_ref.shape[1]
            out_ref[tap * channels : (tap + 1) * channels, :] = term[:, start:end]
            start = end


def second_forward(
    frames, hidden_ref, own_ref, sent_ref, embedding_ref, keep_ref, upstream_ref, temporal_ref, *refs
):
    *spatial_refs, next_ref, normed_ref, activated_ref, pre_grad_ref, back_ref = refs
    rows, channels = hidden_ref.shape
    width = keep_ref.shape[1]
    masks = pixel_masks(rows)
    mixed = own_ref[...].astype(F32) + sent_ref[...].astype(F32)
    hidden = (hidden_ref[...].astype(F32) + mixed).astype(BF16)
    next_ref[...] = hidden
    summed = with_embedding(hidden.astype(F32), embedding_ref, embedding_ref.shape[0])
    normed = (summed * scale_of(summed)).astype(BF16)
    normed_ref[...] = normed
    preact = convolved(normed, spatial_refs, masks)
    activated_ref[...] = (silu_parts(preact)[1] * keep_ref[...]).astype(BF16)
    act_grad = act_grad_of(upstream_ref[...], temporal_ref, width, frames)
    pre_grad = (act_grad * slope_of(preact) * keep_ref[...]).astype(BF16)
    pre_grad_ref[...] = pre_grad
    pre_grad = pre_grad.astype(F32)
    back = None
    for tap in range(9):
        term = dot(
            moved_rows(pre_grad, masks[8 - tap]).astype(BF16),
            tap_weight(spatial_refs, tap, channels),
            ((1,), (1,)),
        )
        back = term if back is None else back + term
    back_ref[...] = back.astype(BF16)


def second_terms(frames, normed_ref, pre_grad_ref, activated_ref, upstream_ref, *outs):
    *spatial_refs, temporal_ref = outs
    store_spatial_terms(normed_ref[...], pre_grad_ref[...], spatial_refs)
    store_temporal_terms(activated_ref[...], upstream_ref[...], frames, temporal_ref)


def first_terms(
    frames, hidden_ref, embedding_ref, upstream_ref, own_ref, sent_ref, normed_ref, preact_ref,
    keep_ref, temporal_ref, *outs
):
    *spatial_outs, temporal_out = outs
    width = keep_ref.shape[1]
    channels = hidden_ref.shape[1]
    summed = with_embedding(hidden_ref[...].astype(F32), embedding_ref, embedding_ref.shape[0])
    scale = scale_of(summed)
    grad = own_ref[...].astype(F32) + sent_ref[...].astype(F32)
    inner = jnp.sum(grad * summed, axis=-1, keepdims=True)
    back = grad * scale - summed * (scale * scale * scale) * (inner / channels)
    upstream = (upstream_ref[...].astype(F32) + back).astype(BF16)
    preact = preact_ref[...]
    activated = (silu_parts(preact)[1] * keep_ref[...]).astype(BF16)
    act_grad = act_grad_of(upstream, temporal_ref, width, frames)
    pre_grad = (act_grad * slope_of(preact) * keep_ref[...]).astype(BF16)
    store_spatial_terms(normed_ref[...], pre_grad, spatial_outs)
    store_temporal_terms(activated, upstream, frames, temporal_out)


def paired_device(samples, timesteps, cotangent, spatial_weight, temporal_weight):
    me = lax.axis_index("pipe")
    first = me == 0
    _, _, c = coordinates()
    count, frames, pixels, channels = samples.shape
    rows = count * frames * pixels
    main = 2 * LANES
    width = main + LANES
    hidden = samples.reshape(rows, channels)
    upstream = cotangent.reshape(rows, channels)
    embedding = jax.vmap(lambda step: embedding_of(step, channels))(timesteps)
    lane = jnp.arange(LANES)
    keep_own = jnp.concatenate([jnp.ones(main), lane < LANES // 2]).astype(F32)[None]
    keep_other = jnp.concatenate([jnp.ones(main), lane >= LANES // 2]).astype(F32)[None]
    keep_first = jnp.where(first, keep_own, keep_other)
    keep_second = jnp.where(first, keep_other, keep_own)
    tail = lane[None] < LANES // 2

    def main_of(value, index, axis):
        return lax.dynamic_slice_in_dim(value, index * main, main, axis)

    spatial_own = spatial_weight[0]
    given = swapped(
        jnp.concatenate([main_of(spatial_own, 1 - me, 1), spatial_own[:, 2 * main :]], 1)
    )
    main_own, main_given = main_of(spatial_own, me, 1), given[:, :main]
    tails = jnp.where(tail, spatial_own[:, 2 * main :], given[:, main:])
    main_first = jnp.where(first, main_own, main_given)
    main_second = jnp.where(first, main_given, main_own)
    chunks = []
    temporal_own = gathered(temporal_weight[0], chunks).reshape(3, channels, channels)
    main_first = gathered(main_first, chunks)
    tails = gathered(tails, chunks)
    spatial_first = [main_first, tails]

    def local_rows(index):
        return jnp.concatenate(
            [main_of(temporal_own, index, 1), temporal_own[:, 2 * main :]], 1
        ).reshape(GRID[2], -1, channels)

    half = swapped(part_of(local_rows(1 - me), c, 0))
    other_half = shifted(half, dc=1)
    temporal_other = jnp.where(
        c == 0, jnp.concatenate([half, other_half]), jnp.concatenate([other_half, half])
    )
    temporal_mine = local_rows(me).reshape(3 * width, channels)
    temporal_first = jnp.where(first, temporal_mine, temporal_other)
    temporal_second = jnp.where(first, temporal_other, temporal_mine)

    def shape(extent, dtype=BF16):
        return jax.ShapeDtypeStruct(extent, dtype)

    spatial_flops = 2 * rows * 9 * channels * width
    temporal_flops = 2 * rows * 3 * channels * width
    spatial_bytes = 2 * 9 * channels * width
    temporal_bytes = 2 * 3 * channels * width
    normed_first, preact_first, mixed = vmem_call(
        functools.partial(first_forward, frames),
        (shape((rows, channels)), shape((rows, width), F32), shape((rows, channels))),
        flops=spatial_flops + temporal_flops,
        moved=spatial_bytes + temporal_bytes,
    )(hidden, embedding, keep_first, temporal_first, *spatial_first)
    mixed_given = swapped(mixed)
    low = gathered(main_second[:, :LANES], chunks)
    high = gathered(main_second[:, LANES:], chunks, mixed, mixed_given)
    spatial_second = [low, high, tails]
    hidden_second, normed_second, activated_second, pre_grad_second, back = vmem_call(
        functools.partial(second_forward, frames),
        (
            shape((rows, channels)),
            shape((rows, channels)),
            shape((rows, width)),
            shape((rows, width)),
            shape((rows, channels)),
        ),
        flops=2 * spatial_flops + temporal_flops,
        moved=spatial_bytes + temporal_bytes,
    )(
        hidden, mixed, mixed_given, embedding, keep_second, upstream, temporal_second,
        *spatial_second,
    )

    def terms_shape():
        return (
            shape((9 * channels, main)),
            shape((9 * channels, width - main)),
            shape((3 * width, channels)),
        )

    def on_chip(terms):
        return summed_on_chip(terms.reshape(*GRID, -1, terms.shape[1]))

    back_given = swapped(back)
    main_terms_second, tail_terms_second, temporal_terms_second = vmem_call(
        functools.partial(second_terms, frames),
        terms_shape(),
        flops=spatial_flops + temporal_flops,
        moved=spatial_bytes + temporal_bytes,
    )(normed_second, pre_grad_second, activated_second, upstream)
    chip_second = on_chip(main_terms_second)
    back_given = after(back_given, chip_second)
    line_low, side_low = summed_over_y(chip_second[..., :LANES], None)
    line_high, side_high = summed_over_y(chip_second[..., LANES:], side_low)
    share_second = jnp.concatenate([summed_over_z(line_low), summed_over_z(line_high)], 1)
    main_terms_first, tail_terms_first, temporal_terms_first = vmem_call(
        functools.partial(first_terms, frames),
        terms_shape(),
        flops=spatial_flops + 2 * temporal_flops,
        moved=spatial_bytes + 2 * temporal_bytes,
    )(
        hidden_second, embedding, upstream, back, back_given, normed_first, preact_first,
        keep_first, temporal_first,
    )
    chip_tails = on_chip(tail_terms_first + tail_terms_second)
    chip_first = on_chip(main_terms_first)

    terms = jnp.stack(
        [
            jnp.where(first, temporal_terms_first, temporal_terms_second),
            jnp.where(first, temporal_terms_second, temporal_terms_first),
        ]
    ).reshape(2, GRID[2], -1, channels)
    sent = shifted(part_of(terms, 1 - c, 1), dc=1)
    halves = added(part_of(terms, c, 1), sent).astype(BF16)
    half_given = swapped(halves[1])
    halves = jnp.stack([halves[0], half_given])
    other_halves = shifted(halves, dc=1)
    both = jnp.where(
        c == 0,
        jnp.stack([halves, other_halves], 1),
        jnp.stack([other_halves, halves], 1),
    ).reshape(2, 3, width, channels)
    mine, theirs = both[0], both[1]
    full = jnp.concatenate(
        [
            jnp.where(first, mine[:, :main], theirs[:, :main]),
            jnp.where(first, theirs[:, :main], mine[:, :main]),
            mine[:, main:] + theirs[:, main:],
        ],
        1,
    )
    full = part_of(full.reshape(*GRID, -1, channels), c, 2)

    line_tails, side = summed_over_y(chip_tails, (side_high, sent))
    share_tails = summed_over_z(line_tails)
    line_low, side = summed_over_y(chip_first[..., :LANES], side)
    line_high, side = summed_over_y(chip_first[..., LANES:], (side, half_given))
    share_first = jnp.concatenate(
        [summed_over_z(line_low), summed_over_z(after(line_high, other_halves))], 1
    )
    line, side = summed_over_y(full[..., : 3 * LANES], side)
    line_end, side = summed_over_y(full[..., 3 * LANES :], side)
    share_temporal = jnp.concatenate([summed_over_z(line), summed_over_z_at_once(line_end)], 1)

    kept = jnp.where(first, share_first, share_second)
    passed = jnp.where(first, share_second, share_first)
    given = jnp.concatenate([passed, share_tails], 1).astype(BF16)
    given = swapped(after(given, side)).astype(F32)
    share_spatial = jnp.concatenate(
        [
            jnp.where(first, kept, given[:, :main]),
            jnp.where(first, given[:, :main], kept),
            jnp.where(tail, share_tails, given[:, main:]),
        ],
        1,
    )
    return (share_spatial[None], share_temporal[None])


def solution(mesh):
    paired = mesh.shape["pipe"] == 2 and mesh.shape["dp"] == math.prod(GRID)
    return jax.shard_map(
        paired_device if paired else per_device,
        mesh=mesh,
        in_specs=(
            P("dp", None, None, None),
            P("dp"),
            P("dp", None, None, None),
            P("pipe", "dp", None),
            P("pipe", "dp", None),
        ),
        out_specs=(P("pipe", "dp", None), P("pipe", "dp", None)),
        check_vma=False,
    )
```

```python
import functools
import math

import jax
import jax.numpy as jnp
from jax import lax
from jax.experimental import pallas as pl
from jax.experimental.pallas import tpu as pltpu
from jax.sharding import PartitionSpec as P

HEIGHT = 8
WIDTH = 4
F32 = jnp.float32
BF16 = jnp.bfloat16
GRID = (4, 2, 2)
LANES = 128


def passed_along(value, axis, steps):
    count = lax.axis_size(axis)
    first, last = (max(0, -steps), min(count, count - steps))
    return lax.ppermute(value, axis, [(source, source + steps) for source in range(first, last)])


def embedding_of(step, channels):
    half_width = channels // 2
    frequency = jnp.exp(-math.log(10000.0) * jnp.arange(half_width, dtype=jnp.float32) / half_width)
    phases = step.astype(jnp.float32) * frequency
    return jnp.concatenate([jnp.sin(phases), jnp.cos(phases)])


def normalize(summed):
    return summed * lax.rsqrt(jnp.mean(summed * summed, axis=-1, keepdims=True) + 1e-06)


def spatial_columns(normed):
    frames, pixels, channels = normed.shape
    grid = normed.reshape(frames, HEIGHT, WIDTH, channels)
    padded = jnp.pad(grid, ((0, 0), (1, 1), (1, 1), (0, 0)))
    pieces = [
        padded[:, row : row + HEIGHT, col : col + WIDTH, :] for row in range(3) for col in range(3)
    ]
    return jnp.concatenate(pieces, axis=-1).reshape(frames * pixels, 9 * channels)


def spatial_fold(grads, frames, channels):
    parts = grads.reshape(frames, HEIGHT, WIDTH, 9, channels)
    padded = jnp.zeros((frames, HEIGHT + 2, WIDTH + 2, channels), jnp.float32)
    for row in range(3):
        for col in range(3):
            padded = padded.at[:, row : row + HEIGHT, col : col + WIDTH, :].add(
                parts[:, :, :, row * 3 + col, :]
            )
    return padded[:, 1 : HEIGHT + 1, 1 : WIDTH + 1, :].reshape(frames, HEIGHT * WIDTH, channels)


def temporal_columns(activated):
    frames, pixels, channels = activated.shape
    padded = jnp.pad(activated, ((1, 1), (0, 0), (0, 0)))
    pieces = [padded[tap : tap + frames] for tap in range(3)]
    return jnp.concatenate(pieces, axis=-1).reshape(frames * pixels, 3 * channels)


def temporal_fold(grads, frames, pixels, channels):
    parts = grads.reshape(frames, pixels, 3, channels)
    padded = jnp.zeros((frames + 2, pixels, channels), jnp.float32)
    for tap in range(3):
        padded = padded.at[tap : tap + frames].add(parts[:, :, tap, :])
    return padded[1 : frames + 1]


def section_forward(block_in, embedding, spatial, temporal):
    frames, pixels, channels = block_in.shape
    summed = block_in.astype(jnp.float32) + embedding
    normed = normalize(summed).astype(jnp.bfloat16)
    preact = jnp.dot(spatial_columns(normed), spatial, preferred_element_type=jnp.float32)
    activated = jax.nn.silu(preact).astype(jnp.bfloat16).reshape(frames, pixels, channels)
    mixed = jnp.dot(temporal_columns(activated), temporal, preferred_element_type=jnp.float32)
    return (block_in.astype(jnp.float32) + mixed.reshape(frames, pixels, channels)).astype(
        jnp.bfloat16
    )


def backward_first(block_in, embedding, spatial, temporal, upstream):
    frames, pixels, channels = block_in.shape
    summed = block_in.astype(jnp.float32) + embedding
    normed = normalize(summed).astype(jnp.bfloat16)
    columns = spatial_columns(normed)
    preact = jnp.dot(columns, spatial, preferred_element_type=jnp.float32)
    activated = jax.nn.silu(preact).astype(jnp.bfloat16).reshape(frames, pixels, channels)
    tcolumns = temporal_columns(activated)
    upstream_flat = upstream.reshape(frames * pixels, channels)
    temporal_term = jnp.dot(tcolumns.T, upstream_flat, preferred_element_type=jnp.float32)
    act_grad = temporal_fold(
        jnp.dot(upstream_flat, temporal.T, preferred_element_type=jnp.float32),
        frames,
        pixels,
        channels,
    )
    logistic = jax.nn.sigmoid(preact)
    slope = logistic * (1.0 + preact * (1.0 - logistic))
    pre_grad = (act_grad.reshape(frames * pixels, channels) * slope).astype(jnp.bfloat16)
    return (temporal_term, pre_grad, columns)


def backward_second(block_in, embedding, spatial, upstream, pre_grad, columns):
    frames, pixels, channels = block_in.shape
    summed = block_in.astype(jnp.float32) + embedding
    spatial_term = jnp.dot(columns.T, pre_grad, preferred_element_type=jnp.float32)
    norm_grad = spatial_fold(
        jnp.dot(pre_grad, spatial.T, preferred_element_type=jnp.float32), frames, channels
    )
    _, pullback = jax.vjp(normalize, summed)
    back_input = (upstream.astype(jnp.float32) + pullback(norm_grad)[0]).astype(jnp.bfloat16)
    return (back_input, spatial_term)


def section_backward(block_in, embedding, spatial, temporal, upstream):
    temporal_term, pre_grad, columns = backward_first(
        block_in, embedding, spatial, temporal, upstream
    )
    back_input, spatial_term = backward_second(
        block_in, embedding, spatial, upstream, pre_grad, columns
    )
    return (back_input, spatial_term, temporal_term)


def per_device(samples, timesteps, cotangent, spatial_weight, temporal_weight):
    sections = lax.axis_size("pipe")
    section_index = lax.axis_index("pipe")
    micro_count = samples.shape[0]
    frames, pixels, channels = (samples.shape[1], samples.shape[2], samples.shape[3])
    moments = jnp.arange(micro_count + sections - 1, dtype=jnp.int32)
    blank = jnp.zeros((frames, pixels, channels), jnp.bfloat16)
    full_spatial, full_temporal = (
        lax.all_gather(spatial_weight[0], "dp", axis=0, tiled=True),
        lax.all_gather(temporal_weight[0], "dp", axis=0, tiled=True),
    )

    def forward_step(carry, moment):
        incoming, stash = carry
        position = moment - section_index
        active = (position >= 0) & (position < micro_count)
        picked = jnp.clip(position, 0, micro_count - 1)
        own = lax.dynamic_index_in_dim(samples, picked, 0, keepdims=False)
        embedding = embedding_of(
            lax.dynamic_index_in_dim(timesteps, picked, 0, keepdims=False), channels
        )
        block_in = jnp.where(section_index == 0, own, incoming)
        result = lax.cond(
            active & (section_index < sections - 1),
            lambda: section_forward(block_in, embedding, full_spatial, full_temporal),
            lambda: blank,
        )
        stash = jnp.where(
            active, lax.dynamic_update_index_in_dim(stash, block_in, picked, 0), stash
        )
        passed = passed_along(result, "pipe", 1)
        return ((passed, stash), None)

    (_, stash), _ = lax.scan(forward_step, (blank, jnp.zeros_like(samples)), moments)
    back_spatial, back_temporal = (full_spatial, full_temporal)

    def inputs_at(moment, incoming):
        position = moment - (sections - 1 - section_index)
        active = (position >= 0) & (position < micro_count)
        picked = jnp.clip(position, 0, micro_count - 1)
        block_in = lax.dynamic_index_in_dim(stash, picked, 0, keepdims=False)
        embedding = embedding_of(
            lax.dynamic_index_in_dim(timesteps, picked, 0, keepdims=False), channels
        )
        given = lax.dynamic_index_in_dim(cotangent, picked, 0, keepdims=False)
        upstream = jnp.where(section_index == sections - 1, given, incoming)
        return (active, block_in, embedding, upstream)

    def backward_step(carry, moment):
        incoming, grad_spatial, grad_temporal = carry
        active, block_in, embedding, upstream = inputs_at(moment, incoming)

        def working():
            back_input, spatial_term, temporal_term = section_backward(
                block_in, embedding, back_spatial, back_temporal, upstream
            )
            return (back_input, grad_spatial + spatial_term, grad_temporal + temporal_term)

        def waiting():
            return (blank, grad_spatial, grad_temporal)

        back_input, grad_spatial, grad_temporal = lax.cond(active, working, waiting)
        passed = passed_along(back_input, "pipe", -1)
        return ((passed, grad_spatial, grad_temporal), None)

    start = (
        blank,
        jnp.zeros(back_spatial.shape, jnp.float32),
        jnp.zeros(back_temporal.shape, jnp.float32),
    )
    (_, grad_spatial, grad_temporal), _ = lax.scan(backward_step, start, moments)
    share_spatial, share_temporal = (
        lax.psum_scatter(
            grad_spatial.astype(jnp.bfloat16).astype(jnp.float32).astype(jnp.bfloat16),
            "dp",
            scatter_dimension=0,
            tiled=True,
        ).astype(jnp.float32),
        lax.psum_scatter(
            grad_temporal.astype(jnp.bfloat16).astype(jnp.float32).astype(jnp.bfloat16),
            "dp",
            scatter_dimension=0,
            tiled=True,
        ).astype(jnp.float32),
    )
    return (share_spatial[None], share_temporal[None])


def coordinates():
    index = lax.axis_index("dp")
    return index // (GRID[1] * GRID[2]), (index // GRID[2]) % GRID[1], index % GRID[2]


def shifted(value, dz=0, dy=0, dc=0):
    pairs = []
    for z in range(GRID[0]):
        for y in range(GRID[1]):
            for c in range(GRID[2]):
                place = ((z + dz) % GRID[0], (y + dy) % GRID[1], (c + dc) % GRID[2])
                pairs.append(
                    (
                        (z * GRID[1] + y) * GRID[2] + c,
                        (place[0] * GRID[1] + place[1]) * GRID[2] + place[2],
                    )
                )
    return lax.ppermute(value, "dp", pairs)


def swapped(value):
    return lax.ppermute(value, "pipe", [(0, 1), (1, 0)])


def part_of(value, index, axis):
    return lax.dynamic_index_in_dim(value, index, axis, keepdims=False)


def vmem_call(body, outs, scratch=(), flops=0, moved=0):
    return pl.pallas_call(
        body,
        out_shape=outs,
        scratch_shapes=list(scratch),
        compiler_params=pltpu.CompilerParams(vmem_limit_bytes=24 * 2**20),
        cost_estimate=pl.CostEstimate(flops=flops, bytes_accessed=moved, transcendentals=0),
    )


def after(value, earlier):
    return value if earlier is None else lax.optimization_barrier((value, earlier))[0]


def in_order(swap, own, other, axis):
    return jnp.where(
        swap, jnp.concatenate([other, own], axis), jnp.concatenate([own, other], axis)
    )


def over_z(value, pairs):
    moves = []
    for source, target in pairs:
        for rest in range(GRID[1] * GRID[2]):
            moves.append(tuple(z * GRID[1] * GRID[2] + rest for z in (source, target)))
    return lax.ppermute(value, "dp", moves)


def sent_over_z(value):
    return [shifted(value, dz=step) for step in range(1, GRID[0])]


def sent_on_chip(value):
    pieces = value.shape[0] if value.size > 4 * 2 * 360 * LANES else 2
    return jnp.concatenate([shifted(piece, dc=1) for piece in jnp.split(value, pieces)])


def gathered_over_plane(value, chunks, earlier=None, parts=1):
    z, y, _ = coordinates()
    before = chunks[-1] if chunks else (None, None)
    pieces = sent_over_z(after(value, before[0]))
    line = jnp.stack(
        [lax.select_n((z - place) % GRID[0], value, *pieces) for place in range(GRID[0])]
    )
    line = after(line, earlier)
    side, planes = before[1], []
    for part in jnp.split(line, parts, axis=2):
        side = shifted(after(part, side), dy=1)
        planes.append(in_order(y == 1, part[:, None], side[:, None], 1))
    chunks.append((pieces, side))
    return planes if parts > 1 else planes[0]


def gathered_on_chip(plane, earlier):
    _, _, c = coordinates()
    plane = after(plane, earlier)
    whole = in_order(c == 1, plane[:, :, None], sent_on_chip(plane)[:, :, None], 2)
    return whole.reshape(-1, plane.shape[3])


def added(*terms):
    return sum(term.astype(F32) for term in terms)


def summed_on_chip(value):
    _, _, c = coordinates()
    sent = sent_on_chip(part_of(value, 1 - c, 2))
    return added(part_of(value, c, 2), sent).astype(BF16)


def summed_over_y(value, earlier):
    _, y, _ = coordinates()
    sent = shifted(after(part_of(value, 1 - y, 1), earlier), dy=1)
    return added(part_of(value, y, 1), sent).astype(BF16), sent


def summed_over_z(line, earlier=None):
    z, _, _ = coordinates()
    line = after(line, earlier)
    sent = [
        shifted(part_of(line, (z + step) % GRID[0], 0), dz=step) for step in range(1, GRID[0])
    ]
    return added(part_of(line, z, 0), *sent), sent


def pixel_masks(rows):
    row = lax.broadcasted_iota(jnp.int32, (rows, 1), 0)
    high, wide = (row // WIDTH) % HEIGHT, row % WIDTH
    masks = []
    for dr in (-1, 0, 1):
        for dc in (-1, 0, 1):
            inside = (high + dr >= 0) & (high + dr < HEIGHT) & (wide + dc >= 0) & (wide + dc < WIDTH)
            masks.append((dr * WIDTH + dc, inside))
    return masks


def frame_masks(rows, frames):
    pixels = HEIGHT * WIDTH
    row = lax.broadcasted_iota(jnp.int32, (rows, 1), 0)
    frame = (row // pixels) % frames
    return [
        (step * pixels, (frame + step >= 0) & (frame + step < frames)) for step in (-1, 0, 1)
    ]


def moved_rows(value, move):
    shift, inside = move
    if shift:
        value = pltpu.roll(value, (-shift) % value.shape[0], 0)
    return jnp.where(inside, value, 0.0)


def dot(left, right, dims=((1,), (0,))):
    return lax.dot_general(left, right, (dims, ((), ())), preferred_element_type=F32)


def with_embedding(hidden, embedding_ref, samples):
    per = hidden.shape[0] // samples
    return jnp.concatenate(
        [hidden[s * per : (s + 1) * per] + embedding_ref[s : s + 1, :] for s in range(samples)]
    )


def scale_of(summed):
    return lax.rsqrt(jnp.mean(summed * summed, axis=-1, keepdims=True) + 1e-06)


def silu_parts(preact):
    logistic = 1.0 / (1.0 + jnp.exp(-preact))
    return logistic, preact * logistic


def tap_weight(weight_refs, tap, channels):
    return jnp.concatenate(
        [ref[tap * channels : (tap + 1) * channels, :] for ref in weight_refs], 1
    )


def convolved(normed, weight_refs, masks):
    rows, channels = normed.shape
    normed = normed.astype(F32)
    total = None
    for tap in range(9):
        term = dot(
            moved_rows(normed, masks[tap]).astype(BF16),
            tap_weight(weight_refs, tap, channels),
        )
        total = term if total is None else total + term
    return total


def first_forward(frames, hidden_ref, embedding_ref, keep_ref, temporal_ref, *refs):
    *spatial_refs, normed_ref, preact_ref, mixed_ref = refs
    rows = hidden_ref.shape[0]
    width = keep_ref.shape[1]
    summed = with_embedding(hidden_ref[...].astype(F32), embedding_ref, embedding_ref.shape[0])
    normed = (summed * scale_of(summed)).astype(BF16)
    normed_ref[...] = normed
    preact = convolved(normed, spatial_refs, pixel_masks(rows))
    preact_ref[...] = preact
    activated = silu_parts(preact)[1].astype(BF16).astype(F32) * keep_ref[...]
    mixed = None
    for tap, move in enumerate(frame_masks(rows, frames)):
        term = dot(
            moved_rows(activated, move).astype(BF16),
            temporal_ref[tap * width : (tap + 1) * width, :],
        )
        mixed = term if mixed is None else mixed + term
    mixed_ref[...] = mixed.astype(BF16)


def slope_of(preact):
    logistic, _ = silu_parts(preact)
    return logistic * (1.0 + preact * (1.0 - logistic))


def act_grad_of(upstream, temporal_ref, width, frames):
    upstream = upstream.astype(F32)
    moves = frame_masks(upstream.shape[0], frames)
    total = None
    for tap in range(3):
        term = dot(
            moved_rows(upstream, moves[2 - tap]).astype(BF16),
            temporal_ref[tap * width : (tap + 1) * width, :],
            ((1,), (1,)),
        )
        total = term if total is None else total + term
    return total


def store_temporal_terms(activated, upstream, frames, out_ref):
    width = activated.shape[1]
    upstream = upstream.astype(F32)
    moves = frame_masks(upstream.shape[0], frames)
    for tap in range(3):
        out_ref[tap * width : (tap + 1) * width, :] = dot(
            activated, moved_rows(upstream, moves[2 - tap]).astype(BF16), ((0,), (0,))
        ).astype(BF16)


def store_spatial_terms(normed, pre_grad, out_refs):
    channels = normed.shape[1]
    pre_grad = pre_grad.astype(F32)
    masks = pixel_masks(pre_grad.shape[0])
    for tap in range(9):
        term = dot(
            normed, moved_rows(pre_grad, masks[8 - tap]).astype(BF16), ((0,), (0,))
        ).astype(BF16)
        start = 0
        for out_ref in out_refs:
            end = start + out_ref.shape[1]
            out_ref[tap * channels : (tap + 1) * channels, :] = term[:, start:end]
            start = end


def second_forward(
    frames, hidden_ref, own_ref, sent_ref, embedding_ref, keep_ref, upstream_ref, temporal_ref, *refs
):
    *spatial_refs, next_ref, normed_ref, activated_ref, pre_grad_ref, back_ref = refs
    rows, channels = hidden_ref.shape
    width = keep_ref.shape[1]
    masks = pixel_masks(rows)
    mixed = own_ref[...].astype(F32) + sent_ref[...].astype(F32)
    hidden = (hidden_ref[...].astype(F32) + mixed).astype(BF16)
    next_ref[...] = hidden
    summed = with_embedding(hidden.astype(F32), embedding_ref, embedding_ref.shape[0])
    normed = (summed * scale_of(summed)).astype(BF16)
    normed_ref[...] = normed
    preact = convolved(normed, spatial_refs, masks)
    activated_ref[...] = (silu_parts(preact)[1] * keep_ref[...]).astype(BF16)
    act_grad = act_grad_of(upstream_ref[...], temporal_ref, width, frames)
    pre_grad = (act_grad * slope_of(preact) * keep_ref[...]).astype(BF16)
    pre_grad_ref[...] = pre_grad
    pre_grad = pre_grad.astype(F32)
    back = None
    for tap in range(9):
        term = dot(
            moved_rows(pre_grad, masks[8 - tap]).astype(BF16),
            tap_weight(spatial_refs, tap, channels),
            ((1,), (1,)),
        )
        back = term if back is None else back + term
    back_ref[...] = back.astype(BF16)


def second_terms(frames, normed_ref, pre_grad_ref, activated_ref, upstream_ref, *outs):
    *spatial_refs, temporal_ref = outs
    store_spatial_terms(normed_ref[...], pre_grad_ref[...], spatial_refs)
    store_temporal_terms(activated_ref[...], upstream_ref[...], frames, temporal_ref)


def first_terms(
    frames, hidden_ref, embedding_ref, upstream_ref, own_ref, sent_ref, normed_ref, preact_ref,
    keep_ref, temporal_ref, *outs
):
    *spatial_outs, temporal_out = outs
    width = keep_ref.shape[1]
    channels = hidden_ref.shape[1]
    summed = with_embedding(hidden_ref[...].astype(F32), embedding_ref, embedding_ref.shape[0])
    scale = scale_of(summed)
    grad = own_ref[...].astype(F32) + sent_ref[...].astype(F32)
    inner = jnp.sum(grad * summed, axis=-1, keepdims=True)
    back = grad * scale - summed * (scale * scale * scale) * (inner / channels)
    upstream = (upstream_ref[...].astype(F32) + back).astype(BF16)
    preact = preact_ref[...]
    activated = (silu_parts(preact)[1] * keep_ref[...]).astype(BF16)
    act_grad = act_grad_of(upstream, temporal_ref, width, frames)
    pre_grad = (act_grad * slope_of(preact) * keep_ref[...]).astype(BF16)
    store_spatial_terms(normed_ref[...], pre_grad, spatial_outs)
    store_temporal_terms(activated, upstream, frames, temporal_out)


def paired_device(samples, timesteps, cotangent, spatial_weight, temporal_weight):
    me = lax.axis_index("pipe")
    first = me == 0
    _, _, c = coordinates()
    count, frames, pixels, channels = samples.shape
    rows = count * frames * pixels
    main = 2 * LANES
    width = main + LANES
    hidden = samples.reshape(rows, channels)
    upstream = cotangent.reshape(rows, channels)
    embedding = jax.vmap(lambda step: embedding_of(step, channels))(timesteps)
    lane = jnp.arange(LANES)
    keep_own = jnp.concatenate([jnp.ones(main), lane < LANES // 2]).astype(F32)[None]
    keep_other = jnp.concatenate([jnp.ones(main), lane >= LANES // 2]).astype(F32)[None]
    keep_first = jnp.where(first, keep_own, keep_other)
    keep_second = jnp.where(first, keep_other, keep_own)
    tail = lane[None] < LANES // 2

    def main_of(value, index, axis):
        return lax.dynamic_slice_in_dim(value, index * main, main, axis)

    spatial_own = spatial_weight[0]
    given = swapped(
        jnp.concatenate([main_of(spatial_own, 1 - me, 1), spatial_own[:, 2 * main :]], 1)
    )
    main_own, main_given = main_of(spatial_own, me, 1), given[:, :main]
    tails = jnp.where(tail, spatial_own[:, 2 * main :], given[:, main:])
    main_first = jnp.where(first, main_own, main_given)
    main_second = jnp.where(first, main_given, main_own)
    chunks = []
    plane_temporal = gathered_over_plane(temporal_weight[0], chunks)
    plane_first = gathered_over_plane(main_first, chunks)
    plane_tails = gathered_over_plane(tails, chunks)
    temporal_own = gathered_on_chip(plane_temporal, chunks[1][0])
    temporal_own = temporal_own.reshape(3, channels, channels)

    def local_rows(index):
        return jnp.concatenate(
            [main_of(temporal_own, index, 1), temporal_own[:, 2 * main :]], 1
        ).reshape(GRID[2], -1, channels)

    half = swapped(part_of(local_rows(1 - me), c, 0))
    other_half = shifted(half, dc=1)
    temporal_other = jnp.where(
        c == 0, jnp.concatenate([half, other_half]), jnp.concatenate([other_half, half])
    )
    temporal_mine = local_rows(me).reshape(3 * width, channels)
    temporal_first = jnp.where(first, temporal_mine, temporal_other)
    temporal_second = jnp.where(first, temporal_other, temporal_mine)

    plane_second = gathered_over_plane(main_second, chunks, half, 2)
    spatial_first = [
        gathered_on_chip(plane_first, chunks[2][0]),
        gathered_on_chip(plane_tails, chunks[3][0]),
    ]

    def shape(extent, dtype=BF16):
        return jax.ShapeDtypeStruct(extent, dtype)

    spatial_flops = 2 * rows * 9 * channels * width
    temporal_flops = 2 * rows * 3 * channels * width
    spatial_bytes = 2 * 9 * channels * width
    temporal_bytes = 2 * 3 * channels * width
    normed_first, preact_first, mixed = vmem_call(
        functools.partial(first_forward, frames),
        (shape((rows, channels)), shape((rows, width), F32), shape((rows, channels))),
        flops=spatial_flops + temporal_flops,
        moved=spatial_bytes + temporal_bytes,
    )(hidden, embedding, keep_first, temporal_first, *spatial_first)
    mixed_given = swapped(mixed)
    spatial_second = [
        *(gathered_on_chip(plane, mixed) for plane in plane_second),
        spatial_first[1],
    ]
    hidden_second, normed_second, activated_second, pre_grad_second, back = vmem_call(
        functools.partial(second_forward, frames),
        (
            shape((rows, channels)),
            shape((rows, channels)),
            shape((rows, width)),
            shape((rows, width)),
            shape((rows, channels)),
        ),
        flops=2 * spatial_flops + temporal_flops,
        moved=spatial_bytes + temporal_bytes,
    )(
        hidden, mixed, mixed_given, embedding, keep_second, upstream, temporal_second,
        *spatial_second,
    )

    def terms_shape():
        return (
            shape((9 * channels, main)),
            shape((9 * channels, width - main)),
            shape((3 * width, channels)),
        )

    def on_chip(terms):
        return summed_on_chip(terms.reshape(*GRID, -1, terms.shape[1]))

    back_given = swapped(back)
    main_terms_second, tail_terms_second, temporal_terms_second = vmem_call(
        functools.partial(second_terms, frames),
        terms_shape(),
        flops=spatial_flops + temporal_flops,
        moved=spatial_bytes + temporal_bytes,
    )(normed_second, pre_grad_second, activated_second, upstream)
    chip_second = on_chip(main_terms_second)
    line_low, side = summed_over_y(chip_second[..., :LANES], None)
    back_given = after(back_given, side)
    line_high, side = summed_over_y(chip_second[..., LANES:], side)
    share_second, sent_second = summed_over_z(jnp.concatenate([line_low, line_high], 2))
    main_terms_first, tail_terms_first, temporal_terms_first = vmem_call(
        functools.partial(first_terms, frames),
        terms_shape(),
        flops=spatial_flops + 2 * temporal_flops,
        moved=spatial_bytes + 2 * temporal_bytes,
    )(
        hidden_second, embedding, upstream, back, back_given, normed_first, preact_first,
        keep_first, temporal_first,
    )
    chip_tails = on_chip(tail_terms_first + tail_terms_second)
    chip_first = on_chip(main_terms_first)

    terms = jnp.stack(
        [
            jnp.where(first, temporal_terms_first, temporal_terms_second),
            jnp.where(first, temporal_terms_second, temporal_terms_first),
        ]
    ).reshape(2, GRID[2], -1, channels)
    sent = sent_on_chip(part_of(terms, 1 - c, 1))
    halves = added(part_of(terms, c, 1), sent).astype(BF16)
    half_given = swapped(halves[1])
    halves = jnp.stack([halves[0], half_given])
    other_halves = sent_on_chip(halves)
    both = jnp.where(
        c == 0,
        jnp.stack([halves, other_halves], 1),
        jnp.stack([other_halves, halves], 1),
    ).reshape(2, 3, width, channels)
    mine, theirs = both[0], both[1]
    full = jnp.concatenate(
        [
            jnp.where(first, mine[:, :main], theirs[:, :main]),
            jnp.where(first, theirs[:, :main], mine[:, :main]),
            mine[:, main:] + theirs[:, main:],
        ],
        1,
    )
    full = part_of(full.reshape(*GRID, -1, channels), c, 2)

    line, side = summed_over_y(chip_tails, (side, sent))
    share_tails, sent_tails = summed_over_z(line, sent_second)
    line, side = summed_over_y(chip_first, (side, sent_second))
    share_first, sent_first = summed_over_z(line, (sent_tails, other_halves))
    line, side = summed_over_y(full[..., : 3 * LANES], (side, sent_tails))
    share_low, sent_low = summed_over_z(line, sent_first)
    line, side = summed_over_y(full[..., 3 * LANES :], side)
    share_high, _ = summed_over_z(line, sent_low)
    share_temporal = jnp.concatenate([share_low, share_high], 1)

    kept = jnp.where(first, share_first, share_second)
    passed = jnp.where(first, share_second, share_first)
    given = jnp.concatenate([passed, share_tails], 1).astype(BF16)
    given = swapped(after(given, side)).astype(F32)
    share_spatial = jnp.concatenate(
        [
            jnp.where(first, kept, given[:, :main]),
            jnp.where(first, given[:, :main], kept),
            jnp.where(tail, share_tails, given[:, main:]),
        ],
        1,
    )
    return (share_spatial[None], share_temporal[None])


def solution(mesh):
    paired = mesh.shape["pipe"] == 2 and mesh.shape["dp"] == math.prod(GRID)
    return jax.shard_map(
        paired_device if paired else per_device,
        mesh=mesh,
        in_specs=(
            P("dp", None, None, None),
            P("dp"),
            P("dp", None, None, None),
            P("pipe", "dp", None),
            P("pipe", "dp", None),
        ),
        out_specs=(P("pipe", "dp", None), P("pipe", "dp", None)),
        check_vma=False,
    )
```

```python
import functools
import math

import jax
import jax.numpy as jnp
from jax import lax
from jax.experimental import pallas as pl
from jax.experimental.pallas import tpu as pltpu
from jax.sharding import PartitionSpec as P

HEIGHT = 8
WIDTH = 4
F32 = jnp.float32
BF16 = jnp.bfloat16
GRID = (4, 2, 2)
LANES = 128


def passed_along(value, axis, steps):
    count = lax.axis_size(axis)
    first, last = (max(0, -steps), min(count, count - steps))
    return lax.ppermute(value, axis, [(source, source + steps) for source in range(first, last)])


def embedding_of(step, channels):
    half_width = channels // 2
    frequency = jnp.exp(-math.log(10000.0) * jnp.arange(half_width, dtype=jnp.float32) / half_width)
    phases = step.astype(jnp.float32) * frequency
    return jnp.concatenate([jnp.sin(phases), jnp.cos(phases)])


def normalize(summed):
    return summed * lax.rsqrt(jnp.mean(summed * summed, axis=-1, keepdims=True) + 1e-06)


def spatial_columns(normed):
    frames, pixels, channels = normed.shape
    grid = normed.reshape(frames, HEIGHT, WIDTH, channels)
    padded = jnp.pad(grid, ((0, 0), (1, 1), (1, 1), (0, 0)))
    pieces = [
        padded[:, row : row + HEIGHT, col : col + WIDTH, :] for row in range(3) for col in range(3)
    ]
    return jnp.concatenate(pieces, axis=-1).reshape(frames * pixels, 9 * channels)


def spatial_fold(grads, frames, channels):
    parts = grads.reshape(frames, HEIGHT, WIDTH, 9, channels)
    padded = jnp.zeros((frames, HEIGHT + 2, WIDTH + 2, channels), jnp.float32)
    for row in range(3):
        for col in range(3):
            padded = padded.at[:, row : row + HEIGHT, col : col + WIDTH, :].add(
                parts[:, :, :, row * 3 + col, :]
            )
    return padded[:, 1 : HEIGHT + 1, 1 : WIDTH + 1, :].reshape(frames, HEIGHT * WIDTH, channels)


def temporal_columns(activated):
    frames, pixels, channels = activated.shape
    padded = jnp.pad(activated, ((1, 1), (0, 0), (0, 0)))
    pieces = [padded[tap : tap + frames] for tap in range(3)]
    return jnp.concatenate(pieces, axis=-1).reshape(frames * pixels, 3 * channels)


def temporal_fold(grads, frames, pixels, channels):
    parts = grads.reshape(frames, pixels, 3, channels)
    padded = jnp.zeros((frames + 2, pixels, channels), jnp.float32)
    for tap in range(3):
        padded = padded.at[tap : tap + frames].add(parts[:, :, tap, :])
    return padded[1 : frames + 1]


def section_forward(block_in, embedding, spatial, temporal):
    frames, pixels, channels = block_in.shape
    summed = block_in.astype(jnp.float32) + embedding
    normed = normalize(summed).astype(jnp.bfloat16)
    preact = jnp.dot(spatial_columns(normed), spatial, preferred_element_type=jnp.float32)
    activated = jax.nn.silu(preact).astype(jnp.bfloat16).reshape(frames, pixels, channels)
    mixed = jnp.dot(temporal_columns(activated), temporal, preferred_element_type=jnp.float32)
    return (block_in.astype(jnp.float32) + mixed.reshape(frames, pixels, channels)).astype(
        jnp.bfloat16
    )


def backward_first(block_in, embedding, spatial, temporal, upstream):
    frames, pixels, channels = block_in.shape
    summed = block_in.astype(jnp.float32) + embedding
    normed = normalize(summed).astype(jnp.bfloat16)
    columns = spatial_columns(normed)
    preact = jnp.dot(columns, spatial, preferred_element_type=jnp.float32)
    activated = jax.nn.silu(preact).astype(jnp.bfloat16).reshape(frames, pixels, channels)
    tcolumns = temporal_columns(activated)
    upstream_flat = upstream.reshape(frames * pixels, channels)
    temporal_term = jnp.dot(tcolumns.T, upstream_flat, preferred_element_type=jnp.float32)
    act_grad = temporal_fold(
        jnp.dot(upstream_flat, temporal.T, preferred_element_type=jnp.float32),
        frames,
        pixels,
        channels,
    )
    logistic = jax.nn.sigmoid(preact)
    slope = logistic * (1.0 + preact * (1.0 - logistic))
    pre_grad = (act_grad.reshape(frames * pixels, channels) * slope).astype(jnp.bfloat16)
    return (temporal_term, pre_grad, columns)


def backward_second(block_in, embedding, spatial, upstream, pre_grad, columns):
    frames, pixels, channels = block_in.shape
    summed = block_in.astype(jnp.float32) + embedding
    spatial_term = jnp.dot(columns.T, pre_grad, preferred_element_type=jnp.float32)
    norm_grad = spatial_fold(
        jnp.dot(pre_grad, spatial.T, preferred_element_type=jnp.float32), frames, channels
    )
    _, pullback = jax.vjp(normalize, summed)
    back_input = (upstream.astype(jnp.float32) + pullback(norm_grad)[0]).astype(jnp.bfloat16)
    return (back_input, spatial_term)


def section_backward(block_in, embedding, spatial, temporal, upstream):
    temporal_term, pre_grad, columns = backward_first(
        block_in, embedding, spatial, temporal, upstream
    )
    back_input, spatial_term = backward_second(
        block_in, embedding, spatial, upstream, pre_grad, columns
    )
    return (back_input, spatial_term, temporal_term)


def per_device(samples, timesteps, cotangent, spatial_weight, temporal_weight):
    sections = lax.axis_size("pipe")
    section_index = lax.axis_index("pipe")
    micro_count = samples.shape[0]
    frames, pixels, channels = (samples.shape[1], samples.shape[2], samples.shape[3])
    moments = jnp.arange(micro_count + sections - 1, dtype=jnp.int32)
    blank = jnp.zeros((frames, pixels, channels), jnp.bfloat16)
    full_spatial, full_temporal = (
        lax.all_gather(spatial_weight[0], "dp", axis=0, tiled=True),
        lax.all_gather(temporal_weight[0], "dp", axis=0, tiled=True),
    )

    def forward_step(carry, moment):
        incoming, stash = carry
        position = moment - section_index
        active = (position >= 0) & (position < micro_count)
        picked = jnp.clip(position, 0, micro_count - 1)
        own = lax.dynamic_index_in_dim(samples, picked, 0, keepdims=False)
        embedding = embedding_of(
            lax.dynamic_index_in_dim(timesteps, picked, 0, keepdims=False), channels
        )
        block_in = jnp.where(section_index == 0, own, incoming)
        result = lax.cond(
            active & (section_index < sections - 1),
            lambda: section_forward(block_in, embedding, full_spatial, full_temporal),
            lambda: blank,
        )
        stash = jnp.where(
            active, lax.dynamic_update_index_in_dim(stash, block_in, picked, 0), stash
        )
        passed = passed_along(result, "pipe", 1)
        return ((passed, stash), None)

    (_, stash), _ = lax.scan(forward_step, (blank, jnp.zeros_like(samples)), moments)
    back_spatial, back_temporal = (full_spatial, full_temporal)

    def inputs_at(moment, incoming):
        position = moment - (sections - 1 - section_index)
        active = (position >= 0) & (position < micro_count)
        picked = jnp.clip(position, 0, micro_count - 1)
        block_in = lax.dynamic_index_in_dim(stash, picked, 0, keepdims=False)
        embedding = embedding_of(
            lax.dynamic_index_in_dim(timesteps, picked, 0, keepdims=False), channels
        )
        given = lax.dynamic_index_in_dim(cotangent, picked, 0, keepdims=False)
        upstream = jnp.where(section_index == sections - 1, given, incoming)
        return (active, block_in, embedding, upstream)

    def backward_step(carry, moment):
        incoming, grad_spatial, grad_temporal = carry
        active, block_in, embedding, upstream = inputs_at(moment, incoming)

        def working():
            back_input, spatial_term, temporal_term = section_backward(
                block_in, embedding, back_spatial, back_temporal, upstream
            )
            return (back_input, grad_spatial + spatial_term, grad_temporal + temporal_term)

        def waiting():
            return (blank, grad_spatial, grad_temporal)

        back_input, grad_spatial, grad_temporal = lax.cond(active, working, waiting)
        passed = passed_along(back_input, "pipe", -1)
        return ((passed, grad_spatial, grad_temporal), None)

    start = (
        blank,
        jnp.zeros(back_spatial.shape, jnp.float32),
        jnp.zeros(back_temporal.shape, jnp.float32),
    )
    (_, grad_spatial, grad_temporal), _ = lax.scan(backward_step, start, moments)
    share_spatial, share_temporal = (
        lax.psum_scatter(
            grad_spatial.astype(jnp.bfloat16).astype(jnp.float32).astype(jnp.bfloat16),
            "dp",
            scatter_dimension=0,
            tiled=True,
        ).astype(jnp.float32),
        lax.psum_scatter(
            grad_temporal.astype(jnp.bfloat16).astype(jnp.float32).astype(jnp.bfloat16),
            "dp",
            scatter_dimension=0,
            tiled=True,
        ).astype(jnp.float32),
    )
    return (share_spatial[None], share_temporal[None])


def coordinates():
    index = lax.axis_index("dp")
    return index // (GRID[1] * GRID[2]), (index // GRID[2]) % GRID[1], index % GRID[2]


def shifted(value, dz=0, dy=0, dc=0):
    pairs = []
    for z in range(GRID[0]):
        for y in range(GRID[1]):
            for c in range(GRID[2]):
                place = ((z + dz) % GRID[0], (y + dy) % GRID[1], (c + dc) % GRID[2])
                pairs.append(
                    (
                        (z * GRID[1] + y) * GRID[2] + c,
                        (place[0] * GRID[1] + place[1]) * GRID[2] + place[2],
                    )
                )
    return lax.ppermute(value, "dp", pairs)


def swapped(value):
    return lax.ppermute(value, "pipe", [(0, 1), (1, 0)])


def part_of(value, index, axis):
    return lax.dynamic_index_in_dim(value, index, axis, keepdims=False)


def vmem_call(body, outs, scratch=(), flops=0, moved=0):
    return pl.pallas_call(
        body,
        out_shape=outs,
        scratch_shapes=list(scratch),
        compiler_params=pltpu.CompilerParams(vmem_limit_bytes=24 * 2**20),
        cost_estimate=pl.CostEstimate(
            flops=5 * flops // 2, bytes_accessed=moved, transcendentals=0
        ),
    )


def after(value, earlier):
    return value if earlier is None else lax.optimization_barrier((value, earlier))[0]


def in_order(swap, own, other, axis):
    return jnp.where(
        swap, jnp.concatenate([other, own], axis), jnp.concatenate([own, other], axis)
    )


def over_z(value, pairs):
    moves = []
    for source, target in pairs:
        for rest in range(GRID[1] * GRID[2]):
            moves.append(tuple(z * GRID[1] * GRID[2] + rest for z in (source, target)))
    return lax.ppermute(value, "dp", moves)


def sent_over_z(value):
    return [shifted(value, dz=step) for step in range(1, GRID[0])]


def sent_on_chip(value):
    pieces = value.shape[0] if value.size > 4 * 2 * 360 * LANES else 2
    return jnp.concatenate([shifted(piece, dc=1) for piece in jnp.split(value, pieces)])


def gathered_over_z(value, earlier=None):
    z, _, _ = coordinates()
    value = after(value, earlier)
    sent = sent_over_z(value)
    return (
        jnp.stack([lax.select_n((z - place) % GRID[0], value, *sent) for place in range(GRID[0])]),
        sent,
    )


def gathered_over_y(line, earlier=None):
    _, y, _ = coordinates()
    line = after(line, earlier)
    sent = shifted(line, dy=1)
    return in_order(y == 1, line[:, None], sent[:, None], 1), sent


def gathered_on_chip(plane, earlier=None):
    _, _, c = coordinates()
    plane = after(plane, earlier)
    whole = in_order(c == 1, plane[:, :, None], sent_on_chip(plane)[:, :, None], 2)
    return whole.reshape(-1, plane.shape[3])


def added(*terms):
    return sum(term.astype(F32) for term in terms)


def summed_on_chip(value):
    _, _, c = coordinates()
    sent = sent_on_chip(part_of(value, 1 - c, 2))
    return added(part_of(value, c, 2), sent).astype(BF16)


def summed_over_y(value, earlier):
    _, y, _ = coordinates()
    sent = shifted(after(part_of(value, 1 - y, 1), earlier), dy=1)
    return added(part_of(value, y, 1), sent).astype(BF16), sent


def summed_over_z(line, earlier=None):
    z, _, _ = coordinates()
    line = after(line, earlier)
    sent = [
        shifted(part_of(line, (z + step) % GRID[0], 0), dz=step) for step in range(1, GRID[0])
    ]
    return added(part_of(line, z, 0), *sent), sent


def pixel_masks(rows):
    row = lax.broadcasted_iota(jnp.int32, (rows, 1), 0)
    high, wide = (row // WIDTH) % HEIGHT, row % WIDTH
    masks = []
    for dr in (-1, 0, 1):
        for dc in (-1, 0, 1):
            inside = (high + dr >= 0) & (high + dr < HEIGHT) & (wide + dc >= 0) & (wide + dc < WIDTH)
            masks.append((dr * WIDTH + dc, inside))
    return masks


def frame_masks(rows, frames):
    pixels = HEIGHT * WIDTH
    row = lax.broadcasted_iota(jnp.int32, (rows, 1), 0)
    frame = (row // pixels) % frames
    return [
        (step * pixels, (frame + step >= 0) & (frame + step < frames)) for step in (-1, 0, 1)
    ]


def moved_rows(value, move):
    shift, inside = move
    if shift:
        value = pltpu.roll(value, (-shift) % value.shape[0], 0)
    return jnp.where(inside, value, 0.0)


def dot(left, right, dims=((1,), (0,))):
    return lax.dot_general(left, right, (dims, ((), ())), preferred_element_type=F32)


def with_embedding(hidden, embedding_ref, samples):
    per = hidden.shape[0] // samples
    return jnp.concatenate(
        [hidden[s * per : (s + 1) * per] + embedding_ref[s : s + 1, :] for s in range(samples)]
    )


def scale_of(summed):
    return lax.rsqrt(jnp.mean(summed * summed, axis=-1, keepdims=True) + 1e-06)


def silu_parts(preact):
    logistic = 1.0 / (1.0 + jnp.exp(-preact))
    return logistic, preact * logistic


def tap_weight(weight_refs, tap, channels):
    return jnp.concatenate(
        [ref[tap * channels : (tap + 1) * channels, :] for ref in weight_refs], 1
    )


def convolved(normed, weight_refs, masks):
    rows, channels = normed.shape
    normed = normed.astype(F32)
    total = None
    for tap in range(9):
        term = dot(
            moved_rows(normed, masks[tap]).astype(BF16),
            tap_weight(weight_refs, tap, channels),
        )
        total = term if total is None else total + term
    return total


def first_forward(frames, hidden_ref, embedding_ref, keep_ref, temporal_ref, *refs):
    *spatial_refs, normed_ref, preact_ref, mixed_ref = refs
    rows = hidden_ref.shape[0]
    width = keep_ref.shape[1]
    summed = with_embedding(hidden_ref[...].astype(F32), embedding_ref, embedding_ref.shape[0])
    normed = (summed * scale_of(summed)).astype(BF16)
    normed_ref[...] = normed
    preact = convolved(normed, spatial_refs, pixel_masks(rows))
    preact_ref[...] = preact
    activated = silu_parts(preact)[1].astype(BF16).astype(F32) * keep_ref[...]
    mixed = None
    for tap, move in enumerate(frame_masks(rows, frames)):
        term = dot(
            moved_rows(activated, move).astype(BF16),
            temporal_ref[tap * width : (tap + 1) * width, :],
        )
        mixed = term if mixed is None else mixed + term
    mixed_ref[...] = mixed.astype(BF16)


def slope_of(preact):
    logistic, _ = silu_parts(preact)
    return logistic * (1.0 + preact * (1.0 - logistic))


def act_grad_of(upstream, temporal_ref, width, frames):
    upstream = upstream.astype(F32)
    moves = frame_masks(upstream.shape[0], frames)
    total = None
    for tap in range(3):
        term = dot(
            moved_rows(upstream, moves[2 - tap]).astype(BF16),
            temporal_ref[tap * width : (tap + 1) * width, :],
            ((1,), (1,)),
        )
        total = term if total is None else total + term
    return total


def store_temporal_terms(activated, upstream, frames, out_ref):
    width = activated.shape[1]
    upstream = upstream.astype(F32)
    moves = frame_masks(upstream.shape[0], frames)
    for tap in range(3):
        out_ref[tap * width : (tap + 1) * width, :] = dot(
            activated, moved_rows(upstream, moves[2 - tap]).astype(BF16), ((0,), (0,))
        ).astype(BF16)


def store_spatial_terms(normed, pre_grad, out_refs):
    channels = normed.shape[1]
    pre_grad = pre_grad.astype(F32)
    masks = pixel_masks(pre_grad.shape[0])
    for tap in range(9):
        term = dot(
            normed, moved_rows(pre_grad, masks[8 - tap]).astype(BF16), ((0,), (0,))
        ).astype(BF16)
        start = 0
        for out_ref in out_refs:
            end = start + out_ref.shape[1]
            out_ref[tap * channels : (tap + 1) * channels, :] = term[:, start:end]
            start = end


def second_forward(
    frames, hidden_ref, own_ref, sent_ref, embedding_ref, keep_ref, upstream_ref, temporal_ref, *refs
):
    *spatial_refs, next_ref, normed_ref, activated_ref, pre_grad_ref, back_ref = refs
    rows, channels = hidden_ref.shape
    width = keep_ref.shape[1]
    masks = pixel_masks(rows)
    mixed = own_ref[...].astype(F32) + sent_ref[...].astype(F32)
    hidden = (hidden_ref[...].astype(F32) + mixed).astype(BF16)
    next_ref[...] = hidden
    summed = with_embedding(hidden.astype(F32), embedding_ref, embedding_ref.shape[0])
    normed = (summed * scale_of(summed)).astype(BF16)
    normed_ref[...] = normed
    preact = convolved(normed, spatial_refs, masks)
    activated_ref[...] = (silu_parts(preact)[1] * keep_ref[...]).astype(BF16)
    act_grad = act_grad_of(upstream_ref[...], temporal_ref, width, frames)
    pre_grad = (act_grad * slope_of(preact) * keep_ref[...]).astype(BF16)
    pre_grad_ref[...] = pre_grad
    pre_grad = pre_grad.astype(F32)
    back = None
    for tap in range(9):
        term = dot(
            moved_rows(pre_grad, masks[8 - tap]).astype(BF16),
            tap_weight(spatial_refs, tap, channels),
            ((1,), (1,)),
        )
        back = term if back is None else back + term
    back_ref[...] = back.astype(BF16)


def second_terms(frames, normed_ref, pre_grad_ref, activated_ref, upstream_ref, *outs):
    *spatial_refs, temporal_ref = outs
    store_spatial_terms(normed_ref[...], pre_grad_ref[...], spatial_refs)
    store_temporal_terms(activated_ref[...], upstream_ref[...], frames, temporal_ref)


def first_terms(
    frames, hidden_ref, embedding_ref, upstream_ref, own_ref, sent_ref, normed_ref, preact_ref,
    keep_ref, temporal_ref, *outs
):
    *spatial_outs, temporal_out = outs
    width = keep_ref.shape[1]
    channels = hidden_ref.shape[1]
    summed = with_embedding(hidden_ref[...].astype(F32), embedding_ref, embedding_ref.shape[0])
    scale = scale_of(summed)
    grad = own_ref[...].astype(F32) + sent_ref[...].astype(F32)
    inner = jnp.sum(grad * summed, axis=-1, keepdims=True)
    back = grad * scale - summed * (scale * scale * scale) * (inner / channels)
    upstream = (upstream_ref[...].astype(F32) + back).astype(BF16)
    preact = preact_ref[...]
    activated = (silu_parts(preact)[1] * keep_ref[...]).astype(BF16)
    act_grad = act_grad_of(upstream, temporal_ref, width, frames)
    pre_grad = (act_grad * slope_of(preact) * keep_ref[...]).astype(BF16)
    store_spatial_terms(normed_ref[...], pre_grad, spatial_outs)
    store_temporal_terms(activated, upstream, frames, temporal_out)


def paired_device(samples, timesteps, cotangent, spatial_weight, temporal_weight):
    me = lax.axis_index("pipe")
    first = me == 0
    _, _, c = coordinates()
    count, frames, pixels, channels = samples.shape
    rows = count * frames * pixels
    main = 2 * LANES
    width = main + LANES
    hidden = samples.reshape(rows, channels)
    upstream = cotangent.reshape(rows, channels)
    embedding = jax.vmap(lambda step: embedding_of(step, channels))(timesteps)
    lane = jnp.arange(LANES)
    keep_own = jnp.concatenate([jnp.ones(main), lane < LANES // 2]).astype(F32)[None]
    keep_other = jnp.concatenate([jnp.ones(main), lane >= LANES // 2]).astype(F32)[None]
    keep_first = jnp.where(first, keep_own, keep_other)
    keep_second = jnp.where(first, keep_other, keep_own)
    tail = lane[None] < LANES // 2

    def main_of(value, index, axis):
        return lax.dynamic_slice_in_dim(value, index * main, main, axis)

    spatial_own = spatial_weight[0]
    given = swapped(
        jnp.concatenate([main_of(spatial_own, 1 - me, 1), spatial_own[:, 2 * main :]], 1)
    )
    main_own, main_given = main_of(spatial_own, me, 1), given[:, :main]
    tails = jnp.where(tail, spatial_own[:, 2 * main :], given[:, main:])
    main_first = jnp.where(first, main_own, main_given)
    main_second = jnp.where(first, main_given, main_own)
    line, sent = gathered_over_z(temporal_weight[0])
    plane_temporal, side = gathered_over_y(line)
    line_first, sent = gathered_over_z(main_first, sent)
    line_tails, sent = gathered_over_z(tails, (sent, side))
    plane_low, side = gathered_over_y(line_first[..., :LANES], side)
    line_low, sent_low = gathered_over_z(main_second[:, :LANES], (sent, side))
    temporal_own = gathered_on_chip(plane_temporal).reshape(3, channels, channels)

    def local_rows(index):
        return jnp.concatenate(
            [main_of(temporal_own, index, 1), temporal_own[:, 2 * main :]], 1
        ).reshape(GRID[2], -1, channels)

    half_low, half_high = jnp.split(part_of(local_rows(1 - me), c, 0), 2)
    half_low = swapped(half_low)
    half_high = swapped(after(half_high, half_low))
    half = jnp.concatenate([half_low, half_high])
    plane_high, side = gathered_over_y(line_first[..., LANES:], side)
    line_high, _ = gathered_over_z(main_second[:, LANES:], (sent_low, side))
    other_half = shifted(half, dc=1)
    temporal_other = jnp.where(
        c == 0, jnp.concatenate([half, other_half]), jnp.concatenate([other_half, half])
    )
    temporal_mine = local_rows(me).reshape(3 * width, channels)
    temporal_first = jnp.where(first, temporal_mine, temporal_other)
    temporal_second = jnp.where(first, temporal_other, temporal_mine)

    plane_tails, side = gathered_over_y(line_tails, (side, half_low, sent_low))
    tails = gathered_on_chip(plane_tails)
    spatial_first = [gathered_on_chip(plane_low), gathered_on_chip(plane_high), tails]
    plane_low, side = gathered_over_y(line_low, (side, half_high))
    plane_high, _ = gathered_over_y(line_high, (side, other_half))

    def shape(extent, dtype=BF16):
        return jax.ShapeDtypeStruct(extent, dtype)

    spatial_flops = 2 * rows * 9 * channels * width
    temporal_flops = 2 * rows * 3 * channels * width
    spatial_bytes = 2 * 9 * channels * width
    temporal_bytes = 2 * 3 * channels * width
    normed_first, preact_first, mixed = vmem_call(
        functools.partial(first_forward, frames),
        (shape((rows, channels)), shape((rows, width), F32), shape((rows, channels))),
        flops=spatial_flops + temporal_flops,
        moved=spatial_bytes + temporal_bytes,
    )(hidden, embedding, keep_first, temporal_first, *spatial_first)
    mixed_given = swapped(mixed)
    spatial_second = [
        *(gathered_on_chip(plane, mixed) for plane in (plane_low, plane_high)),
        tails,
    ]
    hidden_second, normed_second, activated_second, pre_grad_second, back = vmem_call(
        functools.partial(second_forward, frames),
        (
            shape((rows, channels)),
            shape((rows, channels)),
            shape((rows, width)),
            shape((rows, width)),
            shape((rows, channels)),
        ),
        flops=2 * spatial_flops + temporal_flops,
        moved=spatial_bytes + temporal_bytes,
    )(
        hidden, mixed, mixed_given, embedding, keep_second, upstream, temporal_second,
        *spatial_second,
    )

    def terms_shape():
        return (
            shape((9 * channels, main)),
            shape((9 * channels, width - main)),
            shape((3 * width, channels)),
        )

    def on_chip(terms):
        return summed_on_chip(terms.reshape(*GRID, -1, terms.shape[1]))

    back_given = swapped(back)
    main_terms_second, tail_terms_second, temporal_terms_second = vmem_call(
        functools.partial(second_terms, frames),
        terms_shape(),
        flops=spatial_flops + temporal_flops,
        moved=spatial_bytes + temporal_bytes,
    )(normed_second, pre_grad_second, activated_second, upstream)
    chip_second = on_chip(main_terms_second)
    line, side = summed_over_y(chip_second, None)
    share_second, sent_second = summed_over_z(line)
    main_terms_first, tail_terms_first, temporal_terms_first = vmem_call(
        functools.partial(first_terms, frames),
        terms_shape(),
        flops=spatial_flops + 2 * temporal_flops,
        moved=spatial_bytes + 2 * temporal_bytes,
    )(
        hidden_second, embedding, upstream, back, back_given, normed_first, preact_first,
        keep_first, temporal_first,
    )
    chip_tails = on_chip(after(tail_terms_first + tail_terms_second, side))
    chip_first = on_chip(after(main_terms_first, side))

    terms = jnp.stack(
        [
            jnp.where(first, temporal_terms_first, temporal_terms_second),
            jnp.where(first, temporal_terms_second, temporal_terms_first),
        ]
    ).reshape(2, GRID[2], -1, channels)
    sent = sent_on_chip(part_of(terms, 1 - c, 1))
    halves = added(part_of(terms, c, 1), sent).astype(BF16)
    half_given = swapped(halves[1])
    halves = jnp.stack([halves[0], half_given])
    other_halves = sent_on_chip(halves)
    both = jnp.where(
        c == 0,
        jnp.stack([halves, other_halves], 1),
        jnp.stack([other_halves, halves], 1),
    ).reshape(2, 3, width, channels)
    mine, theirs = both[0], both[1]
    full = jnp.concatenate(
        [
            jnp.where(first, mine[:, :main], theirs[:, :main]),
            jnp.where(first, theirs[:, :main], mine[:, :main]),
            mine[:, main:] + theirs[:, main:],
        ],
        1,
    )
    full = part_of(full.reshape(*GRID, -1, channels), c, 2)

    line, side = summed_over_y(chip_tails, (side, sent))
    line_low, side = summed_over_y(chip_first[..., :LANES], side)
    share_tails, sent_tails = summed_over_z(line, (side, sent_second))
    line_high, side = summed_over_y(chip_first[..., LANES:], side)
    share_first, sent_first = summed_over_z(
        jnp.concatenate([line_low, line_high], 2), (sent_tails, other_halves)
    )
    line, side = summed_over_y(full[..., : 3 * LANES], (side, sent_tails))
    share_low, _ = summed_over_z(line, sent_first)
    line, side = summed_over_y(full[..., 3 * LANES :], side)
    share_high, _ = summed_over_z(line, sent_first)
    share_temporal = jnp.concatenate([share_low, share_high], 1)

    kept = jnp.where(first, share_first, share_second)
    passed = jnp.where(first, share_second, share_first)
    given = jnp.concatenate([passed, share_tails], 1).astype(BF16)
    given = swapped(after(given, side)).astype(F32)
    share_spatial = jnp.concatenate(
        [
            jnp.where(first, kept, given[:, :main]),
            jnp.where(first, given[:, :main], kept),
            jnp.where(tail, share_tails, given[:, main:]),
        ],
        1,
    )
    return (share_spatial[None], share_temporal[None])


def solution(mesh):
    paired = mesh.shape["pipe"] == 2 and mesh.shape["dp"] == math.prod(GRID)
    return jax.shard_map(
        paired_device if paired else per_device,
        mesh=mesh,
        in_specs=(
            P("dp", None, None, None),
            P("dp"),
            P("dp", None, None, None),
            P("pipe", "dp", None),
            P("pipe", "dp", None),
        ),
        out_specs=(P("pipe", "dp", None), P("pipe", "dp", None)),
        check_vma=False,
    )
```

```python
import functools
import math

import jax
import jax.numpy as jnp
from jax import lax
from jax.experimental import pallas as pl
from jax.experimental.pallas import tpu as pltpu
from jax.sharding import PartitionSpec as P

HEIGHT = 8
WIDTH = 4
F32 = jnp.float32
BF16 = jnp.bfloat16
GRID = (4, 2, 2)
LANES = 128


def passed_along(value, axis, steps):
    count = lax.axis_size(axis)
    first, last = (max(0, -steps), min(count, count - steps))
    return lax.ppermute(value, axis, [(source, source + steps) for source in range(first, last)])


def embedding_of(step, channels):
    half_width = channels // 2
    frequency = jnp.exp(-math.log(10000.0) * jnp.arange(half_width, dtype=jnp.float32) / half_width)
    phases = step.astype(jnp.float32) * frequency
    return jnp.concatenate([jnp.sin(phases), jnp.cos(phases)])


def normalize(summed):
    return summed * lax.rsqrt(jnp.mean(summed * summed, axis=-1, keepdims=True) + 1e-06)


def spatial_columns(normed):
    frames, pixels, channels = normed.shape
    grid = normed.reshape(frames, HEIGHT, WIDTH, channels)
    padded = jnp.pad(grid, ((0, 0), (1, 1), (1, 1), (0, 0)))
    pieces = [
        padded[:, row : row + HEIGHT, col : col + WIDTH, :] for row in range(3) for col in range(3)
    ]
    return jnp.concatenate(pieces, axis=-1).reshape(frames * pixels, 9 * channels)


def spatial_fold(grads, frames, channels):
    parts = grads.reshape(frames, HEIGHT, WIDTH, 9, channels)
    padded = jnp.zeros((frames, HEIGHT + 2, WIDTH + 2, channels), jnp.float32)
    for row in range(3):
        for col in range(3):
            padded = padded.at[:, row : row + HEIGHT, col : col + WIDTH, :].add(
                parts[:, :, :, row * 3 + col, :]
            )
    return padded[:, 1 : HEIGHT + 1, 1 : WIDTH + 1, :].reshape(frames, HEIGHT * WIDTH, channels)


def temporal_columns(activated):
    frames, pixels, channels = activated.shape
    padded = jnp.pad(activated, ((1, 1), (0, 0), (0, 0)))
    pieces = [padded[tap : tap + frames] for tap in range(3)]
    return jnp.concatenate(pieces, axis=-1).reshape(frames * pixels, 3 * channels)


def temporal_fold(grads, frames, pixels, channels):
    parts = grads.reshape(frames, pixels, 3, channels)
    padded = jnp.zeros((frames + 2, pixels, channels), jnp.float32)
    for tap in range(3):
        padded = padded.at[tap : tap + frames].add(parts[:, :, tap, :])
    return padded[1 : frames + 1]


def section_forward(block_in, embedding, spatial, temporal):
    frames, pixels, channels = block_in.shape
    summed = block_in.astype(jnp.float32) + embedding
    normed = normalize(summed).astype(jnp.bfloat16)
    preact = jnp.dot(spatial_columns(normed), spatial, preferred_element_type=jnp.float32)
    activated = jax.nn.silu(preact).astype(jnp.bfloat16).reshape(frames, pixels, channels)
    mixed = jnp.dot(temporal_columns(activated), temporal, preferred_element_type=jnp.float32)
    return (block_in.astype(jnp.float32) + mixed.reshape(frames, pixels, channels)).astype(
        jnp.bfloat16
    )


def backward_first(block_in, embedding, spatial, temporal, upstream):
    frames, pixels, channels = block_in.shape
    summed = block_in.astype(jnp.float32) + embedding
    normed = normalize(summed).astype(jnp.bfloat16)
    columns = spatial_columns(normed)
    preact = jnp.dot(columns, spatial, preferred_element_type=jnp.float32)
    activated = jax.nn.silu(preact).astype(jnp.bfloat16).reshape(frames, pixels, channels)
    tcolumns = temporal_columns(activated)
    upstream_flat = upstream.reshape(frames * pixels, channels)
    temporal_term = jnp.dot(tcolumns.T, upstream_flat, preferred_element_type=jnp.float32)
    act_grad = temporal_fold(
        jnp.dot(upstream_flat, temporal.T, preferred_element_type=jnp.float32),
        frames,
        pixels,
        channels,
    )
    logistic = jax.nn.sigmoid(preact)
    slope = logistic * (1.0 + preact * (1.0 - logistic))
    pre_grad = (act_grad.reshape(frames * pixels, channels) * slope).astype(jnp.bfloat16)
    return (temporal_term, pre_grad, columns)


def backward_second(block_in, embedding, spatial, upstream, pre_grad, columns):
    frames, pixels, channels = block_in.shape
    summed = block_in.astype(jnp.float32) + embedding
    spatial_term = jnp.dot(columns.T, pre_grad, preferred_element_type=jnp.float32)
    norm_grad = spatial_fold(
        jnp.dot(pre_grad, spatial.T, preferred_element_type=jnp.float32), frames, channels
    )
    _, pullback = jax.vjp(normalize, summed)
    back_input = (upstream.astype(jnp.float32) + pullback(norm_grad)[0]).astype(jnp.bfloat16)
    return (back_input, spatial_term)


def section_backward(block_in, embedding, spatial, temporal, upstream):
    temporal_term, pre_grad, columns = backward_first(
        block_in, embedding, spatial, temporal, upstream
    )
    back_input, spatial_term = backward_second(
        block_in, embedding, spatial, upstream, pre_grad, columns
    )
    return (back_input, spatial_term, temporal_term)


def per_device(samples, timesteps, cotangent, spatial_weight, temporal_weight):
    sections = lax.axis_size("pipe")
    section_index = lax.axis_index("pipe")
    micro_count = samples.shape[0]
    frames, pixels, channels = (samples.shape[1], samples.shape[2], samples.shape[3])
    moments = jnp.arange(micro_count + sections - 1, dtype=jnp.int32)
    blank = jnp.zeros((frames, pixels, channels), jnp.bfloat16)
    full_spatial, full_temporal = (
        lax.all_gather(spatial_weight[0], "dp", axis=0, tiled=True),
        lax.all_gather(temporal_weight[0], "dp", axis=0, tiled=True),
    )

    def forward_step(carry, moment):
        incoming, stash = carry
        position = moment - section_index
        active = (position >= 0) & (position < micro_count)
        picked = jnp.clip(position, 0, micro_count - 1)
        own = lax.dynamic_index_in_dim(samples, picked, 0, keepdims=False)
        embedding = embedding_of(
            lax.dynamic_index_in_dim(timesteps, picked, 0, keepdims=False), channels
        )
        block_in = jnp.where(section_index == 0, own, incoming)
        result = lax.cond(
            active & (section_index < sections - 1),
            lambda: section_forward(block_in, embedding, full_spatial, full_temporal),
            lambda: blank,
        )
        stash = jnp.where(
            active, lax.dynamic_update_index_in_dim(stash, block_in, picked, 0), stash
        )
        passed = passed_along(result, "pipe", 1)
        return ((passed, stash), None)

    (_, stash), _ = lax.scan(forward_step, (blank, jnp.zeros_like(samples)), moments)
    back_spatial, back_temporal = (full_spatial, full_temporal)

    def inputs_at(moment, incoming):
        position = moment - (sections - 1 - section_index)
        active = (position >= 0) & (position < micro_count)
        picked = jnp.clip(position, 0, micro_count - 1)
        block_in = lax.dynamic_index_in_dim(stash, picked, 0, keepdims=False)
        embedding = embedding_of(
            lax.dynamic_index_in_dim(timesteps, picked, 0, keepdims=False), channels
        )
        given = lax.dynamic_index_in_dim(cotangent, picked, 0, keepdims=False)
        upstream = jnp.where(section_index == sections - 1, given, incoming)
        return (active, block_in, embedding, upstream)

    def backward_step(carry, moment):
        incoming, grad_spatial, grad_temporal = carry
        active, block_in, embedding, upstream = inputs_at(moment, incoming)

        def working():
            back_input, spatial_term, temporal_term = section_backward(
                block_in, embedding, back_spatial, back_temporal, upstream
            )
            return (back_input, grad_spatial + spatial_term, grad_temporal + temporal_term)

        def waiting():
            return (blank, grad_spatial, grad_temporal)

        back_input, grad_spatial, grad_temporal = lax.cond(active, working, waiting)
        passed = passed_along(back_input, "pipe", -1)
        return ((passed, grad_spatial, grad_temporal), None)

    start = (
        blank,
        jnp.zeros(back_spatial.shape, jnp.float32),
        jnp.zeros(back_temporal.shape, jnp.float32),
    )
    (_, grad_spatial, grad_temporal), _ = lax.scan(backward_step, start, moments)
    share_spatial, share_temporal = (
        lax.psum_scatter(
            grad_spatial.astype(jnp.bfloat16).astype(jnp.float32).astype(jnp.bfloat16),
            "dp",
            scatter_dimension=0,
            tiled=True,
        ).astype(jnp.float32),
        lax.psum_scatter(
            grad_temporal.astype(jnp.bfloat16).astype(jnp.float32).astype(jnp.bfloat16),
            "dp",
            scatter_dimension=0,
            tiled=True,
        ).astype(jnp.float32),
    )
    return (share_spatial[None], share_temporal[None])


def coordinates():
    index = lax.axis_index("dp")
    return index // (GRID[1] * GRID[2]), (index // GRID[2]) % GRID[1], index % GRID[2]


def shifted(value, dz=0, dy=0, dc=0):
    pairs = []
    for z in range(GRID[0]):
        for y in range(GRID[1]):
            for c in range(GRID[2]):
                place = ((z + dz) % GRID[0], (y + dy) % GRID[1], (c + dc) % GRID[2])
                pairs.append(
                    (
                        (z * GRID[1] + y) * GRID[2] + c,
                        (place[0] * GRID[1] + place[1]) * GRID[2] + place[2],
                    )
                )
    return lax.ppermute(value, "dp", pairs)


def swapped(value):
    return lax.ppermute(value, "pipe", [(0, 1), (1, 0)])


def part_of(value, index, axis):
    return lax.dynamic_index_in_dim(value, index, axis, keepdims=False)


def vmem_call(body, outs, scratch=(), flops=0, moved=0):
    return pl.pallas_call(
        body,
        out_shape=outs,
        scratch_shapes=list(scratch),
        compiler_params=pltpu.CompilerParams(vmem_limit_bytes=24 * 2**20),
        cost_estimate=pl.CostEstimate(
            flops=5 * flops // 2, bytes_accessed=moved, transcendentals=0
        ),
    )


def after(value, earlier):
    return value if earlier is None else lax.optimization_barrier((value, earlier))[0]


def in_order(swap, own, other, axis):
    return jnp.where(
        swap, jnp.concatenate([other, own], axis), jnp.concatenate([own, other], axis)
    )


def over_z(value, pairs):
    moves = []
    for source, target in pairs:
        for rest in range(GRID[1] * GRID[2]):
            moves.append(tuple(z * GRID[1] * GRID[2] + rest for z in (source, target)))
    return lax.ppermute(value, "dp", moves)


def exchanged_over_z(value):
    groups = [
        [z * GRID[1] * GRID[2] + rest for z in range(GRID[0])]
        for rest in range(GRID[1] * GRID[2])
    ]
    return lax.all_to_all(value, "dp", 0, 0, axis_index_groups=groups, tiled=True)


def sent_on_chip(value):
    return shifted(value, dc=1)


def gathered_over_z(value, earlier=None):
    value = after(value, earlier)
    return exchanged_over_z(jnp.broadcast_to(value, (GRID[0], *value.shape)))


def gathered_over_y(line, earlier=None, beside=None):
    _, y, _ = coordinates()
    line = after(line, earlier)
    sent = after(shifted(line, dy=1), beside)
    return in_order(y == 1, line[:, None], sent[:, None], 1), sent


def gathered_on_chip(plane, earlier=None):
    _, _, c = coordinates()
    plane = after(plane, earlier)
    whole = in_order(c == 1, plane[:, :, None], sent_on_chip(plane)[:, :, None], 2)
    return whole.reshape(-1, plane.shape[3])


def added(*terms):
    return sum(term.astype(F32) for term in terms)


def summed_on_chip(value):
    _, _, c = coordinates()
    sent = sent_on_chip(part_of(value, 1 - c, 2))
    return added(part_of(value, c, 2), sent).astype(BF16)


def summed_over_y(value, earlier=None, beside=None):
    _, y, _ = coordinates()
    sent = after(shifted(after(part_of(value, 1 - y, 1), earlier), dy=1), beside)
    return added(part_of(value, y, 1), sent).astype(BF16), sent


def summed_over_z(line, earlier=None):
    return jnp.sum(exchanged_over_z(after(line, earlier)).astype(F32), 0)


def pixel_masks(rows):
    row = lax.broadcasted_iota(jnp.int32, (rows, 1), 0)
    high, wide = (row // WIDTH) % HEIGHT, row % WIDTH
    masks = []
    for dr in (-1, 0, 1):
        for dc in (-1, 0, 1):
            inside = (high + dr >= 0) & (high + dr < HEIGHT) & (wide + dc >= 0) & (wide + dc < WIDTH)
            masks.append((dr * WIDTH + dc, inside))
    return masks


def frame_masks(rows, frames):
    pixels = HEIGHT * WIDTH
    row = lax.broadcasted_iota(jnp.int32, (rows, 1), 0)
    frame = (row // pixels) % frames
    return [
        (step * pixels, (frame + step >= 0) & (frame + step < frames)) for step in (-1, 0, 1)
    ]


def moved_rows(value, move):
    shift, inside = move
    if shift:
        value = pltpu.roll(value, (-shift) % value.shape[0], 0)
    return jnp.where(inside, value, 0.0)


def dot(left, right, dims=((1,), (0,))):
    return lax.dot_general(left, right, (dims, ((), ())), preferred_element_type=F32)


def with_embedding(hidden, embedding_ref, samples):
    per = hidden.shape[0] // samples
    return jnp.concatenate(
        [hidden[s * per : (s + 1) * per] + embedding_ref[s : s + 1, :] for s in range(samples)]
    )


def scale_of(summed):
    return lax.rsqrt(jnp.mean(summed * summed, axis=-1, keepdims=True) + 1e-06)


def silu_parts(preact):
    logistic = 1.0 / (1.0 + jnp.exp(-preact))
    return logistic, preact * logistic


def tap_weight(weight_refs, tap, channels):
    return jnp.concatenate(
        [ref[tap * channels : (tap + 1) * channels, :] for ref in weight_refs], 1
    )


def convolved(normed, weight_refs, masks):
    rows, channels = normed.shape
    normed = normed.astype(F32)
    total = None
    for tap in range(9):
        term = dot(
            moved_rows(normed, masks[tap]).astype(BF16),
            tap_weight(weight_refs, tap, channels),
        )
        total = term if total is None else total + term
    return total


def first_forward(frames, hidden_ref, embedding_ref, keep_ref, temporal_ref, *refs):
    *spatial_refs, normed_ref, preact_ref, mixed_ref = refs
    rows = hidden_ref.shape[0]
    width = keep_ref.shape[1]
    summed = with_embedding(hidden_ref[...].astype(F32), embedding_ref, embedding_ref.shape[0])
    normed = (summed * scale_of(summed)).astype(BF16)
    normed_ref[...] = normed
    preact = convolved(normed, spatial_refs, pixel_masks(rows))
    preact_ref[...] = preact
    activated = silu_parts(preact)[1].astype(BF16).astype(F32) * keep_ref[...]
    mixed = None
    for tap, move in enumerate(frame_masks(rows, frames)):
        term = dot(
            moved_rows(activated, move).astype(BF16),
            temporal_ref[tap * width : (tap + 1) * width, :],
        )
        mixed = term if mixed is None else mixed + term
    mixed_ref[...] = mixed.astype(BF16)


def slope_of(preact):
    logistic, _ = silu_parts(preact)
    return logistic * (1.0 + preact * (1.0 - logistic))


def act_grad_of(upstream, temporal_ref, width, frames):
    upstream = upstream.astype(F32)
    moves = frame_masks(upstream.shape[0], frames)
    total = None
    for tap in range(3):
        term = dot(
            moved_rows(upstream, moves[2 - tap]).astype(BF16),
            temporal_ref[tap * width : (tap + 1) * width, :],
            ((1,), (1,)),
        )
        total = term if total is None else total + term
    return total


def store_temporal_terms(activated, upstream, frames, out_ref):
    width = activated.shape[1]
    upstream = upstream.astype(F32)
    moves = frame_masks(upstream.shape[0], frames)
    for tap in range(3):
        out_ref[tap * width : (tap + 1) * width, :] = dot(
            activated, moved_rows(upstream, moves[2 - tap]).astype(BF16), ((0,), (0,))
        ).astype(BF16)


def store_spatial_terms(normed, pre_grad, out_refs):
    channels = normed.shape[1]
    pre_grad = pre_grad.astype(F32)
    masks = pixel_masks(pre_grad.shape[0])
    for tap in range(9):
        term = dot(
            normed, moved_rows(pre_grad, masks[8 - tap]).astype(BF16), ((0,), (0,))
        ).astype(BF16)
        start = 0
        for out_ref in out_refs:
            end = start + out_ref.shape[1]
            out_ref[tap * channels : (tap + 1) * channels, :] = term[:, start:end]
            start = end


def second_forward(
    frames, hidden_ref, own_ref, sent_ref, embedding_ref, keep_ref, upstream_ref, temporal_ref, *refs
):
    *spatial_refs, next_ref, normed_ref, activated_ref, pre_grad_ref, back_ref = refs
    rows, channels = hidden_ref.shape
    width = keep_ref.shape[1]
    masks = pixel_masks(rows)
    mixed = own_ref[...].astype(F32) + sent_ref[...].astype(F32)
    hidden = (hidden_ref[...].astype(F32) + mixed).astype(BF16)
    next_ref[...] = hidden
    summed = with_embedding(hidden.astype(F32), embedding_ref, embedding_ref.shape[0])
    normed = (summed * scale_of(summed)).astype(BF16)
    normed_ref[...] = normed
    preact = convolved(normed, spatial_refs, masks)
    activated_ref[...] = (silu_parts(preact)[1] * keep_ref[...]).astype(BF16)
    act_grad = act_grad_of(upstream_ref[...], temporal_ref, width, frames)
    pre_grad = (act_grad * slope_of(preact) * keep_ref[...]).astype(BF16)
    pre_grad_ref[...] = pre_grad
    pre_grad = pre_grad.astype(F32)
    back = None
    for tap in range(9):
        term = dot(
            moved_rows(pre_grad, masks[8 - tap]).astype(BF16),
            tap_weight(spatial_refs, tap, channels),
            ((1,), (1,)),
        )
        back = term if back is None else back + term
    back_ref[...] = back.astype(BF16)


def second_terms(frames, normed_ref, pre_grad_ref, activated_ref, upstream_ref, *outs):
    *spatial_refs, temporal_ref = outs
    store_spatial_terms(normed_ref[...], pre_grad_ref[...], spatial_refs)
    store_temporal_terms(activated_ref[...], upstream_ref[...], frames, temporal_ref)


def first_terms(
    frames, hidden_ref, embedding_ref, upstream_ref, own_ref, sent_ref, normed_ref, preact_ref,
    keep_ref, temporal_ref, *outs
):
    *spatial_outs, temporal_out = outs
    width = keep_ref.shape[1]
    channels = hidden_ref.shape[1]
    summed = with_embedding(hidden_ref[...].astype(F32), embedding_ref, embedding_ref.shape[0])
    scale = scale_of(summed)
    grad = own_ref[...].astype(F32) + sent_ref[...].astype(F32)
    inner = jnp.sum(grad * summed, axis=-1, keepdims=True)
    back = grad * scale - summed * (scale * scale * scale) * (inner / channels)
    upstream = (upstream_ref[...].astype(F32) + back).astype(BF16)
    preact = preact_ref[...]
    activated = (silu_parts(preact)[1] * keep_ref[...]).astype(BF16)
    act_grad = act_grad_of(upstream, temporal_ref, width, frames)
    pre_grad = (act_grad * slope_of(preact) * keep_ref[...]).astype(BF16)
    store_spatial_terms(normed_ref[...], pre_grad, spatial_outs)
    store_temporal_terms(activated, upstream, frames, temporal_out)


def paired_device(samples, timesteps, cotangent, spatial_weight, temporal_weight):
    me = lax.axis_index("pipe")
    first = me == 0
    _, _, c = coordinates()
    count, frames, pixels, channels = samples.shape
    rows = count * frames * pixels
    main = 2 * LANES
    width = main + LANES
    hidden = samples.reshape(rows, channels)
    upstream = cotangent.reshape(rows, channels)
    embedding = jax.vmap(lambda step: embedding_of(step, channels))(timesteps)
    lane = jnp.arange(LANES)
    keep_own = jnp.concatenate([jnp.ones(main), lane < LANES // 2]).astype(F32)[None]
    keep_other = jnp.concatenate([jnp.ones(main), lane >= LANES // 2]).astype(F32)[None]
    keep_first = jnp.where(first, keep_own, keep_other)
    keep_second = jnp.where(first, keep_other, keep_own)
    tail = lane[None] < LANES // 2

    def main_of(value, index, axis):
        return lax.dynamic_slice_in_dim(value, index * main, main, axis)

    spatial_own = spatial_weight[0]
    given = swapped(
        jnp.concatenate([main_of(spatial_own, 1 - me, 1), spatial_own[:, 2 * main :]], 1)
    )
    main_own, main_given = main_of(spatial_own, me, 1), given[:, :main]
    tails = jnp.where(tail, spatial_own[:, 2 * main :], given[:, main:])
    main_first = jnp.where(first, main_own, main_given)
    main_second = jnp.where(first, main_given, main_own)
    line_temporal = gathered_over_z(temporal_weight[0])
    line_first = gathered_over_z(jnp.concatenate([main_first, tails], 1), line_temporal)
    plane_temporal, side = gathered_over_y(line_temporal, None, line_first)
    line_second = gathered_over_z(main_second, (line_first, side))
    temporal_own = gathered_on_chip(plane_temporal).reshape(3, channels, channels)

    def local_rows(index):
        return jnp.concatenate(
            [main_of(temporal_own, index, 1), temporal_own[:, 2 * main :]], 1
        ).reshape(GRID[2], -1, channels)

    half = swapped(part_of(local_rows(1 - me), c, 0))
    plane_first, side = gathered_over_y(line_first, side, (line_second, half))
    other_half = shifted(half, dc=1)
    temporal_other = jnp.where(
        c == 0, jnp.concatenate([half, other_half]), jnp.concatenate([other_half, half])
    )
    temporal_mine = local_rows(me).reshape(3 * width, channels)
    temporal_first = jnp.where(first, temporal_mine, temporal_other)
    temporal_second = jnp.where(first, temporal_other, temporal_mine)

    plane_second, _ = gathered_over_y(line_second, side)
    spatial_first = gathered_on_chip(plane_first)

    def shape(extent, dtype=BF16):
        return jax.ShapeDtypeStruct(extent, dtype)

    spatial_flops = 2 * rows * 9 * channels * width
    temporal_flops = 2 * rows * 3 * channels * width
    spatial_bytes = 2 * 9 * channels * width
    temporal_bytes = 2 * 3 * channels * width
    normed_first, preact_first, mixed = vmem_call(
        functools.partial(first_forward, frames),
        (shape((rows, channels)), shape((rows, width), F32), shape((rows, channels))),
        flops=spatial_flops + temporal_flops,
        moved=spatial_bytes + temporal_bytes,
    )(hidden, embedding, keep_first, temporal_first, spatial_first)
    mixed_given = swapped(mixed)
    spatial_second = [
        gathered_on_chip(plane_second, mixed),
        spatial_first[:, main:],
    ]
    hidden_second, normed_second, activated_second, pre_grad_second, back = vmem_call(
        functools.partial(second_forward, frames),
        (
            shape((rows, channels)),
            shape((rows, channels)),
            shape((rows, width)),
            shape((rows, width)),
            shape((rows, channels)),
        ),
        flops=2 * spatial_flops + temporal_flops,
        moved=spatial_bytes + temporal_bytes,
    )(
        hidden, mixed, mixed_given, embedding, keep_second, upstream, temporal_second,
        *spatial_second,
    )

    def terms_shape():
        return (
            shape((9 * channels, main)),
            shape((9 * channels, width - main)),
            shape((3 * width, channels)),
        )

    def on_chip(terms):
        return summed_on_chip(terms.reshape(*GRID, -1, terms.shape[1]))

    back_given = swapped(back)
    main_terms_second, tail_terms_second, temporal_terms_second = vmem_call(
        functools.partial(second_terms, frames),
        terms_shape(),
        flops=spatial_flops + temporal_flops,
        moved=spatial_bytes + temporal_bytes,
    )(normed_second, pre_grad_second, activated_second, upstream)
    chip_second = on_chip(main_terms_second)
    back_given = after(back_given, chip_second)
    main_terms_first, tail_terms_first, temporal_terms_first = vmem_call(
        functools.partial(first_terms, frames),
        terms_shape(),
        flops=spatial_flops + 2 * temporal_flops,
        moved=spatial_bytes + 2 * temporal_bytes,
    )(
        hidden_second, embedding, upstream, back, back_given, normed_first, preact_first,
        keep_first, temporal_first,
    )
    line_second, side = summed_over_y(chip_second, None, temporal_terms_first)
    terms_first = jnp.concatenate([main_terms_first, tail_terms_first + tail_terms_second], 1)
    chip_first = on_chip(terms_first)
    share_second = summed_over_z(line_second, chip_first)

    terms = jnp.stack(
        [
            jnp.where(first, temporal_terms_first, temporal_terms_second),
            jnp.where(first, temporal_terms_second, temporal_terms_first),
        ]
    ).reshape(2, GRID[2], -1, channels)
    sent = sent_on_chip(part_of(terms, 1 - c, 1))
    halves = added(part_of(terms, c, 1), sent).astype(BF16)
    half_given = swapped(halves[1])
    halves = jnp.stack([halves[0], half_given])
    other_halves = sent_on_chip(halves)
    both = jnp.where(
        c == 0,
        jnp.stack([halves, other_halves], 1),
        jnp.stack([other_halves, halves], 1),
    ).reshape(2, 3, width, channels)
    mine, theirs = both[0], both[1]
    full = jnp.concatenate(
        [
            jnp.where(first, mine[:, :main], theirs[:, :main]),
            jnp.where(first, theirs[:, :main], mine[:, :main]),
            mine[:, main:] + theirs[:, main:],
        ],
        1,
    )
    full = part_of(full.reshape(*GRID, -1, channels), c, 2)

    line, side = summed_over_y(chip_first, (side, sent), share_second)
    share_first = summed_over_z(line)
    share_first, share_tails = share_first[:, :main], share_first[:, main:]
    line, side = summed_over_y(full, side, share_first)
    share_temporal = summed_over_z(line)

    kept = jnp.where(first, share_first, share_second)
    passed = jnp.where(first, share_second, share_first)
    given = jnp.concatenate([passed, share_tails], 1).astype(BF16)
    given = swapped(after(given, side)).astype(F32)
    share_spatial = jnp.concatenate(
        [
            jnp.where(first, kept, given[:, :main]),
            jnp.where(first, given[:, :main], kept),
            jnp.where(tail, share_tails, given[:, main:]),
        ],
        1,
    )
    return (share_spatial[None], share_temporal[None])


def solution(mesh):
    paired = mesh.shape["pipe"] == 2 and mesh.shape["dp"] == math.prod(GRID)
    return jax.shard_map(
        paired_device if paired else per_device,
        mesh=mesh,
        in_specs=(
            P("dp", None, None, None),
            P("dp"),
            P("dp", None, None, None),
            P("pipe", "dp", None),
            P("pipe", "dp", None),
        ),
        out_specs=(P("pipe", "dp", None), P("pipe", "dp", None)),
        check_vma=False,
    )
```

```python
import functools
import math

import jax
import jax.numpy as jnp
from jax import lax
from jax.experimental import pallas as pl
from jax.experimental.pallas import tpu as pltpu
from jax.sharding import PartitionSpec as P

HEIGHT = 8
WIDTH = 4
F32 = jnp.float32
BF16 = jnp.bfloat16
GRID = (4, 2, 2)
LANES = 128


def passed_along(value, axis, steps):
    count = lax.axis_size(axis)
    first, last = (max(0, -steps), min(count, count - steps))
    return lax.ppermute(value, axis, [(source, source + steps) for source in range(first, last)])


def embedding_of(step, channels):
    half_width = channels // 2
    frequency = jnp.exp(-math.log(10000.0) * jnp.arange(half_width, dtype=jnp.float32) / half_width)
    phases = step.astype(jnp.float32) * frequency
    return jnp.concatenate([jnp.sin(phases), jnp.cos(phases)])


def normalize(summed):
    return summed * lax.rsqrt(jnp.mean(summed * summed, axis=-1, keepdims=True) + 1e-06)


def spatial_columns(normed):
    frames, pixels, channels = normed.shape
    grid = normed.reshape(frames, HEIGHT, WIDTH, channels)
    padded = jnp.pad(grid, ((0, 0), (1, 1), (1, 1), (0, 0)))
    pieces = [
        padded[:, row : row + HEIGHT, col : col + WIDTH, :] for row in range(3) for col in range(3)
    ]
    return jnp.concatenate(pieces, axis=-1).reshape(frames * pixels, 9 * channels)


def spatial_fold(grads, frames, channels):
    parts = grads.reshape(frames, HEIGHT, WIDTH, 9, channels)
    padded = jnp.zeros((frames, HEIGHT + 2, WIDTH + 2, channels), jnp.float32)
    for row in range(3):
        for col in range(3):
            padded = padded.at[:, row : row + HEIGHT, col : col + WIDTH, :].add(
                parts[:, :, :, row * 3 + col, :]
            )
    return padded[:, 1 : HEIGHT + 1, 1 : WIDTH + 1, :].reshape(frames, HEIGHT * WIDTH, channels)


def temporal_columns(activated):
    frames, pixels, channels = activated.shape
    padded = jnp.pad(activated, ((1, 1), (0, 0), (0, 0)))
    pieces = [padded[tap : tap + frames] for tap in range(3)]
    return jnp.concatenate(pieces, axis=-1).reshape(frames * pixels, 3 * channels)


def temporal_fold(grads, frames, pixels, channels):
    parts = grads.reshape(frames, pixels, 3, channels)
    padded = jnp.zeros((frames + 2, pixels, channels), jnp.float32)
    for tap in range(3):
        padded = padded.at[tap : tap + frames].add(parts[:, :, tap, :])
    return padded[1 : frames + 1]


def section_forward(block_in, embedding, spatial, temporal):
    frames, pixels, channels = block_in.shape
    summed = block_in.astype(jnp.float32) + embedding
    normed = normalize(summed).astype(jnp.bfloat16)
    preact = jnp.dot(spatial_columns(normed), spatial, preferred_element_type=jnp.float32)
    activated = jax.nn.silu(preact).astype(jnp.bfloat16).reshape(frames, pixels, channels)
    mixed = jnp.dot(temporal_columns(activated), temporal, preferred_element_type=jnp.float32)
    return (block_in.astype(jnp.float32) + mixed.reshape(frames, pixels, channels)).astype(
        jnp.bfloat16
    )


def backward_first(block_in, embedding, spatial, temporal, upstream):
    frames, pixels, channels = block_in.shape
    summed = block_in.astype(jnp.float32) + embedding
    normed = normalize(summed).astype(jnp.bfloat16)
    columns = spatial_columns(normed)
    preact = jnp.dot(columns, spatial, preferred_element_type=jnp.float32)
    activated = jax.nn.silu(preact).astype(jnp.bfloat16).reshape(frames, pixels, channels)
    tcolumns = temporal_columns(activated)
    upstream_flat = upstream.reshape(frames * pixels, channels)
    temporal_term = jnp.dot(tcolumns.T, upstream_flat, preferred_element_type=jnp.float32)
    act_grad = temporal_fold(
        jnp.dot(upstream_flat, temporal.T, preferred_element_type=jnp.float32),
        frames,
        pixels,
        channels,
    )
    logistic = jax.nn.sigmoid(preact)
    slope = logistic * (1.0 + preact * (1.0 - logistic))
    pre_grad = (act_grad.reshape(frames * pixels, channels) * slope).astype(jnp.bfloat16)
    return (temporal_term, pre_grad, columns)


def backward_second(block_in, embedding, spatial, upstream, pre_grad, columns):
    frames, pixels, channels = block_in.shape
    summed = block_in.astype(jnp.float32) + embedding
    spatial_term = jnp.dot(columns.T, pre_grad, preferred_element_type=jnp.float32)
    norm_grad = spatial_fold(
        jnp.dot(pre_grad, spatial.T, preferred_element_type=jnp.float32), frames, channels
    )
    _, pullback = jax.vjp(normalize, summed)
    back_input = (upstream.astype(jnp.float32) + pullback(norm_grad)[0]).astype(jnp.bfloat16)
    return (back_input, spatial_term)


def section_backward(block_in, embedding, spatial, temporal, upstream):
    temporal_term, pre_grad, columns = backward_first(
        block_in, embedding, spatial, temporal, upstream
    )
    back_input, spatial_term = backward_second(
        block_in, embedding, spatial, upstream, pre_grad, columns
    )
    return (back_input, spatial_term, temporal_term)


def per_device(samples, timesteps, cotangent, spatial_weight, temporal_weight):
    sections = lax.axis_size("pipe")
    section_index = lax.axis_index("pipe")
    micro_count = samples.shape[0]
    frames, pixels, channels = (samples.shape[1], samples.shape[2], samples.shape[3])
    moments = jnp.arange(micro_count + sections - 1, dtype=jnp.int32)
    blank = jnp.zeros((frames, pixels, channels), jnp.bfloat16)
    full_spatial, full_temporal = (
        lax.all_gather(spatial_weight[0], "dp", axis=0, tiled=True),
        lax.all_gather(temporal_weight[0], "dp", axis=0, tiled=True),
    )

    def forward_step(carry, moment):
        incoming, stash = carry
        position = moment - section_index
        active = (position >= 0) & (position < micro_count)
        picked = jnp.clip(position, 0, micro_count - 1)
        own = lax.dynamic_index_in_dim(samples, picked, 0, keepdims=False)
        embedding = embedding_of(
            lax.dynamic_index_in_dim(timesteps, picked, 0, keepdims=False), channels
        )
        block_in = jnp.where(section_index == 0, own, incoming)
        result = lax.cond(
            active & (section_index < sections - 1),
            lambda: section_forward(block_in, embedding, full_spatial, full_temporal),
            lambda: blank,
        )
        stash = jnp.where(
            active, lax.dynamic_update_index_in_dim(stash, block_in, picked, 0), stash
        )
        passed = passed_along(result, "pipe", 1)
        return ((passed, stash), None)

    (_, stash), _ = lax.scan(forward_step, (blank, jnp.zeros_like(samples)), moments)
    back_spatial, back_temporal = (full_spatial, full_temporal)

    def inputs_at(moment, incoming):
        position = moment - (sections - 1 - section_index)
        active = (position >= 0) & (position < micro_count)
        picked = jnp.clip(position, 0, micro_count - 1)
        block_in = lax.dynamic_index_in_dim(stash, picked, 0, keepdims=False)
        embedding = embedding_of(
            lax.dynamic_index_in_dim(timesteps, picked, 0, keepdims=False), channels
        )
        given = lax.dynamic_index_in_dim(cotangent, picked, 0, keepdims=False)
        upstream = jnp.where(section_index == sections - 1, given, incoming)
        return (active, block_in, embedding, upstream)

    def backward_step(carry, moment):
        incoming, grad_spatial, grad_temporal = carry
        active, block_in, embedding, upstream = inputs_at(moment, incoming)

        def working():
            back_input, spatial_term, temporal_term = section_backward(
                block_in, embedding, back_spatial, back_temporal, upstream
            )
            return (back_input, grad_spatial + spatial_term, grad_temporal + temporal_term)

        def waiting():
            return (blank, grad_spatial, grad_temporal)

        back_input, grad_spatial, grad_temporal = lax.cond(active, working, waiting)
        passed = passed_along(back_input, "pipe", -1)
        return ((passed, grad_spatial, grad_temporal), None)

    start = (
        blank,
        jnp.zeros(back_spatial.shape, jnp.float32),
        jnp.zeros(back_temporal.shape, jnp.float32),
    )
    (_, grad_spatial, grad_temporal), _ = lax.scan(backward_step, start, moments)
    share_spatial, share_temporal = (
        lax.psum_scatter(
            grad_spatial.astype(jnp.bfloat16).astype(jnp.float32).astype(jnp.bfloat16),
            "dp",
            scatter_dimension=0,
            tiled=True,
        ).astype(jnp.float32),
        lax.psum_scatter(
            grad_temporal.astype(jnp.bfloat16).astype(jnp.float32).astype(jnp.bfloat16),
            "dp",
            scatter_dimension=0,
            tiled=True,
        ).astype(jnp.float32),
    )
    return (share_spatial[None], share_temporal[None])


GROUP = 20


def coordinates():
    index = lax.axis_index("dp")
    return index // (GRID[1] * GRID[2]), (index // GRID[2]) % GRID[1], index % GRID[2]


def shifted(value, dz=0, dy=0, dc=0):
    pairs = []
    for z in range(GRID[0]):
        for y in range(GRID[1]):
            for c in range(GRID[2]):
                place = ((z + dz) % GRID[0], (y + dy) % GRID[1], (c + dc) % GRID[2])
                pairs.append(
                    (
                        (z * GRID[1] + y) * GRID[2] + c,
                        (place[0] * GRID[1] + place[1]) * GRID[2] + place[2],
                    )
                )
    return lax.ppermute(value, "dp", pairs)


def swapped(value):
    return lax.ppermute(value, "pipe", [(0, 1), (1, 0)])


def part_of(value, index, axis):
    return lax.dynamic_index_in_dim(value, index, axis, keepdims=False)


def vmem_call(body, outs, scratch=(), flops=0, moved=0):
    return pl.pallas_call(
        body,
        out_shape=outs,
        scratch_shapes=list(scratch),
        compiler_params=pltpu.CompilerParams(vmem_limit_bytes=24 * 2**20),
        cost_estimate=pl.CostEstimate(
            flops=5 * flops // 2, bytes_accessed=moved, transcendentals=0
        ),
    )


def after(value, earlier):
    return value if earlier is None else lax.optimization_barrier((value, earlier))[0]


def in_order(swap, own, other, axis):
    return jnp.where(
        swap, jnp.concatenate([other, own], axis), jnp.concatenate([own, other], axis)
    )


def over_z(value, pairs):
    moves = []
    for source, target in pairs:
        for rest in range(GRID[1] * GRID[2]):
            moves.append(tuple(z * GRID[1] * GRID[2] + rest for z in (source, target)))
    return lax.ppermute(value, "dp", moves)


def sent_over_z(value):
    return [shifted(value, dz=step) for step in range(1, GRID[0])]


def sent_on_chip(value):
    return shifted(value, dc=1)


def places_of(channels, main):
    channel = jnp.arange(channels)
    odd = (channel // GROUP) % 2
    rank = channel // (2 * GROUP) * GROUP + channel % GROUP
    tail = channels // 2 - main
    return jnp.where(rank < main, odd * main + rank, (1 + odd) * main + odd * (tail - main) + rank)


def halves_of(value):
    groups = value.reshape(-1, 2, GROUP, value.shape[1])
    return [groups[:, odd].reshape(-1, value.shape[1]) for odd in range(2)]


def gathered_over_z(value, earlier=None):
    z, _, _ = coordinates()
    value = after(value, earlier)
    sent = sent_over_z(value)
    return (
        jnp.stack([lax.select_n((z - place) % GRID[0], value, *sent) for place in range(GRID[0])]),
        sent,
    )


def gathered_over_y(line):
    _, y, _ = coordinates()
    return in_order(y == 1, line[:, None], shifted(line, dy=1)[:, None], 1)


def gathered_on_chip(plane, earlier=None):
    _, _, c = coordinates()
    plane = after(plane, earlier)
    whole = in_order(c == 1, plane[:, :, None], sent_on_chip(plane)[:, :, None], 2)
    return whole.reshape(-1, plane.shape[3])


def added(*terms):
    return sum(term.astype(F32) for term in terms)


def summed_on_chip(value):
    _, _, c = coordinates()
    sent = sent_on_chip(part_of(value, 1 - c, 2))
    return added(part_of(value, c, 2), sent).astype(BF16)


def summed_over_y(value, earlier):
    _, y, _ = coordinates()
    sent = shifted(after(part_of(value, 1 - y, 1), earlier), dy=1)
    return added(part_of(value, y, 1), sent).astype(BF16), sent


def summed_over_z(line, earlier=None):
    z, _, _ = coordinates()
    line = after(line, earlier)
    sent = [
        shifted(part_of(line, (z + step) % GRID[0], 0), dz=step) for step in range(1, GRID[0])
    ]
    return added(part_of(line, z, 0), *sent), sent


def pixel_masks(rows):
    row = lax.broadcasted_iota(jnp.int32, (rows, 1), 0)
    high, wide = (row // WIDTH) % HEIGHT, row % WIDTH
    masks = []
    for dr in (-1, 0, 1):
        for dc in (-1, 0, 1):
            inside = (high + dr >= 0) & (high + dr < HEIGHT) & (wide + dc >= 0) & (wide + dc < WIDTH)
            masks.append((dr * WIDTH + dc, inside))
    return masks


def frame_masks(rows, frames):
    pixels = HEIGHT * WIDTH
    row = lax.broadcasted_iota(jnp.int32, (rows, 1), 0)
    frame = (row // pixels) % frames
    return [
        (step * pixels, (frame + step >= 0) & (frame + step < frames)) for step in (-1, 0, 1)
    ]


def moved_rows(value, move):
    shift, inside = move
    if shift:
        value = pltpu.roll(value, (-shift) % value.shape[0], 0)
    return jnp.where(inside, value, 0.0)


def dot(left, right, dims=((1,), (0,))):
    return lax.dot_general(left, right, (dims, ((), ())), preferred_element_type=F32)


def with_embedding(hidden, embedding_ref, samples):
    per = hidden.shape[0] // samples
    return jnp.concatenate(
        [hidden[s * per : (s + 1) * per] + embedding_ref[s : s + 1, :] for s in range(samples)]
    )


def scale_of(summed):
    return lax.rsqrt(jnp.mean(summed * summed, axis=-1, keepdims=True) + 1e-06)


def silu_parts(preact):
    logistic = 1.0 / (1.0 + jnp.exp(-preact))
    return logistic, preact * logistic


def tap_weight(weight_refs, tap, channels):
    return jnp.concatenate(
        [ref[tap * channels : (tap + 1) * channels, :] for ref in weight_refs], 1
    )


def convolved(normed, weight_refs, masks):
    rows, channels = normed.shape
    normed = normed.astype(F32)
    total = None
    for tap in range(9):
        term = dot(
            moved_rows(normed, masks[tap]).astype(BF16),
            tap_weight(weight_refs, tap, channels),
        )
        total = term if total is None else total + term
    return total


def first_forward(frames, hidden_ref, embedding_ref, keep_ref, temporal_ref, *refs):
    *spatial_refs, normed_ref, preact_ref, mixed_ref = refs
    rows = hidden_ref.shape[0]
    width = keep_ref.shape[1]
    summed = with_embedding(hidden_ref[...].astype(F32), embedding_ref, embedding_ref.shape[0])
    normed = (summed * scale_of(summed)).astype(BF16)
    normed_ref[...] = normed
    preact = convolved(normed, spatial_refs, pixel_masks(rows))
    preact_ref[...] = preact
    activated = silu_parts(preact)[1].astype(BF16).astype(F32) * keep_ref[...]
    mixed = None
    for tap, move in enumerate(frame_masks(rows, frames)):
        term = dot(
            moved_rows(activated, move).astype(BF16),
            temporal_ref[tap * width : (tap + 1) * width, :],
        )
        mixed = term if mixed is None else mixed + term
    mixed_ref[...] = mixed.astype(BF16)


def slope_of(preact):
    logistic, _ = silu_parts(preact)
    return logistic * (1.0 + preact * (1.0 - logistic))


def act_grad_of(upstream, temporal_ref, width, frames):
    upstream = upstream.astype(F32)
    moves = frame_masks(upstream.shape[0], frames)
    total = None
    for tap in range(3):
        term = dot(
            moved_rows(upstream, moves[2 - tap]).astype(BF16),
            temporal_ref[tap * width : (tap + 1) * width, :],
            ((1,), (1,)),
        )
        total = term if total is None else total + term
    return total


def store_temporal_terms(activated, upstream, frames, out_ref):
    width = activated.shape[1]
    upstream = upstream.astype(F32)
    moves = frame_masks(upstream.shape[0], frames)
    for tap in range(3):
        out_ref[tap * width : (tap + 1) * width, :] = dot(
            activated, moved_rows(upstream, moves[2 - tap]).astype(BF16), ((0,), (0,))
        ).astype(BF16)


def store_spatial_terms(normed, pre_grad, out_refs):
    channels = normed.shape[1]
    pre_grad = pre_grad.astype(F32)
    masks = pixel_masks(pre_grad.shape[0])
    for tap in range(9):
        term = dot(
            normed, moved_rows(pre_grad, masks[8 - tap]).astype(BF16), ((0,), (0,))
        ).astype(BF16)
        start = 0
        for out_ref in out_refs:
            end = start + out_ref.shape[1]
            out_ref[tap * channels : (tap + 1) * channels, :] = term[:, start:end]
            start = end


def second_forward(
    frames, hidden_ref, own_ref, sent_ref, embedding_ref, keep_ref, upstream_ref, temporal_ref, *refs
):
    *spatial_refs, next_ref, normed_ref, activated_ref, pre_grad_ref, back_ref = refs
    rows, channels = hidden_ref.shape
    width = keep_ref.shape[1]
    masks = pixel_masks(rows)
    mixed = own_ref[...].astype(F32) + sent_ref[...].astype(F32)
    hidden = (hidden_ref[...].astype(F32) + mixed).astype(BF16)
    next_ref[...] = hidden
    summed = with_embedding(hidden.astype(F32), embedding_ref, embedding_ref.shape[0])
    normed = (summed * scale_of(summed)).astype(BF16)
    normed_ref[...] = normed
    preact = convolved(normed, spatial_refs, masks)
    activated_ref[...] = (silu_parts(preact)[1] * keep_ref[...]).astype(BF16)
    act_grad = act_grad_of(upstream_ref[...], temporal_ref, width, frames)
    pre_grad = (act_grad * slope_of(preact) * keep_ref[...]).astype(BF16)
    pre_grad_ref[...] = pre_grad
    pre_grad = pre_grad.astype(F32)
    back = None
    for tap in range(9):
        term = dot(
            moved_rows(pre_grad, masks[8 - tap]).astype(BF16),
            tap_weight(spatial_refs, tap, channels),
            ((1,), (1,)),
        )
        back = term if back is None else back + term
    back_ref[...] = back.astype(BF16)


def second_terms(frames, normed_ref, pre_grad_ref, activated_ref, upstream_ref, *outs):
    *spatial_refs, temporal_ref = outs
    store_spatial_terms(normed_ref[...], pre_grad_ref[...], spatial_refs)
    store_temporal_terms(activated_ref[...], upstream_ref[...], frames, temporal_ref)


def first_terms(
    frames, hidden_ref, embedding_ref, upstream_ref, own_ref, sent_ref, normed_ref, preact_ref,
    keep_ref, temporal_ref, *outs
):
    *spatial_outs, temporal_out = outs
    width = keep_ref.shape[1]
    channels = hidden_ref.shape[1]
    summed = with_embedding(hidden_ref[...].astype(F32), embedding_ref, embedding_ref.shape[0])
    scale = scale_of(summed)
    grad = own_ref[...].astype(F32) + sent_ref[...].astype(F32)
    inner = jnp.sum(grad * summed, axis=-1, keepdims=True)
    back = grad * scale - summed * (scale * scale * scale) * (inner / channels)
    upstream = (upstream_ref[...].astype(F32) + back).astype(BF16)
    preact = preact_ref[...]
    activated = (silu_parts(preact)[1] * keep_ref[...]).astype(BF16)
    act_grad = act_grad_of(upstream, temporal_ref, width, frames)
    pre_grad = (act_grad * slope_of(preact) * keep_ref[...]).astype(BF16)
    store_spatial_terms(normed_ref[...], pre_grad, spatial_outs)
    store_temporal_terms(activated, upstream, frames, temporal_out)


def paired_device(samples, timesteps, cotangent, spatial_weight, temporal_weight):
    me = lax.axis_index("pipe")
    first = me == 0
    _, y, _ = coordinates()
    count, frames, pixels, channels = samples.shape
    rows = count * frames * pixels
    main = 2 * LANES
    width = main + LANES
    hidden = samples.reshape(rows, channels)
    upstream = cotangent.reshape(rows, channels)
    embedding = jax.vmap(lambda step: embedding_of(step, channels))(timesteps)
    lane = jnp.arange(LANES)
    keep_own = jnp.concatenate([jnp.ones(main), lane < LANES // 2]).astype(F32)[None]
    keep_other = jnp.concatenate([jnp.ones(main), lane >= LANES // 2]).astype(F32)[None]
    keep_first = jnp.where(first, keep_own, keep_other)
    keep_second = jnp.where(first, keep_other, keep_own)
    tail = lane[None] < LANES // 2

    places = places_of(channels, main)
    order = (places[:, None] == jnp.arange(channels)).astype(BF16)
    temporal_even, temporal_odd = halves_of(temporal_weight[0])
    temporal_given = swapped(temporal_odd)
    line, sent = gathered_over_z(jnp.concatenate([temporal_even, temporal_given]))
    plane_temporal = gathered_over_y(line)
    spatial_own = dot(spatial_weight[0], order).astype(BF16)
    given = swapped(spatial_own[:, main:])
    main_own, main_given = spatial_own[:, :main], given[:, :main]
    tails = jnp.where(tail, spatial_own[:, 2 * main :], given[:, main:])
    line, sent = gathered_over_z(jnp.where(first, main_own, main_given), sent)
    plane_first = gathered_over_y(line)
    line, sent = gathered_over_z(tails, sent)
    plane_tails = gathered_over_y(line)
    line_second, _ = gathered_over_z(jnp.where(first, main_given, main_own), sent)
    side_second = shifted(line_second, dy=1)

    def local_rows(temporal):
        taps = temporal.reshape(3, -1, channels)
        return jnp.concatenate([taps, taps[:, main:]], 1).reshape(3 * width, channels)

    temporal = gathered_on_chip(plane_temporal).reshape(math.prod(GRID), 2, -1, channels)
    temporal_own, temporal_other = local_rows(temporal[:, 0]), local_rows(temporal[:, 1])
    temporal_first = jnp.where(first, temporal_own, temporal_other)
    temporal_second = jnp.where(first, temporal_other, temporal_own)
    tails = gathered_on_chip(plane_tails)
    spatial_first = [gathered_on_chip(plane_first), tails]

    def shape(extent, dtype=BF16):
        return jax.ShapeDtypeStruct(extent, dtype)

    spatial_flops = 2 * rows * 9 * channels * width
    temporal_flops = 2 * rows * 3 * channels * width
    spatial_bytes = 2 * 9 * channels * width
    temporal_bytes = 2 * 3 * channels * width
    normed_first, preact_first, mixed = vmem_call(
        functools.partial(first_forward, frames),
        (shape((rows, channels)), shape((rows, width), F32), shape((rows, channels))),
        flops=spatial_flops + temporal_flops,
        moved=spatial_bytes + temporal_bytes,
    )(hidden, embedding, keep_first, temporal_first, *spatial_first)
    mixed_given = swapped(mixed)
    side_second = after(side_second, mixed)
    plane_second = in_order(y == 1, line_second[:, None], side_second[:, None], 1)
    spatial_second = [gathered_on_chip(plane_second), tails]
    hidden_second, normed_second, activated_second, pre_grad_second, back = vmem_call(
        functools.partial(second_forward, frames),
        (
            shape((rows, channels)),
            shape((rows, channels)),
            shape((rows, width)),
            shape((rows, width)),
            shape((rows, channels)),
        ),
        flops=2 * spatial_flops + temporal_flops,
        moved=spatial_bytes + temporal_bytes,
    )(
        hidden, mixed, mixed_given, embedding, keep_second, upstream, temporal_second,
        *spatial_second,
    )

    def terms_shape():
        return (
            shape((9 * channels, main)),
            shape((9 * channels, width - main)),
            shape((3 * width, channels)),
        )

    def on_chip(terms):
        return summed_on_chip(terms.reshape(*GRID, -1, terms.shape[1]))

    back_given = swapped(back)
    main_terms_second, tail_terms_second, temporal_terms_second = vmem_call(
        functools.partial(second_terms, frames),
        terms_shape(),
        flops=spatial_flops + temporal_flops,
        moved=spatial_bytes + temporal_bytes,
    )(normed_second, pre_grad_second, activated_second, upstream)
    chip_second = on_chip(main_terms_second)
    line, side = summed_over_y(chip_second, None)
    share_second, sent_second = summed_over_z(line)
    main_terms_first, tail_terms_first, temporal_terms_first = vmem_call(
        functools.partial(first_terms, frames),
        terms_shape(),
        flops=spatial_flops + 2 * temporal_flops,
        moved=spatial_bytes + 2 * temporal_bytes,
    )(
        hidden_second, embedding, upstream, back, back_given, normed_first, preact_first,
        keep_first, temporal_first,
    )
    chip_tails = on_chip(after(tail_terms_first + tail_terms_second, side))
    chip_first = on_chip(after(main_terms_first, side))
    terms = [
        jnp.where(first, temporal_terms_first, temporal_terms_second),
        jnp.where(first, temporal_terms_second, temporal_terms_first),
    ]
    own, other = (term.reshape(3, width, channels) for term in terms)
    half = width - LANES // 2
    other = jnp.concatenate([other[:, :main], other[:, half:]], 1)
    parts = (part.reshape(*GRID, -1, channels) for part in (own[:, :half], other))
    chip_temporal = summed_on_chip(jnp.concatenate(list(parts), 3))

    line, side = summed_over_y(chip_tails, side)
    line_low, side = summed_over_y(chip_first[..., :LANES], side)
    share_tails, sent_tails = summed_over_z(line, (side, sent_second))
    line_high, side = summed_over_y(chip_first[..., LANES:], side)
    share_first, sent_first = summed_over_z(
        jnp.concatenate([line_low, line_high], 2), sent_tails
    )
    line, side = summed_over_y(chip_temporal, (side, sent_tails))
    share_temporal, _ = summed_over_z(line, sent_first)

    kept = jnp.where(first, share_first, share_second)
    passed = jnp.where(first, share_second, share_first)
    given = jnp.concatenate([passed, share_tails], 1).astype(BF16)
    given = swapped(after(given, side)).astype(F32)
    share_spatial = jnp.concatenate(
        [kept, given[:, :main], jnp.where(tail, share_tails, given[:, main:])], 1
    )
    share_spatial = lax.dot_general(
        share_spatial, order.astype(F32), (((1,), (1,)), ((), ())), precision=lax.Precision.HIGH
    )
    rows_own = share_temporal.shape[0] // 2
    given = swapped(share_temporal[rows_own:].astype(BF16)).astype(F32)
    share_temporal = jnp.stack(
        [part.reshape(-1, GROUP, channels) for part in (share_temporal[:rows_own], given)], 1
    ).reshape(-1, channels)
    return (share_spatial[None], share_temporal[None])


def solution(mesh):
    paired = mesh.shape["pipe"] == 2 and mesh.shape["dp"] == math.prod(GRID)
    return jax.shard_map(
        paired_device if paired else per_device,
        mesh=mesh,
        in_specs=(
            P("dp", None, None, None),
            P("dp"),
            P("dp", None, None, None),
            P("pipe", "dp", None),
            P("pipe", "dp", None),
        ),
        out_specs=(P("pipe", "dp", None), P("pipe", "dp", None)),
        check_vma=False,
    )
```

```python
import functools
import math

import jax
import jax.numpy as jnp
from jax import lax
from jax.experimental import pallas as pl
from jax.experimental.pallas import tpu as pltpu
from jax.sharding import PartitionSpec as P

HEIGHT = 8
WIDTH = 4
F32 = jnp.float32
BF16 = jnp.bfloat16
GRID = (4, 2, 2)
LANES = 128


def passed_along(value, axis, steps):
    count = lax.axis_size(axis)
    first, last = (max(0, -steps), min(count, count - steps))
    return lax.ppermute(value, axis, [(source, source + steps) for source in range(first, last)])


def embedding_of(step, channels):
    half_width = channels // 2
    frequency = jnp.exp(-math.log(10000.0) * jnp.arange(half_width, dtype=jnp.float32) / half_width)
    phases = step.astype(jnp.float32) * frequency
    return jnp.concatenate([jnp.sin(phases), jnp.cos(phases)])


def normalize(summed):
    return summed * lax.rsqrt(jnp.mean(summed * summed, axis=-1, keepdims=True) + 1e-06)


def spatial_columns(normed):
    frames, pixels, channels = normed.shape
    grid = normed.reshape(frames, HEIGHT, WIDTH, channels)
    padded = jnp.pad(grid, ((0, 0), (1, 1), (1, 1), (0, 0)))
    pieces = [
        padded[:, row : row + HEIGHT, col : col + WIDTH, :] for row in range(3) for col in range(3)
    ]
    return jnp.concatenate(pieces, axis=-1).reshape(frames * pixels, 9 * channels)


def spatial_fold(grads, frames, channels):
    parts = grads.reshape(frames, HEIGHT, WIDTH, 9, channels)
    padded = jnp.zeros((frames, HEIGHT + 2, WIDTH + 2, channels), jnp.float32)
    for row in range(3):
        for col in range(3):
            padded = padded.at[:, row : row + HEIGHT, col : col + WIDTH, :].add(
                parts[:, :, :, row * 3 + col, :]
            )
    return padded[:, 1 : HEIGHT + 1, 1 : WIDTH + 1, :].reshape(frames, HEIGHT * WIDTH, channels)


def temporal_columns(activated):
    frames, pixels, channels = activated.shape
    padded = jnp.pad(activated, ((1, 1), (0, 0), (0, 0)))
    pieces = [padded[tap : tap + frames] for tap in range(3)]
    return jnp.concatenate(pieces, axis=-1).reshape(frames * pixels, 3 * channels)


def temporal_fold(grads, frames, pixels, channels):
    parts = grads.reshape(frames, pixels, 3, channels)
    padded = jnp.zeros((frames + 2, pixels, channels), jnp.float32)
    for tap in range(3):
        padded = padded.at[tap : tap + frames].add(parts[:, :, tap, :])
    return padded[1 : frames + 1]


def section_forward(block_in, embedding, spatial, temporal):
    frames, pixels, channels = block_in.shape
    summed = block_in.astype(jnp.float32) + embedding
    normed = normalize(summed).astype(jnp.bfloat16)
    preact = jnp.dot(spatial_columns(normed), spatial, preferred_element_type=jnp.float32)
    activated = jax.nn.silu(preact).astype(jnp.bfloat16).reshape(frames, pixels, channels)
    mixed = jnp.dot(temporal_columns(activated), temporal, preferred_element_type=jnp.float32)
    return (block_in.astype(jnp.float32) + mixed.reshape(frames, pixels, channels)).astype(
        jnp.bfloat16
    )


def backward_first(block_in, embedding, spatial, temporal, upstream):
    frames, pixels, channels = block_in.shape
    summed = block_in.astype(jnp.float32) + embedding
    normed = normalize(summed).astype(jnp.bfloat16)
    columns = spatial_columns(normed)
    preact = jnp.dot(columns, spatial, preferred_element_type=jnp.float32)
    activated = jax.nn.silu(preact).astype(jnp.bfloat16).reshape(frames, pixels, channels)
    tcolumns = temporal_columns(activated)
    upstream_flat = upstream.reshape(frames * pixels, channels)
    temporal_term = jnp.dot(tcolumns.T, upstream_flat, preferred_element_type=jnp.float32)
    act_grad = temporal_fold(
        jnp.dot(upstream_flat, temporal.T, preferred_element_type=jnp.float32),
        frames,
        pixels,
        channels,
    )
    logistic = jax.nn.sigmoid(preact)
    slope = logistic * (1.0 + preact * (1.0 - logistic))
    pre_grad = (act_grad.reshape(frames * pixels, channels) * slope).astype(jnp.bfloat16)
    return (temporal_term, pre_grad, columns)


def backward_second(block_in, embedding, spatial, upstream, pre_grad, columns):
    frames, pixels, channels = block_in.shape
    summed = block_in.astype(jnp.float32) + embedding
    spatial_term = jnp.dot(columns.T, pre_grad, preferred_element_type=jnp.float32)
    norm_grad = spatial_fold(
        jnp.dot(pre_grad, spatial.T, preferred_element_type=jnp.float32), frames, channels
    )
    _, pullback = jax.vjp(normalize, summed)
    back_input = (upstream.astype(jnp.float32) + pullback(norm_grad)[0]).astype(jnp.bfloat16)
    return (back_input, spatial_term)


def section_backward(block_in, embedding, spatial, temporal, upstream):
    temporal_term, pre_grad, columns = backward_first(
        block_in, embedding, spatial, temporal, upstream
    )
    back_input, spatial_term = backward_second(
        block_in, embedding, spatial, upstream, pre_grad, columns
    )
    return (back_input, spatial_term, temporal_term)


def per_device(samples, timesteps, cotangent, spatial_weight, temporal_weight):
    sections = lax.axis_size("pipe")
    section_index = lax.axis_index("pipe")
    micro_count = samples.shape[0]
    frames, pixels, channels = (samples.shape[1], samples.shape[2], samples.shape[3])
    moments = jnp.arange(micro_count + sections - 1, dtype=jnp.int32)
    blank = jnp.zeros((frames, pixels, channels), jnp.bfloat16)
    full_spatial, full_temporal = (
        lax.all_gather(spatial_weight[0], "dp", axis=0, tiled=True),
        lax.all_gather(temporal_weight[0], "dp", axis=0, tiled=True),
    )

    def forward_step(carry, moment):
        incoming, stash = carry
        position = moment - section_index
        active = (position >= 0) & (position < micro_count)
        picked = jnp.clip(position, 0, micro_count - 1)
        own = lax.dynamic_index_in_dim(samples, picked, 0, keepdims=False)
        embedding = embedding_of(
            lax.dynamic_index_in_dim(timesteps, picked, 0, keepdims=False), channels
        )
        block_in = jnp.where(section_index == 0, own, incoming)
        result = lax.cond(
            active & (section_index < sections - 1),
            lambda: section_forward(block_in, embedding, full_spatial, full_temporal),
            lambda: blank,
        )
        stash = jnp.where(
            active, lax.dynamic_update_index_in_dim(stash, block_in, picked, 0), stash
        )
        passed = passed_along(result, "pipe", 1)
        return ((passed, stash), None)

    (_, stash), _ = lax.scan(forward_step, (blank, jnp.zeros_like(samples)), moments)
    back_spatial, back_temporal = (full_spatial, full_temporal)

    def inputs_at(moment, incoming):
        position = moment - (sections - 1 - section_index)
        active = (position >= 0) & (position < micro_count)
        picked = jnp.clip(position, 0, micro_count - 1)
        block_in = lax.dynamic_index_in_dim(stash, picked, 0, keepdims=False)
        embedding = embedding_of(
            lax.dynamic_index_in_dim(timesteps, picked, 0, keepdims=False), channels
        )
        given = lax.dynamic_index_in_dim(cotangent, picked, 0, keepdims=False)
        upstream = jnp.where(section_index == sections - 1, given, incoming)
        return (active, block_in, embedding, upstream)

    def backward_step(carry, moment):
        incoming, grad_spatial, grad_temporal = carry
        active, block_in, embedding, upstream = inputs_at(moment, incoming)

        def working():
            back_input, spatial_term, temporal_term = section_backward(
                block_in, embedding, back_spatial, back_temporal, upstream
            )
            return (back_input, grad_spatial + spatial_term, grad_temporal + temporal_term)

        def waiting():
            return (blank, grad_spatial, grad_temporal)

        back_input, grad_spatial, grad_temporal = lax.cond(active, working, waiting)
        passed = passed_along(back_input, "pipe", -1)
        return ((passed, grad_spatial, grad_temporal), None)

    start = (
        blank,
        jnp.zeros(back_spatial.shape, jnp.float32),
        jnp.zeros(back_temporal.shape, jnp.float32),
    )
    (_, grad_spatial, grad_temporal), _ = lax.scan(backward_step, start, moments)
    share_spatial, share_temporal = (
        lax.psum_scatter(
            grad_spatial.astype(jnp.bfloat16).astype(jnp.float32).astype(jnp.bfloat16),
            "dp",
            scatter_dimension=0,
            tiled=True,
        ).astype(jnp.float32),
        lax.psum_scatter(
            grad_temporal.astype(jnp.bfloat16).astype(jnp.float32).astype(jnp.bfloat16),
            "dp",
            scatter_dimension=0,
            tiled=True,
        ).astype(jnp.float32),
    )
    return (share_spatial[None], share_temporal[None])


SPAN = 40
CUTS = (24, 16)
PIECE = 64


def coordinates():
    index = lax.axis_index("dp")
    return index // (GRID[1] * GRID[2]), (index // GRID[2]) % GRID[1], index % GRID[2]


def shifted(value, dz=0, dy=0, dc=0):
    pairs = []
    for z in range(GRID[0]):
        for y in range(GRID[1]):
            for c in range(GRID[2]):
                place = ((z + dz) % GRID[0], (y + dy) % GRID[1], (c + dc) % GRID[2])
                pairs.append(
                    (
                        (z * GRID[1] + y) * GRID[2] + c,
                        (place[0] * GRID[1] + place[1]) * GRID[2] + place[2],
                    )
                )
    return lax.ppermute(value, "dp", pairs)


def swapped(value):
    return lax.ppermute(value, "pipe", [(0, 1), (1, 0)])


def part_of(value, index, axis):
    return lax.dynamic_index_in_dim(value, index, axis, keepdims=False)


def vmem_call(body, outs, scratch=(), flops=0, moved=0):
    return pl.pallas_call(
        body,
        out_shape=outs,
        scratch_shapes=list(scratch),
        compiler_params=pltpu.CompilerParams(vmem_limit_bytes=24 * 2**20),
        cost_estimate=pl.CostEstimate(
            flops=5 * flops // 2, bytes_accessed=moved, transcendentals=0
        ),
    )


def after(value, earlier):
    return value if earlier is None else lax.optimization_barrier((value, earlier))[0]


def in_order(swap, own, other, axis):
    return jnp.where(
        swap, jnp.concatenate([other, own], axis), jnp.concatenate([own, other], axis)
    )


def over_z(value, pairs):
    moves = []
    for source, target in pairs:
        for rest in range(GRID[1] * GRID[2]):
            moves.append(tuple(z * GRID[1] * GRID[2] + rest for z in (source, target)))
    return lax.ppermute(value, "dp", moves)


def sent_over_z(value):
    return [shifted(value, dz=step) for step in range(1, GRID[0])]


def sent_on_chip(value):
    return shifted(value, dc=1)


def places_of(channels, main):
    channel = jnp.arange(channels)
    span, inside = channel // SPAN, channel % SPAN
    odd = span % 2
    cut = jnp.where(odd == 0, CUTS[0], CUTS[1])
    second = (inside >= cut).astype(jnp.int32)
    before = span // 2 * SPAN + odd * jnp.where(second == 0, CUTS[0], CUTS[1])
    rank = before + inside - second * cut
    tail = channels // 2 - main
    return jnp.where(
        rank < main, second * main + rank, (1 + second) * main + second * (tail - main) + rank
    )


def spans_of(rows, odd):
    sets = ([], [])
    for index, start in enumerate(range(0, rows, SPAN)):
        cut = start + CUTS[(index + odd) % 2]
        sets[0].append((start, cut))
        sets[1].append((cut, start + SPAN))
    return sets


def sets_of(value):
    _, _, c = coordinates()
    results = []
    for which in range(2):
        by_core = []
        for odd in range(2):
            spans = spans_of(value.shape[0], odd)[which]
            taken = jnp.concatenate([value[start:end] for start, end in spans])
            by_core.append(jnp.pad(taken, ((0, PIECE - taken.shape[0]), (0, 0))))
        results.append(jnp.where(c == 0, by_core[0], by_core[1]))
    return results


def shard_of(own, given, rows):
    _, _, c = coordinates()
    by_core = []
    for odd in range(2):
        taken, pieces = [0, 0], []
        for spans in zip(*spans_of(rows, odd)):
            for which, (start, end) in enumerate(spans):
                source = (own, given)[which]
                pieces.append(source[taken[which] : taken[which] + end - start])
                taken[which] += end - start
        by_core.append(jnp.concatenate(pieces))
    return jnp.where(c == 0, by_core[0], by_core[1])


def compact(pieces, own):
    short = 3 * SPAN - PIECE
    low, high = pieces[:, 0], pieces[:, 1]
    both = jnp.where(
        own,
        jnp.concatenate([low, high[:, :short]], 1),
        jnp.concatenate([low[:, :short], high], 1),
    )
    return both.reshape(-1, pieces.shape[3])


def spread(rows, chips, own):
    rows = rows.reshape(chips, -1, rows.shape[1])
    short = rows.shape[1] - PIECE
    pad = ((0, 0), (0, PIECE - short), (0, 0))
    return jnp.where(
        own,
        jnp.stack([rows[:, :PIECE], jnp.pad(rows[:, PIECE:], pad)], 1),
        jnp.stack([jnp.pad(rows[:, :short], pad), rows[:, short:]], 1),
    )


def gathered_over_z(value, earlier=None):
    z, _, _ = coordinates()
    value = after(value, earlier)
    sent = sent_over_z(value)
    return (
        jnp.stack([lax.select_n((z - place) % GRID[0], value, *sent) for place in range(GRID[0])]),
        sent,
    )


def gathered_over_y(line):
    _, y, _ = coordinates()
    return in_order(y == 1, line[:, None], shifted(line, dy=1)[:, None], 1)


def gathered_on_chip(plane, earlier=None):
    _, _, c = coordinates()
    plane = after(plane, earlier)
    whole = in_order(c == 1, plane[:, :, None], sent_on_chip(plane)[:, :, None], 2)
    return whole.reshape(-1, plane.shape[3])


def added(*terms):
    return sum(term.astype(F32) for term in terms)


def summed_on_chip(value):
    _, _, c = coordinates()
    sent = sent_on_chip(part_of(value, 1 - c, 2))
    return added(part_of(value, c, 2), sent).astype(BF16)


def summed_over_y(value, earlier):
    _, y, _ = coordinates()
    sent = shifted(after(part_of(value, 1 - y, 1), earlier), dy=1)
    return added(part_of(value, y, 1), sent).astype(BF16), sent


def summed_over_z(line, earlier=None):
    z, _, _ = coordinates()
    line = after(line, earlier)
    sent = [
        shifted(part_of(line, (z + step) % GRID[0], 0), dz=step) for step in range(1, GRID[0])
    ]
    return added(part_of(line, z, 0), *sent), sent


def pixel_masks(rows):
    row = lax.broadcasted_iota(jnp.int32, (rows, 1), 0)
    high, wide = (row // WIDTH) % HEIGHT, row % WIDTH
    masks = []
    for dr in (-1, 0, 1):
        for dc in (-1, 0, 1):
            inside = (high + dr >= 0) & (high + dr < HEIGHT) & (wide + dc >= 0) & (wide + dc < WIDTH)
            masks.append((dr * WIDTH + dc, inside))
    return masks


def frame_masks(rows, frames):
    pixels = HEIGHT * WIDTH
    row = lax.broadcasted_iota(jnp.int32, (rows, 1), 0)
    frame = (row // pixels) % frames
    return [
        (step * pixels, (frame + step >= 0) & (frame + step < frames)) for step in (-1, 0, 1)
    ]


def moved_rows(value, move):
    shift, inside = move
    if shift:
        value = pltpu.roll(value, (-shift) % value.shape[0], 0)
    return jnp.where(inside, value, 0.0)


def dot(left, right, dims=((1,), (0,))):
    return lax.dot_general(left, right, (dims, ((), ())), preferred_element_type=F32)


def with_embedding(hidden, embedding_ref, samples):
    per = hidden.shape[0] // samples
    return jnp.concatenate(
        [hidden[s * per : (s + 1) * per] + embedding_ref[s : s + 1, :] for s in range(samples)]
    )


def scale_of(summed):
    return lax.rsqrt(jnp.mean(summed * summed, axis=-1, keepdims=True) + 1e-06)


def silu_parts(preact):
    logistic = 1.0 / (1.0 + jnp.exp(-preact))
    return logistic, preact * logistic


def tap_weight(weight_refs, tap, channels):
    return jnp.concatenate(
        [ref[tap * channels : (tap + 1) * channels, :] for ref in weight_refs], 1
    )


def convolved(normed, weight_refs, masks):
    rows, channels = normed.shape
    normed = normed.astype(F32)
    total = None
    for tap in range(9):
        term = dot(
            moved_rows(normed, masks[tap]).astype(BF16),
            tap_weight(weight_refs, tap, channels),
        )
        total = term if total is None else total + term
    return total


def tap_rows(temporal_ref, tap, width):
    tail = PIECE
    start = tap * (width - tail)
    rows = temporal_ref[start : start + width - tail, :]
    return jnp.concatenate([rows, rows[width - 2 * tail :]], 0)


def first_forward(frames, hidden_ref, embedding_ref, keep_ref, temporal_ref, *refs):
    *spatial_refs, normed_ref, preact_ref, mixed_ref = refs
    rows = hidden_ref.shape[0]
    width = keep_ref.shape[1]
    summed = with_embedding(hidden_ref[...].astype(F32), embedding_ref, embedding_ref.shape[0])
    normed = (summed * scale_of(summed)).astype(BF16)
    normed_ref[...] = normed
    preact = convolved(normed, spatial_refs, pixel_masks(rows))
    preact_ref[...] = preact
    activated = silu_parts(preact)[1].astype(BF16).astype(F32) * keep_ref[...]
    mixed = None
    for tap, move in enumerate(frame_masks(rows, frames)):
        term = dot(
            moved_rows(activated, move).astype(BF16),
            tap_rows(temporal_ref, tap, width),
        )
        mixed = term if mixed is None else mixed + term
    mixed_ref[...] = mixed.astype(BF16)


def slope_of(preact):
    logistic, _ = silu_parts(preact)
    return logistic * (1.0 + preact * (1.0 - logistic))


def act_grad_of(upstream, temporal_ref, width, frames):
    upstream = upstream.astype(F32)
    moves = frame_masks(upstream.shape[0], frames)
    total = None
    for tap in range(3):
        term = dot(
            moved_rows(upstream, moves[2 - tap]).astype(BF16),
            tap_rows(temporal_ref, tap, width),
            ((1,), (1,)),
        )
        total = term if total is None else total + term
    return total


def store_temporal_terms(activated, upstream, frames, out_ref):
    width = activated.shape[1]
    tail = PIECE
    upstream = upstream.astype(F32)
    moves = frame_masks(upstream.shape[0], frames)
    for tap in range(3):
        term = dot(activated, moved_rows(upstream, moves[2 - tap]).astype(BF16), ((0,), (0,)))
        start = tap * (width - tail)
        out_ref[start : start + width - 2 * tail, :] = term[: width - 2 * tail].astype(BF16)
        out_ref[start + width - 2 * tail : start + width - tail, :] = (
            term[width - 2 * tail : width - tail] + term[width - tail :]
        ).astype(BF16)


def store_spatial_terms(normed, pre_grad, out_refs):
    channels = normed.shape[1]
    pre_grad = pre_grad.astype(F32)
    masks = pixel_masks(pre_grad.shape[0])
    for tap in range(9):
        term = dot(
            normed, moved_rows(pre_grad, masks[8 - tap]).astype(BF16), ((0,), (0,))
        ).astype(BF16)
        start = 0
        for out_ref in out_refs:
            end = start + out_ref.shape[1]
            out_ref[tap * channels : (tap + 1) * channels, :] = term[:, start:end]
            start = end


def second_forward(
    frames, hidden_ref, own_ref, sent_ref, embedding_ref, keep_ref, upstream_ref, temporal_ref, *refs
):
    *spatial_refs, next_ref, normed_ref, activated_ref, pre_grad_ref, back_ref = refs
    rows, channels = hidden_ref.shape
    width = keep_ref.shape[1]
    masks = pixel_masks(rows)
    mixed = own_ref[...].astype(F32) + sent_ref[...].astype(F32)
    hidden = (hidden_ref[...].astype(F32) + mixed).astype(BF16)
    next_ref[...] = hidden
    summed = with_embedding(hidden.astype(F32), embedding_ref, embedding_ref.shape[0])
    normed = (summed * scale_of(summed)).astype(BF16)
    normed_ref[...] = normed
    preact = convolved(normed, spatial_refs, masks)
    activated_ref[...] = (silu_parts(preact)[1] * keep_ref[...]).astype(BF16)
    act_grad = act_grad_of(upstream_ref[...], temporal_ref, width, frames)
    pre_grad = (act_grad * slope_of(preact) * keep_ref[...]).astype(BF16)
    pre_grad_ref[...] = pre_grad
    pre_grad = pre_grad.astype(F32)
    back = None
    for tap in range(9):
        term = dot(
            moved_rows(pre_grad, masks[8 - tap]).astype(BF16),
            tap_weight(spatial_refs, tap, channels),
            ((1,), (1,)),
        )
        back = term if back is None else back + term
    back_ref[...] = back.astype(BF16)


def second_terms(frames, normed_ref, pre_grad_ref, activated_ref, upstream_ref, *outs):
    *spatial_refs, temporal_ref = outs
    store_spatial_terms(normed_ref[...], pre_grad_ref[...], spatial_refs)
    store_temporal_terms(activated_ref[...], upstream_ref[...], frames, temporal_ref)


def first_terms(
    frames, hidden_ref, embedding_ref, upstream_ref, own_ref, sent_ref, normed_ref, preact_ref,
    keep_ref, temporal_ref, *outs
):
    *spatial_outs, temporal_out = outs
    width = keep_ref.shape[1]
    channels = hidden_ref.shape[1]
    summed = with_embedding(hidden_ref[...].astype(F32), embedding_ref, embedding_ref.shape[0])
    scale = scale_of(summed)
    grad = own_ref[...].astype(F32) + sent_ref[...].astype(F32)
    inner = jnp.sum(grad * summed, axis=-1, keepdims=True)
    back = grad * scale - summed * (scale * scale * scale) * (inner / channels)
    upstream = (upstream_ref[...].astype(F32) + back).astype(BF16)
    preact = preact_ref[...]
    activated = (silu_parts(preact)[1] * keep_ref[...]).astype(BF16)
    act_grad = act_grad_of(upstream, temporal_ref, width, frames)
    pre_grad = (act_grad * slope_of(preact) * keep_ref[...]).astype(BF16)
    store_spatial_terms(normed_ref[...], pre_grad, spatial_outs)
    store_temporal_terms(activated, upstream, frames, temporal_out)


def paired_device(samples, timesteps, cotangent, spatial_weight, temporal_weight):
    me = lax.axis_index("pipe")
    first = me == 0
    _, y, _ = coordinates()
    count, frames, pixels, channels = samples.shape
    rows = count * frames * pixels
    main = 2 * LANES
    width = main + LANES
    hidden = samples.reshape(rows, channels)
    upstream = cotangent.reshape(rows, channels)
    embedding = jax.vmap(lambda step: embedding_of(step, channels))(timesteps)
    lane = jnp.arange(LANES)
    keep_own = jnp.concatenate([jnp.ones(main), lane < LANES // 2]).astype(F32)[None]
    keep_other = jnp.concatenate([jnp.ones(main), lane >= LANES // 2]).astype(F32)[None]
    keep_first = jnp.where(first, keep_own, keep_other)
    keep_second = jnp.where(first, keep_other, keep_own)
    tail = lane[None] < LANES // 2

    places = places_of(channels, main)
    order = (places[:, None] == jnp.arange(channels)).astype(BF16)
    temporal_own, temporal_sent = sets_of(temporal_weight[0])
    temporal_given = swapped(temporal_sent)
    line, sent = gathered_over_z(in_order(me == 1, temporal_own, temporal_given, 0))
    plane_temporal = gathered_over_y(line)
    spatial_own = dot(spatial_weight[0], order).astype(BF16)
    given = swapped(spatial_own[:, main:])
    main_own, main_given = spatial_own[:, :main], given[:, :main]
    tails = jnp.where(tail, spatial_own[:, 2 * main :], given[:, main:])
    line, sent = gathered_over_z(jnp.where(first, main_own, main_given), sent)
    plane_first = gathered_over_y(line)
    line, sent = gathered_over_z(tails, sent)
    plane_tails = gathered_over_y(line)
    line_second, _ = gathered_over_z(jnp.where(first, main_given, main_own), sent)
    side_second = shifted(line_second, dy=1)

    chips = GRID[0] * GRID[1]
    temporal = gathered_on_chip(plane_temporal).reshape(chips, GRID[2], 2, PIECE, channels)
    temporal_first = compact(temporal[:, :, 0], first)
    temporal_second = compact(temporal[:, :, 1], me == 1)
    tails = gathered_on_chip(plane_tails)
    spatial_first = [gathered_on_chip(plane_first), tails]

    def shape(extent, dtype=BF16):
        return jax.ShapeDtypeStruct(extent, dtype)

    spatial_flops = 2 * rows * 9 * channels * width
    temporal_flops = 2 * rows * 3 * channels * width
    spatial_bytes = 2 * 9 * channels * width
    temporal_bytes = 2 * 3 * channels * width
    normed_first, preact_first, mixed = vmem_call(
        functools.partial(first_forward, frames),
        (shape((rows, channels)), shape((rows, width), F32), shape((rows, channels))),
        flops=spatial_flops + temporal_flops,
        moved=spatial_bytes + temporal_bytes,
    )(hidden, embedding, keep_first, temporal_first, *spatial_first)
    mixed_given = swapped(mixed)
    side_second = after(side_second, mixed)
    plane_second = in_order(y == 1, line_second[:, None], side_second[:, None], 1)
    spatial_second = [gathered_on_chip(plane_second), tails]
    hidden_second, normed_second, activated_second, pre_grad_second, back = vmem_call(
        functools.partial(second_forward, frames),
        (
            shape((rows, channels)),
            shape((rows, channels)),
            shape((rows, width)),
            shape((rows, width)),
            shape((rows, channels)),
        ),
        flops=2 * spatial_flops + temporal_flops,
        moved=spatial_bytes + temporal_bytes,
    )(
        hidden, mixed, mixed_given, embedding, keep_second, upstream, temporal_second,
        *spatial_second,
    )

    def terms_shape():
        return (
            shape((9 * channels, main)),
            shape((9 * channels, width - main)),
            shape((3 * (width - PIECE), channels)),
        )

    def on_chip(terms):
        return summed_on_chip(terms.reshape(*GRID, -1, terms.shape[1]))

    back_given = swapped(back)
    main_terms_second, tail_terms_second, temporal_terms_second = vmem_call(
        functools.partial(second_terms, frames),
        terms_shape(),
        flops=spatial_flops + temporal_flops,
        moved=spatial_bytes + temporal_bytes,
    )(normed_second, pre_grad_second, activated_second, upstream)
    chip_second = on_chip(main_terms_second)
    back_given = after(back_given, chip_second)
    line, side = summed_over_y(chip_second, None)
    share_second, sent_second = summed_over_z(line)
    main_terms_first, tail_terms_first, temporal_terms_first = vmem_call(
        functools.partial(first_terms, frames),
        terms_shape(),
        flops=spatial_flops + 2 * temporal_flops,
        moved=spatial_bytes + 2 * temporal_bytes,
    )(
        hidden_second, embedding, upstream, back, back_given, normed_first, preact_first,
        keep_first, temporal_first,
    )
    chip_tails = on_chip(after(tail_terms_first + tail_terms_second, side))
    chip_first = on_chip(after(main_terms_first, side))
    terms = jnp.concatenate(
        [
            spread(temporal_terms_first, chips, first),
            spread(temporal_terms_second, chips, me == 1),
        ],
        2,
    )
    chip_temporal = summed_on_chip(terms.reshape(*GRID, -1, channels))

    line, side = summed_over_y(chip_tails, side)
    line_low, side = summed_over_y(chip_first[..., :LANES], side)
    share_tails, sent_tails = summed_over_z(line, (side, sent_second))
    line_high, side = summed_over_y(chip_first[..., LANES:], side)
    share_first, sent_first = summed_over_z(
        jnp.concatenate([line_low, line_high], 2), sent_tails
    )
    line, side = summed_over_y(chip_temporal, side)
    share_temporal, _ = summed_over_z(line, sent_first)

    kept = jnp.where(first, share_first, share_second)
    passed = jnp.where(first, share_second, share_first)
    given = jnp.concatenate([passed, share_tails], 1).astype(BF16)
    given = swapped(after(given, side)).astype(F32)
    share_spatial = jnp.concatenate(
        [kept, given[:, :main], jnp.where(tail, share_tails, given[:, main:])], 1
    )
    share_spatial = lax.dot_general(
        share_spatial, order.astype(F32), (((1,), (1,)), ((), ())), precision=lax.Precision.HIGH
    )
    low, high = share_temporal[:PIECE], share_temporal[PIECE:]
    given = swapped(jnp.where(first, high, low).astype(BF16)).astype(F32)
    share_temporal = shard_of(jnp.where(first, low, high), given, temporal_weight.shape[1])
    return (share_spatial[None], share_temporal[None])


def solution(mesh):
    paired = mesh.shape["pipe"] == 2 and mesh.shape["dp"] == math.prod(GRID)
    return jax.shard_map(
        paired_device if paired else per_device,
        mesh=mesh,
        in_specs=(
            P("dp", None, None, None),
            P("dp"),
            P("dp", None, None, None),
            P("pipe", "dp", None),
            P("pipe", "dp", None),
        ),
        out_specs=(P("pipe", "dp", None), P("pipe", "dp", None)),
        check_vma=False,
    )
```

```python
import functools
import math

import jax
import jax.numpy as jnp
from jax import lax
from jax.experimental import pallas as pl
from jax.experimental.pallas import tpu as pltpu
from jax.sharding import PartitionSpec as P

HEIGHT = 8
WIDTH = 4
F32 = jnp.float32
BF16 = jnp.bfloat16
GRID = (4, 2, 2)
LANES = 128


def passed_along(value, axis, steps):
    count = lax.axis_size(axis)
    first, last = (max(0, -steps), min(count, count - steps))
    return lax.ppermute(value, axis, [(source, source + steps) for source in range(first, last)])


def embedding_of(step, channels):
    half_width = channels // 2
    frequency = jnp.exp(-math.log(10000.0) * jnp.arange(half_width, dtype=jnp.float32) / half_width)
    phases = step.astype(jnp.float32) * frequency
    return jnp.concatenate([jnp.sin(phases), jnp.cos(phases)])


def normalize(summed):
    return summed * lax.rsqrt(jnp.mean(summed * summed, axis=-1, keepdims=True) + 1e-06)


def spatial_columns(normed):
    frames, pixels, channels = normed.shape
    grid = normed.reshape(frames, HEIGHT, WIDTH, channels)
    padded = jnp.pad(grid, ((0, 0), (1, 1), (1, 1), (0, 0)))
    pieces = [
        padded[:, row : row + HEIGHT, col : col + WIDTH, :] for row in range(3) for col in range(3)
    ]
    return jnp.concatenate(pieces, axis=-1).reshape(frames * pixels, 9 * channels)


def spatial_fold(grads, frames, channels):
    parts = grads.reshape(frames, HEIGHT, WIDTH, 9, channels)
    padded = jnp.zeros((frames, HEIGHT + 2, WIDTH + 2, channels), jnp.float32)
    for row in range(3):
        for col in range(3):
            padded = padded.at[:, row : row + HEIGHT, col : col + WIDTH, :].add(
                parts[:, :, :, row * 3 + col, :]
            )
    return padded[:, 1 : HEIGHT + 1, 1 : WIDTH + 1, :].reshape(frames, HEIGHT * WIDTH, channels)


def temporal_columns(activated):
    frames, pixels, channels = activated.shape
    padded = jnp.pad(activated, ((1, 1), (0, 0), (0, 0)))
    pieces = [padded[tap : tap + frames] for tap in range(3)]
    return jnp.concatenate(pieces, axis=-1).reshape(frames * pixels, 3 * channels)


def temporal_fold(grads, frames, pixels, channels):
    parts = grads.reshape(frames, pixels, 3, channels)
    padded = jnp.zeros((frames + 2, pixels, channels), jnp.float32)
    for tap in range(3):
        padded = padded.at[tap : tap + frames].add(parts[:, :, tap, :])
    return padded[1 : frames + 1]


def section_forward(block_in, embedding, spatial, temporal):
    frames, pixels, channels = block_in.shape
    summed = block_in.astype(jnp.float32) + embedding
    normed = normalize(summed).astype(jnp.bfloat16)
    preact = jnp.dot(spatial_columns(normed), spatial, preferred_element_type=jnp.float32)
    activated = jax.nn.silu(preact).astype(jnp.bfloat16).reshape(frames, pixels, channels)
    mixed = jnp.dot(temporal_columns(activated), temporal, preferred_element_type=jnp.float32)
    return (block_in.astype(jnp.float32) + mixed.reshape(frames, pixels, channels)).astype(
        jnp.bfloat16
    )


def backward_first(block_in, embedding, spatial, temporal, upstream):
    frames, pixels, channels = block_in.shape
    summed = block_in.astype(jnp.float32) + embedding
    normed = normalize(summed).astype(jnp.bfloat16)
    columns = spatial_columns(normed)
    preact = jnp.dot(columns, spatial, preferred_element_type=jnp.float32)
    activated = jax.nn.silu(preact).astype(jnp.bfloat16).reshape(frames, pixels, channels)
    tcolumns = temporal_columns(activated)
    upstream_flat = upstream.reshape(frames * pixels, channels)
    temporal_term = jnp.dot(tcolumns.T, upstream_flat, preferred_element_type=jnp.float32)
    act_grad = temporal_fold(
        jnp.dot(upstream_flat, temporal.T, preferred_element_type=jnp.float32),
        frames,
        pixels,
        channels,
    )
    logistic = jax.nn.sigmoid(preact)
    slope = logistic * (1.0 + preact * (1.0 - logistic))
    pre_grad = (act_grad.reshape(frames * pixels, channels) * slope).astype(jnp.bfloat16)
    return (temporal_term, pre_grad, columns)


def backward_second(block_in, embedding, spatial, upstream, pre_grad, columns):
    frames, pixels, channels = block_in.shape
    summed = block_in.astype(jnp.float32) + embedding
    spatial_term = jnp.dot(columns.T, pre_grad, preferred_element_type=jnp.float32)
    norm_grad = spatial_fold(
        jnp.dot(pre_grad, spatial.T, preferred_element_type=jnp.float32), frames, channels
    )
    _, pullback = jax.vjp(normalize, summed)
    back_input = (upstream.astype(jnp.float32) + pullback(norm_grad)[0]).astype(jnp.bfloat16)
    return (back_input, spatial_term)


def section_backward(block_in, embedding, spatial, temporal, upstream):
    temporal_term, pre_grad, columns = backward_first(
        block_in, embedding, spatial, temporal, upstream
    )
    back_input, spatial_term = backward_second(
        block_in, embedding, spatial, upstream, pre_grad, columns
    )
    return (back_input, spatial_term, temporal_term)


def per_device(samples, timesteps, cotangent, spatial_weight, temporal_weight):
    sections = lax.axis_size("pipe")
    section_index = lax.axis_index("pipe")
    micro_count = samples.shape[0]
    frames, pixels, channels = (samples.shape[1], samples.shape[2], samples.shape[3])
    moments = jnp.arange(micro_count + sections - 1, dtype=jnp.int32)
    blank = jnp.zeros((frames, pixels, channels), jnp.bfloat16)
    full_spatial, full_temporal = (
        lax.all_gather(spatial_weight[0], "dp", axis=0, tiled=True),
        lax.all_gather(temporal_weight[0], "dp", axis=0, tiled=True),
    )

    def forward_step(carry, moment):
        incoming, stash = carry
        position = moment - section_index
        active = (position >= 0) & (position < micro_count)
        picked = jnp.clip(position, 0, micro_count - 1)
        own = lax.dynamic_index_in_dim(samples, picked, 0, keepdims=False)
        embedding = embedding_of(
            lax.dynamic_index_in_dim(timesteps, picked, 0, keepdims=False), channels
        )
        block_in = jnp.where(section_index == 0, own, incoming)
        result = lax.cond(
            active & (section_index < sections - 1),
            lambda: section_forward(block_in, embedding, full_spatial, full_temporal),
            lambda: blank,
        )
        stash = jnp.where(
            active, lax.dynamic_update_index_in_dim(stash, block_in, picked, 0), stash
        )
        passed = passed_along(result, "pipe", 1)
        return ((passed, stash), None)

    (_, stash), _ = lax.scan(forward_step, (blank, jnp.zeros_like(samples)), moments)
    back_spatial, back_temporal = (full_spatial, full_temporal)

    def inputs_at(moment, incoming):
        position = moment - (sections - 1 - section_index)
        active = (position >= 0) & (position < micro_count)
        picked = jnp.clip(position, 0, micro_count - 1)
        block_in = lax.dynamic_index_in_dim(stash, picked, 0, keepdims=False)
        embedding = embedding_of(
            lax.dynamic_index_in_dim(timesteps, picked, 0, keepdims=False), channels
        )
        given = lax.dynamic_index_in_dim(cotangent, picked, 0, keepdims=False)
        upstream = jnp.where(section_index == sections - 1, given, incoming)
        return (active, block_in, embedding, upstream)

    def backward_step(carry, moment):
        incoming, grad_spatial, grad_temporal = carry
        active, block_in, embedding, upstream = inputs_at(moment, incoming)

        def working():
            back_input, spatial_term, temporal_term = section_backward(
                block_in, embedding, back_spatial, back_temporal, upstream
            )
            return (back_input, grad_spatial + spatial_term, grad_temporal + temporal_term)

        def waiting():
            return (blank, grad_spatial, grad_temporal)

        back_input, grad_spatial, grad_temporal = lax.cond(active, working, waiting)
        passed = passed_along(back_input, "pipe", -1)
        return ((passed, grad_spatial, grad_temporal), None)

    start = (
        blank,
        jnp.zeros(back_spatial.shape, jnp.float32),
        jnp.zeros(back_temporal.shape, jnp.float32),
    )
    (_, grad_spatial, grad_temporal), _ = lax.scan(backward_step, start, moments)
    share_spatial, share_temporal = (
        lax.psum_scatter(
            grad_spatial.astype(jnp.bfloat16).astype(jnp.float32).astype(jnp.bfloat16),
            "dp",
            scatter_dimension=0,
            tiled=True,
        ).astype(jnp.float32),
        lax.psum_scatter(
            grad_temporal.astype(jnp.bfloat16).astype(jnp.float32).astype(jnp.bfloat16),
            "dp",
            scatter_dimension=0,
            tiled=True,
        ).astype(jnp.float32),
    )
    return (share_spatial[None], share_temporal[None])


SPAN = 40
CUTS = (24, 16)
PIECE = 64


def coordinates():
    index = lax.axis_index("dp")
    return index // (GRID[1] * GRID[2]), (index // GRID[2]) % GRID[1], index % GRID[2]


def shifted(value, dz=0, dy=0, dc=0):
    pairs = []
    for z in range(GRID[0]):
        for y in range(GRID[1]):
            for c in range(GRID[2]):
                place = ((z + dz) % GRID[0], (y + dy) % GRID[1], (c + dc) % GRID[2])
                pairs.append(
                    (
                        (z * GRID[1] + y) * GRID[2] + c,
                        (place[0] * GRID[1] + place[1]) * GRID[2] + place[2],
                    )
                )
    return lax.ppermute(value, "dp", pairs)


def swapped(value):
    return lax.ppermute(value, "pipe", [(0, 1), (1, 0)])


def part_of(value, index, axis):
    return lax.dynamic_index_in_dim(value, index, axis, keepdims=False)


def vmem_call(body, outs, scratch=(), flops=0, moved=0):
    return pl.pallas_call(
        body,
        out_shape=outs,
        scratch_shapes=list(scratch),
        compiler_params=pltpu.CompilerParams(vmem_limit_bytes=24 * 2**20),
        cost_estimate=pl.CostEstimate(
            flops=5 * flops // 2, bytes_accessed=moved, transcendentals=0
        ),
    )


def after(value, earlier):
    return value if earlier is None else lax.optimization_barrier((value, earlier))[0]


def in_order(swap, own, other, axis):
    return jnp.where(
        swap, jnp.concatenate([other, own], axis), jnp.concatenate([own, other], axis)
    )


def over_z(value, pairs):
    moves = []
    for source, target in pairs:
        for rest in range(GRID[1] * GRID[2]):
            moves.append(tuple(z * GRID[1] * GRID[2] + rest for z in (source, target)))
    return lax.ppermute(value, "dp", moves)


def sent_over_z(value):
    return [shifted(value, dz=step) for step in range(1, GRID[0])]


def sent_on_chip(value, pieces=1):
    return jnp.concatenate([shifted(piece, dc=1) for piece in jnp.split(value, pieces)])


def places_of(channels, main):
    channel = jnp.arange(channels)
    span, inside = channel // SPAN, channel % SPAN
    odd = span % 2
    cut = jnp.where(odd == 0, CUTS[0], CUTS[1])
    second = (inside >= cut).astype(jnp.int32)
    before = span // 2 * SPAN + odd * jnp.where(second == 0, CUTS[0], CUTS[1])
    rank = before + inside - second * cut
    tail = channels // 2 - main
    return jnp.where(
        rank < main, second * main + rank, (1 + second) * main + second * (tail - main) + rank
    )


def spans_of(rows, odd):
    sets = ([], [])
    for index, start in enumerate(range(0, rows, SPAN)):
        cut = start + CUTS[(index + odd) % 2]
        sets[0].append((start, cut))
        sets[1].append((cut, start + SPAN))
    return sets


def sets_of(value):
    _, _, c = coordinates()
    results = []
    for which in range(2):
        by_core = []
        for odd in range(2):
            spans = spans_of(value.shape[0], odd)[which]
            taken = jnp.concatenate([value[start:end] for start, end in spans])
            by_core.append(jnp.pad(taken, ((0, PIECE - taken.shape[0]), (0, 0))))
        results.append(jnp.where(c == 0, by_core[0], by_core[1]))
    return results


def shard_of(own, given, rows):
    _, _, c = coordinates()
    by_core = []
    for odd in range(2):
        taken, pieces = [0, 0], []
        for spans in zip(*spans_of(rows, odd)):
            for which, (start, end) in enumerate(spans):
                source = (own, given)[which]
                pieces.append(source[taken[which] : taken[which] + end - start])
                taken[which] += end - start
        by_core.append(jnp.concatenate(pieces))
    return jnp.where(c == 0, by_core[0], by_core[1])


def compact(pieces, own):
    short = 3 * SPAN - PIECE
    low, high = pieces[:, 0], pieces[:, 1]
    both = jnp.where(
        own,
        jnp.concatenate([low, high[:, :short]], 1),
        jnp.concatenate([low[:, :short], high], 1),
    )
    return both.reshape(-1, pieces.shape[3])


def spread(rows, chips, own):
    rows = rows.reshape(chips, -1, rows.shape[1])
    short = rows.shape[1] - PIECE
    pad = ((0, 0), (0, PIECE - short), (0, 0))
    return jnp.where(
        own,
        jnp.stack([rows[:, :PIECE], jnp.pad(rows[:, PIECE:], pad)], 1),
        jnp.stack([jnp.pad(rows[:, :short], pad), rows[:, short:]], 1),
    )


def gathered_over_z(value, earlier=None):
    z, _, _ = coordinates()
    value = after(value, earlier)
    sent = sent_over_z(value)
    return (
        jnp.stack([lax.select_n((z - place) % GRID[0], value, *sent) for place in range(GRID[0])]),
        sent,
    )


def gathered_over_y(line):
    _, y, _ = coordinates()
    sent = shifted(line, dy=1)
    return in_order(y == 1, line[:, None], sent[:, None], 1), sent


def gathered_on_chip(plane, earlier=None):
    _, _, c = coordinates()
    plane = after(plane, earlier)
    whole = in_order(c == 1, plane[:, :, None], sent_on_chip(plane)[:, :, None], 2)
    return whole.reshape(-1, plane.shape[3])


def added(*terms):
    return sum(term.astype(F32) for term in terms)


def summed_on_chip(value, pieces=1):
    _, _, c = coordinates()
    sent = sent_on_chip(part_of(value, 1 - c, 2), pieces)
    return added(part_of(value, c, 2), sent).astype(BF16)


def summed_over_y(value, earlier):
    _, y, _ = coordinates()
    sent = shifted(after(part_of(value, 1 - y, 1), earlier), dy=1)
    return added(part_of(value, y, 1), sent).astype(BF16), sent


def summed_over_z(line, earlier=None):
    z, _, _ = coordinates()
    line = after(line, earlier)
    sent = [
        shifted(part_of(line, (z + step) % GRID[0], 0), dz=step) for step in range(1, GRID[0])
    ]
    return added(part_of(line, z, 0), *sent), sent


def pixel_masks(rows):
    row = lax.broadcasted_iota(jnp.int32, (rows, 1), 0)
    high, wide = (row // WIDTH) % HEIGHT, row % WIDTH
    masks = []
    for dr in (-1, 0, 1):
        for dc in (-1, 0, 1):
            inside = (high + dr >= 0) & (high + dr < HEIGHT) & (wide + dc >= 0) & (wide + dc < WIDTH)
            masks.append((dr * WIDTH + dc, inside))
    return masks


def frame_masks(rows, frames):
    pixels = HEIGHT * WIDTH
    row = lax.broadcasted_iota(jnp.int32, (rows, 1), 0)
    frame = (row // pixels) % frames
    return [
        (step * pixels, (frame + step >= 0) & (frame + step < frames)) for step in (-1, 0, 1)
    ]


def moved_rows(value, move):
    shift, inside = move
    if shift:
        value = pltpu.roll(value, (-shift) % value.shape[0], 0)
    return jnp.where(inside, value, 0.0)


def dot(left, right, dims=((1,), (0,))):
    return lax.dot_general(left, right, (dims, ((), ())), preferred_element_type=F32)


def with_embedding(hidden, embedding_ref, samples):
    per = hidden.shape[0] // samples
    return jnp.concatenate(
        [hidden[s * per : (s + 1) * per] + embedding_ref[s : s + 1, :] for s in range(samples)]
    )


def scale_of(summed):
    return lax.rsqrt(jnp.mean(summed * summed, axis=-1, keepdims=True) + 1e-06)


def silu_parts(preact):
    logistic = 1.0 / (1.0 + jnp.exp(-preact))
    return logistic, preact * logistic


def convolved(normed, weight_refs, masks):
    rows, channels = normed.shape
    normed = normed.astype(F32)
    totals = [None] * len(weight_refs)
    for tap in range(9):
        moved = moved_rows(normed, masks[tap]).astype(BF16)
        for index, ref in enumerate(weight_refs):
            term = dot(moved, ref[tap * channels : (tap + 1) * channels, :])
            totals[index] = term if totals[index] is None else totals[index] + term
    return jnp.concatenate(totals, 1)


def back_through(pre_grad, weight_refs, masks, channels):
    pre_grad = pre_grad.astype(F32)
    total = None
    for tap in range(9):
        moved = moved_rows(pre_grad, masks[8 - tap]).astype(BF16)
        start = 0
        for ref in weight_refs:
            end = start + ref.shape[1]
            term = dot(
                moved[:, start:end], ref[tap * channels : (tap + 1) * channels, :], ((1,), (1,))
            )
            total = term if total is None else total + term
            start = end
    return total


def tap_rows(temporal_ref, tap, width):
    tail = PIECE
    start = tap * (width - tail)
    rows = temporal_ref[start : start + width - tail, :]
    return jnp.concatenate([rows, rows[width - 2 * tail :]], 0)


def first_forward(frames, hidden_ref, embedding_ref, keep_ref, temporal_ref, *refs):
    *spatial_refs, normed_ref, preact_ref, mixed_ref = refs
    rows = hidden_ref.shape[0]
    width = keep_ref.shape[1]
    summed = with_embedding(hidden_ref[...].astype(F32), embedding_ref, embedding_ref.shape[0])
    normed = (summed * scale_of(summed)).astype(BF16)
    normed_ref[...] = normed
    preact = convolved(normed, spatial_refs, pixel_masks(rows))
    preact_ref[...] = preact
    activated = silu_parts(preact)[1].astype(BF16).astype(F32) * keep_ref[...]
    mixed = None
    for tap, move in enumerate(frame_masks(rows, frames)):
        term = dot(
            moved_rows(activated, move).astype(BF16),
            tap_rows(temporal_ref, tap, width),
        )
        mixed = term if mixed is None else mixed + term
    mixed_ref[...] = mixed.astype(BF16)


def slope_of(preact):
    logistic, _ = silu_parts(preact)
    return logistic * (1.0 + preact * (1.0 - logistic))


def act_grad_of(upstream, temporal_ref, width, frames):
    upstream = upstream.astype(F32)
    moves = frame_masks(upstream.shape[0], frames)
    total = None
    for tap in range(3):
        term = dot(
            moved_rows(upstream, moves[2 - tap]).astype(BF16),
            tap_rows(temporal_ref, tap, width),
            ((1,), (1,)),
        )
        total = term if total is None else total + term
    return total


def store_temporal_terms(activated, upstream, frames, out_ref):
    width = activated.shape[1]
    tail = PIECE
    upstream = upstream.astype(F32)
    moves = frame_masks(upstream.shape[0], frames)
    for tap in range(3):
        term = dot(activated, moved_rows(upstream, moves[2 - tap]).astype(BF16), ((0,), (0,)))
        start = tap * (width - tail)
        out_ref[start : start + width - 2 * tail, :] = term[: width - 2 * tail].astype(BF16)
        out_ref[start + width - 2 * tail : start + width - tail, :] = (
            term[width - 2 * tail : width - tail] + term[width - tail :]
        ).astype(BF16)


def store_spatial_terms(normed, pre_grad, out_refs):
    channels = normed.shape[1]
    pre_grad = pre_grad.astype(F32)
    masks = pixel_masks(pre_grad.shape[0])
    for tap in range(9):
        term = dot(
            normed, moved_rows(pre_grad, masks[8 - tap]).astype(BF16), ((0,), (0,))
        ).astype(BF16)
        start = 0
        for out_ref in out_refs:
            end = start + out_ref.shape[1]
            out_ref[tap * channels : (tap + 1) * channels, :] = term[:, start:end]
            start = end


def second_forward(
    frames, hidden_ref, own_ref, sent_ref, embedding_ref, keep_ref, upstream_ref, temporal_ref, *refs
):
    *spatial_refs, next_ref, normed_ref, activated_ref, pre_grad_ref, back_ref = refs
    rows, channels = hidden_ref.shape
    width = keep_ref.shape[1]
    masks = pixel_masks(rows)
    mixed = own_ref[...].astype(F32) + sent_ref[...].astype(F32)
    hidden = (hidden_ref[...].astype(F32) + mixed).astype(BF16)
    next_ref[...] = hidden
    summed = with_embedding(hidden.astype(F32), embedding_ref, embedding_ref.shape[0])
    normed = (summed * scale_of(summed)).astype(BF16)
    normed_ref[...] = normed
    preact = convolved(normed, spatial_refs, masks)
    activated_ref[...] = (silu_parts(preact)[1] * keep_ref[...]).astype(BF16)
    act_grad = act_grad_of(upstream_ref[...], temporal_ref, width, frames)
    pre_grad = (act_grad * slope_of(preact) * keep_ref[...]).astype(BF16)
    pre_grad_ref[...] = pre_grad
    back = back_through(pre_grad, spatial_refs, masks, channels)
    back_ref[...] = back.astype(BF16)


def second_terms(frames, normed_ref, pre_grad_ref, activated_ref, upstream_ref, *outs):
    *spatial_refs, temporal_ref = outs
    store_spatial_terms(normed_ref[...], pre_grad_ref[...], spatial_refs)
    store_temporal_terms(activated_ref[...], upstream_ref[...], frames, temporal_ref)


def first_terms(
    frames, hidden_ref, embedding_ref, upstream_ref, own_ref, sent_ref, normed_ref, preact_ref,
    keep_ref, temporal_ref, *outs
):
    *spatial_outs, temporal_out = outs
    width = keep_ref.shape[1]
    channels = hidden_ref.shape[1]
    summed = with_embedding(hidden_ref[...].astype(F32), embedding_ref, embedding_ref.shape[0])
    scale = scale_of(summed)
    grad = own_ref[...].astype(F32) + sent_ref[...].astype(F32)
    inner = jnp.sum(grad * summed, axis=-1, keepdims=True)
    back = grad * scale - summed * (scale * scale * scale) * (inner / channels)
    upstream = (upstream_ref[...].astype(F32) + back).astype(BF16)
    preact = preact_ref[...]
    activated = (silu_parts(preact)[1] * keep_ref[...]).astype(BF16)
    act_grad = act_grad_of(upstream, temporal_ref, width, frames)
    pre_grad = (act_grad * slope_of(preact) * keep_ref[...]).astype(BF16)
    store_spatial_terms(normed_ref[...], pre_grad, spatial_outs)
    store_temporal_terms(activated, upstream, frames, temporal_out)


def paired_device(samples, timesteps, cotangent, spatial_weight, temporal_weight):
    me = lax.axis_index("pipe")
    first = me == 0
    _, y, _ = coordinates()
    count, frames, pixels, channels = samples.shape
    rows = count * frames * pixels
    main = 2 * LANES
    width = main + LANES
    hidden = samples.reshape(rows, channels)
    upstream = cotangent.reshape(rows, channels)
    embedding = jax.vmap(lambda step: embedding_of(step, channels))(timesteps)
    lane = jnp.arange(LANES)
    keep_own = jnp.concatenate([jnp.ones(main), lane < LANES // 2]).astype(F32)[None]
    keep_other = jnp.concatenate([jnp.ones(main), lane >= LANES // 2]).astype(F32)[None]
    keep_first = jnp.where(first, keep_own, keep_other)
    keep_second = jnp.where(first, keep_other, keep_own)
    tail = lane[None] < LANES // 2

    places = places_of(channels, main)
    order = (places[:, None] == jnp.arange(channels)).astype(BF16)
    temporal_own, temporal_sent = sets_of(temporal_weight[0])
    temporal_given = swapped(temporal_sent)
    line, sent = gathered_over_z(in_order(me == 1, temporal_own, temporal_given, 0))
    plane_temporal, side = gathered_over_y(line)
    spatial_own = dot(spatial_weight[0], order).astype(BF16)
    given = swapped(spatial_own[:, main:])
    main_own, main_given = spatial_own[:, :main], given[:, :main]
    tails = jnp.where(tail, spatial_own[:, 2 * main :], given[:, main:])
    line, sent = gathered_over_z(jnp.where(first, main_own, main_given), sent)
    line_tails, sent = gathered_over_z(tails, (sent, side))
    plane_first, side = gathered_over_y(line)
    plane_tails, _ = gathered_over_y(line_tails)
    line_second, _ = gathered_over_z(jnp.where(first, main_given, main_own), (sent, side))
    side_second = shifted(line_second, dy=1)

    chips = GRID[0] * GRID[1]
    temporal = gathered_on_chip(plane_temporal).reshape(chips, GRID[2], 2, PIECE, channels)
    temporal_first = compact(temporal[:, :, 0], first)
    temporal_second = compact(temporal[:, :, 1], me == 1)
    tails = gathered_on_chip(plane_tails)
    spatial_first = [gathered_on_chip(plane_first), tails]

    def shape(extent, dtype=BF16):
        return jax.ShapeDtypeStruct(extent, dtype)

    spatial_flops = 2 * rows * 9 * channels * width
    temporal_flops = 2 * rows * 3 * channels * width
    spatial_bytes = 2 * 9 * channels * width
    temporal_bytes = 2 * 3 * channels * width
    normed_first, preact_first, mixed = vmem_call(
        functools.partial(first_forward, frames),
        (shape((rows, channels)), shape((rows, width), F32), shape((rows, channels))),
        flops=spatial_flops + temporal_flops,
        moved=spatial_bytes + temporal_bytes,
    )(hidden, embedding, keep_first, temporal_first, *spatial_first)
    mixed_given = swapped(mixed)
    side_second = after(side_second, mixed)
    plane_second = in_order(y == 1, line_second[:, None], side_second[:, None], 1)
    spatial_second = [gathered_on_chip(plane_second), tails]
    hidden_second, normed_second, activated_second, pre_grad_second, back = vmem_call(
        functools.partial(second_forward, frames),
        (
            shape((rows, channels)),
            shape((rows, channels)),
            shape((rows, width)),
            shape((rows, width)),
            shape((rows, channels)),
        ),
        flops=2 * spatial_flops + temporal_flops,
        moved=spatial_bytes + temporal_bytes,
    )(
        hidden, mixed, mixed_given, embedding, keep_second, upstream, temporal_second,
        *spatial_second,
    )

    def terms_shape():
        return (
            shape((9 * channels, main)),
            shape((9 * channels, width - main)),
            shape((3 * (width - PIECE), channels)),
        )

    def on_chip(terms, pieces=1):
        return summed_on_chip(terms.reshape(*GRID, -1, terms.shape[1]), pieces)

    back_given = swapped(back)
    main_terms_second, tail_terms_second, temporal_terms_second = vmem_call(
        functools.partial(second_terms, frames),
        terms_shape(),
        flops=spatial_flops + temporal_flops,
        moved=spatial_bytes + temporal_bytes,
    )(normed_second, pre_grad_second, activated_second, upstream)
    chip_second = on_chip(main_terms_second, GRID[0])
    back_given = after(back_given, chip_second)
    line, side = summed_over_y(chip_second, None)
    share_second, sent_second = summed_over_z(line)
    main_terms_first, tail_terms_first, temporal_terms_first = vmem_call(
        functools.partial(first_terms, frames),
        terms_shape(),
        flops=spatial_flops + 2 * temporal_flops,
        moved=spatial_bytes + 2 * temporal_bytes,
    )(
        hidden_second, embedding, upstream, back, back_given, normed_first, preact_first,
        keep_first, temporal_first,
    )
    chip_tails = on_chip(tail_terms_first + tail_terms_second)
    chip_first = on_chip(after(main_terms_first, side))
    terms = jnp.concatenate(
        [
            spread(temporal_terms_first, chips, first),
            spread(temporal_terms_second, chips, me == 1),
        ],
        2,
    )
    chip_temporal = summed_on_chip(terms.reshape(*GRID, -1, channels))

    line, side = summed_over_y(chip_tails, side)
    line_low, side = summed_over_y(chip_first[..., :LANES], side)
    share_tails, sent_tails = summed_over_z(line, (side, sent_second))
    line_high, side = summed_over_y(chip_first[..., LANES:], side)
    share_first, sent_first = summed_over_z(
        jnp.concatenate([line_low, line_high], 2), sent_tails
    )
    line, side = summed_over_y(chip_temporal, side)
    share_temporal, _ = summed_over_z(line, sent_first)

    kept = jnp.where(first, share_first, share_second)
    passed = jnp.where(first, share_second, share_first)
    given = jnp.concatenate([passed, share_tails], 1).astype(BF16)
    given = swapped(after(given, side)).astype(F32)
    share_spatial = jnp.concatenate(
        [kept, given[:, :main], jnp.where(tail, share_tails, given[:, main:])], 1
    )
    share_spatial = lax.dot_general(
        share_spatial, order.astype(F32), (((1,), (1,)), ((), ())), precision=lax.Precision.HIGH
    )
    low, high = share_temporal[:PIECE], share_temporal[PIECE:]
    given = swapped(jnp.where(first, high, low).astype(BF16)).astype(F32)
    share_temporal = shard_of(jnp.where(first, low, high), given, temporal_weight.shape[1])
    return (share_spatial[None], share_temporal[None])


def solution(mesh):
    paired = mesh.shape["pipe"] == 2 and mesh.shape["dp"] == math.prod(GRID)
    return jax.shard_map(
        paired_device if paired else per_device,
        mesh=mesh,
        in_specs=(
            P("dp", None, None, None),
            P("dp"),
            P("dp", None, None, None),
            P("pipe", "dp", None),
            P("pipe", "dp", None),
        ),
        out_specs=(P("pipe", "dp", None), P("pipe", "dp", None)),
        check_vma=False,
    )
```

```python
import functools
import math

import jax
import jax.numpy as jnp
from jax import lax
from jax.experimental import pallas as pl
from jax.experimental.pallas import tpu as pltpu
from jax.sharding import PartitionSpec as P

HEIGHT = 8
WIDTH = 4
F32 = jnp.float32
BF16 = jnp.bfloat16
GRID = (4, 2, 2)
LANES = 128


def passed_along(value, axis, steps):
    count = lax.axis_size(axis)
    first, last = (max(0, -steps), min(count, count - steps))
    return lax.ppermute(value, axis, [(source, source + steps) for source in range(first, last)])


def embedding_of(step, channels):
    half_width = channels // 2
    frequency = jnp.exp(-math.log(10000.0) * jnp.arange(half_width, dtype=jnp.float32) / half_width)
    phases = step.astype(jnp.float32) * frequency
    return jnp.concatenate([jnp.sin(phases), jnp.cos(phases)])


def normalize(summed):
    return summed * lax.rsqrt(jnp.mean(summed * summed, axis=-1, keepdims=True) + 1e-06)


def spatial_columns(normed):
    frames, pixels, channels = normed.shape
    grid = normed.reshape(frames, HEIGHT, WIDTH, channels)
    padded = jnp.pad(grid, ((0, 0), (1, 1), (1, 1), (0, 0)))
    pieces = [
        padded[:, row : row + HEIGHT, col : col + WIDTH, :] for row in range(3) for col in range(3)
    ]
    return jnp.concatenate(pieces, axis=-1).reshape(frames * pixels, 9 * channels)


def spatial_fold(grads, frames, channels):
    parts = grads.reshape(frames, HEIGHT, WIDTH, 9, channels)
    padded = jnp.zeros((frames, HEIGHT + 2, WIDTH + 2, channels), jnp.float32)
    for row in range(3):
        for col in range(3):
            padded = padded.at[:, row : row + HEIGHT, col : col + WIDTH, :].add(
                parts[:, :, :, row * 3 + col, :]
            )
    return padded[:, 1 : HEIGHT + 1, 1 : WIDTH + 1, :].reshape(frames, HEIGHT * WIDTH, channels)


def temporal_columns(activated):
    frames, pixels, channels = activated.shape
    padded = jnp.pad(activated, ((1, 1), (0, 0), (0, 0)))
    pieces = [padded[tap : tap + frames] for tap in range(3)]
    return jnp.concatenate(pieces, axis=-1).reshape(frames * pixels, 3 * channels)


def temporal_fold(grads, frames, pixels, channels):
    parts = grads.reshape(frames, pixels, 3, channels)
    padded = jnp.zeros((frames + 2, pixels, channels), jnp.float32)
    for tap in range(3):
        padded = padded.at[tap : tap + frames].add(parts[:, :, tap, :])
    return padded[1 : frames + 1]


def section_forward(block_in, embedding, spatial, temporal):
    frames, pixels, channels = block_in.shape
    summed = block_in.astype(jnp.float32) + embedding
    normed = normalize(summed).astype(jnp.bfloat16)
    preact = jnp.dot(spatial_columns(normed), spatial, preferred_element_type=jnp.float32)
    activated = jax.nn.silu(preact).astype(jnp.bfloat16).reshape(frames, pixels, channels)
    mixed = jnp.dot(temporal_columns(activated), temporal, preferred_element_type=jnp.float32)
    return (block_in.astype(jnp.float32) + mixed.reshape(frames, pixels, channels)).astype(
        jnp.bfloat16
    )


def backward_first(block_in, embedding, spatial, temporal, upstream):
    frames, pixels, channels = block_in.shape
    summed = block_in.astype(jnp.float32) + embedding
    normed = normalize(summed).astype(jnp.bfloat16)
    columns = spatial_columns(normed)
    preact = jnp.dot(columns, spatial, preferred_element_type=jnp.float32)
    activated = jax.nn.silu(preact).astype(jnp.bfloat16).reshape(frames, pixels, channels)
    tcolumns = temporal_columns(activated)
    upstream_flat = upstream.reshape(frames * pixels, channels)
    temporal_term = jnp.dot(tcolumns.T, upstream_flat, preferred_element_type=jnp.float32)
    act_grad = temporal_fold(
        jnp.dot(upstream_flat, temporal.T, preferred_element_type=jnp.float32),
        frames,
        pixels,
        channels,
    )
    logistic = jax.nn.sigmoid(preact)
    slope = logistic * (1.0 + preact * (1.0 - logistic))
    pre_grad = (act_grad.reshape(frames * pixels, channels) * slope).astype(jnp.bfloat16)
    return (temporal_term, pre_grad, columns)


def backward_second(block_in, embedding, spatial, upstream, pre_grad, columns):
    frames, pixels, channels = block_in.shape
    summed = block_in.astype(jnp.float32) + embedding
    spatial_term = jnp.dot(columns.T, pre_grad, preferred_element_type=jnp.float32)
    norm_grad = spatial_fold(
        jnp.dot(pre_grad, spatial.T, preferred_element_type=jnp.float32), frames, channels
    )
    _, pullback = jax.vjp(normalize, summed)
    back_input = (upstream.astype(jnp.float32) + pullback(norm_grad)[0]).astype(jnp.bfloat16)
    return (back_input, spatial_term)


def section_backward(block_in, embedding, spatial, temporal, upstream):
    temporal_term, pre_grad, columns = backward_first(
        block_in, embedding, spatial, temporal, upstream
    )
    back_input, spatial_term = backward_second(
        block_in, embedding, spatial, upstream, pre_grad, columns
    )
    return (back_input, spatial_term, temporal_term)


def per_device(samples, timesteps, cotangent, spatial_weight, temporal_weight):
    sections = lax.axis_size("pipe")
    section_index = lax.axis_index("pipe")
    micro_count = samples.shape[0]
    frames, pixels, channels = (samples.shape[1], samples.shape[2], samples.shape[3])
    moments = jnp.arange(micro_count + sections - 1, dtype=jnp.int32)
    blank = jnp.zeros((frames, pixels, channels), jnp.bfloat16)
    full_spatial, full_temporal = (
        lax.all_gather(spatial_weight[0], "dp", axis=0, tiled=True),
        lax.all_gather(temporal_weight[0], "dp", axis=0, tiled=True),
    )

    def forward_step(carry, moment):
        incoming, stash = carry
        position = moment - section_index
        active = (position >= 0) & (position < micro_count)
        picked = jnp.clip(position, 0, micro_count - 1)
        own = lax.dynamic_index_in_dim(samples, picked, 0, keepdims=False)
        embedding = embedding_of(
            lax.dynamic_index_in_dim(timesteps, picked, 0, keepdims=False), channels
        )
        block_in = jnp.where(section_index == 0, own, incoming)
        result = lax.cond(
            active & (section_index < sections - 1),
            lambda: section_forward(block_in, embedding, full_spatial, full_temporal),
            lambda: blank,
        )
        stash = jnp.where(
            active, lax.dynamic_update_index_in_dim(stash, block_in, picked, 0), stash
        )
        passed = passed_along(result, "pipe", 1)
        return ((passed, stash), None)

    (_, stash), _ = lax.scan(forward_step, (blank, jnp.zeros_like(samples)), moments)
    back_spatial, back_temporal = (full_spatial, full_temporal)

    def inputs_at(moment, incoming):
        position = moment - (sections - 1 - section_index)
        active = (position >= 0) & (position < micro_count)
        picked = jnp.clip(position, 0, micro_count - 1)
        block_in = lax.dynamic_index_in_dim(stash, picked, 0, keepdims=False)
        embedding = embedding_of(
            lax.dynamic_index_in_dim(timesteps, picked, 0, keepdims=False), channels
        )
        given = lax.dynamic_index_in_dim(cotangent, picked, 0, keepdims=False)
        upstream = jnp.where(section_index == sections - 1, given, incoming)
        return (active, block_in, embedding, upstream)

    def backward_step(carry, moment):
        incoming, grad_spatial, grad_temporal = carry
        active, block_in, embedding, upstream = inputs_at(moment, incoming)

        def working():
            back_input, spatial_term, temporal_term = section_backward(
                block_in, embedding, back_spatial, back_temporal, upstream
            )
            return (back_input, grad_spatial + spatial_term, grad_temporal + temporal_term)

        def waiting():
            return (blank, grad_spatial, grad_temporal)

        back_input, grad_spatial, grad_temporal = lax.cond(active, working, waiting)
        passed = passed_along(back_input, "pipe", -1)
        return ((passed, grad_spatial, grad_temporal), None)

    start = (
        blank,
        jnp.zeros(back_spatial.shape, jnp.float32),
        jnp.zeros(back_temporal.shape, jnp.float32),
    )
    (_, grad_spatial, grad_temporal), _ = lax.scan(backward_step, start, moments)
    share_spatial, share_temporal = (
        lax.psum_scatter(
            grad_spatial.astype(jnp.bfloat16).astype(jnp.float32).astype(jnp.bfloat16),
            "dp",
            scatter_dimension=0,
            tiled=True,
        ).astype(jnp.float32),
        lax.psum_scatter(
            grad_temporal.astype(jnp.bfloat16).astype(jnp.float32).astype(jnp.bfloat16),
            "dp",
            scatter_dimension=0,
            tiled=True,
        ).astype(jnp.float32),
    )
    return (share_spatial[None], share_temporal[None])


SPAN = 40
CUTS = (24, 16)
PIECE = 64


def coordinates():
    index = lax.axis_index("dp")
    return index // (GRID[1] * GRID[2]), (index // GRID[2]) % GRID[1], index % GRID[2]


def shifted(value, dz=0, dy=0, dc=0):
    pairs = []
    for z in range(GRID[0]):
        for y in range(GRID[1]):
            for c in range(GRID[2]):
                place = ((z + dz) % GRID[0], (y + dy) % GRID[1], (c + dc) % GRID[2])
                pairs.append(
                    (
                        (z * GRID[1] + y) * GRID[2] + c,
                        (place[0] * GRID[1] + place[1]) * GRID[2] + place[2],
                    )
                )
    return lax.ppermute(value, "dp", pairs)


def swapped(value):
    return lax.ppermute(value, "pipe", [(0, 1), (1, 0)])


def part_of(value, index, axis):
    return lax.dynamic_index_in_dim(value, index, axis, keepdims=False)


def vmem_call(body, outs, scratch=(), flops=0, moved=0):
    return pl.pallas_call(
        body,
        out_shape=outs,
        scratch_shapes=list(scratch),
        compiler_params=pltpu.CompilerParams(vmem_limit_bytes=24 * 2**20),
        cost_estimate=pl.CostEstimate(
            flops=5 * flops // 2, bytes_accessed=moved, transcendentals=0
        ),
    )


def after(value, earlier):
    return value if earlier is None else lax.optimization_barrier((value, earlier))[0]


def in_order(swap, own, other, axis):
    return jnp.where(
        swap, jnp.concatenate([other, own], axis), jnp.concatenate([own, other], axis)
    )


def over_z(value, pairs):
    moves = []
    for source, target in pairs:
        for rest in range(GRID[1] * GRID[2]):
            moves.append(tuple(z * GRID[1] * GRID[2] + rest for z in (source, target)))
    return lax.ppermute(value, "dp", moves)


def sent_over_z(value):
    return [shifted(value, dz=step) for step in range(1, GRID[0])]


def sent_on_chip(value, pieces=1):
    if pieces == 1:
        return shifted(value, dc=1)
    flat = value.reshape(-1, *value.shape[-2:])
    sent = [shifted(piece, dc=1) for piece in jnp.split(flat, pieces)]
    return jnp.concatenate(sent).reshape(value.shape)


def places_of(channels, main):
    channel = jnp.arange(channels)
    span, inside = channel // SPAN, channel % SPAN
    odd = span % 2
    cut = jnp.where(odd == 0, CUTS[0], CUTS[1])
    second = (inside >= cut).astype(jnp.int32)
    before = span // 2 * SPAN + odd * jnp.where(second == 0, CUTS[0], CUTS[1])
    rank = before + inside - second * cut
    tail = channels // 2 - main
    return jnp.where(
        rank < main, second * main + rank, (1 + second) * main + second * (tail - main) + rank
    )


def spans_of(rows, odd):
    sets = ([], [])
    for index, start in enumerate(range(0, rows, SPAN)):
        cut = start + CUTS[(index + odd) % 2]
        sets[0].append((start, cut))
        sets[1].append((cut, start + SPAN))
    return sets


def sets_of(value):
    _, _, c = coordinates()
    results = []
    for which in range(2):
        by_core = []
        for odd in range(2):
            spans = spans_of(value.shape[0], odd)[which]
            taken = jnp.concatenate([value[start:end] for start, end in spans])
            by_core.append(jnp.pad(taken, ((0, PIECE - taken.shape[0]), (0, 0))))
        results.append(jnp.where(c == 0, by_core[0], by_core[1]))
    return results


def shard_of(own, given, rows):
    _, _, c = coordinates()
    by_core = []
    for odd in range(2):
        taken, pieces = [0, 0], []
        for spans in zip(*spans_of(rows, odd)):
            for which, (start, end) in enumerate(spans):
                source = (own, given)[which]
                pieces.append(source[taken[which] : taken[which] + end - start])
                taken[which] += end - start
        by_core.append(jnp.concatenate(pieces))
    return jnp.where(c == 0, by_core[0], by_core[1])


def compact(pieces, own):
    short = 3 * SPAN - PIECE
    low, high = pieces[:, 0], pieces[:, 1]
    both = jnp.where(
        own,
        jnp.concatenate([low, high[:, :short]], 1),
        jnp.concatenate([low[:, :short], high], 1),
    )
    return both.reshape(-1, pieces.shape[3])


def spread(rows, chips, own):
    rows = rows.reshape(chips, -1, rows.shape[1])
    short = rows.shape[1] - PIECE
    pad = ((0, 0), (0, PIECE - short), (0, 0))
    return jnp.where(
        own,
        jnp.stack([rows[:, :PIECE], jnp.pad(rows[:, PIECE:], pad)], 1),
        jnp.stack([jnp.pad(rows[:, :short], pad), rows[:, short:]], 1),
    )


def gathered_over_z(value, earlier=None):
    z, _, _ = coordinates()
    value = after(value, earlier)
    sent = sent_over_z(value)
    return (
        jnp.stack([lax.select_n((z - place) % GRID[0], value, *sent) for place in range(GRID[0])]),
        sent,
    )


def gathered_over_y(line, earlier=None):
    _, y, _ = coordinates()
    line = after(line, earlier)
    sent = shifted(line, dy=1)
    return in_order(y == 1, line[:, None], sent[:, None], 1), sent


def gathered_on_chip(plane, earlier=None):
    _, _, c = coordinates()
    plane = after(plane, earlier)
    whole = in_order(c == 1, plane[:, :, None], sent_on_chip(plane)[:, :, None], 2)
    return whole.reshape(-1, plane.shape[3])


def added(*terms):
    return sum(term.astype(F32) for term in terms)


def summed_on_chip(value, pieces=1):
    _, _, c = coordinates()
    sent = sent_on_chip(part_of(value, 1 - c, 2), pieces)
    return added(part_of(value, c, 2), sent).astype(BF16)


def summed_over_y(value, earlier):
    _, y, _ = coordinates()
    sent = shifted(after(part_of(value, 1 - y, 1), earlier), dy=1)
    return added(part_of(value, y, 1), sent).astype(BF16), sent


def sent_for_sums(line, earlier=None):
    z, _, _ = coordinates()
    line = after(line, earlier)
    return [
        shifted(part_of(line, (z + step) % GRID[0], 0), dz=step) for step in range(1, GRID[0])
    ]


def summed_over_z(line, earlier=None):
    z, _, _ = coordinates()
    sent = sent_for_sums(line, earlier)
    return added(part_of(line, z, 0), *sent), sent


def pixel_masks(rows):
    row = lax.broadcasted_iota(jnp.int32, (rows, 1), 0)
    high, wide = (row // WIDTH) % HEIGHT, row % WIDTH
    masks = []
    for dr in (-1, 0, 1):
        for dc in (-1, 0, 1):
            inside = (high + dr >= 0) & (high + dr < HEIGHT) & (wide + dc >= 0) & (wide + dc < WIDTH)
            masks.append((dr * WIDTH + dc, inside))
    return masks


def frame_masks(rows, frames):
    pixels = HEIGHT * WIDTH
    row = lax.broadcasted_iota(jnp.int32, (rows, 1), 0)
    frame = (row // pixels) % frames
    return [
        (step * pixels, (frame + step >= 0) & (frame + step < frames)) for step in (-1, 0, 1)
    ]


def moved_rows(value, move):
    shift, inside = move
    if shift:
        value = pltpu.roll(value, (-shift) % value.shape[0], 0)
    return jnp.where(inside, value, 0.0)


def dot(left, right, dims=((1,), (0,))):
    return lax.dot_general(left, right, (dims, ((), ())), preferred_element_type=F32)


def with_embedding(hidden, embedding_ref, samples):
    per = hidden.shape[0] // samples
    return jnp.concatenate(
        [hidden[s * per : (s + 1) * per] + embedding_ref[s : s + 1, :] for s in range(samples)]
    )


def scale_of(summed):
    return lax.rsqrt(jnp.mean(summed * summed, axis=-1, keepdims=True) + 1e-06)


def silu_parts(preact):
    logistic = 1.0 / (1.0 + jnp.exp(-preact))
    return logistic, preact * logistic


def convolved(normed, weight_refs, masks):
    rows, channels = normed.shape
    normed = normed.astype(F32)
    totals = [None] * len(weight_refs)
    for tap in range(9):
        moved = moved_rows(normed, masks[tap]).astype(BF16)
        for index, ref in enumerate(weight_refs):
            term = dot(moved, ref[tap * channels : (tap + 1) * channels, :])
            totals[index] = term if totals[index] is None else totals[index] + term
    return jnp.concatenate(totals, 1)


def back_through(pre_grad, weight_refs, masks, channels):
    pre_grad = pre_grad.astype(F32)
    total = None
    for tap in range(9):
        weights = [ref[tap * channels : (tap + 1) * channels, :] for ref in weight_refs]
        term = dot(
            moved_rows(pre_grad, masks[8 - tap]).astype(BF16),
            jnp.concatenate(weights, 1),
            ((1,), (1,)),
        )
        total = term if total is None else total + term
    return total


def tap_rows(temporal_ref, tap, width):
    tail = PIECE
    start = tap * (width - tail)
    rows = temporal_ref[start : start + width - tail, :]
    return jnp.concatenate([rows, rows[width - 2 * tail :]], 0)


def first_forward(frames, hidden_ref, embedding_ref, keep_ref, temporal_ref, *refs):
    *spatial_refs, normed_ref, preact_ref, mixed_ref = refs
    rows = hidden_ref.shape[0]
    width = keep_ref.shape[1]
    summed = with_embedding(hidden_ref[...].astype(F32), embedding_ref, embedding_ref.shape[0])
    normed = (summed * scale_of(summed)).astype(BF16)
    normed_ref[...] = normed
    preact = convolved(normed, spatial_refs, pixel_masks(rows))
    preact_ref[...] = preact
    activated = silu_parts(preact)[1].astype(BF16).astype(F32) * keep_ref[...]
    mixed = None
    for tap, move in enumerate(frame_masks(rows, frames)):
        term = dot(
            moved_rows(activated, move).astype(BF16),
            tap_rows(temporal_ref, tap, width),
        )
        mixed = term if mixed is None else mixed + term
    mixed_ref[...] = mixed.astype(BF16)


def slope_of(preact):
    logistic, _ = silu_parts(preact)
    return logistic * (1.0 + preact * (1.0 - logistic))


def act_grad_of(upstream, temporal_ref, width, frames):
    upstream = upstream.astype(F32)
    moves = frame_masks(upstream.shape[0], frames)
    total = None
    for tap in range(3):
        term = dot(
            moved_rows(upstream, moves[2 - tap]).astype(BF16),
            tap_rows(temporal_ref, tap, width),
            ((1,), (1,)),
        )
        total = term if total is None else total + term
    return total


def store_temporal_terms(activated, upstream, frames, out_ref):
    width = activated.shape[1]
    tail = PIECE
    upstream = upstream.astype(F32)
    moves = frame_masks(upstream.shape[0], frames)
    for tap in range(3):
        term = dot(activated, moved_rows(upstream, moves[2 - tap]).astype(BF16), ((0,), (0,)))
        start = tap * (width - tail)
        out_ref[start : start + width - 2 * tail, :] = term[: width - 2 * tail].astype(BF16)
        out_ref[start + width - 2 * tail : start + width - tail, :] = (
            term[width - 2 * tail : width - tail] + term[width - tail :]
        ).astype(BF16)


def store_spatial_terms(normed, pre_grad, out_refs):
    channels = normed.shape[1]
    pre_grad = pre_grad.astype(F32)
    masks = pixel_masks(pre_grad.shape[0])
    for tap in range(9):
        term = dot(
            normed, moved_rows(pre_grad, masks[8 - tap]).astype(BF16), ((0,), (0,))
        ).astype(BF16)
        start = 0
        for out_ref in out_refs:
            end = start + out_ref.shape[1]
            out_ref[tap * channels : (tap + 1) * channels, :] = term[:, start:end]
            start = end


def second_forward(
    frames, hidden_ref, own_ref, sent_ref, embedding_ref, keep_ref, upstream_ref, temporal_ref, *refs
):
    *spatial_refs, next_ref, normed_ref, activated_ref, pre_grad_ref, back_ref = refs
    rows, channels = hidden_ref.shape
    width = keep_ref.shape[1]
    masks = pixel_masks(rows)
    mixed = own_ref[...].astype(F32) + sent_ref[...].astype(F32)
    hidden = (hidden_ref[...].astype(F32) + mixed).astype(BF16)
    next_ref[...] = hidden
    summed = with_embedding(hidden.astype(F32), embedding_ref, embedding_ref.shape[0])
    normed = (summed * scale_of(summed)).astype(BF16)
    normed_ref[...] = normed
    preact = convolved(normed, spatial_refs, masks)
    activated_ref[...] = (silu_parts(preact)[1] * keep_ref[...]).astype(BF16)
    act_grad = act_grad_of(upstream_ref[...], temporal_ref, width, frames)
    pre_grad = (act_grad * slope_of(preact) * keep_ref[...]).astype(BF16)
    pre_grad_ref[...] = pre_grad
    back = back_through(pre_grad, spatial_refs, masks, channels)
    back_ref[...] = back.astype(BF16)


def second_terms(frames, normed_ref, pre_grad_ref, activated_ref, upstream_ref, *outs):
    *spatial_refs, temporal_ref = outs
    store_spatial_terms(normed_ref[...], pre_grad_ref[...], spatial_refs)
    store_temporal_terms(activated_ref[...], upstream_ref[...], frames, temporal_ref)


def first_terms(
    frames, hidden_ref, embedding_ref, upstream_ref, own_ref, sent_ref, normed_ref, preact_ref,
    keep_ref, temporal_ref, *outs
):
    *spatial_outs, temporal_out = outs
    width = keep_ref.shape[1]
    channels = hidden_ref.shape[1]
    summed = with_embedding(hidden_ref[...].astype(F32), embedding_ref, embedding_ref.shape[0])
    scale = scale_of(summed)
    grad = own_ref[...].astype(F32) + sent_ref[...].astype(F32)
    inner = jnp.sum(grad * summed, axis=-1, keepdims=True)
    back = grad * scale - summed * (scale * scale * scale) * (inner / channels)
    upstream = (upstream_ref[...].astype(F32) + back).astype(BF16)
    preact = preact_ref[...]
    activated = (silu_parts(preact)[1] * keep_ref[...]).astype(BF16)
    act_grad = act_grad_of(upstream, temporal_ref, width, frames)
    pre_grad = (act_grad * slope_of(preact) * keep_ref[...]).astype(BF16)
    store_spatial_terms(normed_ref[...], pre_grad, spatial_outs)
    store_temporal_terms(activated, upstream, frames, temporal_out)


def paired_device(samples, timesteps, cotangent, spatial_weight, temporal_weight):
    me = lax.axis_index("pipe")
    first = me == 0
    _, y, _ = coordinates()
    count, frames, pixels, channels = samples.shape
    rows = count * frames * pixels
    main = 2 * LANES
    width = main + LANES
    hidden = samples.reshape(rows, channels)
    upstream = cotangent.reshape(rows, channels)
    embedding = jax.vmap(lambda step: embedding_of(step, channels))(timesteps)
    lane = jnp.arange(LANES)
    keep_own = jnp.concatenate([jnp.ones(main), lane < LANES // 2]).astype(F32)[None]
    keep_other = jnp.concatenate([jnp.ones(main), lane >= LANES // 2]).astype(F32)[None]
    keep_first = jnp.where(first, keep_own, keep_other)
    keep_second = jnp.where(first, keep_other, keep_own)
    tail = lane[None] < LANES // 2

    places = places_of(channels, main)
    order = (places[:, None] == jnp.arange(channels)).astype(BF16)
    temporal_own, temporal_sent = sets_of(temporal_weight[0])
    temporal_given = swapped(temporal_sent)
    line, sent = gathered_over_z(in_order(me == 1, temporal_own, temporal_given, 0))
    plane_temporal, side = gathered_over_y(line)
    spatial_own = dot(spatial_weight[0], order).astype(BF16)
    given = swapped(spatial_own[:, main:])
    main_own, main_given = spatial_own[:, :main], given[:, :main]
    tails = jnp.where(tail, spatial_own[:, 2 * main :], given[:, main:])
    line, sent = gathered_over_z(jnp.where(first, main_own, main_given), sent)
    line_tails, sent = gathered_over_z(tails, (sent, side))
    plane_low, side = gathered_over_y(line[..., :LANES])
    plane_high, _ = gathered_over_y(line[..., LANES:], side)
    plane_tails, _ = gathered_over_y(line_tails)
    line_second, _ = gathered_over_z(jnp.where(first, main_given, main_own), (sent, side))
    side_second = shifted(line_second, dy=1)

    chips = GRID[0] * GRID[1]
    temporal = gathered_on_chip(plane_temporal).reshape(chips, GRID[2], 2, PIECE, channels)
    temporal_first = compact(temporal[:, :, 0], first)
    temporal_second = compact(temporal[:, :, 1], me == 1)
    tails = gathered_on_chip(plane_tails)
    spatial_first = [gathered_on_chip(jnp.concatenate([plane_low, plane_high], 3)), tails]

    def shape(extent, dtype=BF16):
        return jax.ShapeDtypeStruct(extent, dtype)

    spatial_flops = 2 * rows * 9 * channels * width
    temporal_flops = 2 * rows * 3 * channels * width
    spatial_bytes = 2 * 9 * channels * width
    temporal_bytes = 2 * 3 * channels * width
    normed_first, preact_first, mixed = vmem_call(
        functools.partial(first_forward, frames),
        (shape((rows, channels)), shape((rows, width), F32), shape((rows, channels))),
        flops=spatial_flops + temporal_flops,
        moved=spatial_bytes + temporal_bytes,
    )(hidden, embedding, keep_first, temporal_first, *spatial_first)
    mixed_given = swapped(mixed)
    side_second = after(side_second, mixed)
    plane_second = in_order(y == 1, line_second[:, None], side_second[:, None], 1)
    spatial_second = [gathered_on_chip(plane_second), tails]
    hidden_second, normed_second, activated_second, pre_grad_second, back = vmem_call(
        functools.partial(second_forward, frames),
        (
            shape((rows, channels)),
            shape((rows, channels)),
            shape((rows, width)),
            shape((rows, width)),
            shape((rows, channels)),
        ),
        flops=2 * spatial_flops + temporal_flops,
        moved=spatial_bytes + temporal_bytes,
    )(
        hidden, mixed, mixed_given, embedding, keep_second, upstream, temporal_second,
        *spatial_second,
    )

    def terms_shape():
        return (
            shape((9 * channels, main)),
            shape((9 * channels, width - main)),
            shape((3 * (width - PIECE), channels)),
        )

    def on_chip(terms, pieces=1):
        return summed_on_chip(terms.reshape(*GRID, -1, terms.shape[1]), pieces)

    back_given = swapped(back)
    main_terms_second, tail_terms_second, temporal_terms_second = vmem_call(
        functools.partial(second_terms, frames),
        terms_shape(),
        flops=spatial_flops + temporal_flops,
        moved=spatial_bytes + temporal_bytes,
    )(normed_second, pre_grad_second, activated_second, upstream)
    chip_second = on_chip(main_terms_second, GRID[0])
    back_given = after(back_given, chip_second)
    line, side = summed_over_y(chip_second, None)
    share_second, sent_second = summed_over_z(line)
    main_terms_first, tail_terms_first, temporal_terms_first = vmem_call(
        functools.partial(first_terms, frames),
        terms_shape(),
        flops=spatial_flops + 2 * temporal_flops,
        moved=spatial_bytes + 2 * temporal_bytes,
    )(
        hidden_second, embedding, upstream, back, back_given, normed_first, preact_first,
        keep_first, temporal_first,
    )
    chip_tails = on_chip(tail_terms_first + tail_terms_second)
    chip_first = on_chip(after(main_terms_first, side))
    terms = jnp.concatenate(
        [
            spread(temporal_terms_first, chips, first),
            spread(temporal_terms_second, chips, me == 1),
        ],
        2,
    )
    chip_temporal = summed_on_chip(terms.reshape(*GRID, -1, channels))

    line_tails, side = summed_over_y(chip_tails, side)
    line_temporal, side = summed_over_y(chip_temporal, side)
    share_tails, sent_tails = summed_over_z(line_tails, sent_second)
    line_low, side = summed_over_y(chip_first[..., :LANES], side)
    share_temporal, sent_temporal = summed_over_z(line_temporal, sent_tails)
    line_high, side = summed_over_y(chip_first[..., LANES:], (side, sent_temporal))
    share_low, sent_low = summed_over_z(line_low)
    share_high, sent_high = summed_over_z(line_high, sent_low)

    def exchanged(own, earlier=None):
        return swapped(after(own.astype(BF16), earlier)).astype(F32)

    low, high = (
        (jnp.where(first, ours, theirs), jnp.where(first, theirs, ours))
        for ours, theirs in (
            (share_low, share_second[:, :LANES]),
            (share_high, share_second[:, LANES:]),
        )
    )
    given = exchanged(jnp.concatenate([low[1], share_tails], 1), sent_high)
    given_high = exchanged(high[1])
    share_spatial = jnp.concatenate(
        [
            low[0],
            high[0],
            given[:, :LANES],
            given_high,
            jnp.where(tail, share_tails, given[:, LANES:]),
        ],
        1,
    )
    share_spatial = lax.dot_general(
        share_spatial, order.astype(F32), (((1,), (1,)), ((), ())), precision=lax.Precision.HIGH
    )
    low, high = share_temporal[:PIECE], share_temporal[PIECE:]
    given = exchanged(jnp.where(first, high, low), sent_low)
    share_temporal = shard_of(jnp.where(first, low, high), given, temporal_weight.shape[1])
    return (share_spatial[None], share_temporal[None])


def solution(mesh):
    paired = mesh.shape["pipe"] == 2 and mesh.shape["dp"] == math.prod(GRID)
    return jax.shard_map(
        paired_device if paired else per_device,
        mesh=mesh,
        in_specs=(
            P("dp", None, None, None),
            P("dp"),
            P("dp", None, None, None),
            P("pipe", "dp", None),
            P("pipe", "dp", None),
        ),
        out_specs=(P("pipe", "dp", None), P("pipe", "dp", None)),
        check_vma=False,
    )
```

```python
import functools
import math

import jax
import jax.numpy as jnp
from jax import lax
from jax.experimental import pallas as pl
from jax.experimental.pallas import tpu as pltpu
from jax.sharding import PartitionSpec as P

HEIGHT = 8
WIDTH = 4
F32 = jnp.float32
BF16 = jnp.bfloat16
GRID = (4, 2, 2)
LANES = 128


def passed_along(value, axis, steps):
    count = lax.axis_size(axis)
    first, last = (max(0, -steps), min(count, count - steps))
    return lax.ppermute(value, axis, [(source, source + steps) for source in range(first, last)])


def embedding_of(step, channels):
    half_width = channels // 2
    frequency = jnp.exp(-math.log(10000.0) * jnp.arange(half_width, dtype=jnp.float32) / half_width)
    phases = step.astype(jnp.float32) * frequency
    return jnp.concatenate([jnp.sin(phases), jnp.cos(phases)])


def normalize(summed):
    return summed * lax.rsqrt(jnp.mean(summed * summed, axis=-1, keepdims=True) + 1e-06)


def spatial_columns(normed):
    frames, pixels, channels = normed.shape
    grid = normed.reshape(frames, HEIGHT, WIDTH, channels)
    padded = jnp.pad(grid, ((0, 0), (1, 1), (1, 1), (0, 0)))
    pieces = [
        padded[:, row : row + HEIGHT, col : col + WIDTH, :] for row in range(3) for col in range(3)
    ]
    return jnp.concatenate(pieces, axis=-1).reshape(frames * pixels, 9 * channels)


def spatial_fold(grads, frames, channels):
    parts = grads.reshape(frames, HEIGHT, WIDTH, 9, channels)
    padded = jnp.zeros((frames, HEIGHT + 2, WIDTH + 2, channels), jnp.float32)
    for row in range(3):
        for col in range(3):
            padded = padded.at[:, row : row + HEIGHT, col : col + WIDTH, :].add(
                parts[:, :, :, row * 3 + col, :]
            )
    return padded[:, 1 : HEIGHT + 1, 1 : WIDTH + 1, :].reshape(frames, HEIGHT * WIDTH, channels)


def temporal_columns(activated):
    frames, pixels, channels = activated.shape
    padded = jnp.pad(activated, ((1, 1), (0, 0), (0, 0)))
    pieces = [padded[tap : tap + frames] for tap in range(3)]
    return jnp.concatenate(pieces, axis=-1).reshape(frames * pixels, 3 * channels)


def temporal_fold(grads, frames, pixels, channels):
    parts = grads.reshape(frames, pixels, 3, channels)
    padded = jnp.zeros((frames + 2, pixels, channels), jnp.float32)
    for tap in range(3):
        padded = padded.at[tap : tap + frames].add(parts[:, :, tap, :])
    return padded[1 : frames + 1]


def section_forward(block_in, embedding, spatial, temporal):
    frames, pixels, channels = block_in.shape
    summed = block_in.astype(jnp.float32) + embedding
    normed = normalize(summed).astype(jnp.bfloat16)
    preact = jnp.dot(spatial_columns(normed), spatial, preferred_element_type=jnp.float32)
    activated = jax.nn.silu(preact).astype(jnp.bfloat16).reshape(frames, pixels, channels)
    mixed = jnp.dot(temporal_columns(activated), temporal, preferred_element_type=jnp.float32)
    return (block_in.astype(jnp.float32) + mixed.reshape(frames, pixels, channels)).astype(
        jnp.bfloat16
    )


def backward_first(block_in, embedding, spatial, temporal, upstream):
    frames, pixels, channels = block_in.shape
    summed = block_in.astype(jnp.float32) + embedding
    normed = normalize(summed).astype(jnp.bfloat16)
    columns = spatial_columns(normed)
    preact = jnp.dot(columns, spatial, preferred_element_type=jnp.float32)
    activated = jax.nn.silu(preact).astype(jnp.bfloat16).reshape(frames, pixels, channels)
    tcolumns = temporal_columns(activated)
    upstream_flat = upstream.reshape(frames * pixels, channels)
    temporal_term = jnp.dot(tcolumns.T, upstream_flat, preferred_element_type=jnp.float32)
    act_grad = temporal_fold(
        jnp.dot(upstream_flat, temporal.T, preferred_element_type=jnp.float32),
        frames,
        pixels,
        channels,
    )
    logistic = jax.nn.sigmoid(preact)
    slope = logistic * (1.0 + preact * (1.0 - logistic))
    pre_grad = (act_grad.reshape(frames * pixels, channels) * slope).astype(jnp.bfloat16)
    return (temporal_term, pre_grad, columns)


def backward_second(block_in, embedding, spatial, upstream, pre_grad, columns):
    frames, pixels, channels = block_in.shape
    summed = block_in.astype(jnp.float32) + embedding
    spatial_term = jnp.dot(columns.T, pre_grad, preferred_element_type=jnp.float32)
    norm_grad = spatial_fold(
        jnp.dot(pre_grad, spatial.T, preferred_element_type=jnp.float32), frames, channels
    )
    _, pullback = jax.vjp(normalize, summed)
    back_input = (upstream.astype(jnp.float32) + pullback(norm_grad)[0]).astype(jnp.bfloat16)
    return (back_input, spatial_term)


def section_backward(block_in, embedding, spatial, temporal, upstream):
    temporal_term, pre_grad, columns = backward_first(
        block_in, embedding, spatial, temporal, upstream
    )
    back_input, spatial_term = backward_second(
        block_in, embedding, spatial, upstream, pre_grad, columns
    )
    return (back_input, spatial_term, temporal_term)


def per_device(samples, timesteps, cotangent, spatial_weight, temporal_weight):
    sections = lax.axis_size("pipe")
    section_index = lax.axis_index("pipe")
    micro_count = samples.shape[0]
    frames, pixels, channels = (samples.shape[1], samples.shape[2], samples.shape[3])
    moments = jnp.arange(micro_count + sections - 1, dtype=jnp.int32)
    blank = jnp.zeros((frames, pixels, channels), jnp.bfloat16)
    full_spatial, full_temporal = (
        lax.all_gather(spatial_weight[0], "dp", axis=0, tiled=True),
        lax.all_gather(temporal_weight[0], "dp", axis=0, tiled=True),
    )

    def forward_step(carry, moment):
        incoming, stash = carry
        position = moment - section_index
        active = (position >= 0) & (position < micro_count)
        picked = jnp.clip(position, 0, micro_count - 1)
        own = lax.dynamic_index_in_dim(samples, picked, 0, keepdims=False)
        embedding = embedding_of(
            lax.dynamic_index_in_dim(timesteps, picked, 0, keepdims=False), channels
        )
        block_in = jnp.where(section_index == 0, own, incoming)
        result = lax.cond(
            active & (section_index < sections - 1),
            lambda: section_forward(block_in, embedding, full_spatial, full_temporal),
            lambda: blank,
        )
        stash = jnp.where(
            active, lax.dynamic_update_index_in_dim(stash, block_in, picked, 0), stash
        )
        passed = passed_along(result, "pipe", 1)
        return ((passed, stash), None)

    (_, stash), _ = lax.scan(forward_step, (blank, jnp.zeros_like(samples)), moments)
    back_spatial, back_temporal = (full_spatial, full_temporal)

    def inputs_at(moment, incoming):
        position = moment - (sections - 1 - section_index)
        active = (position >= 0) & (position < micro_count)
        picked = jnp.clip(position, 0, micro_count - 1)
        block_in = lax.dynamic_index_in_dim(stash, picked, 0, keepdims=False)
        embedding = embedding_of(
            lax.dynamic_index_in_dim(timesteps, picked, 0, keepdims=False), channels
        )
        given = lax.dynamic_index_in_dim(cotangent, picked, 0, keepdims=False)
        upstream = jnp.where(section_index == sections - 1, given, incoming)
        return (active, block_in, embedding, upstream)

    def backward_step(carry, moment):
        incoming, grad_spatial, grad_temporal = carry
        active, block_in, embedding, upstream = inputs_at(moment, incoming)

        def working():
            back_input, spatial_term, temporal_term = section_backward(
                block_in, embedding, back_spatial, back_temporal, upstream
            )
            return (back_input, grad_spatial + spatial_term, grad_temporal + temporal_term)

        def waiting():
            return (blank, grad_spatial, grad_temporal)

        back_input, grad_spatial, grad_temporal = lax.cond(active, working, waiting)
        passed = passed_along(back_input, "pipe", -1)
        return ((passed, grad_spatial, grad_temporal), None)

    start = (
        blank,
        jnp.zeros(back_spatial.shape, jnp.float32),
        jnp.zeros(back_temporal.shape, jnp.float32),
    )
    (_, grad_spatial, grad_temporal), _ = lax.scan(backward_step, start, moments)
    share_spatial, share_temporal = (
        lax.psum_scatter(
            grad_spatial.astype(jnp.bfloat16).astype(jnp.float32).astype(jnp.bfloat16),
            "dp",
            scatter_dimension=0,
            tiled=True,
        ).astype(jnp.float32),
        lax.psum_scatter(
            grad_temporal.astype(jnp.bfloat16).astype(jnp.float32).astype(jnp.bfloat16),
            "dp",
            scatter_dimension=0,
            tiled=True,
        ).astype(jnp.float32),
    )
    return (share_spatial[None], share_temporal[None])


SPAN = 40
CUTS = (24, 16)
PIECE = 64


def coordinates():
    index = lax.axis_index("dp")
    return index // (GRID[1] * GRID[2]), (index // GRID[2]) % GRID[1], index % GRID[2]


def shifted(value, dz=0, dy=0, dc=0):
    pairs = []
    for z in range(GRID[0]):
        for y in range(GRID[1]):
            for c in range(GRID[2]):
                place = ((z + dz) % GRID[0], (y + dy) % GRID[1], (c + dc) % GRID[2])
                pairs.append(
                    (
                        (z * GRID[1] + y) * GRID[2] + c,
                        (place[0] * GRID[1] + place[1]) * GRID[2] + place[2],
                    )
                )
    return lax.ppermute(value, "dp", pairs)


def swapped(value):
    return lax.ppermute(value, "pipe", [(0, 1), (1, 0)])


def part_of(value, index, axis):
    return lax.dynamic_index_in_dim(value, index, axis, keepdims=False)


def vmem_call(body, outs, scratch=(), flops=0, moved=0):
    return pl.pallas_call(
        body,
        out_shape=outs,
        scratch_shapes=list(scratch),
        compiler_params=pltpu.CompilerParams(vmem_limit_bytes=24 * 2**20),
        cost_estimate=pl.CostEstimate(
            flops=5 * flops // 2, bytes_accessed=moved, transcendentals=0
        ),
    )


def after(value, earlier):
    return value if earlier is None else lax.optimization_barrier((value, earlier))[0]


def in_order(swap, own, other, axis):
    return jnp.where(
        swap, jnp.concatenate([other, own], axis), jnp.concatenate([own, other], axis)
    )


def over_z(value, pairs):
    moves = []
    for source, target in pairs:
        for rest in range(GRID[1] * GRID[2]):
            moves.append(tuple(z * GRID[1] * GRID[2] + rest for z in (source, target)))
    return lax.ppermute(value, "dp", moves)


def sent_over_z(value):
    return [shifted(value, dz=step) for step in range(1, GRID[0])]


def sent_on_chip(value, pieces=1):
    if pieces == 1:
        return shifted(value, dc=1)
    flat = value.reshape(-1, *value.shape[-2:])
    sent = [shifted(piece, dc=1) for piece in jnp.split(flat, pieces)]
    return jnp.concatenate(sent).reshape(value.shape)


def places_of(channels, main):
    channel = jnp.arange(channels)
    span, inside = channel // SPAN, channel % SPAN
    odd = span % 2
    cut = jnp.where(odd == 0, CUTS[0], CUTS[1])
    second = (inside >= cut).astype(jnp.int32)
    before = span // 2 * SPAN + odd * jnp.where(second == 0, CUTS[0], CUTS[1])
    rank = before + inside - second * cut
    tail = channels // 2 - main
    return jnp.where(
        rank < main, second * main + rank, (1 + second) * main + second * (tail - main) + rank
    )


def spans_of(rows, odd):
    sets = ([], [])
    for index, start in enumerate(range(0, rows, SPAN)):
        cut = start + CUTS[(index + odd) % 2]
        sets[0].append((start, cut))
        sets[1].append((cut, start + SPAN))
    return sets


def sets_of(value):
    _, _, c = coordinates()
    results = []
    for which in range(2):
        by_core = []
        for odd in range(2):
            spans = spans_of(value.shape[0], odd)[which]
            taken = jnp.concatenate([value[start:end] for start, end in spans])
            by_core.append(jnp.pad(taken, ((0, PIECE - taken.shape[0]), (0, 0))))
        results.append(jnp.where(c == 0, by_core[0], by_core[1]))
    return results


def shard_of(own, given, rows):
    _, _, c = coordinates()
    by_core = []
    for odd in range(2):
        taken, pieces = [0, 0], []
        for spans in zip(*spans_of(rows, odd)):
            for which, (start, end) in enumerate(spans):
                source = (own, given)[which]
                pieces.append(source[taken[which] : taken[which] + end - start])
                taken[which] += end - start
        by_core.append(jnp.concatenate(pieces))
    return jnp.where(c == 0, by_core[0], by_core[1])


def compact(pieces, own):
    short = 3 * SPAN - PIECE
    low, high = pieces[:, 0], pieces[:, 1]
    both = jnp.where(
        own,
        jnp.concatenate([low, high[:, :short]], 1),
        jnp.concatenate([low[:, :short], high], 1),
    )
    return both.reshape(-1, pieces.shape[3])


def spread(rows, chips, own):
    rows = rows.reshape(chips, -1, rows.shape[1])
    short = rows.shape[1] - PIECE
    pad = ((0, 0), (0, PIECE - short), (0, 0))
    return jnp.where(
        own,
        jnp.stack([rows[:, :PIECE], jnp.pad(rows[:, PIECE:], pad)], 1),
        jnp.stack([jnp.pad(rows[:, :short], pad), rows[:, short:]], 1),
    )


def gathered_over_z(value, earlier=None):
    z, _, _ = coordinates()
    value = after(value, earlier)
    sent = sent_over_z(value)
    return (
        jnp.stack([lax.select_n((z - place) % GRID[0], value, *sent) for place in range(GRID[0])]),
        sent,
    )


def sent_over_y(line, earlier=None):
    return shifted(after(line, earlier), dy=1)


def joined_over_y(line, sent):
    _, y, _ = coordinates()
    return in_order(y == 1, line[:, None], sent[:, None], 1)


def gathered_on_chip(plane, earlier=None):
    _, _, c = coordinates()
    plane = after(plane, earlier)
    whole = in_order(c == 1, plane[:, :, None], sent_on_chip(plane)[:, :, None], 2)
    return whole.reshape(-1, plane.shape[3])


def added(*terms):
    return sum(term.astype(F32) for term in terms)


def summed_on_chip(value, pieces=1):
    _, _, c = coordinates()
    sent = sent_on_chip(part_of(value, 1 - c, 2), pieces)
    return added(part_of(value, c, 2), sent).astype(BF16)


def summed_over_y(value, earlier):
    _, y, _ = coordinates()
    sent = shifted(after(part_of(value, 1 - y, 1), earlier), dy=1)
    return added(part_of(value, y, 1), sent).astype(BF16), sent


def sent_for_sums(line, earlier=None):
    z, _, _ = coordinates()
    line = after(line, earlier)
    return [
        shifted(part_of(line, (z + step) % GRID[0], 0), dz=step) for step in range(1, GRID[0])
    ]


def summed_over_z(line, earlier=None):
    z, _, _ = coordinates()
    sent = sent_for_sums(line, earlier)
    return added(part_of(line, z, 0), *sent), sent


def pixel_masks(rows):
    row = lax.broadcasted_iota(jnp.int32, (rows, 1), 0)
    high, wide = (row // WIDTH) % HEIGHT, row % WIDTH
    masks = []
    for dr in (-1, 0, 1):
        for dc in (-1, 0, 1):
            inside = (high + dr >= 0) & (high + dr < HEIGHT) & (wide + dc >= 0) & (wide + dc < WIDTH)
            masks.append((dr * WIDTH + dc, inside))
    return masks


def frame_masks(rows, frames):
    pixels = HEIGHT * WIDTH
    row = lax.broadcasted_iota(jnp.int32, (rows, 1), 0)
    frame = (row // pixels) % frames
    return [
        (step * pixels, (frame + step >= 0) & (frame + step < frames)) for step in (-1, 0, 1)
    ]


def moved_rows(value, move):
    shift, inside = move
    if shift:
        value = pltpu.roll(value, (-shift) % value.shape[0], 0)
    return jnp.where(inside, value, 0.0)


def dot(left, right, dims=((1,), (0,))):
    return lax.dot_general(left, right, (dims, ((), ())), preferred_element_type=F32)


def with_embedding(hidden, embedding_ref, samples):
    per = hidden.shape[0] // samples
    return jnp.concatenate(
        [hidden[s * per : (s + 1) * per] + embedding_ref[s : s + 1, :] for s in range(samples)]
    )


def scale_of(summed):
    return lax.rsqrt(jnp.mean(summed * summed, axis=-1, keepdims=True) + 1e-06)


def silu_parts(preact):
    logistic = 1.0 / (1.0 + jnp.exp(-preact))
    return logistic, preact * logistic


def convolved(normed, weight_refs, masks):
    rows, channels = normed.shape
    normed = normed.astype(F32)
    totals = [None] * len(weight_refs)
    for tap in range(9):
        moved = moved_rows(normed, masks[tap]).astype(BF16)
        for index, ref in enumerate(weight_refs):
            term = dot(moved, ref[tap * channels : (tap + 1) * channels, :])
            totals[index] = term if totals[index] is None else totals[index] + term
    return jnp.concatenate(totals, 1)


def back_through(pre_grad, weight_refs, masks, channels):
    pre_grad = pre_grad.astype(F32)
    total = None
    for tap in range(9):
        weights = [ref[tap * channels : (tap + 1) * channels, :] for ref in weight_refs]
        term = dot(
            moved_rows(pre_grad, masks[8 - tap]).astype(BF16),
            jnp.concatenate(weights, 1),
            ((1,), (1,)),
        )
        total = term if total is None else total + term
    return total


def tap_rows(temporal_ref, tap, width):
    tail = PIECE
    start = tap * (width - tail)
    rows = temporal_ref[start : start + width - tail, :]
    return jnp.concatenate([rows, rows[width - 2 * tail :]], 0)


def first_forward(frames, hidden_ref, embedding_ref, keep_ref, temporal_ref, *refs):
    *spatial_refs, normed_ref, preact_ref, mixed_ref = refs
    rows = hidden_ref.shape[0]
    width = keep_ref.shape[1]
    summed = with_embedding(hidden_ref[...].astype(F32), embedding_ref, embedding_ref.shape[0])
    normed = (summed * scale_of(summed)).astype(BF16)
    normed_ref[...] = normed
    preact = convolved(normed, spatial_refs, pixel_masks(rows))
    preact_ref[...] = preact
    activated = silu_parts(preact)[1].astype(BF16).astype(F32) * keep_ref[...]
    mixed = None
    for tap, move in enumerate(frame_masks(rows, frames)):
        term = dot(
            moved_rows(activated, move).astype(BF16),
            tap_rows(temporal_ref, tap, width),
        )
        mixed = term if mixed is None else mixed + term
    mixed_ref[...] = mixed.astype(BF16)


def slope_of(preact):
    logistic, _ = silu_parts(preact)
    return logistic * (1.0 + preact * (1.0 - logistic))


def act_grad_of(upstream, temporal_ref, width, frames):
    upstream = upstream.astype(F32)
    moves = frame_masks(upstream.shape[0], frames)
    total = None
    for tap in range(3):
        term = dot(
            moved_rows(upstream, moves[2 - tap]).astype(BF16),
            tap_rows(temporal_ref, tap, width),
            ((1,), (1,)),
        )
        total = term if total is None else total + term
    return total


def store_temporal_terms(activated, upstream, frames, out_ref):
    width = activated.shape[1]
    tail = PIECE
    upstream = upstream.astype(F32)
    moves = frame_masks(upstream.shape[0], frames)
    for tap in range(3):
        term = dot(activated, moved_rows(upstream, moves[2 - tap]).astype(BF16), ((0,), (0,)))
        start = tap * (width - tail)
        out_ref[start : start + width - 2 * tail, :] = term[: width - 2 * tail].astype(BF16)
        out_ref[start + width - 2 * tail : start + width - tail, :] = (
            term[width - 2 * tail : width - tail] + term[width - tail :]
        ).astype(BF16)


def store_spatial_terms(normed, pre_grad, out_refs):
    channels = normed.shape[1]
    pre_grad = pre_grad.astype(F32)
    masks = pixel_masks(pre_grad.shape[0])
    for tap in range(9):
        term = dot(
            normed, moved_rows(pre_grad, masks[8 - tap]).astype(BF16), ((0,), (0,))
        ).astype(BF16)
        start = 0
        for out_ref in out_refs:
            end = start + out_ref.shape[1]
            out_ref[tap * channels : (tap + 1) * channels, :] = term[:, start:end]
            start = end


def second_forward(
    frames, hidden_ref, own_ref, sent_ref, embedding_ref, keep_ref, upstream_ref, temporal_ref, *refs
):
    *spatial_refs, next_ref, normed_ref, activated_ref, pre_grad_ref, back_ref = refs
    rows, channels = hidden_ref.shape
    width = keep_ref.shape[1]
    masks = pixel_masks(rows)
    mixed = own_ref[...].astype(F32) + sent_ref[...].astype(F32)
    hidden = (hidden_ref[...].astype(F32) + mixed).astype(BF16)
    next_ref[...] = hidden
    summed = with_embedding(hidden.astype(F32), embedding_ref, embedding_ref.shape[0])
    normed = (summed * scale_of(summed)).astype(BF16)
    normed_ref[...] = normed
    preact = convolved(normed, spatial_refs, masks)
    activated_ref[...] = (silu_parts(preact)[1] * keep_ref[...]).astype(BF16)
    act_grad = act_grad_of(upstream_ref[...], temporal_ref, width, frames)
    pre_grad = (act_grad * slope_of(preact) * keep_ref[...]).astype(BF16)
    pre_grad_ref[...] = pre_grad
    back = back_through(pre_grad, spatial_refs, masks, channels)
    back_ref[...] = back.astype(BF16)


def second_terms(frames, normed_ref, pre_grad_ref, activated_ref, upstream_ref, *outs):
    *spatial_refs, temporal_ref = outs
    store_spatial_terms(normed_ref[...], pre_grad_ref[...], spatial_refs)
    store_temporal_terms(activated_ref[...], upstream_ref[...], frames, temporal_ref)


def first_terms(
    frames, hidden_ref, embedding_ref, upstream_ref, own_ref, sent_ref, normed_ref, preact_ref,
    keep_ref, temporal_ref, *outs
):
    *spatial_outs, temporal_out = outs
    width = keep_ref.shape[1]
    channels = hidden_ref.shape[1]
    summed = with_embedding(hidden_ref[...].astype(F32), embedding_ref, embedding_ref.shape[0])
    scale = scale_of(summed)
    grad = own_ref[...].astype(F32) + sent_ref[...].astype(F32)
    inner = jnp.sum(grad * summed, axis=-1, keepdims=True)
    back = grad * scale - summed * (scale * scale * scale) * (inner / channels)
    upstream = (upstream_ref[...].astype(F32) + back).astype(BF16)
    preact = preact_ref[...]
    activated = (silu_parts(preact)[1] * keep_ref[...]).astype(BF16)
    act_grad = act_grad_of(upstream, temporal_ref, width, frames)
    pre_grad = (act_grad * slope_of(preact) * keep_ref[...]).astype(BF16)
    store_spatial_terms(normed_ref[...], pre_grad, spatial_outs)
    store_temporal_terms(activated, upstream, frames, temporal_out)


def paired_device(samples, timesteps, cotangent, spatial_weight, temporal_weight):
    me = lax.axis_index("pipe")
    first = me == 0
    count, frames, pixels, channels = samples.shape
    rows = count * frames * pixels
    main = 2 * LANES
    width = main + LANES
    hidden = samples.reshape(rows, channels)
    upstream = cotangent.reshape(rows, channels)
    embedding = jax.vmap(lambda step: embedding_of(step, channels))(timesteps)
    lane = jnp.arange(LANES)
    keep_own = jnp.concatenate([jnp.ones(main), lane < LANES // 2]).astype(F32)[None]
    keep_other = jnp.concatenate([jnp.ones(main), lane >= LANES // 2]).astype(F32)[None]
    keep_first = jnp.where(first, keep_own, keep_other)
    keep_second = jnp.where(first, keep_other, keep_own)
    tail = lane[None] < LANES // 2

    places = places_of(channels, main)
    order = (places[:, None] == jnp.arange(channels)).astype(BF16)
    temporal_own, temporal_sent = sets_of(temporal_weight[0])
    temporal_given = swapped(temporal_sent)
    line_temporal, sent = gathered_over_z(in_order(me == 1, temporal_own, temporal_given, 0))
    side_temporal = sent_over_y(line_temporal)
    spatial_own = dot(spatial_weight[0], order).astype(BF16)
    given = swapped(spatial_own[:, main:])
    main_own, main_given = spatial_own[:, :main], given[:, :main]
    tails = jnp.where(tail, spatial_own[:, 2 * main :], given[:, main:])
    line, sent = gathered_over_z(jnp.where(first, main_own, main_given), sent)
    line_tails, sent = gathered_over_z(tails, (sent, side_temporal))
    side_low = sent_over_y(line[..., :LANES])
    side_high = sent_over_y(line[..., LANES:], side_low)
    side_tails = sent_over_y(line_tails)
    line_second, sent = gathered_over_z(
        jnp.where(first, main_given, main_own), (sent, side_low)
    )
    side_first = jnp.concatenate([side_low, after(side_high, sent)], 2)
    plane_first = joined_over_y(line, side_first)
    plane_tails = joined_over_y(line_tails, after(side_tails, sent))
    plane_temporal = joined_over_y(line_temporal, side_temporal)
    side_second = sent_over_y(line_second)

    chips = GRID[0] * GRID[1]
    temporal = gathered_on_chip(plane_temporal).reshape(chips, GRID[2], 2, PIECE, channels)
    temporal_first = compact(temporal[:, :, 0], first)
    temporal_second = compact(temporal[:, :, 1], me == 1)
    tails = gathered_on_chip(plane_tails)
    spatial_first = [gathered_on_chip(plane_first), tails]

    def shape(extent, dtype=BF16):
        return jax.ShapeDtypeStruct(extent, dtype)

    spatial_flops = 2 * rows * 9 * channels * width
    temporal_flops = 2 * rows * 3 * channels * width
    spatial_bytes = 2 * 9 * channels * width
    temporal_bytes = 2 * 3 * channels * width
    normed_first, preact_first, mixed = vmem_call(
        functools.partial(first_forward, frames),
        (shape((rows, channels)), shape((rows, width), F32), shape((rows, channels))),
        flops=spatial_flops + temporal_flops,
        moved=spatial_bytes + temporal_bytes,
    )(hidden, embedding, keep_first, temporal_first, *spatial_first)
    mixed_given = swapped(mixed)
    plane_second = joined_over_y(line_second, after(side_second, mixed))
    spatial_second = [gathered_on_chip(plane_second), tails]
    hidden_second, normed_second, activated_second, pre_grad_second, back = vmem_call(
        functools.partial(second_forward, frames),
        (
            shape((rows, channels)),
            shape((rows, channels)),
            shape((rows, width)),
            shape((rows, width)),
            shape((rows, channels)),
        ),
        flops=2 * spatial_flops + temporal_flops,
        moved=spatial_bytes + temporal_bytes,
    )(
        hidden, mixed, mixed_given, embedding, keep_second, upstream, temporal_second,
        *spatial_second,
    )

    def terms_shape():
        return (
            shape((9 * channels, main)),
            shape((9 * channels, width - main)),
            shape((3 * (width - PIECE), channels)),
        )

    def on_chip(terms, pieces=1):
        return summed_on_chip(terms.reshape(*GRID, -1, terms.shape[1]), pieces)

    back_given = swapped(back)
    main_terms_second, tail_terms_second, temporal_terms_second = vmem_call(
        functools.partial(second_terms, frames),
        terms_shape(),
        flops=spatial_flops + temporal_flops,
        moved=spatial_bytes + temporal_bytes,
    )(normed_second, pre_grad_second, activated_second, upstream)
    chip_second = on_chip(main_terms_second, GRID[0])
    back_given = after(back_given, chip_second)
    line, side = summed_over_y(chip_second, None)
    share_second, sent_second = summed_over_z(line)
    main_terms_first, tail_terms_first, temporal_terms_first = vmem_call(
        functools.partial(first_terms, frames),
        terms_shape(),
        flops=spatial_flops + 2 * temporal_flops,
        moved=spatial_bytes + 2 * temporal_bytes,
    )(
        hidden_second, embedding, upstream, back, back_given, normed_first, preact_first,
        keep_first, temporal_first,
    )
    chip_tails = on_chip(tail_terms_first + tail_terms_second)
    chip_first = on_chip(after(main_terms_first, side))
    terms = jnp.concatenate(
        [
            spread(temporal_terms_first, chips, first),
            spread(temporal_terms_second, chips, me == 1),
        ],
        2,
    )
    chip_temporal = summed_on_chip(terms.reshape(*GRID, -1, channels))

    line, side = summed_over_y(chip_tails, side)
    line_low, side = summed_over_y(chip_first[..., :LANES], side)
    share_tails, sent_tails = summed_over_z(line, (side, sent_second))
    line_high, side = summed_over_y(chip_first[..., LANES:], side)
    share_first, sent_first = summed_over_z(
        jnp.concatenate([line_low, line_high], 2), sent_tails
    )
    line, side = summed_over_y(chip_temporal, side)
    share_temporal, _ = summed_over_z(line, sent_first)

    kept = jnp.where(first, share_first, share_second)
    passed = jnp.where(first, share_second, share_first)
    given = jnp.concatenate([passed, share_tails], 1).astype(BF16)
    given = swapped(after(given, side)).astype(F32)
    share_spatial = jnp.concatenate(
        [kept, given[:, :main], jnp.where(tail, share_tails, given[:, main:])], 1
    )
    share_spatial = lax.dot_general(
        share_spatial, order.astype(F32), (((1,), (1,)), ((), ())), precision=lax.Precision.HIGH
    )
    low, high = share_temporal[:PIECE], share_temporal[PIECE:]
    given = swapped(after(jnp.where(first, high, low).astype(BF16), share_spatial)).astype(F32)
    share_temporal = shard_of(jnp.where(first, low, high), given, temporal_weight.shape[1])
    return (share_spatial[None], share_temporal[None])


def solution(mesh):
    paired = mesh.shape["pipe"] == 2 and mesh.shape["dp"] == math.prod(GRID)
    return jax.shard_map(
        paired_device if paired else per_device,
        mesh=mesh,
        in_specs=(
            P("dp", None, None, None),
            P("dp"),
            P("dp", None, None, None),
            P("pipe", "dp", None),
            P("pipe", "dp", None),
        ),
        out_specs=(P("pipe", "dp", None), P("pipe", "dp", None)),
        check_vma=False,
    )
```

```python
import functools
import math

import jax
import jax.numpy as jnp
from jax import lax
from jax.experimental import pallas as pl
from jax.experimental.pallas import tpu as pltpu
from jax.sharding import PartitionSpec as P

HEIGHT = 8
WIDTH = 4
F32 = jnp.float32
BF16 = jnp.bfloat16
GRID = (4, 2, 2)
LANES = 128


def passed_along(value, axis, steps):
    count = lax.axis_size(axis)
    first, last = (max(0, -steps), min(count, count - steps))
    return lax.ppermute(value, axis, [(source, source + steps) for source in range(first, last)])


def embedding_of(step, channels):
    half_width = channels // 2
    frequency = jnp.exp(-math.log(10000.0) * jnp.arange(half_width, dtype=jnp.float32) / half_width)
    phases = step.astype(jnp.float32) * frequency
    return jnp.concatenate([jnp.sin(phases), jnp.cos(phases)])


def normalize(summed):
    return summed * lax.rsqrt(jnp.mean(summed * summed, axis=-1, keepdims=True) + 1e-06)


def spatial_columns(normed):
    frames, pixels, channels = normed.shape
    grid = normed.reshape(frames, HEIGHT, WIDTH, channels)
    padded = jnp.pad(grid, ((0, 0), (1, 1), (1, 1), (0, 0)))
    pieces = [
        padded[:, row : row + HEIGHT, col : col + WIDTH, :] for row in range(3) for col in range(3)
    ]
    return jnp.concatenate(pieces, axis=-1).reshape(frames * pixels, 9 * channels)


def spatial_fold(grads, frames, channels):
    parts = grads.reshape(frames, HEIGHT, WIDTH, 9, channels)
    padded = jnp.zeros((frames, HEIGHT + 2, WIDTH + 2, channels), jnp.float32)
    for row in range(3):
        for col in range(3):
            padded = padded.at[:, row : row + HEIGHT, col : col + WIDTH, :].add(
                parts[:, :, :, row * 3 + col, :]
            )
    return padded[:, 1 : HEIGHT + 1, 1 : WIDTH + 1, :].reshape(frames, HEIGHT * WIDTH, channels)


def temporal_columns(activated):
    frames, pixels, channels = activated.shape
    padded = jnp.pad(activated, ((1, 1), (0, 0), (0, 0)))
    pieces = [padded[tap : tap + frames] for tap in range(3)]
    return jnp.concatenate(pieces, axis=-1).reshape(frames * pixels, 3 * channels)


def temporal_fold(grads, frames, pixels, channels):
    parts = grads.reshape(frames, pixels, 3, channels)
    padded = jnp.zeros((frames + 2, pixels, channels), jnp.float32)
    for tap in range(3):
        padded = padded.at[tap : tap + frames].add(parts[:, :, tap, :])
    return padded[1 : frames + 1]


def section_forward(block_in, embedding, spatial, temporal):
    frames, pixels, channels = block_in.shape
    summed = block_in.astype(jnp.float32) + embedding
    normed = normalize(summed).astype(jnp.bfloat16)
    preact = jnp.dot(spatial_columns(normed), spatial, preferred_element_type=jnp.float32)
    activated = jax.nn.silu(preact).astype(jnp.bfloat16).reshape(frames, pixels, channels)
    mixed = jnp.dot(temporal_columns(activated), temporal, preferred_element_type=jnp.float32)
    return (block_in.astype(jnp.float32) + mixed.reshape(frames, pixels, channels)).astype(
        jnp.bfloat16
    )


def backward_first(block_in, embedding, spatial, temporal, upstream):
    frames, pixels, channels = block_in.shape
    summed = block_in.astype(jnp.float32) + embedding
    normed = normalize(summed).astype(jnp.bfloat16)
    columns = spatial_columns(normed)
    preact = jnp.dot(columns, spatial, preferred_element_type=jnp.float32)
    activated = jax.nn.silu(preact).astype(jnp.bfloat16).reshape(frames, pixels, channels)
    tcolumns = temporal_columns(activated)
    upstream_flat = upstream.reshape(frames * pixels, channels)
    temporal_term = jnp.dot(tcolumns.T, upstream_flat, preferred_element_type=jnp.float32)
    act_grad = temporal_fold(
        jnp.dot(upstream_flat, temporal.T, preferred_element_type=jnp.float32),
        frames,
        pixels,
        channels,
    )
    logistic = jax.nn.sigmoid(preact)
    slope = logistic * (1.0 + preact * (1.0 - logistic))
    pre_grad = (act_grad.reshape(frames * pixels, channels) * slope).astype(jnp.bfloat16)
    return (temporal_term, pre_grad, columns)


def backward_second(block_in, embedding, spatial, upstream, pre_grad, columns):
    frames, pixels, channels = block_in.shape
    summed = block_in.astype(jnp.float32) + embedding
    spatial_term = jnp.dot(columns.T, pre_grad, preferred_element_type=jnp.float32)
    norm_grad = spatial_fold(
        jnp.dot(pre_grad, spatial.T, preferred_element_type=jnp.float32), frames, channels
    )
    _, pullback = jax.vjp(normalize, summed)
    back_input = (upstream.astype(jnp.float32) + pullback(norm_grad)[0]).astype(jnp.bfloat16)
    return (back_input, spatial_term)


def section_backward(block_in, embedding, spatial, temporal, upstream):
    temporal_term, pre_grad, columns = backward_first(
        block_in, embedding, spatial, temporal, upstream
    )
    back_input, spatial_term = backward_second(
        block_in, embedding, spatial, upstream, pre_grad, columns
    )
    return (back_input, spatial_term, temporal_term)


def per_device(samples, timesteps, cotangent, spatial_weight, temporal_weight):
    sections = lax.axis_size("pipe")
    section_index = lax.axis_index("pipe")
    micro_count = samples.shape[0]
    frames, pixels, channels = (samples.shape[1], samples.shape[2], samples.shape[3])
    moments = jnp.arange(micro_count + sections - 1, dtype=jnp.int32)
    blank = jnp.zeros((frames, pixels, channels), jnp.bfloat16)
    full_spatial, full_temporal = (
        lax.all_gather(spatial_weight[0], "dp", axis=0, tiled=True),
        lax.all_gather(temporal_weight[0], "dp", axis=0, tiled=True),
    )

    def forward_step(carry, moment):
        incoming, stash = carry
        position = moment - section_index
        active = (position >= 0) & (position < micro_count)
        picked = jnp.clip(position, 0, micro_count - 1)
        own = lax.dynamic_index_in_dim(samples, picked, 0, keepdims=False)
        embedding = embedding_of(
            lax.dynamic_index_in_dim(timesteps, picked, 0, keepdims=False), channels
        )
        block_in = jnp.where(section_index == 0, own, incoming)
        result = lax.cond(
            active & (section_index < sections - 1),
            lambda: section_forward(block_in, embedding, full_spatial, full_temporal),
            lambda: blank,
        )
        stash = jnp.where(
            active, lax.dynamic_update_index_in_dim(stash, block_in, picked, 0), stash
        )
        passed = passed_along(result, "pipe", 1)
        return ((passed, stash), None)

    (_, stash), _ = lax.scan(forward_step, (blank, jnp.zeros_like(samples)), moments)
    back_spatial, back_temporal = (full_spatial, full_temporal)

    def inputs_at(moment, incoming):
        position = moment - (sections - 1 - section_index)
        active = (position >= 0) & (position < micro_count)
        picked = jnp.clip(position, 0, micro_count - 1)
        block_in = lax.dynamic_index_in_dim(stash, picked, 0, keepdims=False)
        embedding = embedding_of(
            lax.dynamic_index_in_dim(timesteps, picked, 0, keepdims=False), channels
        )
        given = lax.dynamic_index_in_dim(cotangent, picked, 0, keepdims=False)
        upstream = jnp.where(section_index == sections - 1, given, incoming)
        return (active, block_in, embedding, upstream)

    def backward_step(carry, moment):
        incoming, grad_spatial, grad_temporal = carry
        active, block_in, embedding, upstream = inputs_at(moment, incoming)

        def working():
            back_input, spatial_term, temporal_term = section_backward(
                block_in, embedding, back_spatial, back_temporal, upstream
            )
            return (back_input, grad_spatial + spatial_term, grad_temporal + temporal_term)

        def waiting():
            return (blank, grad_spatial, grad_temporal)

        back_input, grad_spatial, grad_temporal = lax.cond(active, working, waiting)
        passed = passed_along(back_input, "pipe", -1)
        return ((passed, grad_spatial, grad_temporal), None)

    start = (
        blank,
        jnp.zeros(back_spatial.shape, jnp.float32),
        jnp.zeros(back_temporal.shape, jnp.float32),
    )
    (_, grad_spatial, grad_temporal), _ = lax.scan(backward_step, start, moments)
    share_spatial, share_temporal = (
        lax.psum_scatter(
            grad_spatial.astype(jnp.bfloat16).astype(jnp.float32).astype(jnp.bfloat16),
            "dp",
            scatter_dimension=0,
            tiled=True,
        ).astype(jnp.float32),
        lax.psum_scatter(
            grad_temporal.astype(jnp.bfloat16).astype(jnp.float32).astype(jnp.bfloat16),
            "dp",
            scatter_dimension=0,
            tiled=True,
        ).astype(jnp.float32),
    )
    return (share_spatial[None], share_temporal[None])


SPAN = 40
CUTS = (24, 16)
PIECE = 64


def coordinates():
    index = lax.axis_index("dp")
    return index // (GRID[1] * GRID[2]), (index // GRID[2]) % GRID[1], index % GRID[2]


def shifted(value, dz=0, dy=0, dc=0):
    pairs = []
    for z in range(GRID[0]):
        for y in range(GRID[1]):
            for c in range(GRID[2]):
                place = ((z + dz) % GRID[0], (y + dy) % GRID[1], (c + dc) % GRID[2])
                pairs.append(
                    (
                        (z * GRID[1] + y) * GRID[2] + c,
                        (place[0] * GRID[1] + place[1]) * GRID[2] + place[2],
                    )
                )
    return lax.ppermute(value, "dp", pairs)


def swapped(value):
    return lax.ppermute(value, "pipe", [(0, 1), (1, 0)])


def part_of(value, index, axis):
    return lax.dynamic_index_in_dim(value, index, axis, keepdims=False)


def vmem_call(body, outs, scratch=(), flops=0, moved=0):
    return pl.pallas_call(
        body,
        out_shape=outs,
        scratch_shapes=list(scratch),
        compiler_params=pltpu.CompilerParams(vmem_limit_bytes=24 * 2**20),
        cost_estimate=pl.CostEstimate(
            flops=5 * flops // 2, bytes_accessed=moved, transcendentals=0
        ),
    )


def after(value, earlier):
    return value if earlier is None else lax.optimization_barrier((value, earlier))[0]


def in_order(swap, own, other, axis):
    return jnp.where(
        swap, jnp.concatenate([other, own], axis), jnp.concatenate([own, other], axis)
    )


def over_z(value, pairs):
    moves = []
    for source, target in pairs:
        for rest in range(GRID[1] * GRID[2]):
            moves.append(tuple(z * GRID[1] * GRID[2] + rest for z in (source, target)))
    return lax.ppermute(value, "dp", moves)


def sent_over_z(value):
    return [shifted(value, dz=step) for step in range(1, GRID[0])]


def sent_on_chip(value, pieces=1):
    if pieces == 1:
        return shifted(value, dc=1)
    flat = value.reshape(-1, *value.shape[-2:])
    sent = [shifted(piece, dc=1) for piece in jnp.split(flat, pieces)]
    return jnp.concatenate(sent).reshape(value.shape)


def places_of(channels, main):
    channel = jnp.arange(channels)
    span, inside = channel // SPAN, channel % SPAN
    odd = span % 2
    cut = jnp.where(odd == 0, CUTS[0], CUTS[1])
    second = (inside >= cut).astype(jnp.int32)
    before = span // 2 * SPAN + odd * jnp.where(second == 0, CUTS[0], CUTS[1])
    rank = before + inside - second * cut
    tail = channels // 2 - main
    return jnp.where(
        rank < main, second * main + rank, (1 + second) * main + second * (tail - main) + rank
    )


def spans_of(rows, odd):
    sets = ([], [])
    for index, start in enumerate(range(0, rows, SPAN)):
        cut = start + CUTS[(index + odd) % 2]
        sets[0].append((start, cut))
        sets[1].append((cut, start + SPAN))
    return sets


def sets_of(value):
    _, _, c = coordinates()
    results = []
    for which in range(2):
        by_core = []
        for odd in range(2):
            spans = spans_of(value.shape[0], odd)[which]
            taken = jnp.concatenate([value[start:end] for start, end in spans])
            by_core.append(jnp.pad(taken, ((0, PIECE - taken.shape[0]), (0, 0))))
        results.append(jnp.where(c == 0, by_core[0], by_core[1]))
    return results


def shard_of(own, given, rows):
    _, _, c = coordinates()
    by_core = []
    for odd in range(2):
        taken, pieces = [0, 0], []
        for spans in zip(*spans_of(rows, odd)):
            for which, (start, end) in enumerate(spans):
                source = (own, given)[which]
                pieces.append(source[taken[which] : taken[which] + end - start])
                taken[which] += end - start
        by_core.append(jnp.concatenate(pieces))
    return jnp.where(c == 0, by_core[0], by_core[1])


def compact(pieces, own):
    short = 3 * SPAN - PIECE
    low, high = pieces[:, 0], pieces[:, 1]
    both = jnp.where(
        own,
        jnp.concatenate([low, high[:, :short]], 1),
        jnp.concatenate([low[:, :short], high], 1),
    )
    return both.reshape(-1, pieces.shape[3])


def spread(rows, chips, own):
    rows = rows.reshape(chips, -1, rows.shape[1])
    short = rows.shape[1] - PIECE
    pad = ((0, 0), (0, PIECE - short), (0, 0))
    return jnp.where(
        own,
        jnp.stack([rows[:, :PIECE], jnp.pad(rows[:, PIECE:], pad)], 1),
        jnp.stack([jnp.pad(rows[:, :short], pad), rows[:, short:]], 1),
    )


def gathered_over_z(value, earlier=None, beside=None):
    z, _, _ = coordinates()
    value = after(value, earlier)
    sent = after(sent_over_z(value), beside)
    return (
        jnp.stack([lax.select_n((z - place) % GRID[0], value, *sent) for place in range(GRID[0])]),
        sent,
    )


def sent_over_y(line, earlier=None):
    return shifted(after(line, earlier), dy=1)


def joined_over_y(line, sent):
    _, y, _ = coordinates()
    return in_order(y == 1, line[:, None], sent[:, None], 1)


def gathered_on_chip(plane, earlier=None):
    _, _, c = coordinates()
    plane = after(plane, earlier)
    whole = in_order(c == 1, plane[:, :, None], sent_on_chip(plane)[:, :, None], 2)
    return whole.reshape(-1, plane.shape[3])


def added(*terms):
    return sum(term.astype(F32) for term in terms)


def summed_on_chip(value, pieces=1):
    _, _, c = coordinates()
    sent = sent_on_chip(part_of(value, 1 - c, 2), pieces)
    return added(part_of(value, c, 2), sent).astype(BF16)


def summed_over_y(value, earlier):
    _, y, _ = coordinates()
    sent = shifted(after(part_of(value, 1 - y, 1), earlier), dy=1)
    return added(part_of(value, y, 1), sent).astype(BF16), sent


def sent_for_sums(line, earlier=None):
    z, _, _ = coordinates()
    line = after(line, earlier)
    return [
        shifted(part_of(line, (z + step) % GRID[0], 0), dz=step) for step in range(1, GRID[0])
    ]


def summed_over_z(line, earlier=None):
    z, _, _ = coordinates()
    sent = sent_for_sums(line, earlier)
    return added(part_of(line, z, 0), *sent), sent


def pixel_masks(rows):
    row = lax.broadcasted_iota(jnp.int32, (rows, 1), 0)
    high, wide = (row // WIDTH) % HEIGHT, row % WIDTH
    masks = []
    for dr in (-1, 0, 1):
        for dc in (-1, 0, 1):
            inside = (high + dr >= 0) & (high + dr < HEIGHT) & (wide + dc >= 0) & (wide + dc < WIDTH)
            masks.append((dr * WIDTH + dc, inside))
    return masks


def frame_masks(rows, frames):
    pixels = HEIGHT * WIDTH
    row = lax.broadcasted_iota(jnp.int32, (rows, 1), 0)
    frame = (row // pixels) % frames
    return [
        (step * pixels, (frame + step >= 0) & (frame + step < frames)) for step in (-1, 0, 1)
    ]


def moved_rows(value, move):
    shift, inside = move
    if shift:
        value = pltpu.roll(value, (-shift) % value.shape[0], 0)
    return jnp.where(inside, value, 0.0)


def dot(left, right, dims=((1,), (0,))):
    return lax.dot_general(left, right, (dims, ((), ())), preferred_element_type=F32)


def with_embedding(hidden, embedding_ref, samples):
    per = hidden.shape[0] // samples
    return jnp.concatenate(
        [hidden[s * per : (s + 1) * per] + embedding_ref[s : s + 1, :] for s in range(samples)]
    )


def scale_of(summed):
    return lax.rsqrt(jnp.mean(summed * summed, axis=-1, keepdims=True) + 1e-06)


def silu_parts(preact):
    logistic = 1.0 / (1.0 + jnp.exp(-preact))
    return logistic, preact * logistic


def convolved(normed, weight_refs, masks):
    rows, channels = normed.shape
    normed = normed.astype(F32)
    totals = [None] * len(weight_refs)
    for tap in range(9):
        moved = moved_rows(normed, masks[tap]).astype(BF16)
        for index, ref in enumerate(weight_refs):
            term = dot(moved, ref[tap * channels : (tap + 1) * channels, :])
            totals[index] = term if totals[index] is None else totals[index] + term
    return jnp.concatenate(totals, 1)


def back_through(pre_grad, weight_refs, masks, channels):
    pre_grad = pre_grad.astype(F32)
    total = None
    for tap in range(9):
        weights = [ref[tap * channels : (tap + 1) * channels, :] for ref in weight_refs]
        term = dot(
            moved_rows(pre_grad, masks[8 - tap]).astype(BF16),
            jnp.concatenate(weights, 1),
            ((1,), (1,)),
        )
        total = term if total is None else total + term
    return total


def tap_rows(temporal_ref, tap, width):
    tail = PIECE
    start = tap * (width - tail)
    rows = temporal_ref[start : start + width - tail, :]
    return jnp.concatenate([rows, rows[width - 2 * tail :]], 0)


def first_forward(frames, hidden_ref, embedding_ref, keep_ref, temporal_ref, *refs):
    *spatial_refs, normed_ref, preact_ref, mixed_ref = refs
    rows = hidden_ref.shape[0]
    width = keep_ref.shape[1]
    summed = with_embedding(hidden_ref[...].astype(F32), embedding_ref, embedding_ref.shape[0])
    normed = (summed * scale_of(summed)).astype(BF16)
    normed_ref[...] = normed
    preact = convolved(normed, spatial_refs, pixel_masks(rows))
    preact_ref[...] = preact
    activated = silu_parts(preact)[1].astype(BF16).astype(F32) * keep_ref[...]
    mixed = None
    for tap, move in enumerate(frame_masks(rows, frames)):
        term = dot(
            moved_rows(activated, move).astype(BF16),
            tap_rows(temporal_ref, tap, width),
        )
        mixed = term if mixed is None else mixed + term
    mixed_ref[...] = mixed.astype(BF16)


def slope_of(preact):
    logistic, _ = silu_parts(preact)
    return logistic * (1.0 + preact * (1.0 - logistic))


def act_grad_of(upstream, temporal_ref, width, frames):
    upstream = upstream.astype(F32)
    moves = frame_masks(upstream.shape[0], frames)
    total = None
    for tap in range(3):
        term = dot(
            moved_rows(upstream, moves[2 - tap]).astype(BF16),
            tap_rows(temporal_ref, tap, width),
            ((1,), (1,)),
        )
        total = term if total is None else total + term
    return total


def store_temporal_terms(activated, upstream, frames, out_ref):
    width = activated.shape[1]
    tail = PIECE
    upstream = upstream.astype(F32)
    moves = frame_masks(upstream.shape[0], frames)
    for tap in range(3):
        term = dot(activated, moved_rows(upstream, moves[2 - tap]).astype(BF16), ((0,), (0,)))
        start = tap * (width - tail)
        out_ref[start : start + width - 2 * tail, :] = term[: width - 2 * tail].astype(BF16)
        out_ref[start + width - 2 * tail : start + width - tail, :] = (
            term[width - 2 * tail : width - tail] + term[width - tail :]
        ).astype(BF16)


def store_spatial_terms(normed, pre_grad, out_refs):
    channels = normed.shape[1]
    pre_grad = pre_grad.astype(F32)
    masks = pixel_masks(pre_grad.shape[0])
    for tap in range(9):
        term = dot(
            normed, moved_rows(pre_grad, masks[8 - tap]).astype(BF16), ((0,), (0,))
        ).astype(BF16)
        start = 0
        for out_ref in out_refs:
            end = start + out_ref.shape[1]
            out_ref[tap * channels : (tap + 1) * channels, :] = term[:, start:end]
            start = end


def second_forward(
    frames, hidden_ref, own_ref, sent_ref, embedding_ref, keep_ref, upstream_ref, temporal_ref, *refs
):
    *spatial_refs, next_ref, normed_ref, activated_ref, pre_grad_ref, back_ref = refs
    rows, channels = hidden_ref.shape
    width = keep_ref.shape[1]
    masks = pixel_masks(rows)
    mixed = own_ref[...].astype(F32) + sent_ref[...].astype(F32)
    hidden = (hidden_ref[...].astype(F32) + mixed).astype(BF16)
    next_ref[...] = hidden
    summed = with_embedding(hidden.astype(F32), embedding_ref, embedding_ref.shape[0])
    normed = (summed * scale_of(summed)).astype(BF16)
    normed_ref[...] = normed
    preact = convolved(normed, spatial_refs, masks)
    activated_ref[...] = (silu_parts(preact)[1] * keep_ref[...]).astype(BF16)
    act_grad = act_grad_of(upstream_ref[...], temporal_ref, width, frames)
    pre_grad = (act_grad * slope_of(preact) * keep_ref[...]).astype(BF16)
    pre_grad_ref[...] = pre_grad
    back = back_through(pre_grad, spatial_refs, masks, channels)
    back_ref[...] = back.astype(BF16)


def second_terms(frames, normed_ref, pre_grad_ref, activated_ref, upstream_ref, *outs):
    *spatial_refs, temporal_ref = outs
    store_spatial_terms(normed_ref[...], pre_grad_ref[...], spatial_refs)
    store_temporal_terms(activated_ref[...], upstream_ref[...], frames, temporal_ref)


def first_terms(
    frames, hidden_ref, embedding_ref, upstream_ref, own_ref, sent_ref, normed_ref, preact_ref,
    keep_ref, temporal_ref, *outs
):
    *spatial_outs, temporal_out = outs
    width = keep_ref.shape[1]
    channels = hidden_ref.shape[1]
    summed = with_embedding(hidden_ref[...].astype(F32), embedding_ref, embedding_ref.shape[0])
    scale = scale_of(summed)
    grad = own_ref[...].astype(F32) + sent_ref[...].astype(F32)
    inner = jnp.sum(grad * summed, axis=-1, keepdims=True)
    back = grad * scale - summed * (scale * scale * scale) * (inner / channels)
    upstream = (upstream_ref[...].astype(F32) + back).astype(BF16)
    preact = preact_ref[...]
    activated = (silu_parts(preact)[1] * keep_ref[...]).astype(BF16)
    act_grad = act_grad_of(upstream, temporal_ref, width, frames)
    pre_grad = (act_grad * slope_of(preact) * keep_ref[...]).astype(BF16)
    store_spatial_terms(normed_ref[...], pre_grad, spatial_outs)
    store_temporal_terms(activated, upstream, frames, temporal_out)


def paired_device(samples, timesteps, cotangent, spatial_weight, temporal_weight):
    me = lax.axis_index("pipe")
    first = me == 0
    count, frames, pixels, channels = samples.shape
    rows = count * frames * pixels
    main = 2 * LANES
    width = main + LANES
    hidden = samples.reshape(rows, channels)
    upstream = cotangent.reshape(rows, channels)
    embedding = jax.vmap(lambda step: embedding_of(step, channels))(timesteps)
    lane = jnp.arange(LANES)
    keep_own = jnp.concatenate([jnp.ones(main), lane < LANES // 2]).astype(F32)[None]
    keep_other = jnp.concatenate([jnp.ones(main), lane >= LANES // 2]).astype(F32)[None]
    keep_first = jnp.where(first, keep_own, keep_other)
    keep_second = jnp.where(first, keep_other, keep_own)
    tail = lane[None] < LANES // 2

    places = places_of(channels, main)
    order = (places[:, None] == jnp.arange(channels)).astype(BF16)
    temporal_own, temporal_sent = sets_of(temporal_weight[0])
    temporal_given = swapped(temporal_sent)
    line_temporal, sent = gathered_over_z(in_order(me == 1, temporal_own, temporal_given, 0))
    side_temporal = sent_over_y(line_temporal)
    spatial_own = dot(spatial_weight[0], order).astype(BF16)
    given = swapped(spatial_own[:, main:])
    main_own, main_given = spatial_own[:, :main], given[:, :main]
    tails = jnp.where(tail, spatial_own[:, 2 * main :], given[:, main:])
    line, sent = gathered_over_z(jnp.where(first, main_own, main_given), sent, side_temporal)
    line_tails, sent = gathered_over_z(tails, sent)
    side_low = sent_over_y(line[..., :LANES])
    side_high = sent_over_y(line[..., LANES:], side_low)
    side_tails = sent_over_y(line_tails)
    line_second, sent = gathered_over_z(
        jnp.where(first, main_given, main_own), (sent, side_low)
    )
    side_first = jnp.concatenate([side_low, after(side_high, sent)], 2)
    plane_first = joined_over_y(line, side_first)
    plane_tails = joined_over_y(line_tails, after(side_tails, sent))
    plane_temporal = joined_over_y(line_temporal, side_temporal)
    side_second = sent_over_y(line_second)

    chips = GRID[0] * GRID[1]
    temporal = gathered_on_chip(plane_temporal).reshape(chips, GRID[2], 2, PIECE, channels)
    temporal_first = compact(temporal[:, :, 0], first)
    temporal_second = compact(temporal[:, :, 1], me == 1)
    tails = gathered_on_chip(plane_tails)
    spatial_first = [gathered_on_chip(plane_first), tails]

    def shape(extent, dtype=BF16):
        return jax.ShapeDtypeStruct(extent, dtype)

    spatial_flops = 2 * rows * 9 * channels * width
    temporal_flops = 2 * rows * 3 * channels * width
    spatial_bytes = 2 * 9 * channels * width
    temporal_bytes = 2 * 3 * channels * width
    normed_first, preact_first, mixed = vmem_call(
        functools.partial(first_forward, frames),
        (shape((rows, channels)), shape((rows, width), F32), shape((rows, channels))),
        flops=spatial_flops + temporal_flops,
        moved=spatial_bytes + temporal_bytes,
    )(hidden, embedding, keep_first, temporal_first, *spatial_first)
    mixed_given = swapped(mixed)
    plane_second = joined_over_y(line_second, after(side_second, mixed))
    spatial_second = [gathered_on_chip(plane_second), tails]
    hidden_second, normed_second, activated_second, pre_grad_second, back = vmem_call(
        functools.partial(second_forward, frames),
        (
            shape((rows, channels)),
            shape((rows, channels)),
            shape((rows, width)),
            shape((rows, width)),
            shape((rows, channels)),
        ),
        flops=2 * spatial_flops + temporal_flops,
        moved=spatial_bytes + temporal_bytes,
    )(
        hidden, mixed, mixed_given, embedding, keep_second, upstream, temporal_second,
        *spatial_second,
    )

    def terms_shape():
        return (
            shape((9 * channels, main)),
            shape((9 * channels, width - main)),
            shape((3 * (width - PIECE), channels)),
        )

    def on_chip(terms, pieces=1):
        return summed_on_chip(terms.reshape(*GRID, -1, terms.shape[1]), pieces)

    back_given = swapped(back)
    main_terms_second, tail_terms_second, temporal_terms_second = vmem_call(
        functools.partial(second_terms, frames),
        terms_shape(),
        flops=spatial_flops + temporal_flops,
        moved=spatial_bytes + temporal_bytes,
    )(normed_second, pre_grad_second, activated_second, upstream)
    chip_second = on_chip(main_terms_second, GRID[0])
    back_given = after(back_given, chip_second)
    line, side = summed_over_y(chip_second, None)
    share_second, sent_second = summed_over_z(line)
    main_terms_first, tail_terms_first, temporal_terms_first = vmem_call(
        functools.partial(first_terms, frames),
        terms_shape(),
        flops=spatial_flops + 2 * temporal_flops,
        moved=spatial_bytes + 2 * temporal_bytes,
    )(
        hidden_second, embedding, upstream, back, back_given, normed_first, preact_first,
        keep_first, temporal_first,
    )
    chip_tails = on_chip(tail_terms_first + tail_terms_second)
    chip_first = on_chip(after(main_terms_first, side))
    terms = jnp.concatenate(
        [
            spread(temporal_terms_first, chips, first),
            spread(temporal_terms_second, chips, me == 1),
        ],
        2,
    )
    chip_temporal = summed_on_chip(terms.reshape(*GRID, -1, channels))

    line, side = summed_over_y(chip_tails, side)
    line_low, side = summed_over_y(chip_first[..., :LANES], side)
    share_tails, sent_tails = summed_over_z(line, (side, sent_second))
    line_high, side = summed_over_y(chip_first[..., LANES:], side)
    share_first, sent_first = summed_over_z(
        jnp.concatenate([line_low, line_high], 2), sent_tails
    )
    line, side = summed_over_y(chip_temporal, side)
    share_temporal, _ = summed_over_z(line, sent_first)

    kept = jnp.where(first, share_first, share_second)
    passed = jnp.where(first, share_second, share_first)
    given = jnp.concatenate([passed, share_tails], 1).astype(BF16)
    given = swapped(after(given, side)).astype(F32)
    share_spatial = jnp.concatenate(
        [kept, given[:, :main], jnp.where(tail, share_tails, given[:, main:])], 1
    )
    share_spatial = lax.dot_general(
        share_spatial, order.astype(F32), (((1,), (1,)), ((), ())), precision=lax.Precision.HIGH
    )
    low, high = share_temporal[:PIECE], share_temporal[PIECE:]
    given = swapped(jnp.where(first, high, low).astype(BF16))
    given = after(given, share_spatial).astype(F32)
    share_temporal = shard_of(jnp.where(first, low, high), given, temporal_weight.shape[1])
    return (share_spatial[None], share_temporal[None])


def solution(mesh):
    paired = mesh.shape["pipe"] == 2 and mesh.shape["dp"] == math.prod(GRID)
    return jax.shard_map(
        paired_device if paired else per_device,
        mesh=mesh,
        in_specs=(
            P("dp", None, None, None),
            P("dp"),
            P("dp", None, None, None),
            P("pipe", "dp", None),
            P("pipe", "dp", None),
        ),
        out_specs=(P("pipe", "dp", None), P("pipe", "dp", None)),
        check_vma=False,
    )
```

```python
import functools
import math

import jax
import jax.numpy as jnp
from jax import lax
from jax.experimental import pallas as pl
from jax.experimental.pallas import tpu as pltpu
from jax.sharding import PartitionSpec as P

HEIGHT = 8
WIDTH = 4
F32 = jnp.float32
BF16 = jnp.bfloat16
GRID = (4, 2, 2)
LANES = 128


def passed_along(value, axis, steps):
    count = lax.axis_size(axis)
    first, last = (max(0, -steps), min(count, count - steps))
    return lax.ppermute(value, axis, [(source, source + steps) for source in range(first, last)])


def embedding_of(step, channels):
    half_width = channels // 2
    frequency = jnp.exp(-math.log(10000.0) * jnp.arange(half_width, dtype=jnp.float32) / half_width)
    phases = step.astype(jnp.float32) * frequency
    return jnp.concatenate([jnp.sin(phases), jnp.cos(phases)])


def normalize(summed):
    return summed * lax.rsqrt(jnp.mean(summed * summed, axis=-1, keepdims=True) + 1e-06)


def spatial_columns(normed):
    frames, pixels, channels = normed.shape
    grid = normed.reshape(frames, HEIGHT, WIDTH, channels)
    padded = jnp.pad(grid, ((0, 0), (1, 1), (1, 1), (0, 0)))
    pieces = [
        padded[:, row : row + HEIGHT, col : col + WIDTH, :] for row in range(3) for col in range(3)
    ]
    return jnp.concatenate(pieces, axis=-1).reshape(frames * pixels, 9 * channels)


def spatial_fold(grads, frames, channels):
    parts = grads.reshape(frames, HEIGHT, WIDTH, 9, channels)
    padded = jnp.zeros((frames, HEIGHT + 2, WIDTH + 2, channels), jnp.float32)
    for row in range(3):
        for col in range(3):
            padded = padded.at[:, row : row + HEIGHT, col : col + WIDTH, :].add(
                parts[:, :, :, row * 3 + col, :]
            )
    return padded[:, 1 : HEIGHT + 1, 1 : WIDTH + 1, :].reshape(frames, HEIGHT * WIDTH, channels)


def temporal_columns(activated):
    frames, pixels, channels = activated.shape
    padded = jnp.pad(activated, ((1, 1), (0, 0), (0, 0)))
    pieces = [padded[tap : tap + frames] for tap in range(3)]
    return jnp.concatenate(pieces, axis=-1).reshape(frames * pixels, 3 * channels)


def temporal_fold(grads, frames, pixels, channels):
    parts = grads.reshape(frames, pixels, 3, channels)
    padded = jnp.zeros((frames + 2, pixels, channels), jnp.float32)
    for tap in range(3):
        padded = padded.at[tap : tap + frames].add(parts[:, :, tap, :])
    return padded[1 : frames + 1]


def section_forward(block_in, embedding, spatial, temporal):
    frames, pixels, channels = block_in.shape
    summed = block_in.astype(jnp.float32) + embedding
    normed = normalize(summed).astype(jnp.bfloat16)
    preact = jnp.dot(spatial_columns(normed), spatial, preferred_element_type=jnp.float32)
    activated = jax.nn.silu(preact).astype(jnp.bfloat16).reshape(frames, pixels, channels)
    mixed = jnp.dot(temporal_columns(activated), temporal, preferred_element_type=jnp.float32)
    return (block_in.astype(jnp.float32) + mixed.reshape(frames, pixels, channels)).astype(
        jnp.bfloat16
    )


def backward_first(block_in, embedding, spatial, temporal, upstream):
    frames, pixels, channels = block_in.shape
    summed = block_in.astype(jnp.float32) + embedding
    normed = normalize(summed).astype(jnp.bfloat16)
    columns = spatial_columns(normed)
    preact = jnp.dot(columns, spatial, preferred_element_type=jnp.float32)
    activated = jax.nn.silu(preact).astype(jnp.bfloat16).reshape(frames, pixels, channels)
    tcolumns = temporal_columns(activated)
    upstream_flat = upstream.reshape(frames * pixels, channels)
    temporal_term = jnp.dot(tcolumns.T, upstream_flat, preferred_element_type=jnp.float32)
    act_grad = temporal_fold(
        jnp.dot(upstream_flat, temporal.T, preferred_element_type=jnp.float32),
        frames,
        pixels,
        channels,
    )
    logistic = jax.nn.sigmoid(preact)
    slope = logistic * (1.0 + preact * (1.0 - logistic))
    pre_grad = (act_grad.reshape(frames * pixels, channels) * slope).astype(jnp.bfloat16)
    return (temporal_term, pre_grad, columns)


def backward_second(block_in, embedding, spatial, upstream, pre_grad, columns):
    frames, pixels, channels = block_in.shape
    summed = block_in.astype(jnp.float32) + embedding
    spatial_term = jnp.dot(columns.T, pre_grad, preferred_element_type=jnp.float32)
    norm_grad = spatial_fold(
        jnp.dot(pre_grad, spatial.T, preferred_element_type=jnp.float32), frames, channels
    )
    _, pullback = jax.vjp(normalize, summed)
    back_input = (upstream.astype(jnp.float32) + pullback(norm_grad)[0]).astype(jnp.bfloat16)
    return (back_input, spatial_term)


def section_backward(block_in, embedding, spatial, temporal, upstream):
    temporal_term, pre_grad, columns = backward_first(
        block_in, embedding, spatial, temporal, upstream
    )
    back_input, spatial_term = backward_second(
        block_in, embedding, spatial, upstream, pre_grad, columns
    )
    return (back_input, spatial_term, temporal_term)


def per_device(samples, timesteps, cotangent, spatial_weight, temporal_weight):
    sections = lax.axis_size("pipe")
    section_index = lax.axis_index("pipe")
    micro_count = samples.shape[0]
    frames, pixels, channels = (samples.shape[1], samples.shape[2], samples.shape[3])
    moments = jnp.arange(micro_count + sections - 1, dtype=jnp.int32)
    blank = jnp.zeros((frames, pixels, channels), jnp.bfloat16)
    full_spatial, full_temporal = (
        lax.all_gather(spatial_weight[0], "dp", axis=0, tiled=True),
        lax.all_gather(temporal_weight[0], "dp", axis=0, tiled=True),
    )

    def forward_step(carry, moment):
        incoming, stash = carry
        position = moment - section_index
        active = (position >= 0) & (position < micro_count)
        picked = jnp.clip(position, 0, micro_count - 1)
        own = lax.dynamic_index_in_dim(samples, picked, 0, keepdims=False)
        embedding = embedding_of(
            lax.dynamic_index_in_dim(timesteps, picked, 0, keepdims=False), channels
        )
        block_in = jnp.where(section_index == 0, own, incoming)
        result = lax.cond(
            active & (section_index < sections - 1),
            lambda: section_forward(block_in, embedding, full_spatial, full_temporal),
            lambda: blank,
        )
        stash = jnp.where(
            active, lax.dynamic_update_index_in_dim(stash, block_in, picked, 0), stash
        )
        passed = passed_along(result, "pipe", 1)
        return ((passed, stash), None)

    (_, stash), _ = lax.scan(forward_step, (blank, jnp.zeros_like(samples)), moments)
    back_spatial, back_temporal = (full_spatial, full_temporal)

    def inputs_at(moment, incoming):
        position = moment - (sections - 1 - section_index)
        active = (position >= 0) & (position < micro_count)
        picked = jnp.clip(position, 0, micro_count - 1)
        block_in = lax.dynamic_index_in_dim(stash, picked, 0, keepdims=False)
        embedding = embedding_of(
            lax.dynamic_index_in_dim(timesteps, picked, 0, keepdims=False), channels
        )
        given = lax.dynamic_index_in_dim(cotangent, picked, 0, keepdims=False)
        upstream = jnp.where(section_index == sections - 1, given, incoming)
        return (active, block_in, embedding, upstream)

    def backward_step(carry, moment):
        incoming, grad_spatial, grad_temporal = carry
        active, block_in, embedding, upstream = inputs_at(moment, incoming)

        def working():
            back_input, spatial_term, temporal_term = section_backward(
                block_in, embedding, back_spatial, back_temporal, upstream
            )
            return (back_input, grad_spatial + spatial_term, grad_temporal + temporal_term)

        def waiting():
            return (blank, grad_spatial, grad_temporal)

        back_input, grad_spatial, grad_temporal = lax.cond(active, working, waiting)
        passed = passed_along(back_input, "pipe", -1)
        return ((passed, grad_spatial, grad_temporal), None)

    start = (
        blank,
        jnp.zeros(back_spatial.shape, jnp.float32),
        jnp.zeros(back_temporal.shape, jnp.float32),
    )
    (_, grad_spatial, grad_temporal), _ = lax.scan(backward_step, start, moments)
    share_spatial, share_temporal = (
        lax.psum_scatter(
            grad_spatial.astype(jnp.bfloat16).astype(jnp.float32).astype(jnp.bfloat16),
            "dp",
            scatter_dimension=0,
            tiled=True,
        ).astype(jnp.float32),
        lax.psum_scatter(
            grad_temporal.astype(jnp.bfloat16).astype(jnp.float32).astype(jnp.bfloat16),
            "dp",
            scatter_dimension=0,
            tiled=True,
        ).astype(jnp.float32),
    )
    return (share_spatial[None], share_temporal[None])


SPAN = 40
CUTS = (24, 16)
PIECE = 64


def coordinates():
    index = lax.axis_index("dp")
    return index // (GRID[1] * GRID[2]), (index // GRID[2]) % GRID[1], index % GRID[2]


def shifted(value, dz=0, dy=0, dc=0):
    pairs = []
    for z in range(GRID[0]):
        for y in range(GRID[1]):
            for c in range(GRID[2]):
                place = ((z + dz) % GRID[0], (y + dy) % GRID[1], (c + dc) % GRID[2])
                pairs.append(
                    (
                        (z * GRID[1] + y) * GRID[2] + c,
                        (place[0] * GRID[1] + place[1]) * GRID[2] + place[2],
                    )
                )
    return lax.ppermute(value, "dp", pairs)


def swapped(value):
    return lax.ppermute(value, "pipe", [(0, 1), (1, 0)])


def part_of(value, index, axis):
    return lax.dynamic_index_in_dim(value, index, axis, keepdims=False)


def vmem_call(body, outs, scratch=(), flops=0, moved=0):
    return pl.pallas_call(
        body,
        out_shape=outs,
        scratch_shapes=list(scratch),
        compiler_params=pltpu.CompilerParams(vmem_limit_bytes=24 * 2**20),
        cost_estimate=pl.CostEstimate(
            flops=5 * flops // 2, bytes_accessed=moved, transcendentals=0
        ),
    )


def after(value, earlier):
    return value if earlier is None else lax.optimization_barrier((value, earlier))[0]


def in_order(swap, own, other, axis):
    return jnp.where(
        swap, jnp.concatenate([other, own], axis), jnp.concatenate([own, other], axis)
    )


def over_z(value, pairs):
    moves = []
    for source, target in pairs:
        for rest in range(GRID[1] * GRID[2]):
            moves.append(tuple(z * GRID[1] * GRID[2] + rest for z in (source, target)))
    return lax.ppermute(value, "dp", moves)


def sent_over_z(value):
    return [shifted(value, dz=step) for step in range(1, GRID[0])]


def sent_on_chip(value, pieces=1):
    if pieces == 1:
        return shifted(value, dc=1)
    flat = value.reshape(-1, *value.shape[-2:])
    sent = [shifted(piece, dc=1) for piece in jnp.split(flat, pieces)]
    return jnp.concatenate(sent).reshape(value.shape)


def places_of(channels, main):
    channel = jnp.arange(channels)
    span, inside = channel // SPAN, channel % SPAN
    odd = span % 2
    cut = jnp.where(odd == 0, CUTS[0], CUTS[1])
    second = (inside >= cut).astype(jnp.int32)
    before = span // 2 * SPAN + odd * jnp.where(second == 0, CUTS[0], CUTS[1])
    rank = before + inside - second * cut
    tail = channels // 2 - main
    return jnp.where(
        rank < main, second * main + rank, (1 + second) * main + second * (tail - main) + rank
    )


def spans_of(rows, odd):
    sets = ([], [])
    for index, start in enumerate(range(0, rows, SPAN)):
        cut = start + CUTS[(index + odd) % 2]
        sets[0].append((start, cut))
        sets[1].append((cut, start + SPAN))
    return sets


def sets_of(value):
    _, _, c = coordinates()
    results = []
    for which in range(2):
        by_core = []
        for odd in range(2):
            spans = spans_of(value.shape[0], odd)[which]
            taken = jnp.concatenate([value[start:end] for start, end in spans])
            by_core.append(jnp.pad(taken, ((0, PIECE - taken.shape[0]), (0, 0))))
        results.append(jnp.where(c == 0, by_core[0], by_core[1]))
    return results


def shard_of(own, given, rows):
    _, _, c = coordinates()
    by_core = []
    for odd in range(2):
        taken, pieces = [0, 0], []
        for spans in zip(*spans_of(rows, odd)):
            for which, (start, end) in enumerate(spans):
                source = (own, given)[which]
                pieces.append(source[taken[which] : taken[which] + end - start])
                taken[which] += end - start
        by_core.append(jnp.concatenate(pieces))
    return jnp.where(c == 0, by_core[0], by_core[1])


def compact(pieces, own):
    short = 3 * SPAN - PIECE
    low, high = pieces[:, 0], pieces[:, 1]
    both = jnp.where(
        own,
        jnp.concatenate([low, high[:, :short]], 1),
        jnp.concatenate([low[:, :short], high], 1),
    )
    return both.reshape(-1, pieces.shape[3])


def spread(rows, chips, own):
    rows = rows.reshape(chips, -1, rows.shape[1])
    short = rows.shape[1] - PIECE
    pad = ((0, 0), (0, PIECE - short), (0, 0))
    return jnp.where(
        own,
        jnp.stack([rows[:, :PIECE], jnp.pad(rows[:, PIECE:], pad)], 1),
        jnp.stack([jnp.pad(rows[:, :short], pad), rows[:, short:]], 1),
    )


def gathered_over_z(value, earlier=None, beside=None):
    z, _, _ = coordinates()
    value = after(value, earlier)
    sent = after(sent_over_z(value), beside)
    return (
        jnp.stack([lax.select_n((z - place) % GRID[0], value, *sent) for place in range(GRID[0])]),
        sent,
    )


def sent_over_y(line, earlier=None):
    return shifted(after(line, earlier), dy=1)


def joined_over_y(line, sent):
    _, y, _ = coordinates()
    return in_order(y == 1, line[:, None], sent[:, None], 1)


def gathered_on_chip(plane, pieces=1, beside=None):
    _, _, c = coordinates()
    sent = after(sent_on_chip(plane, pieces), beside)
    whole = in_order(c == 1, plane[:, :, None], sent[:, :, None], 2)
    return whole.reshape(-1, plane.shape[3])


def added(*terms):
    return sum(term.astype(F32) for term in terms)


def summed_on_chip(value, pieces=1):
    _, _, c = coordinates()
    sent = sent_on_chip(part_of(value, 1 - c, 2), pieces)
    return added(part_of(value, c, 2), sent).astype(BF16)


def summed_over_y(value, earlier):
    _, y, _ = coordinates()
    sent = shifted(after(part_of(value, 1 - y, 1), earlier), dy=1)
    return added(part_of(value, y, 1), sent).astype(BF16), sent


def sent_for_sums(line, earlier=None):
    z, _, _ = coordinates()
    line = after(line, earlier)
    return [
        shifted(part_of(line, (z + step) % GRID[0], 0), dz=step) for step in range(1, GRID[0])
    ]


def summed_over_z(line, earlier=None):
    z, _, _ = coordinates()
    sent = sent_for_sums(line, earlier)
    return added(part_of(line, z, 0), *sent), sent


def pixel_masks(rows):
    row = lax.broadcasted_iota(jnp.int32, (rows, 1), 0)
    high, wide = (row // WIDTH) % HEIGHT, row % WIDTH
    masks = []
    for dr in (-1, 0, 1):
        for dc in (-1, 0, 1):
            inside = (high + dr >= 0) & (high + dr < HEIGHT) & (wide + dc >= 0) & (wide + dc < WIDTH)
            masks.append((dr * WIDTH + dc, inside))
    return masks


def frame_masks(rows, frames):
    pixels = HEIGHT * WIDTH
    row = lax.broadcasted_iota(jnp.int32, (rows, 1), 0)
    frame = (row // pixels) % frames
    return [
        (step * pixels, (frame + step >= 0) & (frame + step < frames)) for step in (-1, 0, 1)
    ]


def moved_rows(value, move):
    shift, inside = move
    if shift:
        value = pltpu.roll(value, (-shift) % value.shape[0], 0)
    return jnp.where(inside, value, 0.0)


def dot(left, right, dims=((1,), (0,))):
    return lax.dot_general(left, right, (dims, ((), ())), preferred_element_type=F32)


def with_embedding(hidden, embedding_ref, samples):
    per = hidden.shape[0] // samples
    return jnp.concatenate(
        [hidden[s * per : (s + 1) * per] + embedding_ref[s : s + 1, :] for s in range(samples)]
    )


def scale_of(summed):
    return lax.rsqrt(jnp.mean(summed * summed, axis=-1, keepdims=True) + 1e-06)


def silu_parts(preact):
    logistic = 1.0 / (1.0 + jnp.exp(-preact))
    return logistic, preact * logistic


def convolved(normed, weight_refs, masks):
    rows, channels = normed.shape
    normed = normed.astype(F32)
    totals = [None] * len(weight_refs)
    for tap in range(9):
        moved = moved_rows(normed, masks[tap]).astype(BF16)
        for index, ref in enumerate(weight_refs):
            term = dot(moved, ref[tap * channels : (tap + 1) * channels, :])
            totals[index] = term if totals[index] is None else totals[index] + term
    return jnp.concatenate(totals, 1)


def back_through(pre_grad, weight_refs, masks, channels):
    pre_grad = pre_grad.astype(F32)
    total = None
    for tap in range(9):
        weights = [ref[tap * channels : (tap + 1) * channels, :] for ref in weight_refs]
        term = dot(
            moved_rows(pre_grad, masks[8 - tap]).astype(BF16),
            jnp.concatenate(weights, 1),
            ((1,), (1,)),
        )
        total = term if total is None else total + term
    return total


def tap_rows(temporal_ref, tap, width):
    tail = PIECE
    start = tap * (width - tail)
    rows = temporal_ref[start : start + width - tail, :]
    return jnp.concatenate([rows, rows[width - 2 * tail :]], 0)


def first_forward(frames, hidden_ref, embedding_ref, keep_ref, temporal_ref, *refs):
    *spatial_refs, normed_ref, preact_ref, mixed_ref = refs
    rows = hidden_ref.shape[0]
    width = keep_ref.shape[1]
    summed = with_embedding(hidden_ref[...].astype(F32), embedding_ref, embedding_ref.shape[0])
    normed = (summed * scale_of(summed)).astype(BF16)
    normed_ref[...] = normed
    preact = convolved(normed, spatial_refs, pixel_masks(rows))
    preact_ref[...] = preact
    activated = silu_parts(preact)[1].astype(BF16).astype(F32) * keep_ref[...]
    mixed = None
    for tap, move in enumerate(frame_masks(rows, frames)):
        term = dot(
            moved_rows(activated, move).astype(BF16),
            tap_rows(temporal_ref, tap, width),
        )
        mixed = term if mixed is None else mixed + term
    mixed_ref[...] = mixed.astype(BF16)


def slope_of(preact):
    logistic, _ = silu_parts(preact)
    return logistic * (1.0 + preact * (1.0 - logistic))


def act_grad_of(upstream, temporal_ref, width, frames):
    upstream = upstream.astype(F32)
    moves = frame_masks(upstream.shape[0], frames)
    total = None
    for tap in range(3):
        term = dot(
            moved_rows(upstream, moves[2 - tap]).astype(BF16),
            tap_rows(temporal_ref, tap, width),
            ((1,), (1,)),
        )
        total = term if total is None else total + term
    return total


def store_temporal_terms(activated, upstream, frames, out_ref):
    width = activated.shape[1]
    tail = PIECE
    upstream = upstream.astype(F32)
    moves = frame_masks(upstream.shape[0], frames)
    for tap in range(3):
        term = dot(activated, moved_rows(upstream, moves[2 - tap]).astype(BF16), ((0,), (0,)))
        start = tap * (width - tail)
        out_ref[start : start + width - 2 * tail, :] = term[: width - 2 * tail].astype(BF16)
        out_ref[start + width - 2 * tail : start + width - tail, :] = (
            term[width - 2 * tail : width - tail] + term[width - tail :]
        ).astype(BF16)


def store_spatial_terms(normed, pre_grad, out_refs):
    channels = normed.shape[1]
    pre_grad = pre_grad.astype(F32)
    masks = pixel_masks(pre_grad.shape[0])
    for tap in range(9):
        term = dot(
            normed, moved_rows(pre_grad, masks[8 - tap]).astype(BF16), ((0,), (0,))
        ).astype(BF16)
        start = 0
        for out_ref in out_refs:
            end = start + out_ref.shape[1]
            out_ref[tap * channels : (tap + 1) * channels, :] = term[:, start:end]
            start = end


def second_forward(
    frames, hidden_ref, own_ref, sent_ref, embedding_ref, keep_ref, upstream_ref, temporal_ref, *refs
):
    *spatial_refs, next_ref, normed_ref, activated_ref, pre_grad_ref, back_ref = refs
    rows, channels = hidden_ref.shape
    width = keep_ref.shape[1]
    masks = pixel_masks(rows)
    mixed = own_ref[...].astype(F32) + sent_ref[...].astype(F32)
    hidden = (hidden_ref[...].astype(F32) + mixed).astype(BF16)
    next_ref[...] = hidden
    summed = with_embedding(hidden.astype(F32), embedding_ref, embedding_ref.shape[0])
    normed = (summed * scale_of(summed)).astype(BF16)
    normed_ref[...] = normed
    preact = convolved(normed, spatial_refs, masks)
    activated_ref[...] = (silu_parts(preact)[1] * keep_ref[...]).astype(BF16)
    act_grad = act_grad_of(upstream_ref[...], temporal_ref, width, frames)
    pre_grad = (act_grad * slope_of(preact) * keep_ref[...]).astype(BF16)
    pre_grad_ref[...] = pre_grad
    back = back_through(pre_grad, spatial_refs, masks, channels)
    back_ref[...] = back.astype(BF16)


def second_terms(frames, normed_ref, pre_grad_ref, activated_ref, upstream_ref, *outs):
    *spatial_refs, temporal_ref = outs
    store_spatial_terms(normed_ref[...], pre_grad_ref[...], spatial_refs)
    store_temporal_terms(activated_ref[...], upstream_ref[...], frames, temporal_ref)


def first_terms(
    frames, hidden_ref, embedding_ref, upstream_ref, own_ref, sent_ref, normed_ref, preact_ref,
    keep_ref, temporal_ref, *outs
):
    *spatial_outs, temporal_out = outs
    width = keep_ref.shape[1]
    channels = hidden_ref.shape[1]
    summed = with_embedding(hidden_ref[...].astype(F32), embedding_ref, embedding_ref.shape[0])
    scale = scale_of(summed)
    grad = own_ref[...].astype(F32) + sent_ref[...].astype(F32)
    inner = jnp.sum(grad * summed, axis=-1, keepdims=True)
    back = grad * scale - summed * (scale * scale * scale) * (inner / channels)
    upstream = (upstream_ref[...].astype(F32) + back).astype(BF16)
    preact = preact_ref[...]
    activated = (silu_parts(preact)[1] * keep_ref[...]).astype(BF16)
    act_grad = act_grad_of(upstream, temporal_ref, width, frames)
    pre_grad = (act_grad * slope_of(preact) * keep_ref[...]).astype(BF16)
    store_spatial_terms(normed_ref[...], pre_grad, spatial_outs)
    store_temporal_terms(activated, upstream, frames, temporal_out)


def paired_device(samples, timesteps, cotangent, spatial_weight, temporal_weight):
    me = lax.axis_index("pipe")
    first = me == 0
    count, frames, pixels, channels = samples.shape
    rows = count * frames * pixels
    main = 2 * LANES
    width = main + LANES
    hidden = samples.reshape(rows, channels)
    upstream = cotangent.reshape(rows, channels)
    embedding = jax.vmap(lambda step: embedding_of(step, channels))(timesteps)
    lane = jnp.arange(LANES)
    keep_own = jnp.concatenate([jnp.ones(main), lane < LANES // 2]).astype(F32)[None]
    keep_other = jnp.concatenate([jnp.ones(main), lane >= LANES // 2]).astype(F32)[None]
    keep_first = jnp.where(first, keep_own, keep_other)
    keep_second = jnp.where(first, keep_other, keep_own)
    tail = lane[None] < LANES // 2

    places = places_of(channels, main)
    order = (places[:, None] == jnp.arange(channels)).astype(BF16)
    temporal_own, temporal_sent = sets_of(temporal_weight[0])
    temporal_given = swapped(temporal_sent)
    line_temporal, sent = gathered_over_z(in_order(me == 1, temporal_own, temporal_given, 0))
    side_temporal = sent_over_y(line_temporal)
    spatial_own = dot(spatial_weight[0], order).astype(BF16)
    given = swapped(spatial_own[:, main:])
    main_own, main_given = spatial_own[:, :main], given[:, :main]
    tails = jnp.where(tail, spatial_own[:, 2 * main :], given[:, main:])
    line, sent = gathered_over_z(jnp.where(first, main_own, main_given), sent, side_temporal)
    line_tails, sent = gathered_over_z(tails, sent)
    side_low = sent_over_y(line[..., :LANES])
    side_high = sent_over_y(line[..., LANES:], side_low)
    side_tails = sent_over_y(line_tails)
    line_second, sent = gathered_over_z(
        jnp.where(first, main_given, main_own), (sent, side_low)
    )
    side_first = jnp.concatenate([side_low, after(side_high, sent)], 2)
    plane_first = joined_over_y(line, side_first)
    plane_tails = joined_over_y(line_tails, after(side_tails, sent))
    plane_temporal = joined_over_y(line_temporal, side_temporal)
    side_second = sent_over_y(line_second)

    chips = GRID[0] * GRID[1]
    temporal = gathered_on_chip(plane_temporal).reshape(chips, GRID[2], 2, PIECE, channels)
    temporal_first = compact(temporal[:, :, 0], first)
    temporal_second = compact(temporal[:, :, 1], me == 1)
    tails = gathered_on_chip(plane_tails)
    spatial_first = [gathered_on_chip(plane_first), tails]

    def shape(extent, dtype=BF16):
        return jax.ShapeDtypeStruct(extent, dtype)

    spatial_flops = 2 * rows * 9 * channels * width
    temporal_flops = 2 * rows * 3 * channels * width
    spatial_bytes = 2 * 9 * channels * width
    temporal_bytes = 2 * 3 * channels * width
    normed_first, preact_first, mixed = vmem_call(
        functools.partial(first_forward, frames),
        (shape((rows, channels)), shape((rows, width), F32), shape((rows, channels))),
        flops=spatial_flops + temporal_flops,
        moved=spatial_bytes + temporal_bytes,
    )(hidden, embedding, keep_first, temporal_first, *spatial_first)
    mixed_given = swapped(mixed)
    plane_second = joined_over_y(line_second, after(side_second, mixed))
    spatial_second = [gathered_on_chip(plane_second, GRID[0], mixed_given), tails]
    hidden_second, normed_second, activated_second, pre_grad_second, back = vmem_call(
        functools.partial(second_forward, frames),
        (
            shape((rows, channels)),
            shape((rows, channels)),
            shape((rows, width)),
            shape((rows, width)),
            shape((rows, channels)),
        ),
        flops=2 * spatial_flops + temporal_flops,
        moved=spatial_bytes + temporal_bytes,
    )(
        hidden, mixed, mixed_given, embedding, keep_second, upstream, temporal_second,
        *spatial_second,
    )

    def terms_shape():
        return (
            shape((9 * channels, main)),
            shape((9 * channels, width - main)),
            shape((3 * (width - PIECE), channels)),
        )

    def on_chip(terms, pieces=1):
        return summed_on_chip(terms.reshape(*GRID, -1, terms.shape[1]), pieces)

    back_given = swapped(back)
    main_terms_second, tail_terms_second, temporal_terms_second = vmem_call(
        functools.partial(second_terms, frames),
        terms_shape(),
        flops=spatial_flops + temporal_flops,
        moved=spatial_bytes + temporal_bytes,
    )(normed_second, pre_grad_second, activated_second, upstream)
    chip_second = on_chip(main_terms_second, GRID[0])
    back_given = after(back_given, chip_second)
    line, side = summed_over_y(chip_second, None)
    share_second, sent_second = summed_over_z(line)
    main_terms_first, tail_terms_first, temporal_terms_first = vmem_call(
        functools.partial(first_terms, frames),
        terms_shape(),
        flops=spatial_flops + 2 * temporal_flops,
        moved=spatial_bytes + 2 * temporal_bytes,
    )(
        hidden_second, embedding, upstream, back, back_given, normed_first, preact_first,
        keep_first, temporal_first,
    )
    chip_tails = on_chip(tail_terms_first + tail_terms_second)
    chip_first = on_chip(after(main_terms_first, side))
    terms = jnp.concatenate(
        [
            spread(temporal_terms_first, chips, first),
            spread(temporal_terms_second, chips, me == 1),
        ],
        2,
    )
    chip_temporal = summed_on_chip(terms.reshape(*GRID, -1, channels))

    line, side = summed_over_y(chip_tails, side)
    line_low, side = summed_over_y(chip_first[..., :LANES], side)
    share_tails, sent_tails = summed_over_z(line, (side, sent_second))
    line_high, side = summed_over_y(chip_first[..., LANES:], side)
    share_first, sent_first = summed_over_z(
        jnp.concatenate([line_low, line_high], 2), sent_tails
    )
    line, side = summed_over_y(chip_temporal, side)
    share_temporal, _ = summed_over_z(line)

    kept = jnp.where(first, share_first, share_second)
    passed = jnp.where(first, share_second, share_first)
    given = jnp.concatenate([passed, share_tails], 1).astype(BF16)
    given = swapped(after(given, side)).astype(F32)
    share_spatial = jnp.concatenate(
        [kept, given[:, :main], jnp.where(tail, share_tails, given[:, main:])], 1
    )
    share_spatial = lax.dot_general(
        share_spatial, order.astype(F32), (((1,), (1,)), ((), ())), precision=lax.Precision.HIGH
    )
    low, high = share_temporal[:PIECE], share_temporal[PIECE:]
    given = swapped(jnp.where(first, high, low).astype(BF16))
    given = after(given, share_spatial).astype(F32)
    share_temporal = shard_of(jnp.where(first, low, high), given, temporal_weight.shape[1])
    return (share_spatial[None], share_temporal[None])


def solution(mesh):
    paired = mesh.shape["pipe"] == 2 and mesh.shape["dp"] == math.prod(GRID)
    return jax.shard_map(
        paired_device if paired else per_device,
        mesh=mesh,
        in_specs=(
            P("dp", None, None, None),
            P("dp"),
            P("dp", None, None, None),
            P("pipe", "dp", None),
            P("pipe", "dp", None),
        ),
        out_specs=(P("pipe", "dp", None), P("pipe", "dp", None)),
        check_vma=False,
    )
```

```python
import functools
import math

import jax
import jax.numpy as jnp
from jax import lax
from jax.experimental import pallas as pl
from jax.experimental.pallas import tpu as pltpu
from jax.sharding import PartitionSpec as P

HEIGHT = 8
WIDTH = 4
F32 = jnp.float32
BF16 = jnp.bfloat16
GRID = (4, 2, 2)
LANES = 128


def passed_along(value, axis, steps):
    count = lax.axis_size(axis)
    first, last = (max(0, -steps), min(count, count - steps))
    return lax.ppermute(value, axis, [(source, source + steps) for source in range(first, last)])


def embedding_of(step, channels):
    half_width = channels // 2
    frequency = jnp.exp(-math.log(10000.0) * jnp.arange(half_width, dtype=jnp.float32) / half_width)
    phases = step.astype(jnp.float32) * frequency
    return jnp.concatenate([jnp.sin(phases), jnp.cos(phases)])


def normalize(summed):
    return summed * lax.rsqrt(jnp.mean(summed * summed, axis=-1, keepdims=True) + 1e-06)


def spatial_columns(normed):
    frames, pixels, channels = normed.shape
    grid = normed.reshape(frames, HEIGHT, WIDTH, channels)
    padded = jnp.pad(grid, ((0, 0), (1, 1), (1, 1), (0, 0)))
    pieces = [
        padded[:, row : row + HEIGHT, col : col + WIDTH, :] for row in range(3) for col in range(3)
    ]
    return jnp.concatenate(pieces, axis=-1).reshape(frames * pixels, 9 * channels)


def spatial_fold(grads, frames, channels):
    parts = grads.reshape(frames, HEIGHT, WIDTH, 9, channels)
    padded = jnp.zeros((frames, HEIGHT + 2, WIDTH + 2, channels), jnp.float32)
    for row in range(3):
        for col in range(3):
            padded = padded.at[:, row : row + HEIGHT, col : col + WIDTH, :].add(
                parts[:, :, :, row * 3 + col, :]
            )
    return padded[:, 1 : HEIGHT + 1, 1 : WIDTH + 1, :].reshape(frames, HEIGHT * WIDTH, channels)


def temporal_columns(activated):
    frames, pixels, channels = activated.shape
    padded = jnp.pad(activated, ((1, 1), (0, 0), (0, 0)))
    pieces = [padded[tap : tap + frames] for tap in range(3)]
    return jnp.concatenate(pieces, axis=-1).reshape(frames * pixels, 3 * channels)


def temporal_fold(grads, frames, pixels, channels):
    parts = grads.reshape(frames, pixels, 3, channels)
    padded = jnp.zeros((frames + 2, pixels, channels), jnp.float32)
    for tap in range(3):
        padded = padded.at[tap : tap + frames].add(parts[:, :, tap, :])
    return padded[1 : frames + 1]


def section_forward(block_in, embedding, spatial, temporal):
    frames, pixels, channels = block_in.shape
    summed = block_in.astype(jnp.float32) + embedding
    normed = normalize(summed).astype(jnp.bfloat16)
    preact = jnp.dot(spatial_columns(normed), spatial, preferred_element_type=jnp.float32)
    activated = jax.nn.silu(preact).astype(jnp.bfloat16).reshape(frames, pixels, channels)
    mixed = jnp.dot(temporal_columns(activated), temporal, preferred_element_type=jnp.float32)
    return (block_in.astype(jnp.float32) + mixed.reshape(frames, pixels, channels)).astype(
        jnp.bfloat16
    )


def backward_first(block_in, embedding, spatial, temporal, upstream):
    frames, pixels, channels = block_in.shape
    summed = block_in.astype(jnp.float32) + embedding
    normed = normalize(summed).astype(jnp.bfloat16)
    columns = spatial_columns(normed)
    preact = jnp.dot(columns, spatial, preferred_element_type=jnp.float32)
    activated = jax.nn.silu(preact).astype(jnp.bfloat16).reshape(frames, pixels, channels)
    tcolumns = temporal_columns(activated)
    upstream_flat = upstream.reshape(frames * pixels, channels)
    temporal_term = jnp.dot(tcolumns.T, upstream_flat, preferred_element_type=jnp.float32)
    act_grad = temporal_fold(
        jnp.dot(upstream_flat, temporal.T, preferred_element_type=jnp.float32),
        frames,
        pixels,
        channels,
    )
    logistic = jax.nn.sigmoid(preact)
    slope = logistic * (1.0 + preact * (1.0 - logistic))
    pre_grad = (act_grad.reshape(frames * pixels, channels) * slope).astype(jnp.bfloat16)
    return (temporal_term, pre_grad, columns)


def backward_second(block_in, embedding, spatial, upstream, pre_grad, columns):
    frames, pixels, channels = block_in.shape
    summed = block_in.astype(jnp.float32) + embedding
    spatial_term = jnp.dot(columns.T, pre_grad, preferred_element_type=jnp.float32)
    norm_grad = spatial_fold(
        jnp.dot(pre_grad, spatial.T, preferred_element_type=jnp.float32), frames, channels
    )
    _, pullback = jax.vjp(normalize, summed)
    back_input = (upstream.astype(jnp.float32) + pullback(norm_grad)[0]).astype(jnp.bfloat16)
    return (back_input, spatial_term)


def section_backward(block_in, embedding, spatial, temporal, upstream):
    temporal_term, pre_grad, columns = backward_first(
        block_in, embedding, spatial, temporal, upstream
    )
    back_input, spatial_term = backward_second(
        block_in, embedding, spatial, upstream, pre_grad, columns
    )
    return (back_input, spatial_term, temporal_term)


def per_device(samples, timesteps, cotangent, spatial_weight, temporal_weight):
    sections = lax.axis_size("pipe")
    section_index = lax.axis_index("pipe")
    micro_count = samples.shape[0]
    frames, pixels, channels = (samples.shape[1], samples.shape[2], samples.shape[3])
    moments = jnp.arange(micro_count + sections - 1, dtype=jnp.int32)
    blank = jnp.zeros((frames, pixels, channels), jnp.bfloat16)
    full_spatial, full_temporal = (
        lax.all_gather(spatial_weight[0], "dp", axis=0, tiled=True),
        lax.all_gather(temporal_weight[0], "dp", axis=0, tiled=True),
    )

    def forward_step(carry, moment):
        incoming, stash = carry
        position = moment - section_index
        active = (position >= 0) & (position < micro_count)
        picked = jnp.clip(position, 0, micro_count - 1)
        own = lax.dynamic_index_in_dim(samples, picked, 0, keepdims=False)
        embedding = embedding_of(
            lax.dynamic_index_in_dim(timesteps, picked, 0, keepdims=False), channels
        )
        block_in = jnp.where(section_index == 0, own, incoming)
        result = lax.cond(
            active & (section_index < sections - 1),
            lambda: section_forward(block_in, embedding, full_spatial, full_temporal),
            lambda: blank,
        )
        stash = jnp.where(
            active, lax.dynamic_update_index_in_dim(stash, block_in, picked, 0), stash
        )
        passed = passed_along(result, "pipe", 1)
        return ((passed, stash), None)

    (_, stash), _ = lax.scan(forward_step, (blank, jnp.zeros_like(samples)), moments)
    back_spatial, back_temporal = (full_spatial, full_temporal)

    def inputs_at(moment, incoming):
        position = moment - (sections - 1 - section_index)
        active = (position >= 0) & (position < micro_count)
        picked = jnp.clip(position, 0, micro_count - 1)
        block_in = lax.dynamic_index_in_dim(stash, picked, 0, keepdims=False)
        embedding = embedding_of(
            lax.dynamic_index_in_dim(timesteps, picked, 0, keepdims=False), channels
        )
        given = lax.dynamic_index_in_dim(cotangent, picked, 0, keepdims=False)
        upstream = jnp.where(section_index == sections - 1, given, incoming)
        return (active, block_in, embedding, upstream)

    def backward_step(carry, moment):
        incoming, grad_spatial, grad_temporal = carry
        active, block_in, embedding, upstream = inputs_at(moment, incoming)

        def working():
            back_input, spatial_term, temporal_term = section_backward(
                block_in, embedding, back_spatial, back_temporal, upstream
            )
            return (back_input, grad_spatial + spatial_term, grad_temporal + temporal_term)

        def waiting():
            return (blank, grad_spatial, grad_temporal)

        back_input, grad_spatial, grad_temporal = lax.cond(active, working, waiting)
        passed = passed_along(back_input, "pipe", -1)
        return ((passed, grad_spatial, grad_temporal), None)

    start = (
        blank,
        jnp.zeros(back_spatial.shape, jnp.float32),
        jnp.zeros(back_temporal.shape, jnp.float32),
    )
    (_, grad_spatial, grad_temporal), _ = lax.scan(backward_step, start, moments)
    share_spatial, share_temporal = (
        lax.psum_scatter(
            grad_spatial.astype(jnp.bfloat16).astype(jnp.float32).astype(jnp.bfloat16),
            "dp",
            scatter_dimension=0,
            tiled=True,
        ).astype(jnp.float32),
        lax.psum_scatter(
            grad_temporal.astype(jnp.bfloat16).astype(jnp.float32).astype(jnp.bfloat16),
            "dp",
            scatter_dimension=0,
            tiled=True,
        ).astype(jnp.float32),
    )
    return (share_spatial[None], share_temporal[None])


SPAN = 40
CUTS = (24, 16)
PIECE = 64


def coordinates():
    index = lax.axis_index("dp")
    return index // (GRID[1] * GRID[2]), (index // GRID[2]) % GRID[1], index % GRID[2]


def shifted(value, dz=0, dy=0, dc=0):
    pairs = []
    for z in range(GRID[0]):
        for y in range(GRID[1]):
            for c in range(GRID[2]):
                place = ((z + dz) % GRID[0], (y + dy) % GRID[1], (c + dc) % GRID[2])
                pairs.append(
                    (
                        (z * GRID[1] + y) * GRID[2] + c,
                        (place[0] * GRID[1] + place[1]) * GRID[2] + place[2],
                    )
                )
    return lax.ppermute(value, "dp", pairs)


def swapped(value):
    return lax.ppermute(value, "pipe", [(0, 1), (1, 0)])


def part_of(value, index, axis):
    return lax.dynamic_index_in_dim(value, index, axis, keepdims=False)


def vmem_call(body, outs, scratch=(), flops=0, moved=0):
    return pl.pallas_call(
        body,
        out_shape=outs,
        scratch_shapes=list(scratch),
        compiler_params=pltpu.CompilerParams(vmem_limit_bytes=24 * 2**20),
        cost_estimate=pl.CostEstimate(
            flops=5 * flops // 2, bytes_accessed=moved, transcendentals=0
        ),
    )


def after(value, earlier):
    return value if earlier is None else lax.optimization_barrier((value, earlier))[0]


def in_order(swap, own, other, axis):
    return jnp.where(
        swap, jnp.concatenate([other, own], axis), jnp.concatenate([own, other], axis)
    )


def over_z(value, pairs):
    moves = []
    for source, target in pairs:
        for rest in range(GRID[1] * GRID[2]):
            moves.append(tuple(z * GRID[1] * GRID[2] + rest for z in (source, target)))
    return lax.ppermute(value, "dp", moves)


def sent_over_z(value):
    return [shifted(value, dz=step) for step in range(1, GRID[0])]


def sent_on_chip(value, pieces=1):
    if pieces == 1:
        return shifted(value, dc=1)
    flat = value.reshape(-1, *value.shape[-2:])
    sent = [shifted(piece, dc=1) for piece in jnp.split(flat, pieces)]
    return jnp.concatenate(sent).reshape(value.shape)


def places_of(channels, main):
    channel = jnp.arange(channels)
    span, inside = channel // SPAN, channel % SPAN
    odd = span % 2
    cut = jnp.where(odd == 0, CUTS[0], CUTS[1])
    second = (inside >= cut).astype(jnp.int32)
    before = span // 2 * SPAN + odd * jnp.where(second == 0, CUTS[0], CUTS[1])
    rank = before + inside - second * cut
    tail = channels // 2 - main
    return jnp.where(
        rank < main, second * main + rank, (1 + second) * main + second * (tail - main) + rank
    )


def spans_of(rows, odd):
    sets = ([], [])
    for index, start in enumerate(range(0, rows, SPAN)):
        cut = start + CUTS[(index + odd) % 2]
        sets[0].append((start, cut))
        sets[1].append((cut, start + SPAN))
    return sets


def sets_of(value):
    _, _, c = coordinates()
    results = []
    for which in range(2):
        by_core = []
        for odd in range(2):
            spans = spans_of(value.shape[0], odd)[which]
            taken = jnp.concatenate([value[start:end] for start, end in spans])
            by_core.append(jnp.pad(taken, ((0, PIECE - taken.shape[0]), (0, 0))))
        results.append(jnp.where(c == 0, by_core[0], by_core[1]))
    return results


def shard_of(own, given, rows):
    _, _, c = coordinates()
    by_core = []
    for odd in range(2):
        taken, pieces = [0, 0], []
        for spans in zip(*spans_of(rows, odd)):
            for which, (start, end) in enumerate(spans):
                source = (own, given)[which]
                pieces.append(source[taken[which] : taken[which] + end - start])
                taken[which] += end - start
        by_core.append(jnp.concatenate(pieces))
    return jnp.where(c == 0, by_core[0], by_core[1])


def compact(pieces, own):
    short = 3 * SPAN - PIECE
    low, high = pieces[:, 0], pieces[:, 1]
    both = jnp.where(
        own,
        jnp.concatenate([low, high[:, :short]], 1),
        jnp.concatenate([low[:, :short], high], 1),
    )
    return both.reshape(-1, pieces.shape[3])


def spread(rows, chips, own):
    rows = rows.reshape(chips, -1, rows.shape[1])
    short = rows.shape[1] - PIECE
    pad = ((0, 0), (0, PIECE - short), (0, 0))
    return jnp.where(
        own,
        jnp.stack([rows[:, :PIECE], jnp.pad(rows[:, PIECE:], pad)], 1),
        jnp.stack([jnp.pad(rows[:, :short], pad), rows[:, short:]], 1),
    )


def gathered_over_z(value, earlier=None, beside=None):
    z, _, _ = coordinates()
    value = after(value, earlier)
    sent = after(sent_over_z(value), beside)
    return (
        jnp.stack([lax.select_n((z - place) % GRID[0], value, *sent) for place in range(GRID[0])]),
        sent,
    )


def sent_over_y(line, earlier=None):
    return shifted(after(line, earlier), dy=1)


def joined_over_y(line, sent):
    _, y, _ = coordinates()
    return in_order(y == 1, line[:, None], sent[:, None], 1)


def gathered_on_chip(plane, pieces=1, beside=None):
    _, _, c = coordinates()
    sent = after(sent_on_chip(plane, pieces), beside)
    whole = in_order(c == 1, plane[:, :, None], sent[:, :, None], 2)
    return whole.reshape(-1, plane.shape[3])


def added(*terms):
    return sum(term.astype(F32) for term in terms)


def summed_on_chip(value, pieces=1):
    _, _, c = coordinates()
    sent = sent_on_chip(part_of(value, 1 - c, 2), pieces)
    return added(part_of(value, c, 2), sent).astype(BF16)


def summed_over_y(value, earlier):
    _, y, _ = coordinates()
    sent = shifted(after(part_of(value, 1 - y, 1), earlier), dy=1)
    return added(part_of(value, y, 1), sent).astype(BF16), sent


def sent_for_sums(line, earlier=None):
    z, _, _ = coordinates()
    line = after(line, earlier)
    return [
        shifted(part_of(line, (z + step) % GRID[0], 0), dz=step) for step in range(1, GRID[0])
    ]


def summed_over_z(line, earlier=None):
    z, _, _ = coordinates()
    sent = sent_for_sums(line, earlier)
    return added(part_of(line, z, 0), *sent), sent


def pixel_masks(rows):
    row = lax.broadcasted_iota(jnp.int32, (rows, 1), 0)
    high, wide = (row // WIDTH) % HEIGHT, row % WIDTH
    masks = []
    for dr in (-1, 0, 1):
        for dc in (-1, 0, 1):
            inside = (high + dr >= 0) & (high + dr < HEIGHT) & (wide + dc >= 0) & (wide + dc < WIDTH)
            masks.append((dr * WIDTH + dc, inside))
    return masks


def frame_masks(rows, frames):
    pixels = HEIGHT * WIDTH
    row = lax.broadcasted_iota(jnp.int32, (rows, 1), 0)
    frame = (row // pixels) % frames
    return [
        (step * pixels, (frame + step >= 0) & (frame + step < frames)) for step in (-1, 0, 1)
    ]


def moved_rows(value, move):
    shift, inside = move
    if shift:
        value = pltpu.roll(value, (-shift) % value.shape[0], 0)
    return jnp.where(inside, value, 0.0)


def dot(left, right, dims=((1,), (0,))):
    return lax.dot_general(left, right, (dims, ((), ())), preferred_element_type=F32)


def with_embedding(hidden, embedding_ref, samples):
    per = hidden.shape[0] // samples
    return jnp.concatenate(
        [hidden[s * per : (s + 1) * per] + embedding_ref[s : s + 1, :] for s in range(samples)]
    )


def scale_of(summed):
    return lax.rsqrt(jnp.mean(summed * summed, axis=-1, keepdims=True) + 1e-06)


def silu_parts(preact):
    logistic = 1.0 / (1.0 + jnp.exp(-preact))
    return logistic, preact * logistic


def convolved(normed, weight_refs, masks):
    rows, channels = normed.shape
    normed = normed.astype(F32)
    totals = [None] * len(weight_refs)
    for tap in range(9):
        moved = moved_rows(normed, masks[tap]).astype(BF16)
        for index, ref in enumerate(weight_refs):
            term = dot(moved, ref[tap * channels : (tap + 1) * channels, :])
            totals[index] = term if totals[index] is None else totals[index] + term
    return jnp.concatenate(totals, 1)


def back_through(pre_grad, weight_refs, masks, channels):
    pre_grad = pre_grad.astype(F32)
    total = None
    for tap in range(9):
        weights = [ref[tap * channels : (tap + 1) * channels, :] for ref in weight_refs]
        term = dot(
            moved_rows(pre_grad, masks[8 - tap]).astype(BF16),
            jnp.concatenate(weights, 1),
            ((1,), (1,)),
        )
        total = term if total is None else total + term
    return total


def tap_rows(temporal_ref, tap, width):
    tail = PIECE
    start = tap * (width - tail)
    rows = temporal_ref[start : start + width - tail, :]
    return jnp.concatenate([rows, rows[width - 2 * tail :]], 0)


def first_forward(frames, hidden_ref, embedding_ref, keep_ref, temporal_ref, *refs):
    *spatial_refs, normed_ref, preact_ref, mixed_ref = refs
    rows = hidden_ref.shape[0]
    width = keep_ref.shape[1]
    summed = with_embedding(hidden_ref[...].astype(F32), embedding_ref, embedding_ref.shape[0])
    normed = (summed * scale_of(summed)).astype(BF16)
    normed_ref[...] = normed
    preact = convolved(normed, spatial_refs, pixel_masks(rows))
    preact_ref[...] = preact
    activated = silu_parts(preact)[1].astype(BF16).astype(F32) * keep_ref[...]
    mixed = None
    for tap, move in enumerate(frame_masks(rows, frames)):
        term = dot(
            moved_rows(activated, move).astype(BF16),
            tap_rows(temporal_ref, tap, width),
        )
        mixed = term if mixed is None else mixed + term
    mixed_ref[...] = mixed.astype(BF16)


def slope_of(preact):
    logistic, _ = silu_parts(preact)
    return logistic * (1.0 + preact * (1.0 - logistic))


def act_grad_of(upstream, temporal_ref, width, frames):
    upstream = upstream.astype(F32)
    moves = frame_masks(upstream.shape[0], frames)
    total = None
    for tap in range(3):
        term = dot(
            moved_rows(upstream, moves[2 - tap]).astype(BF16),
            tap_rows(temporal_ref, tap, width),
            ((1,), (1,)),
        )
        total = term if total is None else total + term
    return total


def store_temporal_terms(activated, upstream, frames, out_ref):
    width = activated.shape[1]
    tail = PIECE
    upstream = upstream.astype(F32)
    moves = frame_masks(upstream.shape[0], frames)
    for tap in range(3):
        term = dot(activated, moved_rows(upstream, moves[2 - tap]).astype(BF16), ((0,), (0,)))
        start = tap * (width - tail)
        out_ref[start : start + width - 2 * tail, :] = term[: width - 2 * tail].astype(BF16)
        out_ref[start + width - 2 * tail : start + width - tail, :] = (
            term[width - 2 * tail : width - tail] + term[width - tail :]
        ).astype(BF16)


def store_spatial_terms(normed, pre_grad, out_refs):
    channels = normed.shape[1]
    pre_grad = pre_grad.astype(F32)
    masks = pixel_masks(pre_grad.shape[0])
    for tap in range(9):
        term = dot(
            normed, moved_rows(pre_grad, masks[8 - tap]).astype(BF16), ((0,), (0,))
        ).astype(BF16)
        start = 0
        for out_ref in out_refs:
            end = start + out_ref.shape[1]
            out_ref[tap * channels : (tap + 1) * channels, :] = term[:, start:end]
            start = end


def second_act_grad(frames, upstream_ref, temporal_ref, out_ref):
    out_ref[...] = act_grad_of(upstream_ref[...], temporal_ref, out_ref.shape[1], frames)


def second_forward(
    hidden_ref, own_ref, sent_ref, embedding_ref, keep_ref, act_grad_ref, *refs
):
    *spatial_refs, next_ref, normed_ref, activated_ref, pre_grad_ref, back_ref = refs
    rows, channels = hidden_ref.shape
    masks = pixel_masks(rows)
    mixed = own_ref[...].astype(F32) + sent_ref[...].astype(F32)
    hidden = (hidden_ref[...].astype(F32) + mixed).astype(BF16)
    next_ref[...] = hidden
    summed = with_embedding(hidden.astype(F32), embedding_ref, embedding_ref.shape[0])
    normed = (summed * scale_of(summed)).astype(BF16)
    normed_ref[...] = normed
    preact = convolved(normed, spatial_refs, masks)
    activated_ref[...] = (silu_parts(preact)[1] * keep_ref[...]).astype(BF16)
    pre_grad = (act_grad_ref[...] * slope_of(preact) * keep_ref[...]).astype(BF16)
    pre_grad_ref[...] = pre_grad
    back = back_through(pre_grad, spatial_refs, masks, channels)
    back_ref[...] = back.astype(BF16)


def second_terms(frames, normed_ref, pre_grad_ref, activated_ref, upstream_ref, *outs):
    *spatial_refs, temporal_ref = outs
    store_spatial_terms(normed_ref[...], pre_grad_ref[...], spatial_refs)
    store_temporal_terms(activated_ref[...], upstream_ref[...], frames, temporal_ref)


def first_terms(
    frames, hidden_ref, embedding_ref, upstream_ref, own_ref, sent_ref, normed_ref, preact_ref,
    keep_ref, temporal_ref, *outs
):
    *spatial_outs, temporal_out = outs
    width = keep_ref.shape[1]
    channels = hidden_ref.shape[1]
    summed = with_embedding(hidden_ref[...].astype(F32), embedding_ref, embedding_ref.shape[0])
    scale = scale_of(summed)
    grad = own_ref[...].astype(F32) + sent_ref[...].astype(F32)
    inner = jnp.sum(grad * summed, axis=-1, keepdims=True)
    back = grad * scale - summed * (scale * scale * scale) * (inner / channels)
    upstream = (upstream_ref[...].astype(F32) + back).astype(BF16)
    preact = preact_ref[...]
    activated = (silu_parts(preact)[1] * keep_ref[...]).astype(BF16)
    act_grad = act_grad_of(upstream, temporal_ref, width, frames)
    pre_grad = (act_grad * slope_of(preact) * keep_ref[...]).astype(BF16)
    store_spatial_terms(normed_ref[...], pre_grad, spatial_outs)
    store_temporal_terms(activated, upstream, frames, temporal_out)


def paired_device(samples, timesteps, cotangent, spatial_weight, temporal_weight):
    me = lax.axis_index("pipe")
    first = me == 0
    count, frames, pixels, channels = samples.shape
    rows = count * frames * pixels
    main = 2 * LANES
    width = main + LANES
    hidden = samples.reshape(rows, channels)
    upstream = cotangent.reshape(rows, channels)
    embedding = jax.vmap(lambda step: embedding_of(step, channels))(timesteps)
    lane = jnp.arange(LANES)
    keep_own = jnp.concatenate([jnp.ones(main), lane < LANES // 2]).astype(F32)[None]
    keep_other = jnp.concatenate([jnp.ones(main), lane >= LANES // 2]).astype(F32)[None]
    keep_first = jnp.where(first, keep_own, keep_other)
    keep_second = jnp.where(first, keep_other, keep_own)
    tail = lane[None] < LANES // 2

    places = places_of(channels, main)
    order = (places[:, None] == jnp.arange(channels)).astype(BF16)
    temporal_own, temporal_sent = sets_of(temporal_weight[0])
    temporal_given = swapped(temporal_sent)
    line_temporal, sent = gathered_over_z(in_order(me == 1, temporal_own, temporal_given, 0))
    side_temporal = sent_over_y(line_temporal)
    spatial_own = dot(spatial_weight[0], order).astype(BF16)
    given = swapped(spatial_own[:, main:])
    main_own, main_given = spatial_own[:, :main], given[:, :main]
    tails = jnp.where(tail, spatial_own[:, 2 * main :], given[:, main:])
    line, sent = gathered_over_z(jnp.where(first, main_own, main_given), sent, side_temporal)
    line_tails, sent = gathered_over_z(tails, sent)
    side_low = sent_over_y(line[..., :LANES])
    side_high = sent_over_y(line[..., LANES:], side_low)
    side_tails = sent_over_y(line_tails)
    line_second, sent = gathered_over_z(
        jnp.where(first, main_given, main_own), (sent, side_low)
    )
    side_first = jnp.concatenate([side_low, after(side_high, sent)], 2)
    plane_first = joined_over_y(line, side_first)
    plane_tails = joined_over_y(line_tails, after(side_tails, sent))
    plane_temporal = joined_over_y(line_temporal, side_temporal)
    side_second = sent_over_y(line_second)

    chips = GRID[0] * GRID[1]
    temporal = gathered_on_chip(plane_temporal).reshape(chips, GRID[2], 2, PIECE, channels)
    temporal_first = compact(temporal[:, :, 0], first)
    temporal_second = compact(temporal[:, :, 1], me == 1)
    tails = gathered_on_chip(plane_tails)
    spatial_first = [gathered_on_chip(plane_first), tails]

    def shape(extent, dtype=BF16):
        return jax.ShapeDtypeStruct(extent, dtype)

    spatial_flops = 2 * rows * 9 * channels * width
    temporal_flops = 2 * rows * 3 * channels * width
    spatial_bytes = 2 * 9 * channels * width
    temporal_bytes = 2 * 3 * channels * width
    normed_first, preact_first, mixed = vmem_call(
        functools.partial(first_forward, frames),
        (shape((rows, channels)), shape((rows, width), F32), shape((rows, channels))),
        flops=spatial_flops + temporal_flops,
        moved=spatial_bytes + temporal_bytes,
    )(hidden, embedding, keep_first, temporal_first, *spatial_first)
    mixed_given = swapped(mixed)
    plane_second = joined_over_y(line_second, after(side_second, mixed))
    spatial_second = [gathered_on_chip(plane_second, GRID[0], mixed_given), tails]
    act_grad_second = vmem_call(
        functools.partial(second_act_grad, frames),
        shape((rows, width), F32),
        flops=temporal_flops,
        moved=temporal_bytes,
    )(upstream, temporal_second)
    hidden_second, normed_second, activated_second, pre_grad_second, back = vmem_call(
        second_forward,
        (
            shape((rows, channels)),
            shape((rows, channels)),
            shape((rows, width)),
            shape((rows, width)),
            shape((rows, channels)),
        ),
        flops=2 * spatial_flops,
        moved=spatial_bytes,
    )(hidden, mixed, mixed_given, embedding, keep_second, act_grad_second, *spatial_second)

    def terms_shape():
        return (
            shape((9 * channels, main)),
            shape((9 * channels, width - main)),
            shape((3 * (width - PIECE), channels)),
        )

    def on_chip(terms, pieces=1):
        return summed_on_chip(terms.reshape(*GRID, -1, terms.shape[1]), pieces)

    back_given = swapped(back)
    main_terms_second, tail_terms_second, temporal_terms_second = vmem_call(
        functools.partial(second_terms, frames),
        terms_shape(),
        flops=spatial_flops + temporal_flops,
        moved=spatial_bytes + temporal_bytes,
    )(normed_second, pre_grad_second, activated_second, upstream)
    chip_second = on_chip(main_terms_second, GRID[0])
    back_given = after(back_given, chip_second)
    line, side = summed_over_y(chip_second, None)
    share_second, sent_second = summed_over_z(line)
    main_terms_first, tail_terms_first, temporal_terms_first = vmem_call(
        functools.partial(first_terms, frames),
        terms_shape(),
        flops=spatial_flops + 2 * temporal_flops,
        moved=spatial_bytes + 2 * temporal_bytes,
    )(
        hidden_second, embedding, upstream, back, back_given, normed_first, preact_first,
        keep_first, temporal_first,
    )
    chip_tails = on_chip(tail_terms_first + tail_terms_second)
    chip_first = on_chip(after(main_terms_first, side))
    terms = jnp.concatenate(
        [
            spread(temporal_terms_first, chips, first),
            spread(temporal_terms_second, chips, me == 1),
        ],
        2,
    )
    chip_temporal = summed_on_chip(terms.reshape(*GRID, -1, channels))

    line, side = summed_over_y(chip_tails, side)
    line_low, side = summed_over_y(chip_first[..., :LANES], side)
    share_tails, sent_tails = summed_over_z(line, (side, sent_second))
    line_high, side = summed_over_y(chip_first[..., LANES:], side)
    share_first, sent_first = summed_over_z(
        jnp.concatenate([line_low, line_high], 2), sent_tails
    )
    line, side = summed_over_y(chip_temporal, side)
    share_temporal, _ = summed_over_z(line)

    kept = jnp.where(first, share_first, share_second)
    passed = jnp.where(first, share_second, share_first)
    given = jnp.concatenate([passed, share_tails], 1).astype(BF16)
    given = swapped(after(given, side)).astype(F32)
    share_spatial = jnp.concatenate(
        [kept, given[:, :main], jnp.where(tail, share_tails, given[:, main:])], 1
    )
    share_spatial = lax.dot_general(
        share_spatial, order.astype(F32), (((1,), (1,)), ((), ())), precision=lax.Precision.HIGH
    )
    low, high = share_temporal[:PIECE], share_temporal[PIECE:]
    given = swapped(jnp.where(first, high, low).astype(BF16))
    given = after(given, share_spatial).astype(F32)
    share_temporal = shard_of(jnp.where(first, low, high), given, temporal_weight.shape[1])
    return (share_spatial[None], share_temporal[None])


def solution(mesh):
    paired = mesh.shape["pipe"] == 2 and mesh.shape["dp"] == math.prod(GRID)
    return jax.shard_map(
        paired_device if paired else per_device,
        mesh=mesh,
        in_specs=(
            P("dp", None, None, None),
            P("dp"),
            P("dp", None, None, None),
            P("pipe", "dp", None),
            P("pipe", "dp", None),
        ),
        out_specs=(P("pipe", "dp", None), P("pipe", "dp", None)),
        check_vma=False,
    )
```

```python
import functools
import math

import jax
import jax.numpy as jnp
from jax import lax
from jax.experimental import pallas as pl
from jax.experimental.pallas import tpu as pltpu
from jax.sharding import PartitionSpec as P

HEIGHT = 8
WIDTH = 4
F32 = jnp.float32
BF16 = jnp.bfloat16
GRID = (4, 2, 2)
LANES = 128


def passed_along(value, axis, steps):
    count = lax.axis_size(axis)
    first, last = (max(0, -steps), min(count, count - steps))
    return lax.ppermute(value, axis, [(source, source + steps) for source in range(first, last)])


def embedding_of(step, channels):
    half_width = channels // 2
    frequency = jnp.exp(-math.log(10000.0) * jnp.arange(half_width, dtype=jnp.float32) / half_width)
    phases = step.astype(jnp.float32) * frequency
    return jnp.concatenate([jnp.sin(phases), jnp.cos(phases)])


def normalize(summed):
    return summed * lax.rsqrt(jnp.mean(summed * summed, axis=-1, keepdims=True) + 1e-06)


def spatial_columns(normed):
    frames, pixels, channels = normed.shape
    grid = normed.reshape(frames, HEIGHT, WIDTH, channels)
    padded = jnp.pad(grid, ((0, 0), (1, 1), (1, 1), (0, 0)))
    pieces = [
        padded[:, row : row + HEIGHT, col : col + WIDTH, :] for row in range(3) for col in range(3)
    ]
    return jnp.concatenate(pieces, axis=-1).reshape(frames * pixels, 9 * channels)


def spatial_fold(grads, frames, channels):
    parts = grads.reshape(frames, HEIGHT, WIDTH, 9, channels)
    padded = jnp.zeros((frames, HEIGHT + 2, WIDTH + 2, channels), jnp.float32)
    for row in range(3):
        for col in range(3):
            padded = padded.at[:, row : row + HEIGHT, col : col + WIDTH, :].add(
                parts[:, :, :, row * 3 + col, :]
            )
    return padded[:, 1 : HEIGHT + 1, 1 : WIDTH + 1, :].reshape(frames, HEIGHT * WIDTH, channels)


def temporal_columns(activated):
    frames, pixels, channels = activated.shape
    padded = jnp.pad(activated, ((1, 1), (0, 0), (0, 0)))
    pieces = [padded[tap : tap + frames] for tap in range(3)]
    return jnp.concatenate(pieces, axis=-1).reshape(frames * pixels, 3 * channels)


def temporal_fold(grads, frames, pixels, channels):
    parts = grads.reshape(frames, pixels, 3, channels)
    padded = jnp.zeros((frames + 2, pixels, channels), jnp.float32)
    for tap in range(3):
        padded = padded.at[tap : tap + frames].add(parts[:, :, tap, :])
    return padded[1 : frames + 1]


def section_forward(block_in, embedding, spatial, temporal):
    frames, pixels, channels = block_in.shape
    summed = block_in.astype(jnp.float32) + embedding
    normed = normalize(summed).astype(jnp.bfloat16)
    preact = jnp.dot(spatial_columns(normed), spatial, preferred_element_type=jnp.float32)
    activated = jax.nn.silu(preact).astype(jnp.bfloat16).reshape(frames, pixels, channels)
    mixed = jnp.dot(temporal_columns(activated), temporal, preferred_element_type=jnp.float32)
    return (block_in.astype(jnp.float32) + mixed.reshape(frames, pixels, channels)).astype(
        jnp.bfloat16
    )


def backward_first(block_in, embedding, spatial, temporal, upstream):
    frames, pixels, channels = block_in.shape
    summed = block_in.astype(jnp.float32) + embedding
    normed = normalize(summed).astype(jnp.bfloat16)
    columns = spatial_columns(normed)
    preact = jnp.dot(columns, spatial, preferred_element_type=jnp.float32)
    activated = jax.nn.silu(preact).astype(jnp.bfloat16).reshape(frames, pixels, channels)
    tcolumns = temporal_columns(activated)
    upstream_flat = upstream.reshape(frames * pixels, channels)
    temporal_term = jnp.dot(tcolumns.T, upstream_flat, preferred_element_type=jnp.float32)
    act_grad = temporal_fold(
        jnp.dot(upstream_flat, temporal.T, preferred_element_type=jnp.float32),
        frames,
        pixels,
        channels,
    )
    logistic = jax.nn.sigmoid(preact)
    slope = logistic * (1.0 + preact * (1.0 - logistic))
    pre_grad = (act_grad.reshape(frames * pixels, channels) * slope).astype(jnp.bfloat16)
    return (temporal_term, pre_grad, columns)


def backward_second(block_in, embedding, spatial, upstream, pre_grad, columns):
    frames, pixels, channels = block_in.shape
    summed = block_in.astype(jnp.float32) + embedding
    spatial_term = jnp.dot(columns.T, pre_grad, preferred_element_type=jnp.float32)
    norm_grad = spatial_fold(
        jnp.dot(pre_grad, spatial.T, preferred_element_type=jnp.float32), frames, channels
    )
    _, pullback = jax.vjp(normalize, summed)
    back_input = (upstream.astype(jnp.float32) + pullback(norm_grad)[0]).astype(jnp.bfloat16)
    return (back_input, spatial_term)


def section_backward(block_in, embedding, spatial, temporal, upstream):
    temporal_term, pre_grad, columns = backward_first(
        block_in, embedding, spatial, temporal, upstream
    )
    back_input, spatial_term = backward_second(
        block_in, embedding, spatial, upstream, pre_grad, columns
    )
    return (back_input, spatial_term, temporal_term)


def per_device(samples, timesteps, cotangent, spatial_weight, temporal_weight):
    sections = lax.axis_size("pipe")
    section_index = lax.axis_index("pipe")
    micro_count = samples.shape[0]
    frames, pixels, channels = (samples.shape[1], samples.shape[2], samples.shape[3])
    moments = jnp.arange(micro_count + sections - 1, dtype=jnp.int32)
    blank = jnp.zeros((frames, pixels, channels), jnp.bfloat16)
    full_spatial, full_temporal = (
        lax.all_gather(spatial_weight[0], "dp", axis=0, tiled=True),
        lax.all_gather(temporal_weight[0], "dp", axis=0, tiled=True),
    )

    def forward_step(carry, moment):
        incoming, stash = carry
        position = moment - section_index
        active = (position >= 0) & (position < micro_count)
        picked = jnp.clip(position, 0, micro_count - 1)
        own = lax.dynamic_index_in_dim(samples, picked, 0, keepdims=False)
        embedding = embedding_of(
            lax.dynamic_index_in_dim(timesteps, picked, 0, keepdims=False), channels
        )
        block_in = jnp.where(section_index == 0, own, incoming)
        result = lax.cond(
            active & (section_index < sections - 1),
            lambda: section_forward(block_in, embedding, full_spatial, full_temporal),
            lambda: blank,
        )
        stash = jnp.where(
            active, lax.dynamic_update_index_in_dim(stash, block_in, picked, 0), stash
        )
        passed = passed_along(result, "pipe", 1)
        return ((passed, stash), None)

    (_, stash), _ = lax.scan(forward_step, (blank, jnp.zeros_like(samples)), moments)
    back_spatial, back_temporal = (full_spatial, full_temporal)

    def inputs_at(moment, incoming):
        position = moment - (sections - 1 - section_index)
        active = (position >= 0) & (position < micro_count)
        picked = jnp.clip(position, 0, micro_count - 1)
        block_in = lax.dynamic_index_in_dim(stash, picked, 0, keepdims=False)
        embedding = embedding_of(
            lax.dynamic_index_in_dim(timesteps, picked, 0, keepdims=False), channels
        )
        given = lax.dynamic_index_in_dim(cotangent, picked, 0, keepdims=False)
        upstream = jnp.where(section_index == sections - 1, given, incoming)
        return (active, block_in, embedding, upstream)

    def backward_step(carry, moment):
        incoming, grad_spatial, grad_temporal = carry
        active, block_in, embedding, upstream = inputs_at(moment, incoming)

        def working():
            back_input, spatial_term, temporal_term = section_backward(
                block_in, embedding, back_spatial, back_temporal, upstream
            )
            return (back_input, grad_spatial + spatial_term, grad_temporal + temporal_term)

        def waiting():
            return (blank, grad_spatial, grad_temporal)

        back_input, grad_spatial, grad_temporal = lax.cond(active, working, waiting)
        passed = passed_along(back_input, "pipe", -1)
        return ((passed, grad_spatial, grad_temporal), None)

    start = (
        blank,
        jnp.zeros(back_spatial.shape, jnp.float32),
        jnp.zeros(back_temporal.shape, jnp.float32),
    )
    (_, grad_spatial, grad_temporal), _ = lax.scan(backward_step, start, moments)
    share_spatial, share_temporal = (
        lax.psum_scatter(
            grad_spatial.astype(jnp.bfloat16).astype(jnp.float32).astype(jnp.bfloat16),
            "dp",
            scatter_dimension=0,
            tiled=True,
        ).astype(jnp.float32),
        lax.psum_scatter(
            grad_temporal.astype(jnp.bfloat16).astype(jnp.float32).astype(jnp.bfloat16),
            "dp",
            scatter_dimension=0,
            tiled=True,
        ).astype(jnp.float32),
    )
    return (share_spatial[None], share_temporal[None])


SPAN = 40
CUTS = (24, 16)
PIECE = 64


def coordinates():
    index = lax.axis_index("dp")
    return index // (GRID[1] * GRID[2]), (index // GRID[2]) % GRID[1], index % GRID[2]


def shifted(value, dz=0, dy=0, dc=0):
    pairs = []
    for z in range(GRID[0]):
        for y in range(GRID[1]):
            for c in range(GRID[2]):
                place = ((z + dz) % GRID[0], (y + dy) % GRID[1], (c + dc) % GRID[2])
                pairs.append(
                    (
                        (z * GRID[1] + y) * GRID[2] + c,
                        (place[0] * GRID[1] + place[1]) * GRID[2] + place[2],
                    )
                )
    return lax.ppermute(value, "dp", pairs)


def swapped(value):
    return lax.ppermute(value, "pipe", [(0, 1), (1, 0)])


def part_of(value, index, axis):
    return lax.dynamic_index_in_dim(value, index, axis, keepdims=False)


def vmem_call(body, outs, scratch=(), flops=0, moved=0):
    return pl.pallas_call(
        body,
        out_shape=outs,
        scratch_shapes=list(scratch),
        compiler_params=pltpu.CompilerParams(vmem_limit_bytes=24 * 2**20),
        cost_estimate=pl.CostEstimate(
            flops=5 * flops // 2, bytes_accessed=moved, transcendentals=0
        ),
    )


def after(value, earlier):
    return value if earlier is None else lax.optimization_barrier((value, earlier))[0]


def in_order(swap, own, other, axis):
    return jnp.where(
        swap, jnp.concatenate([other, own], axis), jnp.concatenate([own, other], axis)
    )


def over_z(value, pairs):
    moves = []
    for source, target in pairs:
        for rest in range(GRID[1] * GRID[2]):
            moves.append(tuple(z * GRID[1] * GRID[2] + rest for z in (source, target)))
    return lax.ppermute(value, "dp", moves)


def sent_over_z(value):
    return [shifted(value, dz=step) for step in range(1, GRID[0])]


def sent_on_chip(value, pieces=1):
    if pieces == 1:
        return shifted(value, dc=1)
    flat = value.reshape(-1, *value.shape[-2:])
    sent = [shifted(piece, dc=1) for piece in jnp.split(flat, pieces)]
    return jnp.concatenate(sent).reshape(value.shape)


def places_of(channels, main):
    channel = jnp.arange(channels)
    span, inside = channel // SPAN, channel % SPAN
    odd = span % 2
    cut = jnp.where(odd == 0, CUTS[0], CUTS[1])
    second = (inside >= cut).astype(jnp.int32)
    before = span // 2 * SPAN + odd * jnp.where(second == 0, CUTS[0], CUTS[1])
    rank = before + inside - second * cut
    tail = channels // 2 - main
    return jnp.where(
        rank < main, second * main + rank, (1 + second) * main + second * (tail - main) + rank
    )


def spans_of(rows, odd):
    sets = ([], [])
    for index, start in enumerate(range(0, rows, SPAN)):
        cut = start + CUTS[(index + odd) % 2]
        sets[0].append((start, cut))
        sets[1].append((cut, start + SPAN))
    return sets


def sets_of(value):
    _, _, c = coordinates()
    results = []
    for which in range(2):
        by_core = []
        for odd in range(2):
            spans = spans_of(value.shape[0], odd)[which]
            taken = jnp.concatenate([value[start:end] for start, end in spans])
            by_core.append(jnp.pad(taken, ((0, PIECE - taken.shape[0]), (0, 0))))
        results.append(jnp.where(c == 0, by_core[0], by_core[1]))
    return results


def shard_of(own, given, rows):
    _, _, c = coordinates()
    by_core = []
    for odd in range(2):
        taken, pieces = [0, 0], []
        for spans in zip(*spans_of(rows, odd)):
            for which, (start, end) in enumerate(spans):
                source = (own, given)[which]
                pieces.append(source[taken[which] : taken[which] + end - start])
                taken[which] += end - start
        by_core.append(jnp.concatenate(pieces))
    return jnp.where(c == 0, by_core[0], by_core[1])


def compact(pieces, own):
    short = 3 * SPAN - PIECE
    low, high = pieces[:, 0], pieces[:, 1]
    both = jnp.where(
        own,
        jnp.concatenate([low, high[:, :short]], 1),
        jnp.concatenate([low[:, :short], high], 1),
    )
    return both.reshape(-1, pieces.shape[3])


def spread(rows, chips, own):
    rows = rows.reshape(chips, -1, rows.shape[1])
    short = rows.shape[1] - PIECE
    pad = ((0, 0), (0, PIECE - short), (0, 0))
    return jnp.where(
        own,
        jnp.stack([rows[:, :PIECE], jnp.pad(rows[:, PIECE:], pad)], 1),
        jnp.stack([jnp.pad(rows[:, :short], pad), rows[:, short:]], 1),
    )


def gathered_over_z(value, earlier=None, beside=None):
    z, _, _ = coordinates()
    value = after(value, earlier)
    sent = after(sent_over_z(value), beside)
    return (
        jnp.stack([lax.select_n((z - place) % GRID[0], value, *sent) for place in range(GRID[0])]),
        sent,
    )


def sent_over_y(line, earlier=None):
    return shifted(after(line, earlier), dy=1)


def joined_over_y(line, sent):
    _, y, _ = coordinates()
    return in_order(y == 1, line[:, None], sent[:, None], 1)


def gathered_on_chip(plane, pieces=1, beside=None):
    _, _, c = coordinates()
    sent = after(sent_on_chip(plane, pieces), beside)
    whole = in_order(c == 1, plane[:, :, None], sent[:, :, None], 2)
    return whole.reshape(-1, plane.shape[3])


def added(*terms):
    return sum(term.astype(F32) for term in terms)


def summed_on_chip(value, pieces=1):
    _, _, c = coordinates()
    sent = sent_on_chip(part_of(value, 1 - c, 2), pieces)
    return added(part_of(value, c, 2), sent).astype(BF16)


def summed_over_y(value, earlier):
    _, y, _ = coordinates()
    sent = shifted(after(part_of(value, 1 - y, 1), earlier), dy=1)
    return added(part_of(value, y, 1), sent).astype(BF16), sent


def sent_for_sums(line, earlier=None):
    z, _, _ = coordinates()
    line = after(line, earlier)
    return [
        shifted(part_of(line, (z + step) % GRID[0], 0), dz=step) for step in range(1, GRID[0])
    ]


def summed_over_z(line, earlier=None):
    z, _, _ = coordinates()
    sent = sent_for_sums(line, earlier)
    return added(part_of(line, z, 0), *sent), sent


def pixel_masks(rows):
    row = lax.broadcasted_iota(jnp.int32, (rows, 1), 0)
    high, wide = (row // WIDTH) % HEIGHT, row % WIDTH
    masks = []
    for dr in (-1, 0, 1):
        for dc in (-1, 0, 1):
            inside = (high + dr >= 0) & (high + dr < HEIGHT) & (wide + dc >= 0) & (wide + dc < WIDTH)
            masks.append((dr * WIDTH + dc, inside))
    return masks


def frame_masks(rows, frames):
    pixels = HEIGHT * WIDTH
    row = lax.broadcasted_iota(jnp.int32, (rows, 1), 0)
    frame = (row // pixels) % frames
    return [
        (step * pixels, (frame + step >= 0) & (frame + step < frames)) for step in (-1, 0, 1)
    ]


def moved_rows(value, move):
    shift, inside = move
    if shift:
        value = pltpu.roll(value, (-shift) % value.shape[0], 0)
    return jnp.where(inside, value, 0.0)


def dot(left, right, dims=((1,), (0,))):
    return lax.dot_general(left, right, (dims, ((), ())), preferred_element_type=F32)


def with_embedding(hidden, embedding_ref, samples):
    per = hidden.shape[0] // samples
    return jnp.concatenate(
        [hidden[s * per : (s + 1) * per] + embedding_ref[s : s + 1, :] for s in range(samples)]
    )


def scale_of(summed):
    return lax.rsqrt(jnp.mean(summed * summed, axis=-1, keepdims=True) + 1e-06)


def silu_parts(preact):
    logistic = 1.0 / (1.0 + jnp.exp(-preact))
    return logistic, preact * logistic


def convolved(normed, weight_refs, masks):
    rows, channels = normed.shape
    normed = normed.astype(F32)
    totals = [None] * len(weight_refs)
    for tap in range(9):
        moved = moved_rows(normed, masks[tap]).astype(BF16)
        for index, ref in enumerate(weight_refs):
            term = dot(moved, ref[tap * channels : (tap + 1) * channels, :])
            totals[index] = term if totals[index] is None else totals[index] + term
    return jnp.concatenate(totals, 1)


def back_through(pre_grad, weight_refs, masks, channels):
    pre_grad = pre_grad.astype(F32)
    total = None
    for tap in range(9):
        weights = [ref[tap * channels : (tap + 1) * channels, :] for ref in weight_refs]
        term = dot(
            moved_rows(pre_grad, masks[8 - tap]).astype(BF16),
            jnp.concatenate(weights, 1),
            ((1,), (1,)),
        )
        total = term if total is None else total + term
    return total


def tap_rows(temporal_ref, tap, width):
    tail = PIECE
    start = tap * (width - tail)
    rows = temporal_ref[start : start + width - tail, :]
    return jnp.concatenate([rows, rows[width - 2 * tail :]], 0)


def first_forward(frames, hidden_ref, embedding_ref, keep_ref, temporal_ref, *refs):
    *spatial_refs, normed_ref, preact_ref, mixed_ref = refs
    rows = hidden_ref.shape[0]
    width = keep_ref.shape[1]
    summed = with_embedding(hidden_ref[...].astype(F32), embedding_ref, embedding_ref.shape[0])
    normed = (summed * scale_of(summed)).astype(BF16)
    normed_ref[...] = normed
    preact = convolved(normed, spatial_refs, pixel_masks(rows))
    preact_ref[...] = preact
    activated = silu_parts(preact)[1].astype(BF16).astype(F32) * keep_ref[...]
    mixed = None
    for tap, move in enumerate(frame_masks(rows, frames)):
        term = dot(
            moved_rows(activated, move).astype(BF16),
            tap_rows(temporal_ref, tap, width),
        )
        mixed = term if mixed is None else mixed + term
    mixed_ref[...] = mixed.astype(BF16)


def slope_of(preact):
    logistic, _ = silu_parts(preact)
    return logistic * (1.0 + preact * (1.0 - logistic))


def act_grad_of(upstream, temporal_ref, width, frames):
    upstream = upstream.astype(F32)
    moves = frame_masks(upstream.shape[0], frames)
    total = None
    for tap in range(3):
        term = dot(
            moved_rows(upstream, moves[2 - tap]).astype(BF16),
            tap_rows(temporal_ref, tap, width),
            ((1,), (1,)),
        )
        total = term if total is None else total + term
    return total


def store_temporal_terms(activated, upstream, frames, out_ref):
    width = activated.shape[1]
    tail = PIECE
    upstream = upstream.astype(F32)
    moves = frame_masks(upstream.shape[0], frames)
    for tap in range(3):
        term = dot(activated, moved_rows(upstream, moves[2 - tap]).astype(BF16), ((0,), (0,)))
        start = tap * (width - tail)
        out_ref[start : start + width - 2 * tail, :] = term[: width - 2 * tail].astype(BF16)
        out_ref[start + width - 2 * tail : start + width - tail, :] = (
            term[width - 2 * tail : width - tail] + term[width - tail :]
        ).astype(BF16)


def store_spatial_terms(normed, pre_grad, out_refs):
    channels = normed.shape[1]
    pre_grad = pre_grad.astype(F32)
    masks = pixel_masks(pre_grad.shape[0])
    for tap in range(9):
        term = dot(
            normed, moved_rows(pre_grad, masks[8 - tap]).astype(BF16), ((0,), (0,))
        ).astype(BF16)
        start = 0
        for out_ref in out_refs:
            end = start + out_ref.shape[1]
            out_ref[tap * channels : (tap + 1) * channels, :] = term[:, start:end]
            start = end


def second_forward(
    frames, hidden_ref, own_ref, sent_ref, embedding_ref, keep_ref, upstream_ref, temporal_ref, *refs
):
    *spatial_refs, next_ref, normed_ref, activated_ref, pre_grad_ref, back_ref = refs
    rows, channels = hidden_ref.shape
    width = keep_ref.shape[1]
    masks = pixel_masks(rows)
    mixed = own_ref[...].astype(F32) + sent_ref[...].astype(F32)
    hidden = (hidden_ref[...].astype(F32) + mixed).astype(BF16)
    next_ref[...] = hidden
    summed = with_embedding(hidden.astype(F32), embedding_ref, embedding_ref.shape[0])
    normed = (summed * scale_of(summed)).astype(BF16)
    normed_ref[...] = normed
    preact = convolved(normed, spatial_refs, masks)
    activated_ref[...] = (silu_parts(preact)[1] * keep_ref[...]).astype(BF16)
    act_grad = act_grad_of(upstream_ref[...], temporal_ref, width, frames)
    pre_grad = (act_grad * slope_of(preact) * keep_ref[...]).astype(BF16)
    pre_grad_ref[...] = pre_grad
    back = back_through(pre_grad, spatial_refs, masks, channels)
    back_ref[...] = back.astype(BF16)


def second_terms(frames, normed_ref, pre_grad_ref, activated_ref, upstream_ref, *outs):
    *spatial_refs, temporal_ref = outs
    store_spatial_terms(normed_ref[...], pre_grad_ref[...], spatial_refs)
    store_temporal_terms(activated_ref[...], upstream_ref[...], frames, temporal_ref)


def first_terms(
    frames, hidden_ref, embedding_ref, upstream_ref, own_ref, sent_ref, normed_ref, preact_ref,
    keep_ref, temporal_ref, *outs
):
    *spatial_outs, temporal_out = outs
    width = keep_ref.shape[1]
    channels = hidden_ref.shape[1]
    summed = with_embedding(hidden_ref[...].astype(F32), embedding_ref, embedding_ref.shape[0])
    scale = scale_of(summed)
    grad = own_ref[...].astype(F32) + sent_ref[...].astype(F32)
    inner = jnp.sum(grad * summed, axis=-1, keepdims=True)
    back = grad * scale - summed * (scale * scale * scale) * (inner / channels)
    upstream = (upstream_ref[...].astype(F32) + back).astype(BF16)
    preact = preact_ref[...]
    activated = (silu_parts(preact)[1] * keep_ref[...]).astype(BF16)
    act_grad = act_grad_of(upstream, temporal_ref, width, frames)
    pre_grad = (act_grad * slope_of(preact) * keep_ref[...]).astype(BF16)
    store_spatial_terms(normed_ref[...], pre_grad, spatial_outs)
    store_temporal_terms(activated, upstream, frames, temporal_out)


def paired_device(samples, timesteps, cotangent, spatial_weight, temporal_weight):
    me = lax.axis_index("pipe")
    first = me == 0
    count, frames, pixels, channels = samples.shape
    rows = count * frames * pixels
    main = 2 * LANES
    width = main + LANES
    hidden = samples.reshape(rows, channels)
    upstream = cotangent.reshape(rows, channels)
    embedding = jax.vmap(lambda step: embedding_of(step, channels))(timesteps)
    lane = jnp.arange(LANES)
    keep_own = jnp.concatenate([jnp.ones(main), lane < LANES // 2]).astype(F32)[None]
    keep_other = jnp.concatenate([jnp.ones(main), lane >= LANES // 2]).astype(F32)[None]
    keep_first = jnp.where(first, keep_own, keep_other)
    keep_second = jnp.where(first, keep_other, keep_own)
    tail = lane[None] < LANES // 2

    places = places_of(channels, main)
    order = (places[:, None] == jnp.arange(channels)).astype(BF16)
    temporal_own, temporal_sent = sets_of(temporal_weight[0])
    temporal_given = swapped(temporal_sent)
    line_temporal, sent = gathered_over_z(in_order(me == 1, temporal_own, temporal_given, 0))
    side_temporal = sent_over_y(line_temporal)
    spatial_own = dot(spatial_weight[0], order).astype(BF16)
    given = swapped(spatial_own[:, main:])
    main_own, main_given = spatial_own[:, :main], given[:, :main]
    tails = jnp.where(tail, spatial_own[:, 2 * main :], given[:, main:])
    line, sent = gathered_over_z(jnp.where(first, main_own, main_given), sent, side_temporal)
    side_low = sent_over_y(line[..., :LANES])
    line_tails, sent = gathered_over_z(tails, (sent, side_low))
    side_high = sent_over_y(line[..., LANES:], side_low)
    side_tails = sent_over_y(line_tails)
    line_second, sent = gathered_over_z(
        jnp.where(first, main_given, main_own), (sent, side_low)
    )
    side_first = jnp.concatenate([side_low, after(side_high, sent)], 2)
    plane_first = joined_over_y(line, side_first)
    plane_tails = joined_over_y(line_tails, after(side_tails, sent))
    plane_temporal = joined_over_y(line_temporal, side_temporal)
    side_second = sent_over_y(line_second)

    chips = GRID[0] * GRID[1]
    temporal = gathered_on_chip(plane_temporal).reshape(chips, GRID[2], 2, PIECE, channels)
    temporal_first = compact(temporal[:, :, 0], first)
    temporal_second = compact(temporal[:, :, 1], me == 1)
    tails = gathered_on_chip(plane_tails)
    spatial_first = [gathered_on_chip(plane_first), tails]

    def shape(extent, dtype=BF16):
        return jax.ShapeDtypeStruct(extent, dtype)

    spatial_flops = 2 * rows * 9 * channels * width
    temporal_flops = 2 * rows * 3 * channels * width
    spatial_bytes = 2 * 9 * channels * width
    temporal_bytes = 2 * 3 * channels * width
    normed_first, preact_first, mixed = vmem_call(
        functools.partial(first_forward, frames),
        (shape((rows, channels)), shape((rows, width), F32), shape((rows, channels))),
        flops=spatial_flops + temporal_flops,
        moved=spatial_bytes + temporal_bytes,
    )(hidden, embedding, keep_first, temporal_first, *spatial_first)
    mixed_given = swapped(mixed)
    plane_second = joined_over_y(line_second, after(side_second, mixed))
    spatial_second = [gathered_on_chip(plane_second, GRID[0], mixed_given), tails]
    hidden_second, normed_second, activated_second, pre_grad_second, back = vmem_call(
        functools.partial(second_forward, frames),
        (
            shape((rows, channels)),
            shape((rows, channels)),
            shape((rows, width)),
            shape((rows, width)),
            shape((rows, channels)),
        ),
        flops=2 * spatial_flops + temporal_flops,
        moved=spatial_bytes + temporal_bytes,
    )(
        hidden, mixed, mixed_given, embedding, keep_second, upstream, temporal_second,
        *spatial_second,
    )

    def terms_shape():
        return (
            shape((9 * channels, main)),
            shape((9 * channels, width - main)),
            shape((3 * (width - PIECE), channels)),
        )

    def on_chip(terms, pieces=1):
        return summed_on_chip(terms.reshape(*GRID, -1, terms.shape[1]), pieces)

    back_given = swapped(back)
    main_terms_second, tail_terms_second, temporal_terms_second = vmem_call(
        functools.partial(second_terms, frames),
        terms_shape(),
        flops=spatial_flops + temporal_flops,
        moved=spatial_bytes + temporal_bytes,
    )(normed_second, pre_grad_second, activated_second, upstream)
    chip_second = on_chip(main_terms_second, GRID[0])
    back_given = after(back_given, chip_second)
    line, side = summed_over_y(chip_second, None)
    share_second, sent_second = summed_over_z(line)
    main_terms_first, tail_terms_first, temporal_terms_first = vmem_call(
        functools.partial(first_terms, frames),
        terms_shape(),
        flops=spatial_flops + 2 * temporal_flops,
        moved=spatial_bytes + 2 * temporal_bytes,
    )(
        hidden_second, embedding, upstream, back, back_given, normed_first, preact_first,
        keep_first, temporal_first,
    )
    chip_tails = on_chip(tail_terms_first + tail_terms_second)
    chip_first = on_chip(after(main_terms_first, side))
    terms = jnp.concatenate(
        [
            spread(temporal_terms_first, chips, first),
            spread(temporal_terms_second, chips, me == 1),
        ],
        2,
    )
    chip_temporal = summed_on_chip(terms.reshape(*GRID, -1, channels))

    line, side = summed_over_y(chip_tails, side)
    line_low, side = summed_over_y(chip_first[..., :LANES], side)
    share_tails, sent_tails = summed_over_z(line, (side, sent_second))
    line_high, side = summed_over_y(chip_first[..., LANES:], side)
    share_first, sent_first = summed_over_z(
        jnp.concatenate([line_low, line_high], 2), sent_tails
    )
    line, side = summed_over_y(chip_temporal, side)
    share_temporal, _ = summed_over_z(line)

    kept = jnp.where(first, share_first, share_second)
    passed = jnp.where(first, share_second, share_first)
    given = jnp.concatenate([passed, share_tails], 1).astype(BF16)
    given = swapped(after(given, side)).astype(F32)
    share_spatial = jnp.concatenate(
        [kept, given[:, :main], jnp.where(tail, share_tails, given[:, main:])], 1
    )
    share_spatial = lax.dot_general(
        share_spatial, order.astype(F32), (((1,), (1,)), ((), ())), precision=lax.Precision.HIGH
    )
    low, high = share_temporal[:PIECE], share_temporal[PIECE:]
    given = swapped(jnp.where(first, high, low).astype(BF16))
    given = after(given, share_spatial).astype(F32)
    share_temporal = shard_of(jnp.where(first, low, high), given, temporal_weight.shape[1])
    return (share_spatial[None], share_temporal[None])


def solution(mesh):
    paired = mesh.shape["pipe"] == 2 and mesh.shape["dp"] == math.prod(GRID)
    return jax.shard_map(
        paired_device if paired else per_device,
        mesh=mesh,
        in_specs=(
            P("dp", None, None, None),
            P("dp"),
            P("dp", None, None, None),
            P("pipe", "dp", None),
            P("pipe", "dp", None),
        ),
        out_specs=(P("pipe", "dp", None), P("pipe", "dp", None)),
        check_vma=False,
    )
```
